32 devices in a mesh: expert: 8 (over y, x, core), wshard: 4 (over z).
Axes of the slice: x: 2, y: 2, z: 4, core: 2. Of those that a mesh axis runs over, the one named last changes fastest.
Arguments:
- tokens: bfloat16 [8192, 768], P(('expert', 'wshard')), may hold values from -6 to 6
- norm_gain_attn: bfloat16 [768], P('wshard'), may hold values from 0.099609375 to 1.8984375
- w_query: bfloat16 [768, 768], P('wshard'), may hold values from -0.21875 to 0.21875
- w_key: bfloat16 [768, 768], P('wshard'), may hold values from -0.21875 to 0.21875
- w_value: bfloat16 [768, 768], P('wshard'), may hold values from -0.21875 to 0.21875
- w_output: bfloat16 [768, 768], P('wshard'), may hold values from -1.75 to 1.75
- rel_bias: bfloat16 [32, 12], P('wshard'), may hold values from -4 to 4
- norm_gain_ffn: bfloat16 [768], P('wshard'), may hold values from 0.099609375 to 1.8984375
- w_router: bfloat16 [768, 8], P('wshard'), may hold values from -0.109375 to 0.109375
- w_in: bfloat16 [8, 768, 3072], P('expert', None, 'wshard'), may hold values from -0.21875 to 0.21875
- w_out: bfloat16 [8, 3072, 768], P('expert', 'wshard'), may hold values from -1.25 to 1.25
- out_grad: bfloat16 [8192, 768], P(('expert', 'wshard')), may hold values from -6 to 6
- expert_ids: int32 [8192, 1], P(('expert', 'wshard')), may hold values from 0 to 7
- priority: int32 [8192], P(('expert', 'wshard')), may hold values from 0 to 255, as said below
- lengths: int32 [64], replicated, may hold values from 0 to 256, as said below
- seq_order: int32 [64], replicated, may hold values from 0 to 63, as said below
- relpos_table: int32 [511], replicated, may hold values from 0 to 31, as said below
Outputs:
- layer_out: bfloat16 [8192, 768], P(('expert', 'wshard'))
- tokens_grad: float32 [8192, 768], P(('expert', 'wshard'))
- grad_gain_attn: float32 [768], P('wshard')
- grad_query: float32 [768, 768], P('wshard')
- grad_key: float32 [768, 768], P('wshard')
- grad_value: float32 [768, 768], P('wshard')
- grad_output: float32 [768, 768], P('wshard')
- grad_rel_bias: float32 [32, 12], P('wshard')
- grad_gain_ffn: float32 [768], P('wshard')
- grad_router: float32 [768, 8], P('wshard')
- grad_w_in: float32 [8, 768, 3072], P('expert', None, 'wshard')
- grad_w_out: float32 [8, 3072, 768], P('expert', 'wshard')
The draws below stay inside these ranges and needn't reach their ends.
Inputs may be any that keep to these rules, and one draw needn't show every extreme that they name: `priority`: within each block of 256 rows, the priorities are a permutation of 0 to 255. The two lengths dealt to one device (256 / 8) sum to at most 256; some device holds one sequence of 256 tokens and an empty second one. A permutation of all sequence numbers; device d holds sequences seq_order[2 d] and seq_order[2 d + 1], packed in that order from its first row. `relpos_table`: offsets at or below zero have buckets under 32 / 2, offsets above zero have buckets of 16 or more; buckets never fall as the distance grows.
All inputs are finite; a program needn't handle non-finite values.
Results may differ from the reference program's by a relative error of at most 0.014.
Values may be sent and summed in bfloat16 or wider, within the bound.
A program may use at most 128 MiB of HBM per device.

```python
import jax
import jax.numpy as jnp
from jax import lax

D = 768
HEADS = 12
HDIM = 64
FF = 3072
NB = 32
EXPERTS = 8
TOK_DEV = 256
CAP = 32
TOKENS = 8192


def layout_draw(key):
    key = jax.random.fold_in(key, 17)
    dev_count = TOKENS // TOK_DEV
    lowest = TOK_DEV // 8
    key_first, key_second, key_full, key_order = jax.random.split(key, 4)
    first = jax.random.randint(key_first, (dev_count,), lowest, TOK_DEV - lowest + 1, dtype=jnp.int32)
    spread = jax.random.randint(key_second, (dev_count,), 0, 1 << 20, dtype=jnp.int32)
    second = lowest + spread % (TOK_DEV - first - lowest + 1)
    chosen = jax.random.randint(key_full, (), 0, dev_count, dtype=jnp.int32)
    places = jnp.arange(dev_count, dtype=jnp.int32)
    first = jnp.where(places == chosen, TOK_DEV, first)
    second = jnp.where(places == chosen, 0, second)
    order = jax.random.permutation(key_order, 2 * dev_count).astype(jnp.int32)
    slots = jnp.stack([first, second], axis=1).reshape(-1).astype(jnp.int32)
    lengths = jnp.zeros((2 * dev_count,), jnp.int32).at[order].set(slots)
    return (lengths, order)


def draw_lengths(key, part):
    return layout_draw(key)[0]


def draw_seq_order(key, part):
    return layout_draw(key)[1]


def draw_priority(key, part):
    key = jax.random.fold_in(key, 5)
    dev_count = TOKENS // TOK_DEV
    subkeys = jax.random.split(key, dev_count)
    orders = jax.vmap(lambda subkey: jax.random.permutation(subkey, TOK_DEV))(subkeys)
    return orders.reshape(-1).astype(jnp.int32)


def draw_relpos_table(key, part):
    key = jax.random.fold_in(key, 23)
    half = NB // 2
    steps_index = jnp.arange(half, dtype=jnp.int32)
    growth = jnp.power(2, jnp.maximum(steps_index - half // 2 + 1, 0)).astype(jnp.int32) + 1
    noise = jax.random.randint(key, (half,), 0, 1 << 20, dtype=jnp.int32)
    widths = 1 + noise % growth
    cuts = jnp.cumsum(widths, dtype=jnp.int32)
    offsets = jnp.arange(2 * TOK_DEV - 1, dtype=jnp.int32) - (TOK_DEV - 1)
    distance = jnp.abs(offsets)
    count = jnp.sum((cuts[None, :] <= distance[:, None]).astype(jnp.int32), axis=1, dtype=jnp.int32)
    bucket = jnp.minimum(count, half - 1)
    bucket = jnp.where(distance == TOK_DEV - 1, half - 1, bucket)
    return (bucket + half * (offsets > 0).astype(jnp.int32)).astype(jnp.int32)


def levels(rng, extent, cuts, smallest, top_value):
    loudness = 1.0
    for axis_at, parts in cuts:
        draws = jax.random.uniform(jax.random.fold_in(jax.random.fold_in(rng, 6), axis_at), (parts,), jnp.float32, smallest / len(cuts), top_value / len(cuts))
        loudness = loudness * jnp.repeat(jnp.exp(draws), extent[axis_at] // parts).reshape((-1,) + (1,) * (len(extent) - 1 - axis_at))
    return loudness


def distinct(key, rows, amount, top, lift):
    ranking = jax.random.permutation(jax.random.fold_in(key, 1), amount)
    boost = ranking
    for power in range(3):
        boost = boost * boost // amount
    boost = boost * lift // amount
    tickets = jax.random.randint(jax.random.fold_in(key, 2), (rows, amount), 0, 4096) + boost
    fixed_rows = jax.random.permutation(jax.random.fold_in(key, 3), rows)[jnp.arange(amount) % rows]
    tickets = jnp.where(jnp.arange(rows)[:, None] == fixed_rows[None, :], 1 << 14, tickets)
    score = tickets * amount + jnp.arange(amount)
    return lax.top_k(score.astype(jnp.int32), top)[1].astype(jnp.int32)


def centred(rng, dims, width, limit, cuts=(), kind=jnp.bfloat16):
    values = width * jax.random.normal(rng, dims, jnp.float32)
    if cuts:
        values = values * levels(rng, dims, cuts, -0.22, 0.18)
    return jnp.clip(values, -limit, limit).astype(kind)


def setup_inputs(seed: int = 0) -> dict:
    key_list = jax.random.split(jax.random.key(seed), 18)
    tokens = centred(key_list[0], (TOKENS, D), 1.0, 6.0, ((0, 32),))
    norm_gain_attn = jnp.clip(1.0 + 0.18 * jax.random.normal(key_list[1], (D,), jnp.float32), 0.099609375, 1.8984375).astype(jnp.bfloat16)
    w_query = centred(key_list[2], (D, D), D ** -0.5, 0.21875, ((0, 4),))
    w_key = centred(key_list[3], (D, D), D ** -0.5, 0.21875, ((0, 4),))
    w_value = centred(key_list[4], (D, D), D ** -0.5, 0.21875, ((0, 4),))
    w_output = centred(key_list[5], (D, D), (D // 64) ** -0.5, 1.75, ((0, 4),))
    rel_bias = centred(key_list[6], (NB, HEADS), 1.0, 4.0, ((0, 4),))
    norm_gain_ffn = jnp.clip(1.0 + 0.18 * jax.random.normal(key_list[7], (D,), jnp.float32), 0.099609375, 1.8984375).astype(jnp.bfloat16)
    w_router = centred(key_list[8], (D, EXPERTS), (4 * D) ** -0.5, 0.109375, ((0, 4),))
    w_in = centred(key_list[9], (EXPERTS, D, FF), D ** -0.5, 0.21875, ((0, 8), (2, 4)))
    w_out = centred(key_list[10], (EXPERTS, FF, D), (max(1, FF // (2 * EXPERTS * EXPERTS))) ** -0.5, 1.25, ((0, 8), (1, 4)))
    out_grad = centred(key_list[11], (TOKENS, D), 1.0, 6.0, ((0, 32),))
    expert_ids = distinct(key_list[12], TOKENS, EXPERTS, 1, 1024)
    priority = draw_priority(jax.random.fold_in(key_list[17], 71), 0)
    lengths = draw_lengths(jax.random.fold_in(key_list[17], 71), 0)
    seq_order = draw_seq_order(jax.random.fold_in(key_list[17], 71), 0)
    relpos_table = draw_relpos_table(jax.random.fold_in(key_list[17], 71), 0)
    return {"tokens": tokens, "norm_gain_attn": norm_gain_attn, "w_query": w_query, "w_key": w_key, "w_value": w_value, "w_output": w_output, "rel_bias": rel_bias, "norm_gain_ffn": norm_gain_ffn, "w_router": w_router, "w_in": w_in, "w_out": w_out, "out_grad": out_grad, "expert_ids": expert_ids, "priority": priority, "lengths": lengths, "seq_order": seq_order, "relpos_table": relpos_table}


EPSILON = 1e-06
NEG_FILL = -1e+30
HIGHEST_PRECISION = lax.Precision.HIGHEST

@jax.custom_vjp
def low(v):
    return lax.optimization_barrier(v.astype(jnp.bfloat16)).astype(jnp.float32)

@jax.custom_vjp
def low_back(v):
    return v

def low_keep(v):
    return (low(v), None)

def low_pass(kept, grad):
    return (grad,)

def back_keep(v):
    return (v, None)

def back_low(kept, grad):
    return (low(grad),)
low.defvjp(low_keep, low_pass)
low_back.defvjp(back_keep, back_low)

def rms_scale(field):
    return lax.rsqrt(lax.optimization_barrier(jnp.mean(field * field, axis=-1, keepdims=True)) + EPSILON)

def device_layout(lengths, seq_order, device, tok_count):
    first = lengths[seq_order[2 * device]]
    second = lengths[seq_order[2 * device + 1]]
    places = jnp.arange(tok_count, dtype=jnp.int32)
    segment = (places >= first).astype(jnp.int32) + (places >= first + second).astype(jnp.int32)
    valid = (places < first + second).astype(jnp.float32)
    return (segment, valid)

def slot_layout(expert_rows, priority, valid, n_experts, capacity):
    chosen = (expert_rows[:, None] == jnp.arange(n_experts, dtype=jnp.int32)[None, :]).astype(jnp.int32)
    chosen = chosen * (valid[:, None] > 0).astype(jnp.int32)
    ranked = jnp.zeros_like(chosen).at[priority].set(chosen)
    before = jnp.cumsum(ranked, axis=0, dtype=jnp.int32) - ranked
    slot = lax.optimization_barrier(jnp.sum(before[priority] * chosen, axis=1, dtype=jnp.int32))
    keep = (lax.optimization_barrier(jnp.sum(chosen, axis=1, dtype=jnp.int32)) > 0) & (slot < capacity)
    flat = jnp.where(keep, expert_rows * capacity + slot, n_experts * capacity).astype(jnp.int32)
    return (flat, keep.astype(jnp.float32))

def bias_table(rel_bias, relpos_table, tok_count):
    places = jnp.arange(tok_count, dtype=jnp.int32)
    offsets = places[None, :] - places[:, None] + tok_count - 1
    return jnp.transpose(rel_bias[relpos_table[offsets]], (2, 0, 1))

def layer_block(hidden_in, params, segment, valid, expert_rows, priority, relpos_table):
    gain_attn, w_query, w_key, w_value, w_output, rel_bias, gain_ffn, w_router, w_in, w_out = params
    tok_count = hidden_in.shape[0]
    scale = HDIM ** (-0.5)
    normed = low(hidden_in * rms_scale(hidden_in) * gain_attn)

    def project(weight):
        return low_back(low(jnp.dot(normed, weight, precision=HIGHEST_PRECISION))).reshape(tok_count, HEADS, HDIM)
    query = project(w_query)
    keys = project(w_key)
    values = project(w_value)
    scores = jnp.einsum('qhd,khd->hqk', query, keys, precision=HIGHEST_PRECISION) * scale
    scores = low_back(scores + bias_table(rel_bias, relpos_table, tok_count))
    same = segment[:, None] == segment[None, :]
    scores = jnp.where(same[None], scores, NEG_FILL)
    probs = jax.nn.softmax(scores, axis=-1)
    mixed = jnp.einsum('hqk,khd->qhd', low(probs), values, precision=HIGHEST_PRECISION).reshape(tok_count, D)
    mixed = low_back(low(mixed))
    attended = low_back(jnp.dot(mixed, w_output, precision=HIGHEST_PRECISION)) * valid[:, None]
    middle = hidden_in + attended
    normed_ffn = low(middle * rms_scale(middle) * gain_ffn)
    logits = low_back(jnp.dot(normed_ffn, w_router, precision=HIGHEST_PRECISION))
    router = jax.nn.softmax(logits, axis=-1)
    picked = (expert_rows[:, None] == jnp.arange(EXPERTS, dtype=jnp.int32)[None, :]).astype(jnp.float32)
    gate = lax.optimization_barrier(jnp.sum(router * picked, axis=1))
    flat, keep = slot_layout(expert_rows, priority, valid, EXPERTS, CAP)
    sent = low_back(normed_ffn)
    buffer = jnp.zeros((EXPERTS * CAP + 1, D), jnp.float32).at[flat].set(sent)
    buffer = buffer[:EXPERTS * CAP].reshape(EXPERTS, CAP, D)
    inner = low_back(jnp.einsum('ecd,edf->ecf', buffer, w_in, precision=HIGHEST_PRECISION))
    active = low(jax.nn.gelu(inner, approximate=True))
    result = low_back(low(jnp.einsum('ecf,efd->ecd', active, w_out, precision=HIGHEST_PRECISION)))
    back = result.reshape(EXPERTS * CAP, D)[jnp.minimum(flat, EXPERTS * CAP - 1)] * keep[:, None]
    return middle + (keep * gate)[:, None] * back

def reference(tokens, norm_gain_attn, w_query, w_key, w_value, w_output, rel_bias, norm_gain_ffn, w_router, w_in, w_out, out_grad, expert_ids, priority, lengths, seq_order, relpos_table):
    dev_count = TOKENS // TOK_DEV
    weights = tuple((item.astype(jnp.float32) for item in (norm_gain_attn, w_query, w_key, w_value, w_output, rel_bias, norm_gain_ffn, w_router, w_in, w_out)))
    hidden = tokens.astype(jnp.float32)
    id_blocks = expert_ids[:, 0].reshape(dev_count, TOK_DEV)
    order_blocks = priority.reshape(dev_count, TOK_DEV)
    devices = jnp.arange(dev_count, dtype=jnp.int32)

    def whole(hidden_all, *params):

        def step(item):
            device, block, id_block, order_block = item
            segment, valid = device_layout(lengths, seq_order, device, TOK_DEV)
            return layer_block(block, params, segment, valid, id_block, order_block, relpos_table)
        outputs = lax.map(jax.checkpoint(step), (devices, hidden_all.reshape(dev_count, TOK_DEV, D), id_blocks, order_blocks))
        return outputs.reshape(TOKENS, D)
    output, pull = jax.vjp(whole, hidden, *weights)
    grads = pull(out_grad.astype(jnp.float32))
    return (output.astype(jnp.bfloat16), grads[0], grads[1], grads[2], grads[3], grads[4], grads[5], grads[6], grads[7], grads[8], grads[9], grads[10])
```

```python
import jax
import jax.numpy as jnp
from jax import lax
from jax.sharding import PartitionSpec as P

EPSILON = 1e-06
NEG_FILL = -1e30
ROW_BLOCK = 512


def rms_scale(field):
    return lax.rsqrt(jnp.mean(field * field, axis=-1, keepdims=True) + EPSILON)


def device_layout(lengths, seq_order, device, tok_count):
    first = lengths[seq_order[2 * device]]
    second = lengths[seq_order[2 * device + 1]]
    places = jnp.arange(tok_count, dtype=jnp.int32)
    segment = (places >= first).astype(jnp.int32) + (places >= first + second).astype(jnp.int32)
    valid = (places < first + second).astype(jnp.float32)
    return (segment, valid)


def slot_layout(expert_rows, priority, valid, n_experts, capacity):
    chosen = (expert_rows[:, None] == jnp.arange(n_experts, dtype=jnp.int32)[None, :]).astype(
        jnp.int32
    )
    chosen = chosen * (valid[:, None] > 0).astype(jnp.int32)
    ranked = jnp.zeros_like(chosen).at[priority].set(chosen)
    before = jnp.cumsum(ranked, axis=0, dtype=jnp.int32) - ranked
    slot = jnp.sum(before[priority] * chosen, axis=1, dtype=jnp.int32)
    keep = (jnp.sum(chosen, axis=1, dtype=jnp.int32) > 0) & (slot < capacity)
    flat = jnp.where(keep, expert_rows * capacity + slot, n_experts * capacity)
    return (flat, keep.astype(jnp.float32))


def norm_backward(grad, field, scale, gain):
    gain_grad = jnp.sum(grad * field * scale, axis=0)
    direct = grad * gain
    field_grad = scale * direct - field * scale**3 * jnp.mean(
        direct * field, axis=-1, keepdims=True
    )
    return (field_grad, gain_grad)


def gelu_tanh(field):
    return jax.nn.gelu(field, approximate=True)


def block_offsets(tok_count, begin):
    places = jnp.arange(tok_count, dtype=jnp.int32)
    return places[None, :] - (begin + places)[:, None] + tok_count - 1


def skew(table, tok_count):
    heads = table.shape[0]
    span = 2 * tok_count
    padded = jnp.pad(table, ((0, 0), (0, span - table.shape[1])))
    flat = jnp.broadcast_to(padded[:, None, :], (heads, tok_count, span)).reshape(heads, -1)
    body = flat[:, tok_count - 1 : tok_count - 1 + tok_count * (span - 1)]
    return body.reshape(heads, tok_count, span - 1)[:, :, :tok_count]


def unskew_sum(field):
    heads, tok_count, _ = field.shape
    span = 2 * tok_count
    wide = jnp.pad(field, ((0, 0), (0, 0), (0, tok_count - 1))).reshape(heads, -1)
    wide = jnp.pad(wide, ((0, 0), (tok_count - 1, 1))).reshape(heads, tok_count, span)
    return jnp.sum(wide.astype(jnp.float32), axis=1)[:, : span - 1]


def score_block(query_rows, keys, bias_offsets, segment, begin, scale):
    tok_count = keys.shape[0]
    raw = jnp.einsum("qhd,khd->hqk", query_rows, keys, preferred_element_type=jnp.float32) * scale
    looked = skew(bias_offsets, tok_count)
    same = segment[:, None] == segment[None, :]
    return jnp.where(same[None], raw + looked, NEG_FILL)


def fill_buffer(rows, flat, n_experts, capacity):
    width = rows.shape[1]
    buffer = jnp.zeros((n_experts * capacity + 1, width), rows.dtype).at[flat].set(rows)
    return buffer[: n_experts * capacity].reshape(n_experts, capacity, width)


def read_buffer(buffer, flat, keep):
    n_experts, capacity, width = buffer.shape
    picked = buffer.reshape(n_experts * capacity, width)[
        jnp.minimum(flat, n_experts * capacity - 1)
    ]
    return picked.astype(jnp.float32) * keep[:, None]


def to_rows(buffer, source_count, local_experts):
    total, capacity, width = buffer.shape
    shaped = buffer.reshape(source_count, local_experts, capacity, width).transpose(0, 2, 1, 3)
    return shaped.reshape(source_count * capacity, local_experts, width)


def to_buffer(rows, source_count, local_experts):
    total, experts_here, width = rows.shape
    capacity = total // source_count
    shaped = rows.reshape(source_count, capacity, local_experts, width).transpose(0, 2, 1, 3)
    return shaped.reshape(source_count * local_experts, capacity, width)


def local(
    tokens,
    norm_gain_attn,
    w_query,
    w_key,
    w_value,
    w_output,
    rel_bias,
    norm_gain_ffn,
    w_router,
    w_in,
    w_out,
    out_grad,
    expert_ids,
    priority,
    lengths,
    seq_order,
    relpos_table,
):
    tok_count, width = tokens.shape
    shard_count = lax.axis_size("wshard")
    source_count = lax.axis_size("expert")
    n_heads = rel_bias.shape[1]
    head_dim = width // n_heads
    n_buckets = rel_bias.shape[0] * shard_count
    n_experts = w_router.shape[1]
    local_experts = w_in.shape[0]
    capacity = tok_count // n_experts
    scale = head_dim ** (-0.5)
    device = lax.axis_index("expert") * shard_count + lax.axis_index("wshard")
    segment, valid = device_layout(lengths, seq_order, device, tok_count)
    expert_rows = expert_ids[:, 0]
    bucket_range = jnp.arange(n_buckets, dtype=jnp.int32)
    mixer_shards = (
        norm_gain_attn,
        w_query,
        w_key,
        w_value,
        w_output,
        rel_bias,
        norm_gain_ffn,
        w_router,
    )
    gain_attn, full_query, full_key, full_value, full_output, full_bias, gain_ffn, full_router = (
        lax.all_gather(mixer_shards[0], "wshard", axis=0, tiled=True),
        lax.all_gather(mixer_shards[1], "wshard", axis=0, tiled=True),
        lax.all_gather(mixer_shards[2], "wshard", axis=0, tiled=True),
        lax.all_gather(mixer_shards[3], "wshard", axis=0, tiled=True),
        lax.all_gather(mixer_shards[4], "wshard", axis=0, tiled=True),
        lax.all_gather(mixer_shards[5], "wshard", axis=0, tiled=True),
        lax.all_gather(mixer_shards[6], "wshard", axis=0, tiled=True),
        lax.all_gather(mixer_shards[7], "wshard", axis=0, tiled=True),
    )
    table_hot = (relpos_table[:, None] == bucket_range[None, :]).astype(jnp.bfloat16)
    bias_offsets = jnp.dot(table_hot, full_bias, preferred_element_type=jnp.float32).T
    hidden_in = tokens.astype(jnp.float32)
    scale_attn = rms_scale(hidden_in)
    normed = (hidden_in * scale_attn * gain_attn.astype(jnp.float32)).astype(jnp.bfloat16)
    query = (
        jnp.dot(normed, full_query, preferred_element_type=jnp.float32)
        .astype(jnp.bfloat16)
        .reshape(tok_count, n_heads, head_dim)
    )
    keys = (
        jnp.dot(normed, full_key, preferred_element_type=jnp.float32)
        .astype(jnp.bfloat16)
        .reshape(tok_count, n_heads, head_dim)
    )
    values = (
        jnp.dot(normed, full_value, preferred_element_type=jnp.float32)
        .astype(jnp.bfloat16)
        .reshape(tok_count, n_heads, head_dim)
    )
    block_rows = min(ROW_BLOCK, tok_count)
    begin = 0
    scores = score_block(query, keys, bias_offsets, segment, begin, scale)
    top = jnp.max(scores, axis=-1, keepdims=True)
    expo = jnp.exp(scores - top)
    total = jnp.sum(expo, axis=-1, keepdims=True)
    probs_low = (expo / total).astype(jnp.bfloat16)
    mixed_parts = jnp.einsum("hqk,khd->qhd", probs_low, values, preferred_element_type=jnp.float32)
    log_totals = [top + jnp.log(total)]
    mixed = mixed_parts.reshape(tok_count, width).astype(jnp.bfloat16)
    attended = jnp.dot(mixed, full_output, preferred_element_type=jnp.float32) * valid[:, None]
    middle = hidden_in + attended
    scale_ffn = rms_scale(middle)
    normed_ffn = (middle * scale_ffn * gain_ffn.astype(jnp.float32)).astype(jnp.bfloat16)
    logits = jnp.dot(normed_ffn, full_router, preferred_element_type=jnp.float32)
    router = jax.nn.softmax(logits, axis=-1)
    picked = (expert_rows[:, None] == jnp.arange(n_experts, dtype=jnp.int32)[None, :]).astype(
        jnp.float32
    )
    gate = jnp.sum(router * picked, axis=1)
    flat, keep = slot_layout(expert_rows, priority, valid, n_experts, capacity)
    dispatch_buffer = fill_buffer(normed_ffn, flat, n_experts, capacity)
    received = lax.all_to_all(dispatch_buffer, "expert", split_axis=0, concat_axis=0, tiled=True)
    rows_local = to_rows(received, source_count, local_experts)
    rows_all = lax.all_gather(rows_local, "wshard", axis=0, tiled=True)
    inner = jnp.einsum("rxd,xdf->rxf", rows_all, w_in, preferred_element_type=jnp.float32)
    active = gelu_tanh(inner).astype(jnp.bfloat16)
    part = active
    result_rows = lax.psum_scatter(
        jnp.einsum("rxf,xfd->rxd", part, w_out, preferred_element_type=jnp.float32),
        "wshard",
        scatter_dimension=0,
        tiled=True,
    ).astype(jnp.bfloat16)
    returned = lax.all_to_all(
        to_buffer(result_rows, source_count, local_experts),
        "expert",
        split_axis=0,
        concat_axis=0,
        tiled=True,
    )
    result_tok = read_buffer(returned, flat, keep)
    layer_out = (middle + (keep * gate)[:, None] * result_tok).astype(jnp.bfloat16)
    upstream = out_grad.astype(jnp.float32)
    result_grad = ((keep * gate)[:, None] * upstream).astype(jnp.bfloat16)
    gate_grad = keep * jnp.sum(upstream * result_tok, axis=1)
    logit_grad = ((gate * gate_grad)[:, None] * (picked - router)).astype(jnp.bfloat16)
    grad_buffer = fill_buffer(result_grad, flat, n_experts, capacity)
    grad_received = lax.all_to_all(grad_buffer, "expert", split_axis=0, concat_axis=0, tiled=True)
    grad_local = to_rows(grad_received, source_count, local_experts)
    grad_all = lax.all_gather(grad_local, "wshard", axis=0, tiled=True)
    active_grad = jnp.einsum("rxd,xfd->rxf", grad_all, w_out, preferred_element_type=jnp.float32)
    inner_value, gelu_back = jax.vjp(gelu_tanh, inner)
    inner_grad = gelu_back(active_grad)[0].astype(jnp.bfloat16)
    grad_w_out = jnp.einsum("rxf,rxd->xfd", active, grad_all, preferred_element_type=jnp.float32)
    grad_w_in = jnp.einsum("rxd,rxf->xdf", rows_all, inner_grad, preferred_element_type=jnp.float32)
    part = inner_grad
    sent_rows = lax.psum_scatter(
        jnp.einsum("rxf,xdf->rxd", part, w_in, preferred_element_type=jnp.float32),
        "wshard",
        scatter_dimension=0,
        tiled=True,
    ).astype(jnp.bfloat16)
    sent_back = lax.all_to_all(
        to_buffer(sent_rows, source_count, local_experts),
        "expert",
        split_axis=0,
        concat_axis=0,
        tiled=True,
    )
    sent_grad = read_buffer(sent_back, flat, keep)
    gain_attn, full_query, full_key, full_value, full_output, full_bias, gain_ffn, full_router = (
        lax.all_gather(mixer_shards[0], "wshard", axis=0, tiled=True),
        lax.all_gather(mixer_shards[1], "wshard", axis=0, tiled=True),
        lax.all_gather(mixer_shards[2], "wshard", axis=0, tiled=True),
        lax.all_gather(mixer_shards[3], "wshard", axis=0, tiled=True),
        lax.all_gather(mixer_shards[4], "wshard", axis=0, tiled=True),
        lax.all_gather(mixer_shards[5], "wshard", axis=0, tiled=True),
        lax.all_gather(mixer_shards[6], "wshard", axis=0, tiled=True),
        lax.all_gather(mixer_shards[7], "wshard", axis=0, tiled=True),
    )
    grad_router = jnp.dot(normed_ffn.T, logit_grad, preferred_element_type=jnp.float32)
    normed_ffn_grad = (
        jnp.dot(logit_grad, full_router.T, preferred_element_type=jnp.float32) + sent_grad
    )
    middle_norm_grad, grad_gain_ffn = norm_backward(
        normed_ffn_grad, middle, scale_ffn, gain_ffn.astype(jnp.float32)
    )
    middle_grad = upstream + middle_norm_grad
    attended_grad = (middle_grad * valid[:, None]).astype(jnp.bfloat16)
    grad_output = jnp.dot(mixed.T, attended_grad, preferred_element_type=jnp.float32)
    mixed_grad = (
        jnp.dot(attended_grad, full_output.T, preferred_element_type=jnp.float32)
        .astype(jnp.bfloat16)
        .reshape(tok_count, n_heads, head_dim)
    )
    query_parts = []
    keys_grad = jnp.zeros((tok_count, n_heads, head_dim), jnp.float32)
    values_grad = jnp.zeros((tok_count, n_heads, head_dim), jnp.float32)
    bias_grad_heads = jnp.zeros((n_heads, n_buckets), jnp.float32)
    for number, begin in enumerate(range(0, tok_count, block_rows)):
        scores = score_block(query, keys, bias_offsets, segment, begin, scale)
        probs = jnp.exp(scores - log_totals[number])
        prob_grad = jnp.einsum(
            "qhd,khd->hqk", mixed_grad, values, preferred_element_type=jnp.float32
        )
        score_grad = (
            probs * (prob_grad - jnp.sum(probs * prob_grad, axis=-1, keepdims=True))
        ).astype(jnp.bfloat16)
        query_parts.append(
            jnp.einsum("hqk,khd->qhd", score_grad, keys, preferred_element_type=jnp.float32) * scale
        )
        keys_grad = (
            jnp.einsum("hqk,qhd->khd", score_grad, query, preferred_element_type=jnp.float32)
            * scale
        )
        values_grad = jnp.einsum(
            "hqk,qhd->khd",
            probs.astype(jnp.bfloat16),
            mixed_grad,
            preferred_element_type=jnp.float32,
        )
        bias_grad_heads = jnp.dot(
            unskew_sum(score_grad),
            table_hot.astype(jnp.float32),
            precision=lax.Precision.HIGHEST,
        )
    query_grad = query_parts[0].reshape(tok_count, width).astype(jnp.bfloat16)
    keys_grad = keys_grad.reshape(tok_count, width).astype(jnp.bfloat16)
    values_grad = values_grad.reshape(tok_count, width).astype(jnp.bfloat16)
    grad_rel_bias = bias_grad_heads.T
    grad_query = jnp.dot(normed.T, query_grad, preferred_element_type=jnp.float32)
    grad_key = jnp.dot(normed.T, keys_grad, preferred_element_type=jnp.float32)
    grad_value = jnp.dot(normed.T, values_grad, preferred_element_type=jnp.float32)
    normed_grad = jnp.dot(query_grad, full_query.T, preferred_element_type=jnp.float32)
    normed_grad = normed_grad + jnp.dot(keys_grad, full_key.T, preferred_element_type=jnp.float32)
    normed_grad = normed_grad + jnp.dot(
        values_grad, full_value.T, preferred_element_type=jnp.float32
    )
    input_norm_grad, grad_gain_attn = norm_backward(
        normed_grad, hidden_in, scale_attn, gain_attn.astype(jnp.float32)
    )
    tokens_grad = middle_grad + input_norm_grad
    local_grads = (
        grad_gain_attn,
        grad_query,
        grad_key,
        grad_value,
        grad_output,
        grad_rel_bias,
        grad_gain_ffn,
        grad_router,
    )
    shard_grads = (
        lax.psum_scatter(local_grads[0], "wshard", scatter_dimension=0, tiled=True),
        lax.psum_scatter(local_grads[1], "wshard", scatter_dimension=0, tiled=True),
        lax.psum_scatter(local_grads[2], "wshard", scatter_dimension=0, tiled=True),
        lax.psum_scatter(local_grads[3], "wshard", scatter_dimension=0, tiled=True),
        lax.psum_scatter(local_grads[4], "wshard", scatter_dimension=0, tiled=True),
        lax.psum_scatter(local_grads[5], "wshard", scatter_dimension=0, tiled=True),
        lax.psum_scatter(local_grads[6], "wshard", scatter_dimension=0, tiled=True),
        lax.psum_scatter(local_grads[7], "wshard", scatter_dimension=0, tiled=True),
    )
    total_grads = lax.psum(
        (
            shard_grads[0],
            shard_grads[1],
            shard_grads[2],
            shard_grads[3],
            shard_grads[4],
            shard_grads[5],
            shard_grads[6],
            shard_grads[7],
        ),
        "expert",
    )
    return (
        layer_out,
        tokens_grad,
        total_grads[0],
        total_grads[1],
        total_grads[2],
        total_grads[3],
        total_grads[4],
        total_grads[5],
        total_grads[6],
        total_grads[7],
        grad_w_in,
        grad_w_out,
    )


def solution(mesh):
    placed = (
        P(("expert", "wshard"), None),
        P("wshard"),
        P("wshard", None),
        P("wshard", None),
        P("wshard", None),
        P("wshard", None),
        P("wshard", None),
        P("wshard"),
        P("wshard", None),
        P("expert", None, "wshard"),
        P("expert", "wshard", None),
        P(("expert", "wshard"), None),
        P(("expert", "wshard"), None),
        P(("expert", "wshard")),
        P(),
        P(),
        P(),
    )
    return jax.shard_map(
        local,
        mesh=mesh,
        in_specs=placed,
        out_specs=(
            P(("expert", "wshard"), None),
            P(("expert", "wshard"), None),
            P("wshard"),
            P("wshard", None),
            P("wshard", None),
            P("wshard", None),
            P("wshard", None),
            P("wshard", None),
            P("wshard"),
            P("wshard", None),
            P("expert", None, "wshard"),
            P("expert", "wshard", None),
        ),
        check_vma=False,
    )
```

```python
import functools
import types

import jax
import jax.numpy as jnp
import numpy as np
from jax import lax
from jax.experimental import pallas as pl
from jax.experimental.pallas import tpu as pltpu
from jax.sharding import PartitionSpec as P

EPSILON = 1e-06
NEG_FILL = -1e30
GELU_A = 0.79788456
GELU_B = 0.044715
LANES = 128
REL_LANE = 64
GAIN_ATTN_LANE = 126
GAIN_FFN_LANE = 127
MESH = pl.DeviceIdType.MESH
BF = jnp.bfloat16
F32 = jnp.float32
I32 = jnp.int32


def up16(count):
    return -(-count // 16) * 16


def dot(a, b):
    return jnp.dot(a, b, preferred_element_type=F32)


def dot_rt(a, b):
    return lax.dot_general(a, b, (((1,), (1,)), ((), ())), preferred_element_type=F32)


def dot_lt(a, b):
    return lax.dot_general(a, b, (((0,), (0,)), ((), ())), preferred_element_type=F32)


def iota(shape, axis):
    return lax.broadcasted_iota(I32, shape, axis)


def flip(index, offset):
    out = index
    bit = 1
    while bit <= offset:
        if offset & bit:
            out = out + bit * (1 - 2 * lax.rem(lax.div(index, bit), 2))
        bit *= 2
    return out


def aligned(value, step):
    return pl.multiple_of(value, step)


def two_parts(value):
    high = value.astype(BF)
    return high, (value - high.astype(F32)).astype(BF)


def plan(expert_size, shard_size, tok_count, width, heads, buckets_here, n_experts, hidden):
    s = types.SimpleNamespace()
    s.E, s.W = expert_size, shard_size
    s.C = expert_size // 2
    s.T, s.D, s.H = tok_count, width, heads
    s.HD = width // heads
    s.F = hidden
    s.NX = n_experts
    s.cap = tok_count // n_experts
    s.cp = s.cap if s.cap % 8 == 0 else up16(s.cap)
    s.dt = BF if s.cp % 16 == 0 else F32
    s.S = n_experts * s.cp
    s.R = s.E * s.cp
    s.SR = width // shard_size
    s.NBH = buckets_here
    s.NBP = up16(buckets_here)
    s.half = width // 2
    team = s.C
    while s.SR % team or (s.SR // team) % 16:
        team //= 2
    s.team = team
    s.pw = s.SR // team
    s.pr = up16(s.SR // s.C)
    s.CP = s.C * s.pr
    s.Dp = s.W * s.CP
    s.padded = s.CP != s.SR
    s.tile = LANES
    s.slots = 2 if s.padded else max(width, hidden) // s.tile
    return s


def pieces_shape(s):
    return (4, s.C - 1, s.W * s.pr, s.half)


def arrivals(s):
    return (("Ga", s.D), ("Na", s.D), ("Ta", LANES)) if s.dt == F32 else ()


def scratch_list(s):
    V = pltpu.VMEM
    dma = pltpu.SemaphoreType.DMA
    return [
        ("wfull", V((4, s.D, s.D), BF)),
        ("smg", V((s.W, s.SR + s.NBP, LANES), BF)),
        ("xb", V((s.T, s.D), BF)),
        ("og", V((s.T, s.D), BF)),
        ("wi", V((s.D, s.F), BF)),
        ("wo", V((s.F, s.D), BF)),
        ("pm", V((s.S, s.T), BF)),
        ("pt", V((s.T, s.S), BF)),
        ("gsend", V((s.NX, s.cp, s.D), s.dt)),
        ("nsend", V((s.NX, s.cp, s.D), s.dt)),
        ("tsend", V((s.NX, s.cp, LANES), s.dt)),
        ("Gr", V((s.W * s.R, s.D), BF)),
        ("Nr", V((s.W * s.R, s.D), BF)),
        ("Tr", V((s.W * s.R, LANES), BF)),
        ("agr", V((s.W * s.R, s.F), BF)),
        ("act", V((s.W * s.R, s.F), BF)),
        ("ig", V((s.W * s.R, s.F), BF)),
        ("SS", V((s.W, s.R, s.D + LANES), BF)),
        ("Sr", V((s.W - 1, s.R, s.D + LANES), BF)),
        ("Sb", V((s.R, s.D + LANES), s.dt)),
        ("Sk", V((s.S, s.D + LANES), s.dt)),
        ("Rb", V((s.R, s.D), s.dt)),
        ("Rk", V((s.S, s.D), s.dt)),
        ("tb", V((LANES, 2 * s.T), F32)),
        ("oh", V((s.W * s.NBP, 2 * s.T), BF)),
        ("ohm", V((s.W * s.NBP, 2 * s.T), BF)),
        ("rows", V((8, s.D), F32)),
        ("Rw", V((s.D, LANES), BF)),
        ("probs", V((s.H, s.T, s.T), F32)),
        ("q", V((s.T, s.D), BF)),
        ("kk", V((s.T, s.D), BF)),
        ("v", V((s.T, s.D), BF)),
        ("mixed", V((s.T, s.D), BF)),
        ("nf", V((s.T, s.D), BF)),
        ("middle", V((s.T, s.D), F32)),
        ("mg", V((s.T, s.D), F32)),
        ("att", V((s.T, s.D), BF)),
        ("dq", V((s.T, s.D), BF)),
        ("dk", V((s.T, s.D), BF)),
        ("dv", V((s.T, s.D), BF)),
        ("nT", V((s.Dp, 2 * s.T), BF)),
        ("mT", V((s.Dp, 2 * s.T), BF)),
        ("fac", V((4, s.T, s.half), BF)),
        ("GS", V((4, s.C, s.W * s.pr, s.half), BF)),
        ("ZS", V((4, s.W * s.pr, s.half), BF)),
        ("ZR", V((4, s.W - 1, s.pr, s.half), BF)),
        ("FG", V((4, s.CP, s.D), BF)),
        ("smo", V((s.Dp, LANES), BF)),
        ("sms", V((s.Dp, LANES), BF)),
        ("hGS", V((s.C, s.W * s.pr, LANES), BF)),
        ("hGR", V((s.C - 1, s.W * s.pr, LANES), BF)),
        ("hZS", V((s.W * s.pr, LANES), BF)),
        ("hZR", V((s.W - 1, s.pr, LANES), BF)),
        ("hFG", V((s.CP, LANES), BF)),
        ("bt", V((LANES, 2 * s.T), F32)),
        ("gwi", V((s.slots, s.tile, s.F), F32)),
        ("gwo", V((s.slots, s.tile, s.D), F32)),
        ("gwi_sem", dma((s.slots,))),
        ("gwo_sem", dma((s.slots,))),
        ("lsem", dma((9,))),
        ("smr", dma((s.W,))),
        ("wa", dma((4, s.W))),
        ("wb", dma((4,))),
        ("wc", dma((4,))),
        ("g1", dma((s.C,))),
        ("g2", dma((s.W,))),
        ("n1", dma((s.C,))),
        ("n2", dma((s.W,))),
        ("t1", dma((s.C,))),
        ("t2", dma((s.W,))),
        ("s3", dma((s.W,))),
        ("r3", dma((s.W,))),
        ("back", dma((2,))),
        ("sibT", dma((2,))),
        ("sibF", dma((4,))),
        ("ra", dma((5,))),
        ("rb", dma((5,))),
        ("rc", dma((5,))),
        ("rd", dma((5,))),
        ("x_sm", dma),
        ("x_wa", dma((4,))),
        ("x_wb", dma((4,))),
        ("x_wc", dma((4,))),
        ("x_d1", dma((3,))),
        ("x_d2", dma((3,))),
        ("x_s3", dma((s.W,))),
        ("x_r3", dma((s.W,))),
        ("x_back", dma((2,))),
        ("x_sibT", dma((2,))),
        ("x_sibF", dma((4,))),
        ("x_ra", dma((5,))),
        ("x_rb", dma((5,))),
        ("x_rc", dma((5,))),
        ("x_rd", dma((5,))),
        ("credit", pltpu.SemaphoreType.REGULAR),
    ] + (
        [("gst", V((s.W * s.pr, s.half), BF))]
        + [(name, V((s.R, width), F32)) for name, width in arrivals(s)]
        if s.padded
        else [("GR", V(pieces_shape(s), BF))]
    )


IN_NAMES = (
    "lengths", "seq", "small", "ids", "prio", "table",
    "tokens", "out_grad", "w0", "w1", "w2", "w3", "w_in", "w_out",
)
PAD_NAMES = ("unsel",)
OUT_NAMES = ("layer_out", "tokens_grad", "grads", "smalls", "grad_w_in", "grad_w_out")


def kernel(s, names, *refs):
    r = types.SimpleNamespace(**dict(zip(names, refs, strict=True)))
    e = lax.axis_index("expert")
    z = lax.axis_index("wshard")
    c = lax.div(e, 2)
    k = lax.rem(e, 2)
    T, D, E, W, C, R, cp, half = s.T, s.D, s.E, s.W, s.C, s.R, s.cp, s.half
    sib = (flip(e, 1), z)
    here = pl.ds(aligned(k * half, LANES), half)
    there = pl.ds(aligned((1 - k) * half, LANES), half)

    def zpeer(offset):
        return (e, flip(z, offset))

    def cpeer(offset):
        return (flip(c, offset) * 2 + k, z)

    def remote(src, dst, send, recv, device):
        return pltpu.make_async_remote_copy(
            src_ref=src, dst_ref=dst, send_sem=send, recv_sem=recv, device_id=device, device_id_type=MESH
        )

    def got(ref, sem):
        remote(ref, ref, sem, sem, sib).wait_recv()

    def sent(ref, sem):
        remote(ref, ref, sem, sem, sib).wait_send()

    shards = (r.w0, r.w1, r.w2, r.w3)
    own_rows = pl.ds(aligned(z * s.SR, 16), s.SR)
    load_w = [
        pltpu.make_async_copy(shards[m].at[:, here], r.wfull.at[m, own_rows, here], r.lsem.at[m])
        for m in range(4)
    ]
    load_og = pltpu.make_async_copy(r.out_grad, r.og, r.lsem.at[4])
    load_x = pltpu.make_async_copy(r.tokens, r.xb, r.lsem.at[5])
    load_wo = pltpu.make_async_copy(r.w_out.at[0], r.wo, r.lsem.at[6])
    load_wi = pltpu.make_async_copy(r.w_in.at[0], r.wi, r.lsem.at[7])
    for copy in (*load_w, load_og, load_x, load_wo, load_wi):
        copy.start()

    barrier = pltpu.get_barrier_semaphore()
    peers = [(flip(e, o), z) for o in range(1, E)] + [zpeer(o) for o in range(1, W)]
    for peer in peers:
        pl.semaphore_signal(barrier, inc=1, device_id=peer, device_id_type=MESH)
    pl.semaphore_wait(barrier, len(peers))

    team_c = lax.rem(c, s.team)
    r.smg[z] = r.small[...]
    for o in range(1, W):
        remote(r.small, r.smg.at[z], r.x_sm, r.smr.at[o], zpeer(o)).start()
    piece = pl.ds(aligned(z * s.SR + team_c * s.pw, 16), s.pw)
    for m in range(4):
        load_w[m].wait()
        for o in range(1, W):
            part = r.wfull.at[m, piece, here]
            remote(part, part, r.x_wa.at[m], r.wa.at[m, o], zpeer(o)).start()

    device = e * W + z
    first = r.lengths[r.seq[2 * device]]
    both = first + r.lengths[r.seq[2 * device + 1]]
    col = iota((T, 1), 0)
    row = iota((1, T), 1)
    seg_col = (col >= first).astype(I32) + (col >= both).astype(I32)
    seg_row = (row >= first).astype(I32) + (row >= both).astype(I32)
    same = seg_col == seg_row
    valid = (col < both).astype(F32)
    eye = iota((T, T), 0) == iota((T, T), 1)
    id_col = r.ids[...].astype(F32)
    id_row = jnp.sum(jnp.where(eye, id_col, 0.0), axis=0, keepdims=True)
    prio_row = r.prio[...].astype(F32)
    prio_col = jnp.sum(jnp.where(eye, prio_row, 0.0), axis=1, keepdims=True)
    ahead = (id_col == id_row) & (prio_col < prio_row)
    slot_row = jnp.sum(jnp.where(ahead, valid, 0.0), axis=0, keepdims=True)
    kept = (row < both) & (slot_row < s.cap)
    flat_row = jnp.where(kept, id_row * cp + slot_row, -1.0)
    flat_col = jnp.sum(jnp.where(eye, flat_row, 0.0), axis=1, keepdims=True)
    r.pm[...] = (iota((s.S, T), 0).astype(F32) == flat_row).astype(F32).astype(BF)
    r.pt[...] = (iota((T, s.S), 1).astype(F32) == flat_col).astype(F32).astype(BF)

    plane_step = 16 if s.dt == BF else 8

    def dispatch(index, send, rows, first_sem, value):
        width = rows.shape[1]
        buffer = dot(r.pm[...], value)
        send[...] = buffer.astype(s.dt).reshape(s.NX, cp, width)
        mine = pl.ds(aligned(e * cp, plane_step), cp)
        for o in range(1, E):
            x = flip(e, o)
            remote(
                send.at[x], rows.at[mine], r.x_d1.at[index], first_sem.at[o // 2], (x, z)
            ).start()
        rows[mine, :] = send[e]

    def forward(index, rows, arrived, first_sem, second_sem):
        for oc in range(C):
            got(arrived.at[pl.ds(0, (2 if oc else 1) * cp)], first_sem.at[oc])
            at = flip(c, oc) * 2 * cp
            if s.dt != BF:
                block = pl.ds(aligned(at, 16), 2 * cp)
                rows[block, :] = arrived[block, :].astype(BF)
            for o in range(1, W):
                remote(
                    rows.at[pl.ds(aligned(at, 16), 2 * cp)],
                    rows.at[pl.ds(aligned(o * R + at, 16), 2 * cp)],
                    r.x_d2.at[index],
                    second_sem.at[o],
                    zpeer(o),
                ).start()

    Ga, Na, Ta = (r.Gr, r.Nr, r.Tr) if s.dt == BF else (r.Ga, r.Na, r.Ta)
    load_og.wait()
    dispatch(0, r.gsend, Ga, r.g1, r.og[...])

    def pass_on(m):
        for o in range(1, W):
            begin = flip(z, o) * s.SR + team_c * s.pw
            part = r.wfull.at[m, pl.ds(aligned(begin, 16), s.pw), here]
            got(part, r.wa.at[m, o])
            for oc in range(1, s.team):
                remote(part, part, r.x_wb.at[m], r.wb.at[m], cpeer(oc)).start()

    def to_sibling(m):
        if s.team > 1:
            got(r.wfull.at[m, pl.ds(0, (W - 1) * (s.team - 1) * s.pw), here], r.wb.at[m])
        part = r.wfull.at[m, :, here]
        remote(part, part, r.x_wc.at[m], r.wc.at[m], sib).start()

    def weight_ready(m):
        got(r.wfull.at[m, :, there], r.wc.at[m])

    for o in range(1, W):
        got(r.small, r.smr.at[o])
    pass_on(0)
    router_rows = r.smg[:, : s.SR, :].reshape(D, LANES)
    turned = router_rows.astype(F32).T
    r.rows[0:1, :] = turned[GAIN_ATTN_LANE : GAIN_ATTN_LANE + 1, :]
    r.rows[1:2, :] = turned[GAIN_FFN_LANE : GAIN_FFN_LANE + 1, :]
    lane_row = iota((1, LANES), 1)
    r.Rw[...] = router_rows * (lane_row < s.NX).astype(F32).astype(BF)
    bucket = r.table[...]
    shift = s.NBH.bit_length() - 1
    bucket = lax.shift_right_logical(bucket, shift) * s.NBP + lax.bitwise_and(bucket, s.NBH - 1)
    bucket_at = iota((W * s.NBP, 2 * T), 0)
    r.oh[...] = (bucket_at == bucket[0:1]).astype(F32).astype(BF)
    r.ohm[...] = (bucket_at == bucket[1:2]).astype(F32).astype(BF)
    bias_rows = r.smg[:, s.SR :, :].reshape(W * s.NBP, LANES)
    r.tb[...] = dot_lt(bias_rows, r.oh[...])

    def bias_head(h, carry):
        wide = jnp.broadcast_to(r.tb[pl.ds(h, 1), :], (T, 2 * T))
        turned = pltpu.roll(wide, T + 1, 1, stride=1, stride_axis=0)
        r.probs[h] = jnp.where(same, turned[:, :T], NEG_FILL)
        return carry

    third = s.H // 3
    pass_on(1)
    lax.fori_loop(0, third, bias_head, 0)
    pass_on(2)
    to_sibling(0)
    lax.fori_loop(third, 2 * third, bias_head, 0)
    to_sibling(1)
    pass_on(3)
    lax.fori_loop(2 * third, s.H, bias_head, 0)
    to_sibling(2)

    load_x.wait()
    x = r.xb[...].astype(F32)
    scale1 = lax.rsqrt(jnp.mean(x * x, axis=1, keepdims=True) + EPSILON)
    normed = (x * scale1 * r.rows[0:1, :]).astype(BF)

    def spread_rows(value):
        if not s.padded:
            return value
        shards = [value[at : at + s.SR] for at in range(0, D, s.SR)]
        return jnp.concatenate([dot_lt(r.unsel[...], shard) for shard in shards], axis=0).astype(BF)

    def turn_out(index, value, target):
        target[:, :T] = spread_rows(value.T)
        remote(
            target.at[:, pl.ds(0, T)], target.at[:, pl.ds(T, T)], r.x_sibT.at[index], r.sibT.at[index], sib
        ).start()

    turn_out(0, normed, r.nT)
    weight_ready(0)
    r.q[...] = dot(normed, r.wfull[0]).astype(BF)
    weight_ready(1)
    r.kk[...] = dot(normed, r.wfull[1]).astype(BF)
    to_sibling(3)
    weight_ready(2)
    r.v[...] = dot(normed, r.wfull[2]).astype(BF)
    forward(0, r.Gr, Ga, r.g1, r.g2)

    scale = s.HD ** (-0.5)
    low_lane = (lane_row < s.HD).astype(F32)
    lane_masks = (low_lane.astype(BF), (1.0 - low_lane).astype(BF))

    def attend(p, carry):
        cols = pl.ds(aligned(p * LANES, LANES), LANES)
        q, kk, v = r.q[:, cols], r.kk[:, cols], r.v[:, cols]
        outs = []
        for side in range(2):
            h = 2 * p + side
            scores = dot_rt(q * lane_masks[side], kk) * scale + r.probs[h]
            expo = jnp.exp(scores - jnp.max(scores, axis=1, keepdims=True))
            probs = expo * (1.0 / jnp.sum(expo, axis=1, keepdims=True))
            r.probs[h] = probs
            outs.append(dot(probs.astype(BF), v))
        r.mixed[:, cols] = jnp.where(lane_row < s.HD, outs[0], outs[1]).astype(BF)
        return carry

    lax.fori_loop(0, s.H // 2, attend, 0)
    mixed = r.mixed[...]
    weight_ready(3)
    middle = r.xb[...].astype(F32) + dot(mixed, r.wfull[3]) * valid
    r.middle[...] = middle
    scale2 = lax.rsqrt(jnp.mean(middle * middle, axis=1, keepdims=True) + EPSILON)
    nf = (middle * scale2 * r.rows[1:2, :]).astype(BF)
    r.nf[...] = nf
    dispatch(1, r.nsend, Na, r.n1, nf)
    logits = jnp.where(lane_row < s.NX, dot(nf, r.Rw[...]), NEG_FILL)
    raised = jnp.exp(logits - jnp.max(logits, axis=1, keepdims=True))
    router = raised / jnp.sum(raised, axis=1, keepdims=True)
    picked = (lane_row.astype(F32) == id_col).astype(F32)
    gate = jnp.sum(router * picked, axis=1, keepdims=True)
    gate_high, gate_rest = two_parts(gate)
    gate_mid, gate_low = two_parts(gate - gate_high.astype(F32))
    gate_lanes = jnp.where(
        lane_row == 0,
        gate_high.astype(F32),
        jnp.where(lane_row == 1, gate_mid.astype(F32), jnp.where(lane_row == 2, gate_low.astype(F32), 0.0)),
    )
    dispatch(2, r.tsend, Ta, r.t1, gate_lanes.astype(BF))
    forward(1, r.Nr, Na, r.n1, r.n2)
    forward(2, r.Tr, Ta, r.t1, r.t2)
    turn_out(1, mixed, r.mT)

    load_wo.wait()
    for o in range(1, W):
        got(r.Gr.at[pl.ds(0, R)], r.g2.at[o])

    def back_rows(step, carry):
        at = pl.ds(aligned(step * R, 16), R)
        r.agr[at, :] = dot_rt(r.Gr[at, :], r.wo[...]).astype(BF)
        return carry

    lax.fori_loop(0, W, back_rows, 0)
    load_wi.wait()

    def expert(step, carry):
        at = pl.ds(aligned(step * R, 16), R)

        @pl.when(step > 0)
        def _():
            got(r.Nr.at[pl.ds(0, R)], r.n2.at[step])

        inner = dot(r.Nr[at, :], r.wi[...])
        square = inner * inner
        tanh = jnp.tanh(GELU_A * inner * (1.0 + GELU_B * square))
        active = (0.5 * inner * (1.0 + tanh)).astype(BF)
        slope = 0.5 * (1.0 + tanh) + (0.5 * GELU_A) * inner * (1.0 - tanh * tanh) * (
            1.0 + (3.0 * GELU_B) * square
        )
        back = r.agr[at, :].astype(F32)
        inner_grad = (back * slope).astype(BF)
        r.act[at, :] = active
        r.ig[at, :] = inner_grad
        r.SS[step, :, :D] = dot_rt(inner_grad, r.wi[...]).astype(BF)
        high, rest = two_parts(jnp.sum(active.astype(F32) * back, axis=1, keepdims=True))
        r.SS[step, :, D:] = jnp.where(
            lane_row == 0, high.astype(F32), jnp.where(lane_row == 1, rest.astype(F32), 0.0)
        ).astype(BF)
        for o in range(1, W):

            @pl.when(step == o)
            def _():
                remote(r.SS.at[o], r.Sr.at[o - 1], r.x_s3.at[o], r.s3.at[o], zpeer(o)).start()

        return carry

    lax.fori_loop(0, W, expert, 0)

    sent(r.Gr.at[pl.ds(0, (W - 1) * R)], r.x_d2.at[0])
    sent(r.Nr.at[pl.ds(0, (W - 1) * R)], r.x_d2.at[1])
    for o in range(1, W):
        got(r.Tr.at[pl.ds(0, R)], r.t2.at[o])

    def scale_rows(step, carry):
        at = pl.ds(aligned(step * R, 16), R)
        gates = jnp.sum(r.Tr[at, :].astype(F32), axis=1, keepdims=True)
        r.Gr[at, :] = (r.Gr[at, :].astype(F32) * gates).astype(BF)
        r.ig[at, :] = (r.ig[at, :].astype(F32) * gates).astype(BF)
        return carry

    lax.fori_loop(0, W, scale_rows, 0)
    tile, slots = s.tile, s.slots

    def save_out(step):
        slot = lax.rem(step, slots)
        at = pl.ds(aligned(step * tile, LANES), tile)
        return pltpu.make_async_copy(r.gwo.at[slot], r.grad_w_out.at[0, at], r.gwo_sem.at[slot])

    def save_in(step):
        slot = lax.rem(step, slots)
        at = pl.ds(aligned(step * tile, LANES), tile)
        return pltpu.make_async_copy(r.gwi.at[slot], r.grad_w_in.at[0, at], r.gwi_sem.at[slot])

    def grad_out_tile(step, carry):
        @pl.when(step >= slots)
        def _():
            save_out(step - slots).wait()

        at = pl.ds(aligned(step * tile, LANES), tile)
        r.gwo[lax.rem(step, slots)] = dot_lt(r.act[:, at], r.Gr[...])
        save_out(step).start()
        return carry

    def grad_in_tile(step, carry):
        @pl.when(step >= slots)
        def _():
            save_in(step - slots).wait()

        at = pl.ds(aligned(step * tile, LANES), tile)
        r.gwi[lax.rem(step, slots)] = dot_lt(r.Nr[:, at], r.ig[...])
        save_in(step).start()
        return carry

    lax.fori_loop(0, s.F // tile, grad_out_tile, 0)
    lax.fori_loop(0, D // tile, grad_in_tile, 0)

    def plane_back(index, source, target):
        mine = pl.ds(aligned(e * cp, plane_step), cp)
        for o in range(1, E):
            x = flip(e, o)
            remote(
                source.at[pl.ds(aligned(x * cp, plane_step), cp)],
                target.at[mine],
                r.x_back.at[index],
                r.back.at[index],
                (x, z),
            ).start()
        target[mine, :] = source[mine, :]

    total = r.SS[0].astype(F32)
    for o in range(1, W):
        got(r.Sr.at[o - 1], r.s3.at[o])
        total = total + r.Sr[o - 1].astype(F32)
    high, rest = two_parts(jnp.sum(total[:, D:], axis=1, keepdims=True))
    r.Sb[:, :D] = total[:, :D].astype(BF).astype(s.dt)
    r.Sb[:, D:] = jnp.where(
        lane_row == 0, high.astype(F32), jnp.where(lane_row == 1, rest.astype(F32), 0.0)
    ).astype(s.dt)
    for o in range(1, W):
        pl.semaphore_signal(r.credit, inc=1, device_id=zpeer(o), device_id_type=MESH)
    plane_back(0, r.Sb, r.Sk)

    for o in range(1, W):
        sent(r.SS.at[o], r.x_s3.at[o])
    pl.semaphore_wait(r.credit, W - 1)

    def results(step, carry):
        at = pl.ds(aligned(step * R, 16), R)
        r.SS[step, :, :D] = dot(r.act[at, :], r.wo[...]).astype(BF)
        for o in range(1, W):

            @pl.when(step == o)
            def _():
                remote(
                    r.SS.at[o, :, pl.ds(0, D)],
                    r.Sr.at[o - 1, :, pl.ds(0, D)],
                    r.x_r3.at[o],
                    r.r3.at[o],
                    zpeer(o),
                ).start()

        return carry

    lax.fori_loop(0, W, results, 0)

    got(r.Sk.at[pl.ds(0, (E - 1) * cp)], r.back.at[0])
    returned = dot(r.pt[...], r.Sk[...].astype(BF))
    gate_grad = jnp.sum(returned[:, D:], axis=1, keepdims=True)
    logit_grad = (gate * gate_grad * (picked - router)).astype(BF)
    nf_grad = dot_rt(logit_grad, r.Rw[...]) + gate * returned[:, :D]
    middle = r.middle[...]
    along = nf_grad * r.rows[1:2, :]
    middle_grad = (
        r.og[...].astype(F32)
        + scale2 * along
        - middle * (scale2 * scale2 * scale2 * jnp.mean(along * middle, axis=1, keepdims=True))
    )
    r.mg[...] = middle_grad
    r.rows[2:3, :] = jnp.sum(nf_grad * middle * scale2, axis=0, keepdims=True)
    r.att[...] = (middle_grad * valid).astype(BF)
    attended_grad = r.att[...]

    def share(m, source):
        remote(source.at[:, there], r.fac.at[m], r.x_sibF.at[m], r.sibF.at[m], sib).start()

    share(3, r.att)
    r.mixed[...] = dot_rt(attended_grad, r.wfull[3]).astype(BF)
    router_grad = dot_lt(logit_grad, r.nf[...])

    def plane_sum(m, left, source):
        got(r.fac.at[m], r.sibF.at[m])

        def block(step, carry):
            at = pl.ds(aligned(step * s.CP, 16), s.CP)
            part = dot(left[at, :T], source[:, here]) + dot(left[at, T:], r.fac[m])
            part = part.astype(BF)
            for chip in range(C):
                r.GS[m, chip, pl.ds(aligned(step * s.pr, 16), s.pr), :] = part[
                    chip * s.pr : (chip + 1) * s.pr
                ]
            return carry

        lax.fori_loop(0, W, block, 0)
        for oc in range(1, C):
            remote(
                r.GS.at[m, flip(c, oc)], r.GR.at[m, oc - 1], r.x_ra.at[m], r.ra.at[m], cpeer(oc)
            ).start()

    got(r.mT.at[:, pl.ds(T, T)], r.sibT.at[1])
    plane_sum(3, r.mT, r.att)

    def attend_back(p, carry):
        cols = pl.ds(aligned(p * LANES, LANES), LANES)
        q, kk, v, mixg = r.q[:, cols], r.kk[:, cols], r.v[:, cols], r.mixed[:, cols]
        outs = []
        for side in range(2):
            h = 2 * p + side
            probs = r.probs[h]
            prob_grad = dot_rt(mixg * lane_masks[side], v)
            inside = jnp.sum(probs * prob_grad, axis=1, keepdims=True)
            score_grad = (probs * (prob_grad - inside)).astype(BF)
            r.probs[h] = score_grad.astype(F32)
            outs.append(
                (
                    dot(score_grad, kk) * scale,
                    dot_lt(score_grad, q) * scale,
                    dot_lt(probs.astype(BF), mixg),
                )
            )
        low = lane_row < s.HD
        r.dq[:, cols] = jnp.where(low, outs[0][0], outs[1][0]).astype(BF)
        r.dk[:, cols] = jnp.where(low, outs[0][1], outs[1][1]).astype(BF)
        r.dv[:, cols] = jnp.where(low, outs[0][2], outs[1][2]).astype(BF)
        return carry

    lax.fori_loop(0, s.H // 2, attend_back, 0)
    share(0, r.dq)
    share(1, r.dk)
    share(2, r.dv)
    got(r.nT.at[:, pl.ds(T, T)], r.sibT.at[0])
    plane_sum(0, r.nT, r.dq)
    plane_sum(1, r.nT, r.dk)
    plane_sum(2, r.nT, r.dv)

    def shard_sum(m):
        got(r.GR.at[m], r.ra.at[m])
        total = r.GS[m, c].astype(F32)
        for oc in range(1, C):
            if s.padded:
                fetch = pltpu.make_async_copy(r.GR.at[m, oc - 1], r.gst, r.lsem.at[8])
                fetch.start()
                fetch.wait()
            part = r.gst[...] if s.padded else r.GR[m, oc - 1]
            total = total + part.astype(F32)
        r.ZS[m] = total.astype(BF)
        for o in range(1, W):
            remote(
                r.ZS.at[m, pl.ds(aligned(flip(z, o) * s.pr, 16), s.pr)],
                r.ZR.at[m, o - 1],
                r.x_rb.at[m],
                r.rb.at[m],
                zpeer(o),
            ).start()

    def spread(m):
        got(r.ZR.at[m], r.rb.at[m])
        total = r.ZS[m, pl.ds(aligned(z * s.pr, 16), s.pr), :].astype(F32)
        for o in range(1, W):
            total = total + r.ZR[m, o - 1].astype(F32)
        mine = pl.ds(aligned(c * s.pr, 16), s.pr)
        r.FG[m, mine, here] = total.astype(BF)
        part = r.FG.at[m, mine, here]
        for oc in range(1, C):
            remote(part, part, r.x_rc.at[m], r.rc.at[m], cpeer(oc)).start()

    def share_sum(m):
        got(r.FG.at[m, pl.ds(0, (C - 1) * s.pr), here], r.rc.at[m])
        part = r.FG.at[m, :, here]
        remote(part, part, r.x_rd.at[m], r.rd.at[m], sib).start()

    shard_sum(3)

    normed_grad = (
        dot_rt(r.dq[...], r.wfull[0]) + dot_rt(r.dk[...], r.wfull[1]) + dot_rt(r.dv[...], r.wfull[2])
    )
    x = r.xb[...].astype(F32)
    along = normed_grad * r.rows[0:1, :]
    r.tokens_grad[...] = (
        r.mg[...]
        + scale1 * along
        - x * (scale1 * scale1 * scale1 * jnp.mean(along * x, axis=1, keepdims=True))
    )
    r.rows[3:4, :] = jnp.sum(normed_grad * x * scale1, axis=0, keepdims=True)

    r.bt[...] = jnp.zeros_like(r.bt)
    mirror = (iota((T, T), 0) + iota((T, T), 1) == T - 1).astype(F32).astype(BF)

    def bias_back(h, carry):
        mirrored = dot(r.probs[h].astype(BF), mirror)
        wide = jnp.concatenate([mirrored, jnp.zeros((T, T), F32)], axis=1)
        turned = pltpu.roll(wide, 0, 1, stride=1, stride_axis=0)
        r.bt[pl.ds(REL_LANE + h, 1), :] = jnp.sum(turned, axis=0, keepdims=True)
        return carry

    lax.fori_loop(0, s.H, bias_back, 0)
    high, rest = two_parts(r.bt[...])
    rel_grad = dot_rt(r.ohm[...], high) + dot_rt(r.ohm[...], rest)
    lane_col = iota((LANES, 1), 0)
    small = jnp.where(
        lane_col == GAIN_ATTN_LANE,
        r.rows[3:4, :],
        jnp.where(lane_col == GAIN_FFN_LANE, r.rows[2:3, :], router_grad),
    ).T
    blocks = []
    for block in range(W):
        part = small[block * s.SR : (block + 1) * s.SR]
        head = part[: s.NBP] + rel_grad[block * s.NBP : (block + 1) * s.NBP]
        blocks.append(jnp.concatenate([head, part[s.NBP :]], axis=0))
    small = jnp.concatenate(blocks, axis=0).astype(BF)
    r.smo[...] = spread_rows(small)
    remote(r.smo, r.sms, r.x_rd.at[4], r.rd.at[4], sib).start()
    shard_sum(0)
    shard_sum(1)
    shard_sum(2)
    got(r.sms, r.rd.at[4])
    pair = (r.smo[...].astype(F32) + r.sms[...].astype(F32)).astype(BF)
    for block in range(W):
        for chip in range(C):
            at = block * s.CP + chip * s.pr
            r.hGS[chip, block * s.pr : (block + 1) * s.pr, :] = pair[at : at + s.pr]
    for oc in range(1, C):
        remote(r.hGS.at[flip(c, oc)], r.hGR.at[oc - 1], r.x_ra.at[4], r.ra.at[4], cpeer(oc)).start()
    spread(3)

    total = r.SS[0, :, :D].astype(F32)
    for o in range(1, W):
        got(r.Sr.at[o - 1, :, pl.ds(0, D)], r.r3.at[o])
        total = total + r.Sr[o - 1, :, :D].astype(F32)
    r.Rb[...] = total.astype(BF).astype(s.dt)
    plane_back(1, r.Rb, r.Rk)

    got(r.hGR, r.ra.at[4])
    total = r.hGS[c].astype(F32)
    for oc in range(1, C):
        total = total + r.hGR[oc - 1].astype(F32)
    r.hZS[...] = total.astype(BF)
    for o in range(1, W):
        remote(
            r.hZS.at[pl.ds(aligned(flip(z, o) * s.pr, 16), s.pr)],
            r.hZR.at[o - 1],
            r.x_rb.at[4],
            r.rb.at[4],
            zpeer(o),
        ).start()
    spread(0)
    spread(1)
    spread(2)
    share_sum(3)
    got(r.hZR, r.rb.at[4])
    total = r.hZS[pl.ds(aligned(z * s.pr, 16), s.pr), :].astype(F32)
    for o in range(1, W):
        total = total + r.hZR[o - 1].astype(F32)
    mine = pl.ds(aligned(c * s.pr, 16), s.pr)
    r.hFG[mine, :] = total.astype(BF)
    for oc in range(1, C):
        part = r.hFG.at[mine]
        remote(part, part, r.x_rc.at[4], r.rc.at[4], cpeer(oc)).start()

    got(r.Rk.at[pl.ds(0, (E - 1) * cp)], r.back.at[1])
    r.layer_out[...] = (r.middle[...] + gate * dot(r.pt[...], r.Rk[...].astype(BF))).astype(BF)

    share_sum(0)
    share_sum(1)
    share_sum(2)
    got(r.hFG.at[pl.ds(0, (C - 1) * s.pr)], r.rc.at[4])

    def unpad(value):
        return dot(r.unsel[...], value) if s.padded else value.astype(F32)

    r.smalls[...] = unpad(r.hFG[...])
    for m in (3, 0, 1, 2):
        got(r.FG.at[m, :, there], r.rd.at[m])
        r.grads[m] = unpad(r.FG[m]).astype(r.grads.dtype)

    for step in range(max(0, s.F // tile - slots), s.F // tile):
        save_out(step).wait()
    for step in range(max(0, D // tile - slots), D // tile):
        save_in(step).wait()
    sent(r.smg.at[pl.ds(0, W - 1)], r.x_sm)
    for m in range(4):
        sent(r.wfull.at[m, pl.ds(0, (W - 1) * s.pw), here], r.x_wa.at[m])
        if s.team > 1:
            sent(r.wfull.at[m, pl.ds(0, (W - 1) * (s.team - 1) * s.pw), here], r.x_wb.at[m])
        sent(r.wfull.at[m, :, here], r.x_wc.at[m])
        sent(r.fac.at[m], r.x_sibF.at[m])
        sent(r.GR.at[m], r.x_ra.at[m])
        sent(r.ZR.at[m], r.x_rb.at[m])
        sent(r.FG.at[m, pl.ds(0, (C - 1) * s.pr), here], r.x_rc.at[m])
        sent(r.FG.at[m, :, here], r.x_rd.at[m])
    for index, buffer in enumerate((r.gsend, r.nsend, r.tsend)):
        sent(buffer.at[pl.ds(0, E - 1)], r.x_d1.at[index])
    sent(r.Tr.at[pl.ds(0, (W - 1) * R)], r.x_d2.at[2])
    for o in range(1, W):
        sent(r.SS.at[o, :, pl.ds(0, D)], r.x_r3.at[o])
    sent(r.Sk.at[pl.ds(0, (E - 1) * cp)], r.x_back.at[0])
    sent(r.Rk.at[pl.ds(0, (E - 1) * cp)], r.x_back.at[1])
    sent(r.nT.at[:, pl.ds(0, T)], r.x_sibT.at[0])
    sent(r.mT.at[:, pl.ds(0, T)], r.x_sibT.at[1])
    sent(r.hGR, r.x_ra.at[4])
    sent(r.hZR, r.x_rb.at[4])
    sent(r.hFG.at[pl.ds(0, (C - 1) * s.pr)], r.x_rc.at[4])
    sent(r.smo, r.x_rd.at[4])


def selection(s):
    share = s.SR // s.C
    unsel = np.zeros((s.SR, s.CP), np.float32)
    for chip in range(s.C):
        for at in range(share):
            unsel[chip * share + at, chip * s.pr + at] = 1
    return jnp.asarray(unsel, BF)


def local(
    tokens,
    norm_gain_attn,
    w_query,
    w_key,
    w_value,
    w_output,
    rel_bias,
    norm_gain_ffn,
    w_router,
    w_in,
    w_out,
    out_grad,
    expert_ids,
    priority,
    lengths,
    seq_order,
    relpos_table,
):
    tok_count, width = tokens.shape
    buckets_here, heads = rel_bias.shape
    n_experts = w_router.shape[1]
    s = plan(
        lax.axis_size("expert"),
        lax.axis_size("wshard"),
        tok_count,
        width,
        heads,
        buckets_here,
        n_experts,
        w_in.shape[2],
    )
    gap = jnp.zeros((s.SR, GAIN_ATTN_LANE - n_experts), BF)
    small = jnp.concatenate(
        [w_router, gap, norm_gain_attn[:, None], norm_gain_ffn[:, None]], axis=1
    )
    bias = jnp.pad(rel_bias, ((0, s.NBP - buckets_here), (0, LANES - heads)))
    small = jnp.concatenate([small, bias], axis=0)
    table = jnp.pad(jnp.stack([relpos_table, relpos_table[::-1]]), ((0, 0), (0, 1)))
    operands = [
        lengths, seq_order, small, expert_ids, priority.reshape(1, tok_count), table,
        tokens, out_grad, w_query, w_key, w_value, w_output, w_in, w_out,
    ]
    smem, vmem, anywhere = (
        pl.BlockSpec(memory_space=space) for space in (pltpu.SMEM, pltpu.VMEM, pl.ANY)
    )
    in_specs = [smem] * 2 + [vmem] * 4 + [anywhere] * 8
    names = IN_NAMES
    if s.padded:
        operands.append(selection(s))
        in_specs.append(vmem)
        names = names + PAD_NAMES
    spilled = (jax.ShapeDtypeStruct(pieces_shape(s), BF),) if s.padded else ()
    scratch = scratch_list(s)
    names = names + OUT_NAMES + ("GR",) * len(spilled) + tuple(name for name, _ in scratch)
    outs = pl.pallas_call(
        functools.partial(kernel, s, names),
        name="layer",
        out_shape=(
            jax.ShapeDtypeStruct((s.T, s.D), BF),
            jax.ShapeDtypeStruct((s.T, s.D), F32),
            jax.ShapeDtypeStruct((4, s.SR, s.D), BF),
            jax.ShapeDtypeStruct((s.SR, LANES), F32),
            jax.ShapeDtypeStruct((1, s.D, s.F), F32),
            jax.ShapeDtypeStruct((1, s.F, s.D), F32),
            *spilled,
        ),
        in_specs=in_specs,
        out_specs=(vmem, vmem, vmem, vmem, anywhere, anywhere) + (anywhere,) * len(spilled),
        scratch_shapes=[shape for _, shape in scratch],
        compiler_params=pltpu.CompilerParams(
            collective_id=0, has_side_effects=True, vmem_limit_bytes=62 * 2**20
        ),
    )(*operands)
    layer_out, tokens_grad, grads, smalls, grad_w_in, grad_w_out = outs[:6]
    return (
        layer_out,
        tokens_grad,
        smalls[:, GAIN_ATTN_LANE],
        grads[0].astype(F32),
        grads[1].astype(F32),
        grads[2].astype(F32),
        grads[3].astype(F32),
        smalls[:buckets_here, REL_LANE : REL_LANE + heads],
        smalls[:, GAIN_FFN_LANE],
        smalls[:, :n_experts],
        grad_w_in,
        grad_w_out,
    )


def solution(mesh):
    rows = P(("expert", "wshard"), None)
    shard = P("wshard", None)
    into, outof = P("expert", None, "wshard"), P("expert", "wshard", None)
    return jax.shard_map(
        local,
        mesh=mesh,
        in_specs=(
            rows,
            P("wshard"),
            shard,
            shard,
            shard,
            shard,
            shard,
            P("wshard"),
            shard,
            into,
            outof,
            rows,
            rows,
            P(("expert", "wshard")),
            P(),
            P(),
            P(),
        ),
        out_specs=(
            rows,
            rows,
            P("wshard"),
            shard,
            shard,
            shard,
            shard,
            shard,
            P("wshard"),
            shard,
            into,
            outof,
        ),
        check_vma=False,
    )
```

```python
import functools
import types

import jax
import jax.numpy as jnp
import numpy as np
from jax import lax
from jax.experimental import pallas as pl
from jax.experimental.pallas import tpu as pltpu
from jax.sharding import PartitionSpec as P

EPSILON = 1e-06
NEG_FILL = -1e30
GELU_A = 0.79788456
GELU_B = 0.044715
LANES = 128
REL_LANE = 64
GAIN_ATTN_LANE = 126
GAIN_FFN_LANE = 127
MESH = pl.DeviceIdType.MESH
BF = jnp.bfloat16
F32 = jnp.float32
I32 = jnp.int32


def up16(count):
    return -(-count // 16) * 16


def dot(a, b):
    return jnp.dot(a, b, preferred_element_type=F32)


def dot_rt(a, b):
    return lax.dot_general(a, b, (((1,), (1,)), ((), ())), preferred_element_type=F32)


def dot_lt(a, b):
    return lax.dot_general(a, b, (((0,), (0,)), ((), ())), preferred_element_type=F32)


def iota(shape, axis):
    return lax.broadcasted_iota(I32, shape, axis)


def flip(index, offset):
    out = index
    bit = 1
    while bit <= offset:
        if offset & bit:
            out = out + bit * (1 - 2 * lax.rem(lax.div(index, bit), 2))
        bit *= 2
    return out


def aligned(value, step):
    return pl.multiple_of(value, step)


def two_parts(value):
    high = value.astype(BF)
    return high, (value - high.astype(F32)).astype(BF)


def plan(expert_size, shard_size, tok_count, width, heads, buckets_here, n_experts, hidden):
    s = types.SimpleNamespace()
    s.E, s.W = expert_size, shard_size
    s.C = expert_size // 2
    s.T, s.D, s.H = tok_count, width, heads
    s.HD = width // heads
    s.F = hidden
    s.NX = n_experts
    s.cap = tok_count // n_experts
    s.cp = s.cap if s.cap % 8 == 0 else up16(s.cap)
    s.dt = BF if s.cp % 16 == 0 else F32
    s.S = n_experts * s.cp
    s.R = s.E * s.cp
    s.SR = width // shard_size
    s.NBH = buckets_here
    s.NBP = up16(buckets_here)
    s.half = width // 2
    team = s.C
    while s.SR % team or (s.SR // team) % 16:
        team //= 2
    s.team = team
    s.pw = s.SR // team
    s.pr = up16(s.SR // s.C)
    s.CP = s.C * s.pr
    s.Dp = s.W * s.CP
    s.padded = s.CP != s.SR
    s.tile = LANES
    s.slots = 2 if s.padded else max(width, hidden) // s.tile
    return s


def pieces_shape(s):
    return (4, s.C - 1, s.W * s.pr, s.half)


def arrivals(s):
    return (("Ga", s.D), ("Na", s.D), ("Ta", LANES)) if s.dt == F32 else ()


def scratch_list(s):
    V = pltpu.VMEM
    dma = pltpu.SemaphoreType.DMA
    return [
        ("wfull", V((4, s.D, s.D), BF)),
        ("smg", V((s.W, s.SR + s.NBP, LANES), BF)),
        ("xb", V((s.T, s.D), BF)),
        ("og", V((s.T, s.D), BF)),
        ("wi", V((s.D, s.F), BF)),
        ("wo", V((s.F, s.D), BF)),
        ("pm", V((s.S, s.T), BF)),
        ("pt", V((s.T, s.S), BF)),
        ("gsend", V((s.NX, s.cp, s.D), s.dt)),
        ("nsend", V((s.NX, s.cp, s.D), s.dt)),
        ("tsend", V((s.NX, s.cp, LANES), s.dt)),
        ("Gr", V((s.W * s.R, s.D), BF)),
        ("Nr", V((s.W * s.R, s.D), BF)),
        ("Tr", V((s.W * s.R, LANES), BF)),
        ("agr", V((s.W * s.R, s.F), BF)),
        ("act", V((s.W * s.R, s.F), BF)),
        ("ig", V((s.W * s.R, s.F), BF)),
        ("SS", V((s.W, s.R, s.D + LANES), BF)),
        ("Sin", V((s.W + 1, s.R, s.D + LANES), BF)),
        ("Sb", V((s.R, s.D + LANES), s.dt)),
        ("Sk", V((s.S, s.D + LANES), s.dt)),
        ("Rb", V((s.R, s.D), s.dt)),
        ("Rk", V((s.S, s.D), s.dt)),
        ("tb", V((LANES, 2 * s.T), F32)),
        ("oh", V((s.W * s.NBP, 2 * s.T), BF)),
        ("ohm", V((s.W * s.NBP, 2 * s.T), BF)),
        ("rows", V((8, s.D), F32)),
        ("Rw", V((s.D, LANES), BF)),
        ("probs", V((s.H, s.T, s.T), F32)),
        ("q", V((s.T, s.D), BF)),
        ("kk", V((s.T, s.D), BF)),
        ("v", V((s.T, s.D), BF)),
        ("mixed", V((s.T, s.D), BF)),
        ("nf", V((s.T, s.D), BF)),
        ("middle", V((s.T, s.D), F32)),
        ("mg", V((s.T, s.D), F32)),
        ("att", V((s.T, s.D), BF)),
        ("dq", V((s.T, s.D), BF)),
        ("dk", V((s.T, s.D), BF)),
        ("dv", V((s.T, s.D), BF)),
        ("nT", V((s.Dp, 2 * s.T), BF)),
        ("mT", V((s.Dp, 2 * s.T), BF)),
        ("fac", V((4, s.T, s.half), BF)),
        ("GS", V((4, s.C, s.W * s.pr, s.half), BF)),
        ("ZS", V((4, s.W * s.pr, s.half), BF)),
        ("ZR", V((4, s.W - 1, s.pr, s.half), BF)),
        ("FG", V((4, s.CP, s.D), BF)),
        ("smo", V((s.Dp, LANES), BF)),
        ("sms", V((s.Dp, LANES), BF)),
        ("hGS", V((s.C, s.W * s.pr, LANES), BF)),
        ("hGR", V((s.C - 1, s.W * s.pr, LANES), BF)),
        ("hZS", V((s.W * s.pr, LANES), BF)),
        ("hZR", V((s.W - 1, s.pr, LANES), BF)),
        ("hFG", V((s.CP, LANES), BF)),
        ("bt", V((LANES, 2 * s.T), F32)),
        ("gwi", V((s.slots, s.tile, s.F), F32)),
        ("gwo", V((s.slots, s.tile, s.D), F32)),
        ("gwi_sem", dma((s.slots,))),
        ("gwo_sem", dma((s.slots,))),
        ("lsem", dma((9,))),
        ("smr", dma((s.W,))),
        ("wa", dma((4, s.W))),
        ("wb", dma((4,))),
        ("wc", dma((4,))),
        ("g1", dma((s.C,))),
        ("gu", dma((s.W, s.C))),
        ("gd", dma((s.W, s.C))),
        ("n1", dma((s.C,))),
        ("nu", dma((s.W, s.C))),
        ("nd", dma((s.W, s.C))),
        ("t1", dma((s.C,))),
        ("t2", dma((s.W,))),
        ("su", dma((s.W, s.C))),
        ("sd", dma((s.W, s.C))),
        ("r3", dma((s.W,))),
        ("back", dma((2,))),
        ("sibT", dma((2,))),
        ("sibF", dma((4,))),
        ("ra", dma((5,))),
        ("rb", dma((5,))),
        ("rc", dma((5,))),
        ("rd", dma((5,))),
        ("x_sm", dma),
        ("x_wa", dma((4,))),
        ("x_wb", dma((4,))),
        ("x_wc", dma((4,))),
        ("x_d1", dma((3,))),
        ("x_t2", dma),
        ("x_gu", dma((s.W,))),
        ("x_gd", dma((s.W,))),
        ("x_nu", dma((s.W,))),
        ("x_nd", dma((s.W,))),
        ("x_su", dma((s.W,))),
        ("x_sd", dma((s.W,))),
        ("x_r3", dma((s.W,))),
        ("x_back", dma((2,))),
        ("x_sibT", dma((2,))),
        ("x_sibF", dma((4,))),
        ("x_ra", dma((5,))),
        ("x_rb", dma((5,))),
        ("x_rc", dma((5,))),
        ("x_rd", dma((5,))),
        ("credit", pltpu.SemaphoreType.REGULAR),
    ] + (
        [("gst", V((s.W * s.pr, s.half), BF))]
        + [(name, V((s.R, width), F32)) for name, width in arrivals(s)]
        if s.padded
        else [("GR", V(pieces_shape(s), BF))]
    )


IN_NAMES = (
    "lengths", "seq", "small", "ids", "prio", "table",
    "tokens", "out_grad", "w0", "w1", "w2", "w3", "w_in", "w_out",
)
PAD_NAMES = ("unsel",)
OUT_NAMES = ("layer_out", "tokens_grad", "grads", "smalls", "grad_w_in", "grad_w_out")


def kernel(s, names, *refs):
    r = types.SimpleNamespace(**dict(zip(names, refs, strict=True)))
    e = lax.axis_index("expert")
    z = lax.axis_index("wshard")
    c = lax.div(e, 2)
    k = lax.rem(e, 2)
    T, D, E, W, C, R, cp, half = s.T, s.D, s.E, s.W, s.C, s.R, s.cp, s.half
    sib = (flip(e, 1), z)
    here = pl.ds(aligned(k * half, LANES), half)
    there = pl.ds(aligned((1 - k) * half, LANES), half)

    def zpeer(offset):
        return (e, flip(z, offset))

    def cpeer(offset):
        return (flip(c, offset) * 2 + k, z)

    def remote(src, dst, send, recv, device):
        return pltpu.make_async_remote_copy(
            src_ref=src, dst_ref=dst, send_sem=send, recv_sem=recv, device_id=device, device_id_type=MESH
        )

    def got(ref, sem):
        remote(ref, ref, sem, sem, sib).wait_recv()

    def sent(ref, sem):
        remote(ref, ref, sem, sem, sib).wait_send()

    shards = (r.w0, r.w1, r.w2, r.w3)
    own_rows = pl.ds(aligned(z * s.SR, 16), s.SR)
    load_w = [
        pltpu.make_async_copy(shards[m].at[:, here], r.wfull.at[m, own_rows, here], r.lsem.at[m])
        for m in range(4)
    ]
    load_og = pltpu.make_async_copy(r.out_grad, r.og, r.lsem.at[4])
    load_x = pltpu.make_async_copy(r.tokens, r.xb, r.lsem.at[5])
    load_wo = pltpu.make_async_copy(r.w_out.at[0], r.wo, r.lsem.at[6])
    load_wi = pltpu.make_async_copy(r.w_in.at[0], r.wi, r.lsem.at[7])
    for copy in (*load_w, load_og, load_x, load_wo, load_wi):
        copy.start()

    barrier = pltpu.get_barrier_semaphore()
    peers = [(flip(e, o), z) for o in range(1, E)] + [zpeer(o) for o in range(1, W)]
    for peer in peers:
        pl.semaphore_signal(barrier, inc=1, device_id=peer, device_id_type=MESH)
    pl.semaphore_wait(barrier, len(peers))

    team_c = lax.rem(c, s.team)
    r.smg[z] = r.small[...]
    for o in range(1, W):
        remote(r.small, r.smg.at[z], r.x_sm, r.smr.at[o], zpeer(o)).start()
    piece = pl.ds(aligned(z * s.SR + team_c * s.pw, 16), s.pw)
    share_rows = pl.ds(aligned(team_c * s.pw, 16), s.pw)
    for m in range(4):
        for o in range(1, W):
            remote(
                shards[m].at[share_rows, here],
                r.wfull.at[m, piece, here],
                r.x_wa.at[m],
                r.wa.at[m, o],
                zpeer(o),
            ).start()

    device = e * W + z
    first = r.lengths[r.seq[2 * device]]
    both = first + r.lengths[r.seq[2 * device + 1]]
    col = iota((T, 1), 0)
    row = iota((1, T), 1)
    seg_col = (col >= first).astype(I32) + (col >= both).astype(I32)
    seg_row = (row >= first).astype(I32) + (row >= both).astype(I32)
    same = seg_col == seg_row
    valid = (col < both).astype(F32)
    eye = iota((T, T), 0) == iota((T, T), 1)
    id_col = r.ids[...].astype(F32)
    id_row = jnp.sum(jnp.where(eye, id_col, 0.0), axis=0, keepdims=True)
    prio_row = r.prio[...].astype(F32)
    prio_col = jnp.sum(jnp.where(eye, prio_row, 0.0), axis=1, keepdims=True)
    ahead = (id_col == id_row) & (prio_col < prio_row)
    slot_row = jnp.sum(jnp.where(ahead, valid, 0.0), axis=0, keepdims=True)
    kept = (row < both) & (slot_row < s.cap)
    flat_row = jnp.where(kept, id_row * cp + slot_row, -1.0)
    flat_col = jnp.sum(jnp.where(eye, flat_row, 0.0), axis=1, keepdims=True)
    r.pm[...] = (iota((s.S, T), 0).astype(F32) == flat_row).astype(F32).astype(BF)
    r.pt[...] = (iota((T, s.S), 1).astype(F32) == flat_col).astype(F32).astype(BF)

    plane_step = 16 if s.dt == BF else 8
    plane_rows = z * R if s.dt == BF else 0

    def dispatch(index, send, rows, first_sem, value):
        width = rows.shape[1]
        buffer = dot(r.pm[...], value)
        send[...] = buffer.astype(s.dt).reshape(s.NX, cp, width)
        mine = pl.ds(aligned(plane_rows + e * cp, plane_step), cp)
        for o in range(1, E):
            x = flip(e, o)
            remote(
                send.at[x], rows.at[mine], r.x_d1.at[index], first_sem.at[o // 2], (x, z)
            ).start()
        rows[mine, :] = send[e]

    def block_at(plane, oc):
        return pl.ds(aligned(plane * R + flip(c, oc) * 2 * cp, 16), 2 * cp)

    def landed(rows, arrived, first_sem, oc):
        got(arrived.at[pl.ds(0, (2 if oc else 1) * cp)], first_sem.at[oc])
        if s.dt != BF:
            rows[block_at(z, oc), :] = arrived[block_at(0, oc), :].astype(BF)

    def move(part, send, recv, to):
        remote(part, part, send, recv, (e, to)).start()

    def line_own(rows, arrived, first_sem, up, down, x_up, x_down):
        for oc in range(C):
            landed(rows, arrived, first_sem, oc)
            part = rows.at[block_at(z, oc)]
            pl.when(z < W - 1)(functools.partial(move, part, x_up.at[0], up.at[1, oc], z + 1))
            pl.when(z > 0)(functools.partial(move, part, x_down.at[0], down.at[1, oc], z - 1))

    def line_pass(rows, d, up, down, x_up, x_down):
        for oc in range(C):

            @pl.when(z >= d)
            def _():
                part = rows.at[block_at(z - d, oc)]
                got(part, up.at[d, oc])
                if d < W - 1:
                    pl.when(z < W - 1)(
                        functools.partial(move, part, x_up.at[d], up.at[d + 1, oc], z + 1)
                    )

            @pl.when(z + d <= W - 1)
            def _():
                part = rows.at[block_at(z + d, oc)]
                got(part, down.at[d, oc])
                if d < W - 1:
                    pl.when(z > 0)(
                        functools.partial(move, part, x_down.at[d], down.at[d + 1, oc], z - 1)
                    )

    def line_sent(rows, x_up, x_down):
        for d in range(W - 1):
            whole = rows.at[pl.ds(0, R)]
            pl.when((z >= d) & (z < W - 1))(functools.partial(sent, whole, x_up.at[d]))
            pl.when((z + d <= W - 1) & (z > 0))(functools.partial(sent, whole, x_down.at[d]))

    g_line = (r.gu, r.gd, r.x_gu, r.x_gd)
    n_line = (r.nu, r.nd, r.x_nu, r.x_nd)
    Ga, Na, Ta = (r.Gr, r.Nr, r.Tr) if s.dt == BF else (r.Ga, r.Na, r.Ta)
    load_og.wait()
    dispatch(0, r.gsend, Ga, r.g1, r.og[...])

    def pass_on(m):
        for o in range(1, W):
            begin = flip(z, o) * s.SR + team_c * s.pw
            part = r.wfull.at[m, pl.ds(aligned(begin, 16), s.pw), here]
            got(part, r.wa.at[m, o])
            for oc in range(1, s.team):
                remote(part, part, r.x_wb.at[m], r.wb.at[m], cpeer(oc)).start()

    def to_sibling(m):
        if s.team > 1:
            got(r.wfull.at[m, pl.ds(0, (W - 1) * (s.team - 1) * s.pw), here], r.wb.at[m])
        load_w[m].wait()
        part = r.wfull.at[m, :, here]
        remote(part, part, r.x_wc.at[m], r.wc.at[m], sib).start()

    def weight_ready(m):
        got(r.wfull.at[m, :, there], r.wc.at[m])

    for o in range(1, W):
        got(r.small, r.smr.at[o])
    pass_on(0)
    router_rows = r.smg[:, : s.SR, :].reshape(D, LANES)
    turned = router_rows.astype(F32).T
    r.rows[0:1, :] = turned[GAIN_ATTN_LANE : GAIN_ATTN_LANE + 1, :]
    r.rows[1:2, :] = turned[GAIN_FFN_LANE : GAIN_FFN_LANE + 1, :]
    lane_row = iota((1, LANES), 1)
    r.Rw[...] = router_rows * (lane_row < s.NX).astype(F32).astype(BF)
    bucket = r.table[...]
    shift = s.NBH.bit_length() - 1
    bucket = lax.shift_right_logical(bucket, shift) * s.NBP + lax.bitwise_and(bucket, s.NBH - 1)
    bucket_at = iota((W * s.NBP, 2 * T), 0)
    r.oh[...] = (bucket_at == bucket[0:1]).astype(F32).astype(BF)
    r.ohm[...] = (bucket_at == bucket[1:2]).astype(F32).astype(BF)
    bias_rows = r.smg[:, s.SR :, :].reshape(W * s.NBP, LANES)
    r.tb[...] = dot_lt(bias_rows, r.oh[...])

    def bias_head(h, carry):
        wide = jnp.broadcast_to(r.tb[pl.ds(h, 1), :], (T, 2 * T))
        turned = pltpu.roll(wide, T + 1, 1, stride=1, stride_axis=0)
        r.probs[h] = jnp.where(same, turned[:, :T], NEG_FILL)
        return carry

    third = s.H // 3
    pass_on(1)
    lax.fori_loop(0, third, bias_head, 0)
    pass_on(2)
    to_sibling(0)
    lax.fori_loop(third, 2 * third, bias_head, 0)
    to_sibling(1)
    line_own(r.Gr, Ga, r.g1, *g_line)
    pass_on(3)
    lax.fori_loop(2 * third, s.H, bias_head, 0)
    to_sibling(2)

    load_x.wait()
    x = r.xb[...].astype(F32)
    scale1 = lax.rsqrt(jnp.mean(x * x, axis=1, keepdims=True) + EPSILON)
    normed = (x * scale1 * r.rows[0:1, :]).astype(BF)

    def spread_rows(value):
        if not s.padded:
            return value
        shards = [value[at : at + s.SR] for at in range(0, D, s.SR)]
        return jnp.concatenate([dot_lt(r.unsel[...], shard) for shard in shards], axis=0).astype(BF)

    def turn_out(index, value, target):
        target[:, :T] = spread_rows(value.T)
        remote(
            target.at[:, pl.ds(0, T)], target.at[:, pl.ds(T, T)], r.x_sibT.at[index], r.sibT.at[index], sib
        ).start()

    turn_out(0, normed, r.nT)
    weight_ready(0)
    r.q[...] = dot(normed, r.wfull[0]).astype(BF)
    weight_ready(1)
    r.kk[...] = dot(normed, r.wfull[1]).astype(BF)
    to_sibling(3)
    weight_ready(2)
    r.v[...] = dot(normed, r.wfull[2]).astype(BF)
    line_pass(r.Gr, 1, *g_line)

    scale = s.HD ** (-0.5)
    low_lane = (lane_row < s.HD).astype(F32)
    lane_masks = (low_lane.astype(BF), (1.0 - low_lane).astype(BF))

    def attend(p, carry):
        cols = pl.ds(aligned(p * LANES, LANES), LANES)
        q, kk, v = r.q[:, cols], r.kk[:, cols], r.v[:, cols]
        outs = []
        for side in range(2):
            h = 2 * p + side
            scores = dot_rt(q * lane_masks[side], kk) * scale + r.probs[h]
            expo = jnp.exp(scores - jnp.max(scores, axis=1, keepdims=True))
            probs = expo * (1.0 / jnp.sum(expo, axis=1, keepdims=True))
            r.probs[h] = probs
            outs.append(dot(probs.astype(BF), v))
        r.mixed[:, cols] = jnp.where(lane_row < s.HD, outs[0], outs[1]).astype(BF)
        return carry

    lax.fori_loop(0, s.H // 2, attend, 0)
    mixed = r.mixed[...]
    if W > 2:
        line_pass(r.Gr, 2, *g_line)
    weight_ready(3)
    middle = r.xb[...].astype(F32) + dot(mixed, r.wfull[3]) * valid
    r.middle[...] = middle
    scale2 = lax.rsqrt(jnp.mean(middle * middle, axis=1, keepdims=True) + EPSILON)
    nf = (middle * scale2 * r.rows[1:2, :]).astype(BF)
    r.nf[...] = nf
    dispatch(1, r.nsend, Na, r.n1, nf)
    logits = jnp.where(lane_row < s.NX, dot(nf, r.Rw[...]), NEG_FILL)
    raised = jnp.exp(logits - jnp.max(logits, axis=1, keepdims=True))
    router = raised / jnp.sum(raised, axis=1, keepdims=True)
    picked = (lane_row.astype(F32) == id_col).astype(F32)
    gate = jnp.sum(router * picked, axis=1, keepdims=True)
    gate_high, gate_rest = two_parts(gate)
    gate_mid, gate_low = two_parts(gate - gate_high.astype(F32))
    gate_lanes = jnp.where(
        lane_row == 0,
        gate_high.astype(F32),
        jnp.where(lane_row == 1, gate_mid.astype(F32), jnp.where(lane_row == 2, gate_low.astype(F32), 0.0)),
    )
    dispatch(2, r.tsend, Ta, r.t1, gate_lanes.astype(BF))
    line_own(r.Nr, Na, r.n1, *n_line)
    for oc in range(C):
        landed(r.Tr, Ta, r.t1, oc)
        for o in range(1, W):
            part = r.Tr.at[block_at(z, oc)]
            remote(part, part, r.x_t2, r.t2.at[o], zpeer(o)).start()
    turn_out(1, mixed, r.mT)

    load_wo.wait()
    for d in range(3, W):
        line_pass(r.Gr, d, *g_line)

    def back_rows(step, carry):
        at = pl.ds(aligned(step * R, 16), R)
        r.agr[at, :] = dot_rt(r.Gr[at, :], r.wo[...]).astype(BF)
        return carry

    lax.fori_loop(0, W, back_rows, 0)
    load_wi.wait()

    def lanes_of(value):
        high, rest = two_parts(value)
        return jnp.where(
            lane_row == 0, high.astype(F32), jnp.where(lane_row == 1, rest.astype(F32), 0.0)
        )

    def expert(plane):
        at = pl.ds(aligned(plane * R, 16), R)
        inner = dot(r.Nr[at, :], r.wi[...])
        square = inner * inner
        tanh = jnp.tanh(GELU_A * inner * (1.0 + GELU_B * square))
        active = (0.5 * inner * (1.0 + tanh)).astype(BF)
        slope = 0.5 * (1.0 + tanh) + (0.5 * GELU_A) * inner * (1.0 - tanh * tanh) * (
            1.0 + (3.0 * GELU_B) * square
        )
        back = r.agr[at, :].astype(F32)
        inner_grad = (back * slope).astype(BF)
        r.act[at, :] = active
        r.ig[at, :] = inner_grad
        r.SS[plane, :, :D] = dot_rt(inner_grad, r.wi[...]).astype(BF)
        r.SS[plane, :, D:] = lanes_of(
            jnp.sum(active.astype(F32) * back, axis=1, keepdims=True)
        ).astype(BF)

    def merge(plane, slot, block):
        own, other = r.SS[plane, block, :].astype(F32), r.Sin[slot, block, :].astype(F32)
        r.SS[plane, block, :D] = (own[:, :D] + other[:, :D]).astype(BF)
        r.SS[plane, block, D:] = lanes_of(
            jnp.sum(own[:, D:] + other[:, D:], axis=1, keepdims=True)
        ).astype(BF)

    def plane_back(index, source, target, offsets):
        mine = pl.ds(aligned(e * cp, plane_step), cp)
        for o in offsets:
            if o == 0:
                target[mine, :] = source[mine, :]
                continue
            x = flip(e, o)
            remote(
                source.at[pl.ds(aligned(x * cp, plane_step), cp)],
                target.at[mine],
                r.x_back.at[index],
                r.back.at[index],
                (x, z),
            ).start()

    expert(z)
    for step in range(1, 2 * W - 2):
        if step < W:
            line_pass(r.Nr, step, *n_line)

            def sides(side, carry, step=step):
                plane = z + (2 * side - 1) * step
                pl.when((plane >= 0) & (plane < W))(functools.partial(expert, plane))
                return carry

            lax.fori_loop(0, 2, sides, 0)

        plane_down = 2 * W - 2 - z - step
        gap_down = z - plane_down
        plane_up = step - z
        gap_up = plane_up - z

        @pl.when((plane_down >= 0) & (gap_down >= 1))
        def _():
            for oc in range(C):
                block = block_at(0, oc)

                @pl.when(z < W - 1)
                def _():
                    got(r.Sin.at[plane_down, block], r.sd.at[gap_down, oc])
                    merge(plane_down, plane_down, block)

                remote(
                    r.SS.at[plane_down, block],
                    r.Sin.at[plane_down, block],
                    r.x_sd.at[gap_down],
                    r.sd.at[gap_down - 1, oc],
                    (e, z - 1),
                ).start()

        @pl.when((plane_up <= W - 1) & (gap_up >= 1))
        def _():
            for oc in range(C):
                block = block_at(0, oc)

                @pl.when(z > 0)
                def _():
                    got(r.Sin.at[plane_up + 1, block], r.su.at[gap_up, oc])
                    merge(plane_up, plane_up + 1, block)

                remote(
                    r.SS.at[plane_up, block],
                    r.Sin.at[plane_up + 1, block],
                    r.x_su.at[gap_up],
                    r.su.at[gap_up - 1, oc],
                    (e, z + 1),
                ).start()

    for oc in range(C):
        block = block_at(0, oc)

        @pl.when(z < W - 1)
        def _():
            got(r.Sin.at[z, block], r.sd.at[0, oc])
            merge(z, z, block)

        @pl.when(z > 0)
        def _():
            got(r.Sin.at[z + 1, block], r.su.at[0, oc])
            merge(z, z + 1, block)

        r.Sb[block, :] = r.SS[z, block, :].astype(s.dt)
        plane_back(0, r.Sb, r.Sk, (2 * oc, 2 * oc + 1))

    line_sent(r.Gr, r.x_gu, r.x_gd)
    for o in range(1, W):
        got(r.Tr.at[pl.ds(0, R)], r.t2.at[o])

    def scale_rows(step, carry):
        at = pl.ds(aligned(step * R, 16), R)
        gates = jnp.sum(r.Tr[at, :].astype(F32), axis=1, keepdims=True)
        r.Gr[at, :] = (r.Gr[at, :].astype(F32) * gates).astype(BF)
        r.ig[at, :] = (r.ig[at, :].astype(F32) * gates).astype(BF)
        return carry

    lax.fori_loop(0, W, scale_rows, 0)
    tile, slots = s.tile, s.slots

    def save_out(step):
        slot = lax.rem(step, slots)
        at = pl.ds(aligned(step * tile, LANES), tile)
        return pltpu.make_async_copy(r.gwo.at[slot], r.grad_w_out.at[0, at], r.gwo_sem.at[slot])

    def save_in(step):
        slot = lax.rem(step, slots)
        at = pl.ds(aligned(step * tile, LANES), tile)
        return pltpu.make_async_copy(r.gwi.at[slot], r.grad_w_in.at[0, at], r.gwi_sem.at[slot])

    def grad_out_tile(step, carry):
        @pl.when(step >= slots)
        def _():
            save_out(step - slots).wait()

        at = pl.ds(aligned(step * tile, LANES), tile)
        r.gwo[lax.rem(step, slots)] = dot_lt(r.act[:, at], r.Gr[...])
        save_out(step).start()
        return carry

    def grad_in_tile(step, carry):
        @pl.when(step >= slots)
        def _():
            save_in(step - slots).wait()

        at = pl.ds(aligned(step * tile, LANES), tile)
        r.gwi[lax.rem(step, slots)] = dot_lt(r.Nr[:, at], r.ig[...])
        save_in(step).start()
        return carry

    lax.fori_loop(0, s.F // tile, grad_out_tile, 0)
    lax.fori_loop(0, D // tile, grad_in_tile, 0)

    for o in range(1, W):
        pl.semaphore_signal(r.credit, inc=1, device_id=zpeer(o), device_id_type=MESH)
    for d in range(1, W):
        pl.when(z >= d)(functools.partial(sent, r.SS.at[0], r.x_sd.at[d]))
        pl.when(z + d <= W - 1)(functools.partial(sent, r.SS.at[0], r.x_su.at[d]))
    pl.semaphore_wait(r.credit, W - 1)

    def results(step, carry):
        at = pl.ds(aligned(step * R, 16), R)
        r.SS[step, :, :D] = dot(r.act[at, :], r.wo[...]).astype(BF)
        return carry

    lax.fori_loop(0, W, results, 0)
    for o in range(1, W):
        remote(
            r.SS.at[flip(z, o), :, pl.ds(0, D)],
            r.Sin.at[z, :, pl.ds(0, D)],
            r.x_r3.at[o],
            r.r3.at[o],
            zpeer(o),
        ).start()

    got(r.Sk.at[pl.ds(0, (E - 1) * cp)], r.back.at[0])
    returned = dot(r.pt[...], r.Sk[...].astype(BF))
    gate_grad = jnp.sum(returned[:, D:], axis=1, keepdims=True)
    logit_grad = (gate * gate_grad * (picked - router)).astype(BF)
    nf_grad = dot_rt(logit_grad, r.Rw[...]) + gate * returned[:, :D]
    middle = r.middle[...]
    along = nf_grad * r.rows[1:2, :]
    middle_grad = (
        r.og[...].astype(F32)
        + scale2 * along
        - middle * (scale2 * scale2 * scale2 * jnp.mean(along * middle, axis=1, keepdims=True))
    )
    r.mg[...] = middle_grad
    r.rows[2:3, :] = jnp.sum(nf_grad * middle * scale2, axis=0, keepdims=True)
    r.att[...] = (middle_grad * valid).astype(BF)
    attended_grad = r.att[...]

    def share(m, source):
        remote(source.at[:, there], r.fac.at[m], r.x_sibF.at[m], r.sibF.at[m], sib).start()

    share(3, r.att)
    r.mixed[...] = dot_rt(attended_grad, r.wfull[3]).astype(BF)
    router_grad = dot_lt(logit_grad, r.nf[...])

    def plane_sum(m, left, source):
        got(r.fac.at[m], r.sibF.at[m])

        def block(step, carry):
            at = pl.ds(aligned(step * s.CP, 16), s.CP)
            part = dot(left[at, :T], source[:, here]) + dot(left[at, T:], r.fac[m])
            part = part.astype(BF)
            for chip in range(C):
                r.GS[m, chip, pl.ds(aligned(step * s.pr, 16), s.pr), :] = part[
                    chip * s.pr : (chip + 1) * s.pr
                ]
            return carry

        lax.fori_loop(0, W, block, 0)
        for oc in range(1, C):
            remote(
                r.GS.at[m, flip(c, oc)], r.GR.at[m, oc - 1], r.x_ra.at[m], r.ra.at[m], cpeer(oc)
            ).start()

    got(r.mT.at[:, pl.ds(T, T)], r.sibT.at[1])
    plane_sum(3, r.mT, r.att)

    def attend_back(p, carry):
        cols = pl.ds(aligned(p * LANES, LANES), LANES)
        q, kk, v, mixg = r.q[:, cols], r.kk[:, cols], r.v[:, cols], r.mixed[:, cols]
        outs = []
        for side in range(2):
            h = 2 * p + side
            probs = r.probs[h]
            prob_grad = dot_rt(mixg * lane_masks[side], v)
            inside = jnp.sum(probs * prob_grad, axis=1, keepdims=True)
            score_grad = (probs * (prob_grad - inside)).astype(BF)
            r.probs[h] = score_grad.astype(F32)
            outs.append(
                (
                    dot(score_grad, kk) * scale,
                    dot_lt(score_grad, q) * scale,
                    dot_lt(probs.astype(BF), mixg),
                )
            )
        low = lane_row < s.HD
        r.dq[:, cols] = jnp.where(low, outs[0][0], outs[1][0]).astype(BF)
        r.dk[:, cols] = jnp.where(low, outs[0][1], outs[1][1]).astype(BF)
        r.dv[:, cols] = jnp.where(low, outs[0][2], outs[1][2]).astype(BF)
        return carry

    lax.fori_loop(0, s.H // 2, attend_back, 0)
    share(0, r.dq)
    share(1, r.dk)
    share(2, r.dv)
    got(r.nT.at[:, pl.ds(T, T)], r.sibT.at[0])
    plane_sum(0, r.nT, r.dq)
    plane_sum(1, r.nT, r.dk)
    plane_sum(2, r.nT, r.dv)

    def shard_sum(m):
        got(r.GR.at[m], r.ra.at[m])
        total = r.GS[m, c].astype(F32)
        for oc in range(1, C):
            if s.padded:
                fetch = pltpu.make_async_copy(r.GR.at[m, oc - 1], r.gst, r.lsem.at[8])
                fetch.start()
                fetch.wait()
            part = r.gst[...] if s.padded else r.GR[m, oc - 1]
            total = total + part.astype(F32)
        r.ZS[m] = total.astype(BF)
        for o in range(1, W):
            remote(
                r.ZS.at[m, pl.ds(aligned(flip(z, o) * s.pr, 16), s.pr)],
                r.ZR.at[m, o - 1],
                r.x_rb.at[m],
                r.rb.at[m],
                zpeer(o),
            ).start()

    def spread(m):
        got(r.ZR.at[m], r.rb.at[m])
        total = r.ZS[m, pl.ds(aligned(z * s.pr, 16), s.pr), :].astype(F32)
        for o in range(1, W):
            total = total + r.ZR[m, o - 1].astype(F32)
        mine = pl.ds(aligned(c * s.pr, 16), s.pr)
        r.FG[m, mine, here] = total.astype(BF)
        part = r.FG.at[m, mine, here]
        for oc in range(1, C):
            remote(part, part, r.x_rc.at[m], r.rc.at[m], cpeer(oc)).start()

    def share_sum(m):
        got(r.FG.at[m, pl.ds(0, (C - 1) * s.pr), here], r.rc.at[m])
        part = r.FG.at[m, :, here]
        remote(part, part, r.x_rd.at[m], r.rd.at[m], sib).start()

    shard_sum(3)

    normed_grad = (
        dot_rt(r.dq[...], r.wfull[0]) + dot_rt(r.dk[...], r.wfull[1]) + dot_rt(r.dv[...], r.wfull[2])
    )
    x = r.xb[...].astype(F32)
    along = normed_grad * r.rows[0:1, :]
    r.tokens_grad[...] = (
        r.mg[...]
        + scale1 * along
        - x * (scale1 * scale1 * scale1 * jnp.mean(along * x, axis=1, keepdims=True))
    )
    r.rows[3:4, :] = jnp.sum(normed_grad * x * scale1, axis=0, keepdims=True)

    r.bt[...] = jnp.zeros_like(r.bt)
    mirror = (iota((T, T), 0) + iota((T, T), 1) == T - 1).astype(F32).astype(BF)

    def bias_back(h, carry):
        mirrored = dot(r.probs[h].astype(BF), mirror)
        wide = jnp.concatenate([mirrored, jnp.zeros((T, T), F32)], axis=1)
        turned = pltpu.roll(wide, 0, 1, stride=1, stride_axis=0)
        r.bt[pl.ds(REL_LANE + h, 1), :] = jnp.sum(turned, axis=0, keepdims=True)
        return carry

    lax.fori_loop(0, s.H, bias_back, 0)
    high, rest = two_parts(r.bt[...])
    rel_grad = dot_rt(r.ohm[...], high) + dot_rt(r.ohm[...], rest)
    lane_col = iota((LANES, 1), 0)
    small = jnp.where(
        lane_col == GAIN_ATTN_LANE,
        r.rows[3:4, :],
        jnp.where(lane_col == GAIN_FFN_LANE, r.rows[2:3, :], router_grad),
    ).T
    blocks = []
    for block in range(W):
        part = small[block * s.SR : (block + 1) * s.SR]
        head = part[: s.NBP] + rel_grad[block * s.NBP : (block + 1) * s.NBP]
        blocks.append(jnp.concatenate([head, part[s.NBP :]], axis=0))
    small = jnp.concatenate(blocks, axis=0).astype(BF)
    r.smo[...] = spread_rows(small)
    remote(r.smo, r.sms, r.x_rd.at[4], r.rd.at[4], sib).start()
    shard_sum(0)
    shard_sum(1)
    shard_sum(2)
    got(r.sms, r.rd.at[4])
    pair = (r.smo[...].astype(F32) + r.sms[...].astype(F32)).astype(BF)
    for block in range(W):
        for chip in range(C):
            at = block * s.CP + chip * s.pr
            r.hGS[chip, block * s.pr : (block + 1) * s.pr, :] = pair[at : at + s.pr]
    for oc in range(1, C):
        remote(r.hGS.at[flip(c, oc)], r.hGR.at[oc - 1], r.x_ra.at[4], r.ra.at[4], cpeer(oc)).start()
    spread(3)

    total = r.SS[z, :, :D].astype(F32)
    for o in range(1, W):
        got(r.Sin.at[flip(z, o), :, pl.ds(0, D)], r.r3.at[o])
        total = total + r.Sin[flip(z, o), :, :D].astype(F32)
    r.Rb[...] = total.astype(BF).astype(s.dt)
    plane_back(1, r.Rb, r.Rk, range(E))

    got(r.hGR, r.ra.at[4])
    total = r.hGS[c].astype(F32)
    for oc in range(1, C):
        total = total + r.hGR[oc - 1].astype(F32)
    r.hZS[...] = total.astype(BF)
    for o in range(1, W):
        remote(
            r.hZS.at[pl.ds(aligned(flip(z, o) * s.pr, 16), s.pr)],
            r.hZR.at[o - 1],
            r.x_rb.at[4],
            r.rb.at[4],
            zpeer(o),
        ).start()
    spread(0)
    spread(1)
    spread(2)
    share_sum(3)
    got(r.hZR, r.rb.at[4])
    total = r.hZS[pl.ds(aligned(z * s.pr, 16), s.pr), :].astype(F32)
    for o in range(1, W):
        total = total + r.hZR[o - 1].astype(F32)
    mine = pl.ds(aligned(c * s.pr, 16), s.pr)
    r.hFG[mine, :] = total.astype(BF)
    for oc in range(1, C):
        part = r.hFG.at[mine]
        remote(part, part, r.x_rc.at[4], r.rc.at[4], cpeer(oc)).start()

    got(r.Rk.at[pl.ds(0, (E - 1) * cp)], r.back.at[1])
    r.layer_out[...] = (r.middle[...] + gate * dot(r.pt[...], r.Rk[...].astype(BF))).astype(BF)

    share_sum(0)
    share_sum(1)
    share_sum(2)
    got(r.hFG.at[pl.ds(0, (C - 1) * s.pr)], r.rc.at[4])

    def unpad(value):
        return dot(r.unsel[...], value) if s.padded else value.astype(F32)

    r.smalls[...] = unpad(r.hFG[...])
    for m in (3, 0, 1, 2):
        got(r.FG.at[m, :, there], r.rd.at[m])
        r.grads[m] = unpad(r.FG[m]).astype(r.grads.dtype)

    for step in range(max(0, s.F // tile - slots), s.F // tile):
        save_out(step).wait()
    for step in range(max(0, D // tile - slots), D // tile):
        save_in(step).wait()
    sent(r.smg.at[pl.ds(0, W - 1)], r.x_sm)
    for m in range(4):
        sent(r.wfull.at[m, pl.ds(0, (W - 1) * s.pw), here], r.x_wa.at[m])
        if s.team > 1:
            sent(r.wfull.at[m, pl.ds(0, (W - 1) * (s.team - 1) * s.pw), here], r.x_wb.at[m])
        sent(r.wfull.at[m, :, here], r.x_wc.at[m])
        sent(r.fac.at[m], r.x_sibF.at[m])
        sent(r.GR.at[m], r.x_ra.at[m])
        sent(r.ZR.at[m], r.x_rb.at[m])
        sent(r.FG.at[m, pl.ds(0, (C - 1) * s.pr), here], r.x_rc.at[m])
        sent(r.FG.at[m, :, here], r.x_rd.at[m])
    for index, buffer in enumerate((r.gsend, r.nsend, r.tsend)):
        sent(buffer.at[pl.ds(0, E - 1)], r.x_d1.at[index])
    line_sent(r.Nr, r.x_nu, r.x_nd)
    sent(r.Tr.at[pl.ds(0, (W - 1) * R)], r.x_t2)
    for o in range(1, W):
        sent(r.SS.at[0, :, pl.ds(0, D)], r.x_r3.at[o])
    sent(r.Sk.at[pl.ds(0, (E - 1) * cp)], r.x_back.at[0])
    sent(r.Rk.at[pl.ds(0, (E - 1) * cp)], r.x_back.at[1])
    sent(r.nT.at[:, pl.ds(0, T)], r.x_sibT.at[0])
    sent(r.mT.at[:, pl.ds(0, T)], r.x_sibT.at[1])
    sent(r.hGR, r.x_ra.at[4])
    sent(r.hZR, r.x_rb.at[4])
    sent(r.hFG.at[pl.ds(0, (C - 1) * s.pr)], r.x_rc.at[4])
    sent(r.smo, r.x_rd.at[4])


def selection(s):
    share = s.SR // s.C
    unsel = np.zeros((s.SR, s.CP), np.float32)
    for chip in range(s.C):
        for at in range(share):
            unsel[chip * share + at, chip * s.pr + at] = 1
    return jnp.asarray(unsel, BF)


def local(
    tokens,
    norm_gain_attn,
    w_query,
    w_key,
    w_value,
    w_output,
    rel_bias,
    norm_gain_ffn,
    w_router,
    w_in,
    w_out,
    out_grad,
    expert_ids,
    priority,
    lengths,
    seq_order,
    relpos_table,
):
    tok_count, width = tokens.shape
    buckets_here, heads = rel_bias.shape
    n_experts = w_router.shape[1]
    s = plan(
        lax.axis_size("expert"),
        lax.axis_size("wshard"),
        tok_count,
        width,
        heads,
        buckets_here,
        n_experts,
        w_in.shape[2],
    )
    gap = jnp.zeros((s.SR, GAIN_ATTN_LANE - n_experts), BF)
    small = jnp.concatenate(
        [w_router, gap, norm_gain_attn[:, None], norm_gain_ffn[:, None]], axis=1
    )
    bias = jnp.pad(rel_bias, ((0, s.NBP - buckets_here), (0, LANES - heads)))
    small = jnp.concatenate([small, bias], axis=0)
    table = jnp.pad(jnp.stack([relpos_table, relpos_table[::-1]]), ((0, 0), (0, 1)))
    operands = [
        lengths, seq_order, small, expert_ids, priority.reshape(1, tok_count), table,
        tokens, out_grad, w_query, w_key, w_value, w_output, w_in, w_out,
    ]
    smem, vmem, anywhere = (
        pl.BlockSpec(memory_space=space) for space in (pltpu.SMEM, pltpu.VMEM, pl.ANY)
    )
    in_specs = [smem] * 2 + [vmem] * 4 + [anywhere] * 8
    names = IN_NAMES
    if s.padded:
        operands.append(selection(s))
        in_specs.append(vmem)
        names = names + PAD_NAMES
    spilled = (jax.ShapeDtypeStruct(pieces_shape(s), BF),) if s.padded else ()
    scratch = scratch_list(s)
    names = names + OUT_NAMES + ("GR",) * len(spilled) + tuple(name for name, _ in scratch)
    outs = pl.pallas_call(
        functools.partial(kernel, s, names),
        name="layer",
        out_shape=(
            jax.ShapeDtypeStruct((s.T, s.D), BF),
            jax.ShapeDtypeStruct((s.T, s.D), F32),
            jax.ShapeDtypeStruct((4, s.SR, s.D), BF),
            jax.ShapeDtypeStruct((s.SR, LANES), F32),
            jax.ShapeDtypeStruct((1, s.D, s.F), F32),
            jax.ShapeDtypeStruct((1, s.F, s.D), F32),
            *spilled,
        ),
        in_specs=in_specs,
        out_specs=(vmem, vmem, vmem, vmem, anywhere, anywhere) + (anywhere,) * len(spilled),
        scratch_shapes=[shape for _, shape in scratch],
        compiler_params=pltpu.CompilerParams(
            collective_id=0, has_side_effects=True, vmem_limit_bytes=62 * 2**20
        ),
    )(*operands)
    layer_out, tokens_grad, grads, smalls, grad_w_in, grad_w_out = outs[:6]
    return (
        layer_out,
        tokens_grad,
        smalls[:, GAIN_ATTN_LANE],
        grads[0].astype(F32),
        grads[1].astype(F32),
        grads[2].astype(F32),
        grads[3].astype(F32),
        smalls[:buckets_here, REL_LANE : REL_LANE + heads],
        smalls[:, GAIN_FFN_LANE],
        smalls[:, :n_experts],
        grad_w_in,
        grad_w_out,
    )


def solution(mesh):
    rows = P(("expert", "wshard"), None)
    shard = P("wshard", None)
    into, outof = P("expert", None, "wshard"), P("expert", "wshard", None)
    return jax.shard_map(
        local,
        mesh=mesh,
        in_specs=(
            rows,
            P("wshard"),
            shard,
            shard,
            shard,
            shard,
            shard,
            P("wshard"),
            shard,
            into,
            outof,
            rows,
            rows,
            P(("expert", "wshard")),
            P(),
            P(),
            P(),
        ),
        out_specs=(
            rows,
            rows,
            P("wshard"),
            shard,
            shard,
            shard,
            shard,
            shard,
            P("wshard"),
            shard,
            into,
            outof,
        ),
        check_vma=False,
    )
```

```python
import functools
import types

import jax
import jax.numpy as jnp
import numpy as np
from jax import lax
from jax.experimental import pallas as pl
from jax.experimental.pallas import tpu as pltpu
from jax.sharding import PartitionSpec as P

EPSILON = 1e-06
NEG_FILL = -1e30
GELU_A = 0.79788456
GELU_B = 0.044715
LANES = 128
REL_LANE = 64
GAIN_ATTN_LANE = 126
GAIN_FFN_LANE = 127
MESH = pl.DeviceIdType.MESH
BF = jnp.bfloat16
F32 = jnp.float32
I32 = jnp.int32


def up16(count):
    return -(-count // 16) * 16


def dot(a, b):
    return jnp.dot(a, b, preferred_element_type=F32)


def dot_rt(a, b):
    return lax.dot_general(a, b, (((1,), (1,)), ((), ())), preferred_element_type=F32)


def dot_lt(a, b):
    return lax.dot_general(a, b, (((0,), (0,)), ((), ())), preferred_element_type=F32)


def iota(shape, axis):
    return lax.broadcasted_iota(I32, shape, axis)


def flip(index, offset):
    out = index
    bit = 1
    while bit <= offset:
        if offset & bit:
            out = out + bit * (1 - 2 * lax.rem(lax.div(index, bit), 2))
        bit *= 2
    return out


def aligned(value, step):
    return pl.multiple_of(value, step)


def two_parts(value):
    high = value.astype(BF)
    return high, (value - high.astype(F32)).astype(BF)


def plan(expert_size, shard_size, tok_count, width, heads, buckets_here, n_experts, hidden):
    s = types.SimpleNamespace()
    s.E, s.W = expert_size, shard_size
    s.C = expert_size // 2
    s.T, s.D, s.H = tok_count, width, heads
    s.HD = width // heads
    s.F = hidden
    s.NX = n_experts
    s.cap = tok_count // n_experts
    s.cp = s.cap if s.cap % 8 == 0 else up16(s.cap)
    s.dt = BF if s.cp % 16 == 0 else F32
    s.S = n_experts * s.cp
    s.R = s.E * s.cp
    s.SR = width // shard_size
    s.NBH = buckets_here
    s.NBP = up16(buckets_here)
    s.half = width // 2
    s.P1 = up16(n_experts + 2)
    s.LW = -(-s.SR // LANES) * LANES
    team = s.C
    while s.SR % team or (s.SR // team) % 16:
        team //= 2
    s.team = team
    s.pw = s.SR // team
    s.pr = up16(s.SR // s.C)
    s.CP = s.C * s.pr
    s.Dp = s.W * s.CP
    s.padded = s.CP != s.SR
    s.tile = LANES
    s.slots = 2 if s.padded else max(width, hidden) // s.tile
    return s


def pieces_shape(s):
    return (4, s.C - 1, s.W * s.pr, s.half)


def arrivals(s):
    return (("Ga", s.D), ("Na", s.D), ("Ta", LANES)) if s.dt == F32 else ()


def scratch_list(s):
    V = pltpu.VMEM
    dma = pltpu.SemaphoreType.DMA
    return [
        ("wfull", V((4, s.D, s.D), BF)),
        ("smf", V((s.P1 + s.NBP, s.LW), F32)),
        ("smg", V((s.W, s.P1 + s.NBP, s.LW), BF)),
        ("tab", V((8, 2 * s.T), I32)),
        ("xb", V((s.T, s.D), BF)),
        ("og", V((s.T, s.D), BF)),
        ("wi", V((s.D, s.F), BF)),
        ("wo", V((s.F, s.D), BF)),
        ("pm", V((s.S, s.T), BF)),
        ("pt", V((s.T, s.S), BF)),
        ("gsend", V((s.NX, s.cp, s.D), s.dt)),
        ("nsend", V((s.NX, s.cp, s.D), s.dt)),
        ("tsend", V((s.NX, s.cp, LANES), s.dt)),
        ("Gr", V((s.W * s.R, s.D), BF)),
        ("Nr", V((s.W * s.R, s.D), BF)),
        ("Tr", V((s.W * s.R, LANES), BF)),
        ("agr", V((s.W * s.R, s.F), BF)),
        ("act", V((s.W * s.R, s.F), BF)),
        ("ig", V((s.W * s.R, s.F), BF)),
        ("SS", V((s.W, s.R, s.D + LANES), BF)),
        ("Sin", V((s.W + 1, s.R, s.D + LANES), BF)),
        ("Sb", V((s.R, s.D + LANES), s.dt)),
        ("Sk", V((s.S, s.D + LANES), s.dt)),
        ("Rb", V((s.R, s.D), s.dt)),
        ("Rk", V((s.S, s.D), s.dt)),
        ("tb", V((LANES, 2 * s.T), F32)),
        ("ohm", V((s.W * s.NBP, 2 * s.T), BF)),
        ("rows", V((8, s.D), F32)),
        ("RwT", V((LANES, s.D), BF)),
        ("probs", V((s.H, s.T, s.T), F32)),
        ("q", V((s.T, s.D), BF)),
        ("kk", V((s.T, s.D), BF)),
        ("v", V((s.T, s.D), BF)),
        ("mixed", V((s.T, s.D), BF)),
        ("nf", V((s.T, s.D), BF)),
        ("middle", V((s.T, s.D), F32)),
        ("mg", V((s.T, s.D), F32)),
        ("att", V((s.T, s.D), BF)),
        ("dq", V((s.T, s.D), BF)),
        ("dk", V((s.T, s.D), BF)),
        ("dv", V((s.T, s.D), BF)),
        ("nT", V((s.Dp, 2 * s.T), BF)),
        ("mT", V((s.Dp, 2 * s.T), BF)),
        ("fac", V((4, s.T, s.half), BF)),
        ("GS", V((4, s.C, s.W * s.pr, s.half), BF)),
        ("ZS", V((4, s.W * s.pr, s.half), BF)),
        ("ZR", V((4, s.W - 1, s.pr, s.half), BF)),
        ("FG", V((4, s.CP, s.D), BF)),
        ("smo", V((s.Dp, LANES), BF)),
        ("sms", V((s.Dp, LANES), BF)),
        ("hGS", V((s.C, s.W * s.pr, LANES), BF)),
        ("hGR", V((s.C - 1, s.W * s.pr, LANES), BF)),
        ("hZS", V((s.W * s.pr, LANES), BF)),
        ("hZR", V((s.W - 1, s.pr, LANES), BF)),
        ("hFG", V((s.CP, LANES), BF)),
        ("bt", V((LANES, 2 * s.T), F32)),
        ("gwi", V((s.slots, s.tile, s.F), BF)),
        ("gwo", V((s.slots, s.tile, s.D), BF)),
        ("gwi_sem", dma((s.slots,))),
        ("gwo_sem", dma((s.slots,))),
        ("lsem", dma((9,))),
        ("smr", dma((s.W,))),
        ("wu", dma((2, s.W))),
        ("wd", dma((2, s.W))),
        ("wb", dma((2,))),
        ("wc", dma((2,))),
        ("g1", dma((s.C,))),
        ("gu", dma((s.W, s.C))),
        ("gd", dma((s.W, s.C))),
        ("n1", dma((s.C,))),
        ("nu", dma((s.W, s.C))),
        ("nd", dma((s.W, s.C))),
        ("t1", dma((s.C,))),
        ("t2", dma((s.W,))),
        ("su", dma((s.W, s.C))),
        ("sd", dma((s.W, s.C))),
        ("ru", dma((s.W,))),
        ("rdn", dma((s.W,))),
        ("back", dma((2,))),
        ("sibT", dma((2,))),
        ("sibF", dma((4,))),
        ("ra", dma((5,))),
        ("rb", dma((5,))),
        ("rc", dma((5,))),
        ("rd", dma((5,))),
        ("x_sm", dma),
        ("x_wu", dma((2, s.W))),
        ("x_wd", dma((2, s.W))),
        ("x_wb", dma((2,))),
        ("x_wc", dma((2,))),
        ("x_d1", dma((3,))),
        ("x_t2", dma),
        ("x_gu", dma((s.W,))),
        ("x_gd", dma((s.W,))),
        ("x_nu", dma((s.W,))),
        ("x_nd", dma((s.W,))),
        ("x_su", dma((s.W,))),
        ("x_sd", dma((s.W,))),
        ("x_ru", dma((s.W,))),
        ("x_rdn", dma((s.W,))),
        ("x_back", dma((2,))),
        ("x_sibT", dma((2,))),
        ("x_sibF", dma((4,))),
        ("x_ra", dma((5,))),
        ("x_rb", dma((5,))),
        ("x_rc", dma((5,))),
        ("x_rd", dma((5,))),
        ("credit", pltpu.SemaphoreType.REGULAR),
    ] + (
        [("gst", V((s.W * s.pr, s.half), BF))]
        + [(name, V((s.R, width), F32)) for name, width in arrivals(s)]
        if s.padded
        else [("GR", V(pieces_shape(s), BF))]
    )


IN_NAMES = (
    "lengths", "seq", "ids", "prio", "table", "router", "gain_attn", "gain_ffn", "bias",
    "tokens", "out_grad", "w0", "w1", "w2", "w3", "w_in", "w_out",
)
PAD_NAMES = ("unsel",)
OUT_NAMES = ("layer_out", "tokens_grad", "grads", "smalls", "grad_w_in", "grad_w_out")


def kernel(s, names, *refs):
    r = types.SimpleNamespace(**dict(zip(names, refs, strict=True)))
    e = lax.axis_index("expert")
    z = lax.axis_index("wshard")
    c = lax.div(e, 2)
    k = lax.rem(e, 2)
    T, D, E, W, C, R, cp, half = s.T, s.D, s.E, s.W, s.C, s.R, s.cp, s.half
    sib = (flip(e, 1), z)
    here = pl.ds(aligned(k * half, LANES), half)
    there = pl.ds(aligned((1 - k) * half, LANES), half)

    def zpeer(offset):
        return (e, flip(z, offset))

    def cpeer(offset):
        return (flip(c, offset) * 2 + k, z)

    def remote(src, dst, send, recv, device):
        return pltpu.make_async_remote_copy(
            src_ref=src, dst_ref=dst, send_sem=send, recv_sem=recv, device_id=device, device_id_type=MESH
        )

    def got(ref, sem):
        remote(ref, ref, sem, sem, sib).wait_recv()

    def sent(ref, sem):
        remote(ref, ref, sem, sem, sib).wait_send()

    shards = (r.w0, r.w1, r.w2, r.w3)
    own_rows = pl.ds(aligned(z * s.SR, 16), s.SR)
    load_w = [
        pltpu.make_async_copy(shards[m].at[:, here], r.wfull.at[m, own_rows, here], r.lsem.at[m])
        for m in range(4)
    ]
    load_og = pltpu.make_async_copy(r.out_grad, r.og, r.lsem.at[4])
    load_x = pltpu.make_async_copy(r.tokens, r.xb, r.lsem.at[5])
    load_wo = pltpu.make_async_copy(r.w_out.at[0], r.wo, r.lsem.at[6])
    load_wi = pltpu.make_async_copy(r.w_in.at[0], r.wi, r.lsem.at[7])
    for copy in (*load_w, load_og, load_x, load_wo, load_wi):
        copy.start()

    r.smf[...] = jnp.zeros_like(r.smf)
    r.smf[0 : s.NX, 0 : s.SR] = r.router[...].astype(F32)
    r.smf[s.NX : s.NX + 1, 0 : s.SR] = r.gain_attn[...].astype(F32).reshape(1, s.SR)
    r.smf[s.NX + 1 : s.NX + 2, 0 : s.SR] = r.gain_ffn[...].astype(F32).reshape(1, s.SR)
    r.smf[s.P1 : s.P1 + s.NBH, 0 : s.H] = r.bias[...].astype(F32)
    r.smg[z] = r.smf[...].astype(BF)

    barrier = pltpu.get_barrier_semaphore()
    peers = [(flip(e, o), z) for o in range(1, E)] + [zpeer(o) for o in range(1, W)]
    for peer in peers:
        pl.semaphore_signal(barrier, inc=1, device_id=peer, device_id_type=MESH)
    pl.semaphore_wait(barrier, len(peers))

    team_c = lax.rem(c, s.team)
    for o in range(1, W):
        remote(r.smg.at[z], r.smg.at[z], r.x_sm, r.smr.at[o], zpeer(o)).start()
    share_rows = pl.ds(aligned(team_c * s.pw, 16), s.pw)
    groups = (pl.ds(0, 3), pl.ds(3, 1))
    members = ((0, 1, 2), (3,))

    def weight_at(plane):
        return pl.ds(aligned(plane * s.SR + team_c * s.pw, 16), s.pw)

    def weight_own(g):
        def send(sender, receiver, to):
            for m in members[g]:
                source = shards[m].at[share_rows, here]
                remote(source, r.wfull.at[m, weight_at(z), here], sender, receiver, (e, to)).start()

        pl.when(z < W - 1)(functools.partial(send, r.x_wu.at[g, 0], r.wu.at[g, 1], z + 1))
        pl.when(z > 0)(functools.partial(send, r.x_wd.at[g, 0], r.wd.at[g, 1], z - 1))

    weight_own(0)
    device = e * W + z
    first = r.lengths[r.seq[2 * device]]
    both = first + r.lengths[r.seq[2 * device + 1]]
    col = iota((T, 1), 0)
    row = iota((1, T), 1)
    seg_col = (col >= first).astype(I32) + (col >= both).astype(I32)
    seg_row = (row >= first).astype(I32) + (row >= both).astype(I32)
    same = seg_col == seg_row
    valid = (col < both).astype(F32)
    eye = iota((T, T), 0) == iota((T, T), 1)
    id_row = r.ids[...].astype(F32)
    id_col = jnp.sum(jnp.where(eye, id_row, 0.0), axis=1, keepdims=True)
    prio_row = r.prio[...].astype(F32)
    prio_col = jnp.sum(jnp.where(eye, prio_row, 0.0), axis=1, keepdims=True)
    ahead = (id_col == id_row) & (prio_col < prio_row)
    slot_row = jnp.sum(jnp.where(ahead, valid, 0.0), axis=0, keepdims=True)
    kept = (row < both) & (slot_row < s.cap)
    flat_row = jnp.where(kept, id_row * cp + slot_row, -1.0)
    flat_col = jnp.sum(jnp.where(eye, flat_row, 0.0), axis=1, keepdims=True)
    r.pm[...] = (iota((s.S, T), 0).astype(F32) == flat_row).astype(F32).astype(BF)
    r.pt[...] = (iota((T, s.S), 1).astype(F32) == flat_col).astype(F32).astype(BF)

    plane_step = 16 if s.dt == BF else 8
    plane_rows = z * R if s.dt == BF else 0

    def dispatch(index, send, rows, first_sem, value):
        width = rows.shape[1]
        buffer = dot(r.pm[...], value)
        send[...] = buffer.astype(s.dt).reshape(s.NX, cp, width)
        mine = pl.ds(aligned(plane_rows + e * cp, plane_step), cp)
        for o in range(1, E):
            x = flip(e, o)
            remote(
                send.at[x], rows.at[mine], r.x_d1.at[index], first_sem.at[o // 2], (x, z)
            ).start()
        rows[mine, :] = send[e]

    def block_at(plane, oc):
        return pl.ds(aligned(plane * R + flip(c, oc) * 2 * cp, 16), 2 * cp)

    def landed(rows, arrived, first_sem, oc):
        got(arrived.at[pl.ds(0, (2 if oc else 1) * cp)], first_sem.at[oc])
        if s.dt != BF:
            rows[block_at(z, oc), :] = arrived[block_at(0, oc), :].astype(BF)

    def move(part, send, recv, to):
        remote(part, part, send, recv, (e, to)).start()

    def line_own(rows, arrived, first_sem, up, down, x_up, x_down):
        for oc in range(C):
            landed(rows, arrived, first_sem, oc)
            part = rows.at[block_at(z, oc)]
            pl.when(z < W - 1)(functools.partial(move, part, x_up.at[0], up.at[1, oc], z + 1))
            pl.when(z > 0)(functools.partial(move, part, x_down.at[0], down.at[1, oc], z - 1))

    def line_pass(rows, d, up, down, x_up, x_down):
        for oc in range(C):

            @pl.when(z >= d)
            def _():
                part = rows.at[block_at(z - d, oc)]
                got(part, up.at[d, oc])
                if d < W - 1:
                    pl.when(z < W - 1)(
                        functools.partial(move, part, x_up.at[d], up.at[d + 1, oc], z + 1)
                    )

            @pl.when(z + d <= W - 1)
            def _():
                part = rows.at[block_at(z + d, oc)]
                got(part, down.at[d, oc])
                if d < W - 1:
                    pl.when(z > 0)(
                        functools.partial(move, part, x_down.at[d], down.at[d + 1, oc], z - 1)
                    )

    def line_sent(rows, x_up, x_down):
        for d in range(W - 1):
            whole = rows.at[pl.ds(0, R)]
            pl.when((z >= d) & (z < W - 1))(functools.partial(sent, whole, x_up.at[d]))
            pl.when((z + d <= W - 1) & (z > 0))(functools.partial(sent, whole, x_down.at[d]))

    g_line = (r.gu, r.gd, r.x_gu, r.x_gd)
    n_line = (r.nu, r.nd, r.x_nu, r.x_nd)
    Ga, Na, Ta = (r.Gr, r.Nr, r.Tr) if s.dt == BF else (r.Ga, r.Na, r.Ta)
    load_og.wait()
    dispatch(0, r.gsend, Ga, r.g1, r.og[...])

    def weight_pass(g, d):
        def handle(plane, arrived, onward, sender, receiver, to):
            part = r.wfull.at[groups[g], weight_at(plane), here]
            got(part, arrived)
            if d < W - 1:
                pl.when(onward)(functools.partial(move, part, sender, receiver, to))
            for oc in range(1, s.team):
                remote(part, part, r.x_wb.at[g], r.wb.at[g], cpeer(oc)).start()

        after = min(d + 1, W - 1)
        pl.when(z >= d)(
            functools.partial(
                handle, z - d, r.wu.at[g, d], z < W - 1, r.x_wu.at[g, d], r.wu.at[g, after], z + 1
            )
        )
        pl.when(z + d <= W - 1)(
            functools.partial(
                handle, z + d, r.wd.at[g, d], z > 0, r.x_wd.at[g, d], r.wd.at[g, after], z - 1
            )
        )

    team_rows = pl.ds(0, (W - 1) * (s.team - 1) * s.pw)

    def to_sibling(g):
        if s.team > 1:
            got(r.wfull.at[groups[g], team_rows, here], r.wb.at[g])
        for m in members[g]:
            load_w[m].wait()
        part = r.wfull.at[groups[g], :, here]
        remote(part, part, r.x_wc.at[g], r.wc.at[g], sib).start()

    def weight_ready(g):
        got(r.wfull.at[groups[g], :, there], r.wc.at[g])

    for d in range(1, W):
        weight_pass(0, d)
        if d == 1:
            weight_own(1)
        else:
            weight_pass(1, d - 1)
        if d == min(2, W - 1):
            line_own(r.Gr, Ga, r.g1, *g_line)
    weight_pass(1, W - 1)
    for o in range(1, W):
        got(r.smg.at[0], r.smr.at[o])
    gathered = jnp.concatenate(
        [r.smg[w, : s.P1, : s.SR].astype(F32) for w in range(W)], axis=1
    )
    r.rows[0:1, :] = gathered[s.NX : s.NX + 1]
    r.rows[1:2, :] = gathered[s.NX + 1 : s.NX + 2]
    r.RwT[...] = jnp.zeros_like(r.RwT)
    r.RwT[: s.P1, :] = jnp.where(iota((s.P1, D), 0) < s.NX, gathered, 0.0).astype(BF)
    lane_row = iota((1, LANES), 1)
    r.tab[...] = jnp.full(r.tab.shape, -1, I32)
    r.tab[0:1, 0 : 2 * T - 1] = r.table[...]
    bucket = r.tab[0:1, :]
    shift = s.NBH.bit_length() - 1
    bucket = lax.shift_right_logical(bucket, shift) * s.NBP + lax.bitwise_and(bucket, s.NBH - 1)
    bucket = jnp.where(r.tab[0:1, :] < 0, -1, bucket)
    hot = (iota((W * s.NBP, 2 * T), 0) == bucket).astype(F32).astype(BF)
    backwards = (iota((2 * T, 2 * T), 0) + iota((2 * T, 2 * T), 1) == 2 * T - 2).astype(F32)
    r.ohm[...] = dot(hot, backwards.astype(BF)).astype(BF)
    bias_rows = r.smg[:, s.P1 :, :LANES].reshape(W * s.NBP, LANES)
    r.tb[...] = dot_lt(bias_rows, hot)

    def bias_head(h, carry):
        wide = jnp.broadcast_to(r.tb[pl.ds(h, 1), :], (T, 2 * T))
        turned = pltpu.roll(wide, T + 1, 1, stride=1, stride_axis=0)
        r.probs[h] = jnp.where(same, turned[:, :T], NEG_FILL)
        return carry

    lax.fori_loop(0, s.H, bias_head, 0)
    to_sibling(0)
    load_x.wait()
    x = r.xb[...].astype(F32)
    scale1 = lax.rsqrt(jnp.mean(x * x, axis=1, keepdims=True) + EPSILON)
    normed = (x * scale1 * r.rows[0:1, :]).astype(BF)

    def spread_rows(value):
        if not s.padded:
            return value
        shards = [value[at : at + s.SR] for at in range(0, D, s.SR)]
        return jnp.concatenate([dot_lt(r.unsel[...], shard) for shard in shards], axis=0).astype(BF)

    def turn_out(index, value, target):
        target[:, :T] = spread_rows(value.T)
        remote(
            target.at[:, pl.ds(0, T)], target.at[:, pl.ds(T, T)], r.x_sibT.at[index], r.sibT.at[index], sib
        ).start()

    turn_out(0, normed, r.nT)
    weight_ready(0)
    r.q[...] = dot(normed, r.wfull[0]).astype(BF)
    r.kk[...] = dot(normed, r.wfull[1]).astype(BF)
    r.v[...] = dot(normed, r.wfull[2]).astype(BF)
    to_sibling(1)
    line_pass(r.Gr, 1, *g_line)

    scale = s.HD ** (-0.5)
    low_lane = (lane_row < s.HD).astype(F32)
    lane_masks = (low_lane.astype(BF), (1.0 - low_lane).astype(BF))

    def attend(p, carry):
        cols = pl.ds(aligned(p * LANES, LANES), LANES)
        q, kk, v = r.q[:, cols], r.kk[:, cols], r.v[:, cols]
        outs = []
        for side in range(2):
            h = 2 * p + side
            scores = dot_rt(q * lane_masks[side], kk) * scale + r.probs[h]
            expo = jnp.exp(scores - jnp.max(scores, axis=1, keepdims=True))
            probs = expo * (1.0 / jnp.sum(expo, axis=1, keepdims=True))
            r.probs[h] = probs
            outs.append(dot(probs.astype(BF), v))
        r.mixed[:, cols] = jnp.where(lane_row < s.HD, outs[0], outs[1]).astype(BF)
        return carry

    lax.fori_loop(0, s.H // 2, attend, 0)
    mixed = r.mixed[...]
    weight_ready(1)
    middle = r.xb[...].astype(F32) + dot(mixed, r.wfull[3]) * valid
    r.middle[...] = middle
    scale2 = lax.rsqrt(jnp.mean(middle * middle, axis=1, keepdims=True) + EPSILON)
    nf = (middle * scale2 * r.rows[1:2, :]).astype(BF)
    r.nf[...] = nf
    dispatch(1, r.nsend, Na, r.n1, nf)
    logits = jnp.where(lane_row < s.NX, dot_rt(nf, r.RwT[...]), NEG_FILL)
    raised = jnp.exp(logits - jnp.max(logits, axis=1, keepdims=True))
    router = raised / jnp.sum(raised, axis=1, keepdims=True)
    picked = (lane_row.astype(F32) == id_col).astype(F32)
    gate = jnp.sum(router * picked, axis=1, keepdims=True)
    gate_high, gate_rest = two_parts(gate)
    gate_mid, gate_low = two_parts(gate - gate_high.astype(F32))
    gate_lanes = jnp.where(
        lane_row == 0,
        gate_high.astype(F32),
        jnp.where(lane_row == 1, gate_mid.astype(F32), jnp.where(lane_row == 2, gate_low.astype(F32), 0.0)),
    )
    dispatch(2, r.tsend, Ta, r.t1, gate_lanes.astype(BF))
    if W > 2:
        line_pass(r.Gr, 2, *g_line)
    line_own(r.Nr, Na, r.n1, *n_line)
    for oc in range(C):
        landed(r.Tr, Ta, r.t1, oc)
        for o in range(1, W):
            part = r.Tr.at[block_at(z, oc)]
            remote(part, part, r.x_t2, r.t2.at[o], zpeer(o)).start()
    turn_out(1, mixed, r.mT)

    load_wo.wait()
    for d in range(3, W):
        line_pass(r.Gr, d, *g_line)

    def back_rows(step, carry):
        at = pl.ds(aligned(step * R, 16), R)
        r.agr[at, :] = dot_rt(r.Gr[at, :], r.wo[...]).astype(BF)
        return carry

    lax.fori_loop(0, W, back_rows, 0)
    load_wi.wait()

    def lanes_of(value):
        high, rest = two_parts(value)
        return jnp.where(
            lane_row == 0, high.astype(F32), jnp.where(lane_row == 1, rest.astype(F32), 0.0)
        )

    def expert(plane):
        at = pl.ds(aligned(plane * R, 16), R)
        inner = dot(r.Nr[at, :], r.wi[...])
        square = inner * inner
        tanh = jnp.tanh(GELU_A * inner * (1.0 + GELU_B * square))
        active = (0.5 * inner * (1.0 + tanh)).astype(BF)
        slope = 0.5 * (1.0 + tanh) + (0.5 * GELU_A) * inner * (1.0 - tanh * tanh) * (
            1.0 + (3.0 * GELU_B) * square
        )
        back = r.agr[at, :].astype(F32)
        inner_grad = (back * slope).astype(BF)
        r.act[at, :] = active
        r.ig[at, :] = inner_grad
        r.SS[plane, :, :D] = dot_rt(inner_grad, r.wi[...]).astype(BF)
        r.SS[plane, :, D:] = lanes_of(
            jnp.sum(active.astype(F32) * back, axis=1, keepdims=True)
        ).astype(BF)

    def merge(plane, slot, block):
        own, other = r.SS[plane, block, :].astype(F32), r.Sin[slot, block, :].astype(F32)
        r.SS[plane, block, :D] = (own[:, :D] + other[:, :D]).astype(BF)
        r.SS[plane, block, D:] = lanes_of(
            jnp.sum(own[:, D:] + other[:, D:], axis=1, keepdims=True)
        ).astype(BF)

    def plane_back(index, source, target, offsets):
        mine = pl.ds(aligned(e * cp, plane_step), cp)
        for o in offsets:
            if o == 0:
                target[mine, :] = source[mine, :]
                continue
            x = flip(e, o)
            remote(
                source.at[pl.ds(aligned(x * cp, plane_step), cp)],
                target.at[mine],
                r.x_back.at[index],
                r.back.at[index],
                (x, z),
            ).start()

    expert(z)
    for step in range(1, 2 * W - 2):
        if step < W:
            line_pass(r.Nr, step, *n_line)

            def sides(side, carry, step=step):
                plane = z + (2 * side - 1) * step
                pl.when((plane >= 0) & (plane < W))(functools.partial(expert, plane))
                return carry

            lax.fori_loop(0, 2, sides, 0)

        plane_down = 2 * W - 2 - z - step
        gap_down = z - plane_down
        plane_up = step - z
        gap_up = plane_up - z

        @pl.when((plane_down >= 0) & (gap_down >= 1))
        def _():
            for oc in range(C):
                block = block_at(0, oc)

                @pl.when(z < W - 1)
                def _():
                    got(r.Sin.at[plane_down, block], r.sd.at[gap_down, oc])
                    merge(plane_down, plane_down, block)

                remote(
                    r.SS.at[plane_down, block],
                    r.Sin.at[plane_down, block],
                    r.x_sd.at[gap_down],
                    r.sd.at[gap_down - 1, oc],
                    (e, z - 1),
                ).start()

        @pl.when((plane_up <= W - 1) & (gap_up >= 1))
        def _():
            for oc in range(C):
                block = block_at(0, oc)

                @pl.when(z > 0)
                def _():
                    got(r.Sin.at[plane_up + 1, block], r.su.at[gap_up, oc])
                    merge(plane_up, plane_up + 1, block)

                remote(
                    r.SS.at[plane_up, block],
                    r.Sin.at[plane_up + 1, block],
                    r.x_su.at[gap_up],
                    r.su.at[gap_up - 1, oc],
                    (e, z + 1),
                ).start()

    for oc in range(C):
        block = block_at(0, oc)

        @pl.when(z < W - 1)
        def _():
            got(r.Sin.at[z, block], r.sd.at[0, oc])
            merge(z, z, block)

        @pl.when(z > 0)
        def _():
            got(r.Sin.at[z + 1, block], r.su.at[0, oc])
            merge(z, z + 1, block)

        r.Sb[block, :] = r.SS[z, block, :].astype(s.dt)
        plane_back(0, r.Sb, r.Sk, (2 * oc, 2 * oc + 1))

    line_sent(r.Gr, r.x_gu, r.x_gd)
    for o in range(1, W):
        got(r.Tr.at[pl.ds(0, R)], r.t2.at[o])

    def scale_rows(step, carry):
        at = pl.ds(aligned(step * R, 16), R)
        gates = jnp.sum(r.Tr[at, :].astype(F32), axis=1, keepdims=True)
        r.Gr[at, :] = (r.Gr[at, :].astype(F32) * gates).astype(BF)
        r.ig[at, :] = (r.ig[at, :].astype(F32) * gates).astype(BF)
        return carry

    lax.fori_loop(0, W, scale_rows, 0)
    tile, slots = s.tile, s.slots

    def save_out(step):
        slot = lax.rem(step, slots)
        at = pl.ds(aligned(step * tile, LANES), tile)
        return pltpu.make_async_copy(r.gwo.at[slot], r.grad_w_out.at[at], r.gwo_sem.at[slot])

    def save_in(step):
        slot = lax.rem(step, slots)
        at = pl.ds(aligned(step * tile, LANES), tile)
        return pltpu.make_async_copy(r.gwi.at[slot], r.grad_w_in.at[at], r.gwi_sem.at[slot])

    def grad_out_tile(step, carry):
        @pl.when(step >= slots)
        def _():
            save_out(step - slots).wait()

        at = pl.ds(aligned(step * tile, LANES), tile)
        r.gwo[lax.rem(step, slots)] = dot_lt(r.act[:, at], r.Gr[...]).astype(BF)
        save_out(step).start()
        return carry

    def grad_in_tile(step, carry):
        @pl.when(step >= slots)
        def _():
            save_in(step - slots).wait()

        at = pl.ds(aligned(step * tile, LANES), tile)
        r.gwi[lax.rem(step, slots)] = dot_lt(r.Nr[:, at], r.ig[...]).astype(BF)
        save_in(step).start()
        return carry

    lax.fori_loop(0, s.F // tile, grad_out_tile, 0)
    lax.fori_loop(0, D // tile, grad_in_tile, 0)

    for o in range(1, W):
        pl.semaphore_signal(r.credit, inc=1, device_id=zpeer(o), device_id_type=MESH)
    for d in range(1, W):
        pl.when(z >= d)(functools.partial(sent, r.SS.at[0], r.x_sd.at[d]))
        pl.when(z + d <= W - 1)(functools.partial(sent, r.SS.at[0], r.x_su.at[d]))
    pl.semaphore_wait(r.credit, W - 1)

    def results(step, carry):
        at = pl.ds(aligned(step * R, 16), R)
        r.SS[step, :, :D] = dot(r.act[at, :], r.wo[...]).astype(BF)
        return carry

    lax.fori_loop(0, W, results, 0)
    body = pl.ds(0, D)

    def result_down(plane):
        remote(
            r.SS.at[plane, :, body],
            r.Sin.at[plane, :, body],
            r.x_rdn.at[z - plane],
            r.rdn.at[z - plane - 1],
            (e, z - 1),
        ).start()

    def result_up(plane):
        remote(
            r.SS.at[plane, :, body],
            r.Sin.at[plane + 1, :, body],
            r.x_ru.at[plane - z],
            r.ru.at[plane - z - 1],
            (e, z + 1),
        ).start()

    def result_merge(plane, slot, sem):
        got(r.Sin.at[slot, :, body], sem)
        r.SS[plane, :, :D] = (
            r.SS[plane, :, :D].astype(F32) + r.Sin[slot, :, :D].astype(F32)
        ).astype(BF)

    def results_pass(step):
        if step == 0:

            @pl.when(z == W - 1)
            def _():
                for plane in range(W - 1):
                    result_down(plane)

            @pl.when(z == 0)
            def _():
                for plane in range(W - 1, 0, -1):
                    result_up(plane)

            return
        below = step - (W - 1 - z)
        above = W - 1 - step + z

        @pl.when((z < W - 1) & (below >= 0) & (below < z))
        def _():
            result_merge(below, below, r.rdn.at[z - below])
            result_down(below)

        @pl.when((z > 0) & (above <= W - 1) & (above > z))
        def _():
            result_merge(above, above + 1, r.ru.at[above - z])
            result_up(above)

    results_pass(0)
    got(r.Sk.at[pl.ds(0, (E - 1) * cp)], r.back.at[0])
    returned = dot(r.pt[...], r.Sk[...].astype(BF))
    gate_grad = jnp.sum(returned[:, D:], axis=1, keepdims=True)
    logit_grad = (gate * gate_grad * (picked - router)).astype(BF)
    nf_grad = dot(logit_grad, r.RwT[...]) + gate * returned[:, :D]
    middle = r.middle[...]
    along = nf_grad * r.rows[1:2, :]
    middle_grad = (
        r.og[...].astype(F32)
        + scale2 * along
        - middle * (scale2 * scale2 * scale2 * jnp.mean(along * middle, axis=1, keepdims=True))
    )
    r.mg[...] = middle_grad
    r.rows[2:3, :] = jnp.sum(nf_grad * middle * scale2, axis=0, keepdims=True)
    r.att[...] = (middle_grad * valid).astype(BF)
    attended_grad = r.att[...]

    def share(m, source):
        remote(source.at[:, there], r.fac.at[m], r.x_sibF.at[m], r.sibF.at[m], sib).start()

    share(3, r.att)
    r.mixed[...] = dot_rt(attended_grad, r.wfull[3]).astype(BF)
    router_grad = dot_lt(logit_grad, r.nf[...])

    def plane_sum(m, left, source):
        got(r.fac.at[m], r.sibF.at[m])

        def block(step, carry):
            at = pl.ds(aligned(step * s.CP, 16), s.CP)
            part = dot(left[at, :T], source[:, here]) + dot(left[at, T:], r.fac[m])
            part = part.astype(BF)
            for chip in range(C):
                r.GS[m, chip, pl.ds(aligned(step * s.pr, 16), s.pr), :] = part[
                    chip * s.pr : (chip + 1) * s.pr
                ]
            return carry

        lax.fori_loop(0, W, block, 0)
        for oc in range(1, C):
            remote(
                r.GS.at[m, flip(c, oc)], r.GR.at[m, oc - 1], r.x_ra.at[m], r.ra.at[m], cpeer(oc)
            ).start()

    got(r.mT.at[:, pl.ds(T, T)], r.sibT.at[1])
    plane_sum(3, r.mT, r.att)

    def attend_back(p, carry):
        cols = pl.ds(aligned(p * LANES, LANES), LANES)
        q, kk, v, mixg = r.q[:, cols], r.kk[:, cols], r.v[:, cols], r.mixed[:, cols]
        outs = []
        for side in range(2):
            h = 2 * p + side
            probs = r.probs[h]
            prob_grad = dot_rt(mixg * lane_masks[side], v)
            inside = jnp.sum(probs * prob_grad, axis=1, keepdims=True)
            score_grad = (probs * (prob_grad - inside)).astype(BF)
            r.probs[h] = score_grad.astype(F32)
            outs.append(
                (
                    dot(score_grad, kk) * scale,
                    dot_lt(score_grad, q) * scale,
                    dot_lt(probs.astype(BF), mixg),
                )
            )
        low = lane_row < s.HD
        r.dq[:, cols] = jnp.where(low, outs[0][0], outs[1][0]).astype(BF)
        r.dk[:, cols] = jnp.where(low, outs[0][1], outs[1][1]).astype(BF)
        r.dv[:, cols] = jnp.where(low, outs[0][2], outs[1][2]).astype(BF)
        return carry

    lax.fori_loop(0, s.H // 2, attend_back, 0)
    share(0, r.dq)
    share(1, r.dk)
    share(2, r.dv)
    got(r.nT.at[:, pl.ds(T, T)], r.sibT.at[0])
    plane_sum(0, r.nT, r.dq)
    for step in range(1, W - 2):
        results_pass(step)

    def shard_sum(m):
        got(r.GR.at[m], r.ra.at[m])
        total = r.GS[m, c].astype(F32)
        for oc in range(1, C):
            if s.padded:
                fetch = pltpu.make_async_copy(r.GR.at[m, oc - 1], r.gst, r.lsem.at[8])
                fetch.start()
                fetch.wait()
            part = r.gst[...] if s.padded else r.GR[m, oc - 1]
            total = total + part.astype(F32)
        r.ZS[m] = total.astype(BF)
        for o in range(1, W):
            remote(
                r.ZS.at[m, pl.ds(aligned(flip(z, o) * s.pr, 16), s.pr)],
                r.ZR.at[m, o - 1],
                r.x_rb.at[m],
                r.rb.at[m],
                zpeer(o),
            ).start()

    def spread(m):
        got(r.ZR.at[m], r.rb.at[m])
        total = r.ZS[m, pl.ds(aligned(z * s.pr, 16), s.pr), :].astype(F32)
        for o in range(1, W):
            total = total + r.ZR[m, o - 1].astype(F32)
        mine = pl.ds(aligned(c * s.pr, 16), s.pr)
        r.FG[m, mine, here] = total.astype(BF)
        part = r.FG.at[m, mine, here]
        for oc in range(1, C):
            remote(part, part, r.x_rc.at[m], r.rc.at[m], cpeer(oc)).start()

    def share_sum(m):
        got(r.FG.at[m, pl.ds(0, (C - 1) * s.pr), here], r.rc.at[m])
        part = r.FG.at[m, :, here]
        remote(part, part, r.x_rd.at[m], r.rd.at[m], sib).start()

    normed_grad = (
        dot_rt(r.dq[...], r.wfull[0]) + dot_rt(r.dk[...], r.wfull[1]) + dot_rt(r.dv[...], r.wfull[2])
    )
    x = r.xb[...].astype(F32)
    along = normed_grad * r.rows[0:1, :]
    r.tokens_grad[...] = (
        r.mg[...]
        + scale1 * along
        - x * (scale1 * scale1 * scale1 * jnp.mean(along * x, axis=1, keepdims=True))
    )
    r.rows[3:4, :] = jnp.sum(normed_grad * x * scale1, axis=0, keepdims=True)
    shard_sum(3)
    plane_sum(1, r.nT, r.dk)

    r.bt[...] = jnp.zeros_like(r.bt)
    mirror = (iota((T, T), 0) + iota((T, T), 1) == T - 1).astype(F32).astype(BF)

    def bias_back(h, carry):
        mirrored = dot(r.probs[h].astype(BF), mirror)
        wide = jnp.concatenate([mirrored, jnp.zeros((T, T), F32)], axis=1)
        turned = pltpu.roll(wide, 0, 1, stride=1, stride_axis=0)
        r.bt[pl.ds(REL_LANE + h, 1), :] = jnp.sum(turned, axis=0, keepdims=True)
        return carry

    lax.fori_loop(0, s.H, bias_back, 0)
    shard_sum(0)
    plane_sum(2, r.nT, r.dv)
    high, rest = two_parts(r.bt[...])
    rel_grad = dot_rt(r.ohm[...], high) + dot_rt(r.ohm[...], rest)
    lane_col = iota((LANES, 1), 0)
    small = jnp.where(
        lane_col == GAIN_ATTN_LANE,
        r.rows[3:4, :],
        jnp.where(lane_col == GAIN_FFN_LANE, r.rows[2:3, :], router_grad),
    ).T
    blocks = []
    for block in range(W):
        part = small[block * s.SR : (block + 1) * s.SR]
        head = part[: s.NBP] + rel_grad[block * s.NBP : (block + 1) * s.NBP]
        blocks.append(jnp.concatenate([head, part[s.NBP :]], axis=0))
    small = jnp.concatenate(blocks, axis=0).astype(BF)
    r.smo[...] = spread_rows(small)
    remote(r.smo, r.sms, r.x_rd.at[4], r.rd.at[4], sib).start()
    if W > 2:
        results_pass(W - 2)
    spread(3)
    shard_sum(1)
    spread(0)
    got(r.sms, r.rd.at[4])
    pair = (r.smo[...].astype(F32) + r.sms[...].astype(F32)).astype(BF)
    for block in range(W):
        for chip in range(C):
            at = block * s.CP + chip * s.pr
            r.hGS[chip, block * s.pr : (block + 1) * s.pr, :] = pair[at : at + s.pr]
    for oc in range(1, C):
        remote(r.hGS.at[flip(c, oc)], r.hGR.at[oc - 1], r.x_ra.at[4], r.ra.at[4], cpeer(oc)).start()
    shard_sum(2)
    share_sum(3)
    spread(1)
    share_sum(0)
    pl.when(z < W - 1)(functools.partial(result_merge, z, z, r.rdn.at[0]))
    pl.when(z > 0)(functools.partial(result_merge, z, z + 1, r.ru.at[0]))
    r.Rb[...] = r.SS[z, :, :D].astype(s.dt)
    plane_back(1, r.Rb, r.Rk, range(E))

    got(r.hGR, r.ra.at[4])
    total = r.hGS[c].astype(F32)
    for oc in range(1, C):
        total = total + r.hGR[oc - 1].astype(F32)
    r.hZS[...] = total.astype(BF)
    for o in range(1, W):
        remote(
            r.hZS.at[pl.ds(aligned(flip(z, o) * s.pr, 16), s.pr)],
            r.hZR.at[o - 1],
            r.x_rb.at[4],
            r.rb.at[4],
            zpeer(o),
        ).start()
    share_sum(1)
    spread(2)
    got(r.hZR, r.rb.at[4])
    total = r.hZS[pl.ds(aligned(z * s.pr, 16), s.pr), :].astype(F32)
    for o in range(1, W):
        total = total + r.hZR[o - 1].astype(F32)
    mine = pl.ds(aligned(c * s.pr, 16), s.pr)
    r.hFG[mine, :] = total.astype(BF)
    for oc in range(1, C):
        part = r.hFG.at[mine]
        remote(part, part, r.x_rc.at[4], r.rc.at[4], cpeer(oc)).start()

    got(r.Rk.at[pl.ds(0, (E - 1) * cp)], r.back.at[1])
    r.layer_out[...] = (r.middle[...] + gate * dot(r.pt[...], r.Rk[...].astype(BF))).astype(BF)

    share_sum(2)
    got(r.hFG.at[pl.ds(0, (C - 1) * s.pr)], r.rc.at[4])

    def unpad(value):
        return dot(r.unsel[...], value) if s.padded else value.astype(F32)

    r.smalls[...] = unpad(r.hFG[...])
    for m in (3, 0, 1, 2):
        got(r.FG.at[m, :, there], r.rd.at[m])
        r.grads[m] = unpad(r.FG[m]).astype(r.grads.dtype)

    for step in range(max(0, s.F // tile - slots), s.F // tile):
        save_out(step).wait()
    for step in range(max(0, D // tile - slots), D // tile):
        save_in(step).wait()
    sent(r.smg.at[pl.ds(0, W - 1)], r.x_sm)
    for g in range(2):
        part = r.wfull.at[groups[g], pl.ds(0, s.pw), here]
        for d in range(W - 1):
            pl.when((z >= d) & (z < W - 1))(functools.partial(sent, part, r.x_wu.at[g, d]))
            pl.when((z + d <= W - 1) & (z > 0))(functools.partial(sent, part, r.x_wd.at[g, d]))
        if s.team > 1:
            sent(r.wfull.at[groups[g], team_rows, here], r.x_wb.at[g])
        sent(r.wfull.at[groups[g], :, here], r.x_wc.at[g])
    for m in range(4):
        sent(r.fac.at[m], r.x_sibF.at[m])
        sent(r.GR.at[m], r.x_ra.at[m])
        sent(r.ZR.at[m], r.x_rb.at[m])
        sent(r.FG.at[m, pl.ds(0, (C - 1) * s.pr), here], r.x_rc.at[m])
        sent(r.FG.at[m, :, here], r.x_rd.at[m])
    for index, buffer in enumerate((r.gsend, r.nsend, r.tsend)):
        sent(buffer.at[pl.ds(0, E - 1)], r.x_d1.at[index])
    line_sent(r.Nr, r.x_nu, r.x_nd)
    sent(r.Tr.at[pl.ds(0, (W - 1) * R)], r.x_t2)
    for d in range(1, W):
        pl.when(z >= d)(functools.partial(sent, r.SS.at[0, :, body], r.x_rdn.at[d]))
        pl.when(z + d <= W - 1)(functools.partial(sent, r.SS.at[0, :, body], r.x_ru.at[d]))
    sent(r.Sk.at[pl.ds(0, (E - 1) * cp)], r.x_back.at[0])
    sent(r.Rk.at[pl.ds(0, (E - 1) * cp)], r.x_back.at[1])
    sent(r.nT.at[:, pl.ds(0, T)], r.x_sibT.at[0])
    sent(r.mT.at[:, pl.ds(0, T)], r.x_sibT.at[1])
    sent(r.hGR, r.x_ra.at[4])
    sent(r.hZR, r.x_rb.at[4])
    sent(r.hFG.at[pl.ds(0, (C - 1) * s.pr)], r.x_rc.at[4])
    sent(r.smo, r.x_rd.at[4])


def selection(s):
    share = s.SR // s.C
    unsel = np.zeros((s.SR, s.CP), np.float32)
    for chip in range(s.C):
        for at in range(share):
            unsel[chip * share + at, chip * s.pr + at] = 1
    return jnp.asarray(unsel, BF)


PARTS = 3


def finish(s, *refs):
    layer_out, tokens_grad, grads, smalls, grad_in, grad_out = refs[:6]
    out_layer, out_tokens, *out_mixers = refs[6:12]
    out_in, out_out, out_gain1, out_gain2, out_rel, out_router = refs[12:18]
    low_mix, low_in, low_out, mix, into, outof, held_layer, held_tokens = refs[18:26]
    pass_sem, load_sem, save_sem, load2, save2 = refs[26:]
    through = (
        (layer_out, held_layer, out_layer),
        (tokens_grad, held_tokens, out_tokens),
    )
    loads = [
        pltpu.make_async_copy(source, held, pass_sem.at[0, index])
        for index, (source, held, _) in enumerate(through)
    ]
    saves = [
        pltpu.make_async_copy(held, target, pass_sem.at[1, index])
        for index, (_, held, target) in enumerate(through)
    ]
    for m in range(4):
        loads.append(pltpu.make_async_copy(grads.at[m], low_mix.at[m], load_sem.at[m]))
        saves.append(pltpu.make_async_copy(mix.at[m], out_mixers[m], save_sem.at[m]))
    steps = [None, None] + [(low_mix, mix, m) for m in range(4)]
    for index, (source, low, high, target) in enumerate(
        ((grad_in, low_in, into, out_in), (grad_out, low_out, outof, out_out))
    ):
        rows = source.shape[0] // PARTS
        for part in range(PARTS):
            at = pl.ds(part * rows, rows)
            loads.append(
                pltpu.make_async_copy(source.at[at], low.at[at], load2.at[index, part])
            )
            saves.append(
                pltpu.make_async_copy(high.at[at], target.at[0, at], save2.at[index, part])
            )
            steps.append((low, high, at))
    for copy in loads:
        copy.start()
    turned = smalls[...].T
    out_router[...] = turned[: s.NX]
    out_gain1[...] = turned[GAIN_ATTN_LANE : GAIN_ATTN_LANE + 1]
    out_gain2[...] = turned[GAIN_FFN_LANE : GAIN_FFN_LANE + 1]
    out_rel[...] = smalls[: s.NBH, REL_LANE : REL_LANE + s.H]
    for load, save, step in zip(loads, saves, steps, strict=True):
        load.wait()
        if step is not None:
            low, high, at = step
            high[at] = low[at].astype(F32)
        save.start()
    for copy in saves:
        copy.wait()


def local(
    tokens,
    norm_gain_attn,
    w_query,
    w_key,
    w_value,
    w_output,
    rel_bias,
    norm_gain_ffn,
    w_router,
    w_in,
    w_out,
    out_grad,
    expert_ids,
    priority,
    lengths,
    seq_order,
    relpos_table,
):
    tok_count, width = tokens.shape
    buckets_here, heads = rel_bias.shape
    n_experts = w_router.shape[1]
    s = plan(
        lax.axis_size("expert"),
        lax.axis_size("wshard"),
        tok_count,
        width,
        heads,
        buckets_here,
        n_experts,
        w_in.shape[2],
    )
    operands = [
        lengths, seq_order, expert_ids.reshape(1, tok_count), priority.reshape(1, tok_count),
        relpos_table.reshape(1, -1), w_router.T, norm_gain_attn,
        norm_gain_ffn, rel_bias,
        tokens, out_grad, w_query, w_key, w_value, w_output, w_in, w_out,
    ]
    smem, vmem, anywhere = (
        pl.BlockSpec(memory_space=space) for space in (pltpu.SMEM, pltpu.VMEM, pl.ANY)
    )
    in_specs = [smem] * 2 + [vmem] * 7 + [anywhere] * 8
    names = IN_NAMES
    if s.padded:
        operands.append(selection(s))
        in_specs.append(vmem)
        names = names + PAD_NAMES
    spilled = (jax.ShapeDtypeStruct(pieces_shape(s), BF),) if s.padded else ()
    scratch = scratch_list(s)
    names = names + OUT_NAMES + ("GR",) * len(spilled) + tuple(name for name, _ in scratch)
    outs = pl.pallas_call(
        functools.partial(kernel, s, names),
        name="layer",
        out_shape=(
            jax.ShapeDtypeStruct((s.T, s.D), BF),
            jax.ShapeDtypeStruct((s.T, s.D), F32),
            jax.ShapeDtypeStruct((4, s.SR, s.D), BF),
            jax.ShapeDtypeStruct((s.SR, LANES), F32),
            jax.ShapeDtypeStruct((s.D, s.F), BF),
            jax.ShapeDtypeStruct((s.F, s.D), BF),
            *spilled,
        ),
        in_specs=in_specs,
        out_specs=(vmem, vmem, vmem, vmem, anywhere, anywhere) + (anywhere,) * len(spilled),
        scratch_shapes=[shape for _, shape in scratch],
        compiler_params=pltpu.CompilerParams(
            collective_id=0, has_side_effects=True, vmem_limit_bytes=62 * 2**20
        ),
    )(*operands)
    done = pl.pallas_call(
        functools.partial(finish, s),
        name="finish",
        out_shape=(
            jax.ShapeDtypeStruct((s.T, s.D), BF),
            jax.ShapeDtypeStruct((s.T, s.D), F32),
            *[jax.ShapeDtypeStruct((s.SR, s.D), F32)] * 4,
            jax.ShapeDtypeStruct((1, s.D, s.F), F32),
            jax.ShapeDtypeStruct((1, s.F, s.D), F32),
            jax.ShapeDtypeStruct((1, s.SR), F32),
            jax.ShapeDtypeStruct((1, s.SR), F32),
            jax.ShapeDtypeStruct((buckets_here, heads), F32),
            jax.ShapeDtypeStruct((n_experts, s.SR), F32),
        ),
        in_specs=[anywhere, anywhere, anywhere, vmem, anywhere, anywhere],
        out_specs=(anywhere,) * 8 + (vmem,) * 4,
        scratch_shapes=[
            pltpu.VMEM((4, s.SR, s.D), BF),
            pltpu.VMEM((s.D, s.F), BF),
            pltpu.VMEM((s.F, s.D), BF),
            pltpu.VMEM((4, s.SR, s.D), F32),
            pltpu.VMEM((s.D, s.F), F32),
            pltpu.VMEM((s.F, s.D), F32),
            pltpu.VMEM((s.T, s.D), BF),
            pltpu.VMEM((s.T, s.D), F32),
            pltpu.SemaphoreType.DMA((2, 2)),
            pltpu.SemaphoreType.DMA((4,)),
            pltpu.SemaphoreType.DMA((4,)),
            pltpu.SemaphoreType.DMA((2, PARTS)),
            pltpu.SemaphoreType.DMA((2, PARTS)),
        ],
        compiler_params=pltpu.CompilerParams(vmem_limit_bytes=62 * 2**20),
    )(*outs[:6])
    layer_out, tokens_grad, gq, gk, gv, go, grad_w_in, grad_w_out, gain1, gain2, rel, router = done
    return (
        layer_out,
        tokens_grad,
        gain1.reshape(s.SR),
        gq,
        gk,
        gv,
        go,
        rel,
        gain2.reshape(s.SR),
        router.T,
        grad_w_in,
        grad_w_out,
    )


def solution(mesh):
    rows = P(("expert", "wshard"), None)
    shard = P("wshard", None)
    into, outof = P("expert", None, "wshard"), P("expert", "wshard", None)
    return jax.shard_map(
        local,
        mesh=mesh,
        in_specs=(
            rows,
            P("wshard"),
            shard,
            shard,
            shard,
            shard,
            shard,
            P("wshard"),
            shard,
            into,
            outof,
            rows,
            rows,
            P(("expert", "wshard")),
            P(),
            P(),
            P(),
        ),
        out_specs=(
            rows,
            rows,
            P("wshard"),
            shard,
            shard,
            shard,
            shard,
            shard,
            P("wshard"),
            shard,
            into,
            outof,
        ),
        check_vma=False,
    )
```

```python
import functools
import types

import jax
import jax.numpy as jnp
import numpy as np
from jax import lax
from jax.experimental import pallas as pl
from jax.experimental.pallas import tpu as pltpu
from jax.sharding import PartitionSpec as P

EPSILON = 1e-06
NEG_FILL = -1e30
GELU_A = 0.79788456
GELU_B = 0.044715
LANES = 128
REL_LANE = 64
GAIN_ATTN_LANE = 126
GAIN_FFN_LANE = 127
MESH = pl.DeviceIdType.MESH
BF = jnp.bfloat16
F32 = jnp.float32
I32 = jnp.int32


def up16(count):
    return -(-count // 16) * 16


def dot(a, b):
    return jnp.dot(a, b, preferred_element_type=F32)


def dot_rt(a, b):
    return lax.dot_general(a, b, (((1,), (1,)), ((), ())), preferred_element_type=F32)


def dot_lt(a, b):
    return lax.dot_general(a, b, (((0,), (0,)), ((), ())), preferred_element_type=F32)


def iota(shape, axis):
    return lax.broadcasted_iota(I32, shape, axis)


def flip(index, offset):
    out = index
    bit = 1
    while bit <= offset:
        if offset & bit:
            out = out + bit * (1 - 2 * lax.rem(lax.div(index, bit), 2))
        bit *= 2
    return out


def aligned(value, step):
    return pl.multiple_of(value, step)


def two_parts(value):
    high = value.astype(BF)
    return high, (value - high.astype(F32)).astype(BF)


def plan(expert_size, shard_size, tok_count, width, heads, buckets_here, n_experts, hidden):
    s = types.SimpleNamespace()
    s.E, s.W = expert_size, shard_size
    s.C = expert_size // 2
    s.T, s.D, s.H = tok_count, width, heads
    s.HD = width // heads
    s.F = hidden
    s.NX = n_experts
    s.cap = tok_count // n_experts
    s.cp = s.cap if s.cap % 8 == 0 else up16(s.cap)
    s.dt = BF if s.cp % 16 == 0 else F32
    s.S = n_experts * s.cp
    s.R = s.E * s.cp
    s.SR = width // shard_size
    s.NBH = buckets_here
    s.NBP = up16(buckets_here)
    s.half = width // 2
    s.P1 = up16(n_experts + 2)
    s.LW = -(-s.SR // LANES) * LANES
    team = s.C
    while s.SR % team or (s.SR // team) % 16:
        team //= 2
    s.team = team
    s.pw = s.SR // team
    s.pr = up16(s.SR // s.C)
    s.CP = s.C * s.pr
    s.Dp = s.W * s.CP
    s.padded = s.CP != s.SR
    s.tile = LANES
    s.slots = 2 if s.padded else max(width, hidden) // s.tile
    return s


def pieces_shape(s):
    return (4, s.C - 1, s.W * s.pr, s.half)


def arrivals(s):
    return (("Ga", s.D), ("Na", s.D), ("Ta", LANES)) if s.dt == F32 else ()


def scratch_list(s):
    V = pltpu.VMEM
    dma = pltpu.SemaphoreType.DMA
    return [
        ("wfull", V((4, s.D, s.D), BF)),
        ("smf", V((s.P1 + s.NBP, s.LW), F32)),
        ("smg", V((s.W, s.P1 + s.NBP, s.LW), BF)),
        ("tab", V((8, 2 * s.T), I32)),
        ("xb", V((s.T, s.D), BF)),
        ("og", V((s.T, s.D), BF)),
        ("wi", V((s.D, s.F), BF)),
        ("wo", V((s.F, s.D), BF)),
        ("pm", V((s.S, s.T), BF)),
        ("pt", V((s.T, s.S), BF)),
        ("gsend", V((s.NX, s.cp, s.D), s.dt)),
        ("nsend", V((s.NX, s.cp, s.D), s.dt)),
        ("tsend", V((s.NX, s.cp, LANES), s.dt)),
        ("Gr", V((s.W * s.R, s.D), BF)),
        ("Nr", V((s.W * s.R, s.D), BF)),
        ("Tr", V((s.W * s.R, LANES), BF)),
        ("agr", V((s.W * s.R, s.F), BF)),
        ("act", V((s.W * s.R, s.F), BF)),
        ("ig", V((s.W * s.R, s.F), BF)),
        ("SS", V((s.W, s.R, s.D), BF)),
        ("Sin", V((s.W + 1, s.R, s.D), BF)),
        ("Sb", V((s.R, s.D), s.dt)),
        ("Sk", V((s.S, s.D), s.dt)),
        ("HS", V((s.W, 8, s.R), F32)),
        ("Hr", V((s.W, 8, s.R), F32)),
        ("Hb", V((8, s.R), F32)),
        ("Hk", V((s.E, 8, s.R), F32)),
        ("Hm", V((LANES, s.R), F32)),
        ("Rb", V((s.R, s.D), s.dt)),
        ("Rk", V((s.S, s.D), s.dt)),
        ("tb", V((LANES, 2 * s.T), F32)),
        ("ohm", V((s.W * s.NBP, 2 * s.T), BF)),
        ("rows", V((8, s.D), F32)),
        ("RwT", V((LANES, s.D), BF)),
        ("probs", V((s.H, s.T, s.T), F32)),
        ("q", V((s.T, s.D), BF)),
        ("kk", V((s.T, s.D), BF)),
        ("v", V((s.T, s.D), BF)),
        ("mixed", V((s.T, s.D), BF)),
        ("nf", V((s.T, s.D), BF)),
        ("middle", V((s.T, s.D), F32)),
        ("mg", V((s.T, s.D), F32)),
        ("att", V((s.T, s.D), BF)),
        ("dq", V((s.T, s.D), BF)),
        ("dk", V((s.T, s.D), BF)),
        ("dv", V((s.T, s.D), BF)),
        ("nT", V((s.Dp, 2 * s.T), BF)),
        ("mT", V((s.Dp, 2 * s.T), BF)),
        ("fac", V((4, s.T, s.half), BF)),
        ("GS", V((4, s.C, s.W * s.pr, s.half), BF)),
        ("ZS", V((4, s.W * s.pr, s.half), BF)),
        ("ZR", V((4, s.W - 1, s.pr, s.half), BF)),
        ("FG", V((4, s.CP, s.D), BF)),
        ("smo", V((s.Dp, LANES), BF)),
        ("sms", V((s.Dp, LANES), BF)),
        ("hGS", V((s.C, s.W * s.pr, LANES), BF)),
        ("hGR", V((s.C - 1, s.W * s.pr, LANES), BF)),
        ("hZS", V((s.W * s.pr, LANES), BF)),
        ("hZR", V((s.W - 1, s.pr, LANES), BF)),
        ("hFG", V((s.CP, LANES), BF)),
        ("bt", V((LANES, 2 * s.T), F32)),
        ("gwi", V((s.slots, s.tile, s.F), BF)),
        ("gwo", V((s.slots, s.tile, s.D), BF)),
        ("gwi_sem", dma((s.slots,))),
        ("gwo_sem", dma((s.slots,))),
        ("lsem", dma((9,))),
        ("smr", dma((s.W,))),
        ("wu", dma((4, s.W))),
        ("wd", dma((4, s.W))),
        ("wbu", dma((4, s.W))),
        ("wbd", dma((4, s.W))),
        ("wc", dma((4,))),
        ("g1", dma((s.C,))),
        ("gu", dma((s.W, s.C))),
        ("gd", dma((s.W, s.C))),
        ("n1", dma((s.C,))),
        ("nu", dma((s.W, s.C))),
        ("nd", dma((s.W, s.C))),
        ("t1", dma((s.C,))),
        ("t2", dma((s.W,))),
        ("hz", dma((s.W,))),
        ("hp", dma),
        ("x_hz", dma((s.W,))),
        ("x_hp", dma),
        ("su", dma((s.W, s.C))),
        ("sd", dma((s.W, s.C))),
        ("ru", dma((s.W,))),
        ("rdn", dma((s.W,))),
        ("back", dma((2,))),
        ("sibT", dma((2,))),
        ("sibF", dma((4,))),
        ("ra", dma((5,))),
        ("rb", dma((5,))),
        ("rc", dma((5,))),
        ("rd", dma((5,))),
        ("x_sm", dma),
        ("x_wu", dma((4, s.W))),
        ("x_wd", dma((4, s.W))),
        ("x_wb", dma((4,))),
        ("x_wc", dma((4,))),
        ("x_d1", dma((3,))),
        ("x_t2", dma),
        ("x_gu", dma((s.W,))),
        ("x_gd", dma((s.W,))),
        ("x_nu", dma((s.W,))),
        ("x_nd", dma((s.W,))),
        ("x_su", dma((s.W,))),
        ("x_sd", dma((s.W,))),
        ("x_ru", dma((s.W,))),
        ("x_rdn", dma((s.W,))),
        ("x_back", dma((2,))),
        ("x_sibT", dma((2,))),
        ("x_sibF", dma((4,))),
        ("x_ra", dma((5,))),
        ("x_rb", dma((5,))),
        ("x_rc", dma((5,))),
        ("x_rd", dma((5,))),
        ("credit", pltpu.SemaphoreType.REGULAR),
    ] + (
        [("gst", V((s.W * s.pr, s.half), BF))]
        + [(name, V((s.R, width), F32)) for name, width in arrivals(s)]
        if s.padded
        else [
            ("GR", V(pieces_shape(s), BF)),
            ("RS", V((s.W, s.R, s.D), BF)),
            ("Rin", V((s.W + 1, s.R, s.D), BF)),
        ]
    )


IN_NAMES = (
    "lengths", "seq", "ids", "prio", "table", "router", "gain_attn", "gain_ffn", "bias",
    "tokens", "out_grad", "w0", "w1", "w2", "w3", "w_in", "w_out",
)
PAD_NAMES = ("unsel",)
OUT_NAMES = ("layer_out", "tokens_grad", "grads", "smalls", "grad_w_in", "grad_w_out")


def kernel(s, names, *refs):
    r = types.SimpleNamespace(**dict(zip(names, refs, strict=True)))
    e = lax.axis_index("expert")
    z = lax.axis_index("wshard")
    c = lax.div(e, 2)
    k = lax.rem(e, 2)
    T, D, E, W, C, R, cp, half = s.T, s.D, s.E, s.W, s.C, s.R, s.cp, s.half
    sib = (flip(e, 1), z)
    here = pl.ds(aligned(k * half, LANES), half)
    there = pl.ds(aligned((1 - k) * half, LANES), half)

    def zpeer(offset):
        return (e, flip(z, offset))

    def cpeer(offset):
        return (flip(c, offset) * 2 + k, z)

    def remote(src, dst, send, recv, device):
        return pltpu.make_async_remote_copy(
            src_ref=src, dst_ref=dst, send_sem=send, recv_sem=recv, device_id=device, device_id_type=MESH
        )

    def got(ref, sem):
        remote(ref, ref, sem, sem, sib).wait_recv()

    def sent(ref, sem):
        remote(ref, ref, sem, sem, sib).wait_send()

    shards = (r.w0, r.w1, r.w2, r.w3)
    own_rows = pl.ds(aligned(z * s.SR, 16), s.SR)
    load_w = [
        pltpu.make_async_copy(shards[m], r.wfull.at[m, own_rows], r.lsem.at[m])
        for m in range(4)
    ]
    load_og = pltpu.make_async_copy(r.out_grad, r.og, r.lsem.at[4])
    load_x = pltpu.make_async_copy(r.tokens, r.xb, r.lsem.at[5])
    load_wo = pltpu.make_async_copy(r.w_out.at[0], r.wo, r.lsem.at[6])
    load_wi = pltpu.make_async_copy(r.w_in.at[0], r.wi, r.lsem.at[7])
    load_og.start()

    r.smf[...] = jnp.zeros_like(r.smf)
    r.smf[0 : s.NX, 0 : s.SR] = r.router[...].astype(F32)
    r.smf[s.NX : s.NX + 1, 0 : s.SR] = r.gain_attn[...].astype(F32).reshape(1, s.SR)
    r.smf[s.NX + 1 : s.NX + 2, 0 : s.SR] = r.gain_ffn[...].astype(F32).reshape(1, s.SR)
    r.smf[s.P1 : s.P1 + s.NBH, 0 : s.H] = r.bias[...].astype(F32)
    r.smg[z] = r.smf[...].astype(BF)

    barrier = pltpu.get_barrier_semaphore()
    peers = [(flip(e, o), z) for o in range(1, E)] + [zpeer(o) for o in range(1, W)]
    for peer in peers:
        pl.semaphore_signal(barrier, inc=1, device_id=peer, device_id_type=MESH)
    pl.semaphore_wait(barrier, len(peers))

    team_c = lax.rem(c, s.team)
    for o in range(1, W):
        remote(r.smg.at[z], r.smg.at[z], r.x_sm, r.smr.at[o], zpeer(o)).start()
    share_rows = pl.ds(aligned(team_c * s.pw, 16), s.pw)
    def weight_at(plane):
        return pl.ds(aligned(plane * s.SR + team_c * s.pw, 16), s.pw)

    def weight_own(m):
        def send(sender, receiver, to):
            source = shards[m].at[share_rows, here]
            remote(source, r.wfull.at[m, weight_at(z), here], sender, receiver, (e, to)).start()

        pl.when(z < W - 1)(functools.partial(send, r.x_wu.at[m, 0], r.wu.at[m, 1], z + 1))
        pl.when(z > 0)(functools.partial(send, r.x_wd.at[m, 0], r.wd.at[m, 1], z - 1))

    for m in range(3):
        weight_own(m)
    for copy in (load_x, *load_w, load_wo, load_wi):
        copy.start()
    device = e * W + z
    first = r.lengths[r.seq[2 * device]]
    both = first + r.lengths[r.seq[2 * device + 1]]
    col = iota((T, 1), 0)
    row = iota((1, T), 1)
    seg_col = (col >= first).astype(I32) + (col >= both).astype(I32)
    seg_row = (row >= first).astype(I32) + (row >= both).astype(I32)
    same = seg_col == seg_row
    valid = (col < both).astype(F32)
    eye = iota((T, T), 0) == iota((T, T), 1)
    id_row = r.ids[...].astype(F32)
    id_col = jnp.sum(jnp.where(eye, id_row, 0.0), axis=1, keepdims=True)
    prio_row = r.prio[...].astype(F32)
    prio_col = jnp.sum(jnp.where(eye, prio_row, 0.0), axis=1, keepdims=True)
    ahead = (id_col == id_row) & (prio_col < prio_row)
    slot_row = jnp.sum(jnp.where(ahead, valid, 0.0), axis=0, keepdims=True)
    kept = (row < both) & (slot_row < s.cap)
    flat_row = jnp.where(kept, id_row * cp + slot_row, -1.0)
    flat_col = jnp.sum(jnp.where(eye, flat_row, 0.0), axis=1, keepdims=True)
    r.pm[...] = (iota((s.S, T), 0).astype(F32) == flat_row).astype(F32).astype(BF)
    r.pt[...] = (iota((T, s.S), 1).astype(F32) == flat_col).astype(F32).astype(BF)

    plane_step = 16 if s.dt == BF else 8
    plane_rows = z * R if s.dt == BF else 0

    def dispatch(index, send, rows, first_sem, value):
        width = rows.shape[1]
        buffer = dot(r.pm[...], value)
        send[...] = buffer.astype(s.dt).reshape(s.NX, cp, width)
        mine = pl.ds(aligned(plane_rows + e * cp, plane_step), cp)
        for o in range(1, E):
            x = flip(e, o)
            remote(
                send.at[x], rows.at[mine], r.x_d1.at[index], first_sem.at[o // 2], (x, z)
            ).start()
        rows[mine, :] = send[e]

    def block_at(plane, oc):
        return pl.ds(aligned(plane * R + flip(c, oc) * 2 * cp, 16), 2 * cp)

    def landed(rows, arrived, first_sem, oc):
        got(arrived.at[pl.ds(0, (2 if oc else 1) * cp)], first_sem.at[oc])
        if s.dt != BF:
            rows[block_at(z, oc), :] = arrived[block_at(0, oc), :].astype(BF)

    def move(part, send, recv, to):
        remote(part, part, send, recv, (e, to)).start()

    def line_own(rows, arrived, first_sem, up, down, x_up, x_down):
        for oc in range(C):
            landed(rows, arrived, first_sem, oc)
            part = rows.at[block_at(z, oc)]
            pl.when(z < W - 1)(functools.partial(move, part, x_up.at[0], up.at[1, oc], z + 1))
            pl.when(z > 0)(functools.partial(move, part, x_down.at[0], down.at[1, oc], z - 1))

    def line_pass(rows, d, up, down, x_up, x_down):
        for oc in range(C):

            @pl.when(z >= d)
            def _():
                part = rows.at[block_at(z - d, oc)]
                got(part, up.at[d, oc])
                if d < W - 1:
                    pl.when(z < W - 1)(
                        functools.partial(move, part, x_up.at[d], up.at[d + 1, oc], z + 1)
                    )

            @pl.when(z + d <= W - 1)
            def _():
                part = rows.at[block_at(z + d, oc)]
                got(part, down.at[d, oc])
                if d < W - 1:
                    pl.when(z > 0)(
                        functools.partial(move, part, x_down.at[d], down.at[d + 1, oc], z - 1)
                    )

    def line_sent(rows, x_up, x_down):
        for d in range(W - 1):
            whole = rows.at[pl.ds(0, R)]
            pl.when((z >= d) & (z < W - 1))(functools.partial(sent, whole, x_up.at[d]))
            pl.when((z + d <= W - 1) & (z > 0))(functools.partial(sent, whole, x_down.at[d]))

    g_line = (r.gu, r.gd, r.x_gu, r.x_gd)
    n_line = (r.nu, r.nd, r.x_nu, r.x_nd)
    Ga, Na, Ta = (r.Gr, r.Nr, r.Tr) if s.dt == BF else (r.Ga, r.Na, r.Ta)
    load_og.wait()
    dispatch(0, r.gsend, Ga, r.g1, r.og[...])

    def weight_pass(m, d):
        def handle(plane, arrived, onward, sender, receiver, to, beside):
            part = r.wfull.at[m, weight_at(plane), here]
            got(part, arrived)
            if d < W - 1:
                pl.when(onward)(functools.partial(move, part, sender, receiver, to))
            for oc in range(1, s.team):
                remote(part, part, r.x_wb.at[m], beside, cpeer(oc)).start()

        up, down, after = (m, d), (m, d), (m, min(d + 1, W - 1))
        pl.when(z >= d)(
            functools.partial(
                handle, z - d, r.wu.at[up], z < W - 1, r.x_wu.at[up], r.wu.at[after], z + 1, r.wbu.at[up]
            )
        )
        pl.when(z + d <= W - 1)(
            functools.partial(
                handle, z + d, r.wd.at[down], z > 0, r.x_wd.at[down], r.wd.at[after], z - 1, r.wbd.at[down]
            )
        )

    def weight_share(m, d):
        def handle(plane, beside):
            if s.team > 1:
                got(r.wfull.at[m, pl.ds(0, (s.team - 1) * s.pw), here], beside)
            part = r.wfull.at[m, pl.ds(aligned(plane * s.SR, 16), s.SR), here]
            remote(part, part, r.x_wc.at[m], r.wc.at[m], sib).start()

        pl.when(z >= d)(functools.partial(handle, z - d, r.wbu.at[m, d]))
        pl.when(z + d <= W - 1)(functools.partial(handle, z + d, r.wbd.at[m, d]))

    others = pl.ds(0, (W - 1) * s.SR)

    def weight_ready(m):
        load_w[m].wait()
        got(r.wfull.at[m, others, there], r.wc.at[m])

    for d in range(1, W):
        for m in range(3):
            weight_pass(m, d)
        if d == 1:
            weight_own(3)
        else:
            weight_pass(3, d - 1)
            for m in range(3):
                weight_share(m, d - 1)
        if d == min(2, W - 1):
            line_own(r.Gr, Ga, r.g1, *g_line)
    weight_pass(3, W - 1)
    for m in range(3):
        weight_share(m, W - 1)
    for o in range(1, W):
        got(r.smg.at[0], r.smr.at[o])
    gathered = jnp.concatenate(
        [r.smg[w, : s.P1, : s.SR].astype(F32) for w in range(W)], axis=1
    )
    r.rows[0:1, :] = gathered[s.NX : s.NX + 1]
    r.rows[1:2, :] = gathered[s.NX + 1 : s.NX + 2]
    r.RwT[...] = jnp.zeros_like(r.RwT)
    r.RwT[: s.P1, :] = jnp.where(iota((s.P1, D), 0) < s.NX, gathered, 0.0).astype(BF)
    lane_row = iota((1, LANES), 1)
    r.tab[...] = jnp.full(r.tab.shape, -1, I32)
    r.tab[0:1, 0 : 2 * T - 1] = r.table[...]
    bucket = r.tab[0:1, :]
    shift = s.NBH.bit_length() - 1
    bucket = lax.shift_right_logical(bucket, shift) * s.NBP + lax.bitwise_and(bucket, s.NBH - 1)
    bucket = jnp.where(r.tab[0:1, :] < 0, -1, bucket)
    hot = (iota((W * s.NBP, 2 * T), 0) == bucket).astype(F32).astype(BF)
    backwards = (iota((2 * T, 2 * T), 0) + iota((2 * T, 2 * T), 1) == 2 * T - 2).astype(F32)
    r.ohm[...] = dot(hot, backwards.astype(BF)).astype(BF)
    bias_rows = r.smg[:, s.P1 :, :LANES].reshape(W * s.NBP, LANES)
    r.tb[...] = dot_lt(bias_rows, hot)

    def bias_head(h, carry):
        wide = jnp.broadcast_to(r.tb[pl.ds(h, 1), :], (T, 2 * T))
        turned = pltpu.roll(wide, T + 1, 1, stride=1, stride_axis=0)
        r.probs[h] = jnp.where(same, turned[:, :T], NEG_FILL)
        return carry

    lax.fori_loop(0, s.H, bias_head, 0)
    load_x.wait()
    x = r.xb[...].astype(F32)
    scale1 = lax.rsqrt(jnp.mean(x * x, axis=1, keepdims=True) + EPSILON)
    normed = (x * scale1 * r.rows[0:1, :]).astype(BF)

    def spread_rows(value):
        if not s.padded:
            return value
        shards = [value[at : at + s.SR] for at in range(0, D, s.SR)]
        return jnp.concatenate([dot_lt(r.unsel[...], shard) for shard in shards], axis=0).astype(BF)

    def turn_out(index, value, target):
        target[:, :T] = spread_rows(value.T)
        remote(
            target.at[:, pl.ds(0, T)], target.at[:, pl.ds(T, T)], r.x_sibT.at[index], r.sibT.at[index], sib
        ).start()

    turn_out(0, normed, r.nT)
    weight_ready(0)
    r.q[...] = dot(normed, r.wfull[0]).astype(BF)
    weight_ready(1)
    r.kk[...] = dot(normed, r.wfull[1]).astype(BF)
    weight_ready(2)
    r.v[...] = dot(normed, r.wfull[2]).astype(BF)
    for d in range(1, W):
        weight_share(3, d)
    line_pass(r.Gr, 1, *g_line)

    scale = s.HD ** (-0.5)
    low_lane = (lane_row < s.HD).astype(F32)
    lane_masks = (low_lane.astype(BF), (1.0 - low_lane).astype(BF))

    def attend(p, carry):
        cols = pl.ds(aligned(p * LANES, LANES), LANES)
        q, kk, v = r.q[:, cols], r.kk[:, cols], r.v[:, cols]
        outs = []
        for side in range(2):
            h = 2 * p + side
            scores = dot_rt(q * lane_masks[side], kk) * scale + r.probs[h]
            expo = jnp.exp(scores - jnp.max(scores, axis=1, keepdims=True))
            probs = expo * (1.0 / jnp.sum(expo, axis=1, keepdims=True))
            r.probs[h] = probs
            outs.append(dot(probs.astype(BF), v))
        r.mixed[:, cols] = jnp.where(lane_row < s.HD, outs[0], outs[1]).astype(BF)
        return carry

    lax.fori_loop(0, s.H // 2, attend, 0)
    mixed = r.mixed[...]
    weight_ready(3)
    middle = r.xb[...].astype(F32) + dot(mixed, r.wfull[3]) * valid
    r.middle[...] = middle
    scale2 = lax.rsqrt(jnp.mean(middle * middle, axis=1, keepdims=True) + EPSILON)
    nf = (middle * scale2 * r.rows[1:2, :]).astype(BF)
    r.nf[...] = nf
    dispatch(1, r.nsend, Na, r.n1, nf)
    logits = jnp.where(lane_row < s.NX, dot_rt(nf, r.RwT[...]), NEG_FILL)
    raised = jnp.exp(logits - jnp.max(logits, axis=1, keepdims=True))
    router = raised / jnp.sum(raised, axis=1, keepdims=True)
    picked = (lane_row.astype(F32) == id_col).astype(F32)
    gate = jnp.sum(router * picked, axis=1, keepdims=True)
    gate_high, gate_rest = two_parts(gate)
    gate_mid, gate_low = two_parts(gate - gate_high.astype(F32))
    gate_lanes = jnp.where(
        lane_row == 0,
        gate_high.astype(F32),
        jnp.where(lane_row == 1, gate_mid.astype(F32), jnp.where(lane_row == 2, gate_low.astype(F32), 0.0)),
    )
    dispatch(2, r.tsend, Ta, r.t1, gate_lanes.astype(BF))
    if W > 2:
        line_pass(r.Gr, 2, *g_line)
    line_own(r.Nr, Na, r.n1, *n_line)
    for oc in range(C):
        landed(r.Tr, Ta, r.t1, oc)
        for o in range(1, W):
            part = r.Tr.at[block_at(z, oc)]
            remote(part, part, r.x_t2, r.t2.at[o], zpeer(o)).start()
    turn_out(1, mixed, r.mT)

    load_wo.wait()
    for d in range(3, W):
        line_pass(r.Gr, d, *g_line)

    def back_rows(step, carry):
        at = pl.ds(aligned(step * R, 16), R)
        r.agr[at, :] = dot_rt(r.Gr[at, :], r.wo[...]).astype(BF)
        return carry

    lax.fori_loop(0, W, back_rows, 0)
    load_wi.wait()

    def expert_rows(plane, at, block):
        inner = dot(r.Nr[at, :], r.wi[...])
        square = inner * inner
        tanh = jnp.tanh(GELU_A * inner * (1.0 + GELU_B * square))
        active = (0.5 * inner * (1.0 + tanh)).astype(BF)
        slope = 0.5 * (1.0 + tanh) + (0.5 * GELU_A) * inner * (1.0 - tanh * tanh) * (
            1.0 + (3.0 * GELU_B) * square
        )
        inner_grad = (r.agr[at, :].astype(F32) * slope).astype(BF)
        r.act[at, :] = active
        r.ig[at, :] = inner_grad
        r.SS[plane, block, :] = dot_rt(inner_grad, r.wi[...]).astype(BF)

    def expert(plane):
        expert_rows(plane, pl.ds(aligned(plane * R, 16), R), pl.ds(0, R))

    def gate_sums(plane, carry):
        at = pl.ds(aligned(plane * R, 16), R)
        part = jnp.sum(
            r.act[at, :].astype(F32) * r.agr[at, :].astype(F32), axis=1, keepdims=True
        )
        diagonal = iota((R, R), 0) == iota((R, R), 1)
        r.HS[plane, 0:1, :] = jnp.sum(jnp.where(diagonal, part, 0.0), axis=0, keepdims=True)

        @pl.when(plane != z)
        def _():
            remote(r.HS.at[plane], r.Hr.at[z], r.x_hz.at[plane], r.hz.at[z], (e, plane)).start()

        return carry

    def merge(plane, slot, block):
        r.SS[plane, block, :] = (
            r.SS[plane, block, :].astype(F32) + r.Sin[slot, block, :].astype(F32)
        ).astype(BF)

    def sum_down(plane, gap, oc):
        block = block_at(0, oc)
        remote(
            r.SS.at[plane, block],
            r.Sin.at[plane, block],
            r.x_sd.at[gap],
            r.sd.at[gap - 1, oc],
            (e, z - 1),
        ).start()

    def sum_up(plane, gap, oc):
        block = block_at(0, oc)
        remote(
            r.SS.at[plane, block],
            r.Sin.at[plane + 1, block],
            r.x_su.at[gap],
            r.su.at[gap - 1, oc],
            (e, z + 1),
        ).start()

    def plane_back(index, source, target, offsets):
        mine = pl.ds(aligned(e * cp, plane_step), cp)
        for o in offsets:
            if o == 0:
                target[mine, :] = source[mine, :]
                continue
            x = flip(e, o)
            remote(
                source.at[pl.ds(aligned(x * cp, plane_step), cp)],
                target.at[mine],
                r.x_back.at[index],
                r.back.at[index],
                (x, z),
            ).start()

    early = not s.padded
    RS, Rin = (r.RS, r.Rin) if early else (r.SS, r.Sin)

    def results_begin():
        if not early:
            for d in range(1, W):
                pl.when(z >= d)(functools.partial(sent, r.SS.at[0], r.x_sd.at[d]))
                pl.when(z + d <= W - 1)(functools.partial(sent, r.SS.at[0], r.x_su.at[d]))
            pl.semaphore_wait(r.credit, W - 1)

        def results(step, carry):
            at = pl.ds(aligned(step * R, 16), R)
            RS[step] = dot(r.act[at, :], r.wo[...]).astype(BF)
            return carry

        lax.fori_loop(0, W, results, 0)

    def result_merge(plane, slot, sem):
        got(Rin.at[slot], sem)
        RS[plane] = (RS[plane].astype(F32) + Rin[slot].astype(F32)).astype(BF)

    def results_pass(step):
        below = step - (W - 1 - z)
        above = W - 1 - step + z

        @pl.when((below >= 0) & (below < z))
        def _():
            @pl.when(z < W - 1)
            def _():
                result_merge(below, below, r.rdn.at[z - below])

            remote(
                RS.at[below],
                Rin.at[below],
                r.x_rdn.at[z - below],
                r.rdn.at[z - below - 1],
                (e, z - 1),
            ).start()

        @pl.when((above <= W - 1) & (above > z))
        def _():
            @pl.when(z > 0)
            def _():
                result_merge(above, above + 1, r.ru.at[above - z])

            remote(
                RS.at[above],
                Rin.at[above + 1],
                r.x_ru.at[above - z],
                r.ru.at[above - z - 1],
                (e, z + 1),
            ).start()

    passes = iter(range(W - 1))

    def next_pass():
        for step in passes:
            results_pass(step)
            break

    expert(z)
    for step in range(1, 2 * W - 2):
        if step < W - 1:
            line_pass(r.Nr, step, *n_line)

            def sides(side, carry, step=step):
                plane = z + (2 * side - 1) * step
                pl.when((plane >= 0) & (plane < W))(functools.partial(expert, plane))
                return carry

            lax.fori_loop(0, 2, sides, 0)

        if step == W - 1:
            @pl.when((z == 0) | (z == W - 1))
            def _():
                plane = W - 1 - z
                for oc in range(C):
                    at = block_at(plane, oc)
                    top = functools.partial(got, r.Nr.at[at], r.nu.at[W - 1, oc])
                    bottom = functools.partial(got, r.Nr.at[at], r.nd.at[W - 1, oc])
                    pl.when(z > 0)(top)
                    pl.when(z == 0)(bottom)
                    expert_rows(plane, at, block_at(0, oc))
                    pl.when(z > 0)(functools.partial(sum_down, plane, W - 1, oc))
                    pl.when(z == 0)(functools.partial(sum_up, plane, W - 1, oc))

        plane_down = 2 * W - 2 - z - step
        gap_down = z - plane_down
        plane_up = step - z
        gap_up = plane_up - z
        inner_down = (plane_down >= 0) & (gap_down >= 1)
        inner_up = (plane_up <= W - 1) & (gap_up >= 1)
        if step == W - 1:
            inner_down, inner_up = inner_down & (z < W - 1), inner_up & (z > 0)

        @pl.when(inner_down)
        def _():
            for oc in range(C):

                @pl.when(z < W - 1)
                def _():
                    got(r.Sin.at[plane_down, block_at(0, oc)], r.sd.at[gap_down, oc])
                    merge(plane_down, plane_down, block_at(0, oc))

                sum_down(plane_down, gap_down, oc)

        @pl.when(inner_up)
        def _():
            for oc in range(C):

                @pl.when(z > 0)
                def _():
                    got(r.Sin.at[plane_up + 1, block_at(0, oc)], r.su.at[gap_up, oc])
                    merge(plane_up, plane_up + 1, block_at(0, oc))

                sum_up(plane_up, gap_up, oc)

        if step == W - 1:
            if early:
                results_begin()
                next_pass()
            lax.fori_loop(0, W, gate_sums, 0)

    for oc in range(C):
        block = block_at(0, oc)

        @pl.when(z < W - 1)
        def _():
            got(r.Sin.at[z, block], r.sd.at[0, oc])
            merge(z, z, block)

        @pl.when(z > 0)
        def _():
            got(r.Sin.at[z + 1, block], r.su.at[0, oc])
            merge(z, z + 1, block)

        r.Sb[block, :] = r.SS[z, block, :].astype(s.dt)
        plane_back(0, r.Sb, r.Sk, (2 * oc, 2 * oc + 1))

    total = r.HS[z]
    for o in range(1, W):
        other = flip(z, o)
        got(r.Hr.at[0], r.hz.at[other])
        total = total + r.Hr[other]
    r.Hb[...] = total
    r.Hk[e] = total
    for o in range(1, E):
        remote(r.Hb, r.Hk.at[e], r.x_hp, r.hp, (flip(e, o), z)).start()

    if not early:
        for o in range(1, W):
            pl.semaphore_signal(r.credit, inc=1, device_id=zpeer(o), device_id_type=MESH)
        results_begin()
    next_pass()
    got(r.Sk.at[pl.ds(0, (E - 1) * cp)], r.back.at[0])
    got(r.Hk.at[pl.ds(0, E - 1)], r.hp)
    r.Hm[...] = jnp.zeros_like(r.Hm)
    for x in range(E):
        r.Hm[x : x + 1, :] = r.Hk[x, 0:1, :]
    slot_col = jnp.sum(jnp.where(eye, jnp.where(kept, slot_row, -1.0), 0.0), axis=1, keepdims=True)
    slot_lane = jnp.where(slot_col < 0, -1.0, slot_col + (e * cp).astype(F32))
    chosen = (iota((T, R), 1).astype(F32) == slot_lane).astype(F32).astype(BF)
    high, rest = two_parts(r.Hm[...])
    gate_grad = jnp.sum(
        picked * (dot_rt(chosen, high) + dot_rt(chosen, rest)), axis=1, keepdims=True
    )
    returned = dot(r.pt[...], r.Sk[...].astype(BF))
    logit_grad = (gate * gate_grad * (picked - router)).astype(BF)
    nf_grad = dot(logit_grad, r.RwT[...]) + gate * returned
    middle = r.middle[...]
    along = nf_grad * r.rows[1:2, :]
    middle_grad = (
        r.og[...].astype(F32)
        + scale2 * along
        - middle * (scale2 * scale2 * scale2 * jnp.mean(along * middle, axis=1, keepdims=True))
    )
    r.mg[...] = middle_grad
    r.rows[2:3, :] = jnp.sum(nf_grad * middle * scale2, axis=0, keepdims=True)
    r.att[...] = (middle_grad * valid).astype(BF)
    attended_grad = r.att[...]

    def share(m, source):
        remote(source.at[:, there], r.fac.at[m], r.x_sibF.at[m], r.sibF.at[m], sib).start()

    share(3, r.att)
    r.mixed[...] = dot_rt(attended_grad, r.wfull[3]).astype(BF)
    router_grad = dot_lt(logit_grad, r.nf[...])
    def plane_sum(m, left, source):
        got(r.fac.at[m], r.sibF.at[m])

        def block(step, carry):
            at = pl.ds(aligned(step * s.CP, 16), s.CP)
            part = dot(left[at, :T], source[:, here]) + dot(left[at, T:], r.fac[m])
            part = part.astype(BF)
            for chip in range(C):
                r.GS[m, chip, pl.ds(aligned(step * s.pr, 16), s.pr), :] = part[
                    chip * s.pr : (chip + 1) * s.pr
                ]
            return carry

        lax.fori_loop(0, W, block, 0)
        for oc in range(1, C):
            remote(
                r.GS.at[m, flip(c, oc)], r.GR.at[m, oc - 1], r.x_ra.at[m], r.ra.at[m], cpeer(oc)
            ).start()

    low_side = lane_row < s.HD

    def values_back(p, carry):
        cols = pl.ds(aligned(p * LANES, LANES), LANES)
        mixg = r.mixed[:, cols]
        outs = [dot_lt(r.probs[2 * p + side].astype(BF), mixg) for side in range(2)]
        r.dv[:, cols] = jnp.where(low_side, outs[0], outs[1]).astype(BF)
        return carry

    lax.fori_loop(0, s.H // 2, values_back, 0)
    share(2, r.dv)
    got(r.mT.at[:, pl.ds(T, T)], r.sibT.at[1])
    plane_sum(3, r.mT, r.att)
    got(r.nT.at[:, pl.ds(T, T)], r.sibT.at[0])
    plane_sum(2, r.nT, r.dv)

    def attend_back(p, carry):
        cols = pl.ds(aligned(p * LANES, LANES), LANES)
        q, kk, v, mixg = r.q[:, cols], r.kk[:, cols], r.v[:, cols], r.mixed[:, cols]
        outs = []
        for side in range(2):
            h = 2 * p + side
            probs = r.probs[h]
            prob_grad = dot_rt(mixg * lane_masks[side], v)
            inside = jnp.sum(probs * prob_grad, axis=1, keepdims=True)
            score_grad = (probs * (prob_grad - inside)).astype(BF)
            r.probs[h] = score_grad.astype(F32)
            outs.append((dot(score_grad, kk) * scale, dot_lt(score_grad, q) * scale))
        r.dq[:, cols] = jnp.where(low_side, outs[0][0], outs[1][0]).astype(BF)
        r.dk[:, cols] = jnp.where(low_side, outs[0][1], outs[1][1]).astype(BF)
        return carry

    lax.fori_loop(0, s.H // 2, attend_back, 0)
    share(0, r.dq)
    share(1, r.dk)
    next_pass()

    def shard_sum(m):
        got(r.GR.at[m], r.ra.at[m])
        total = r.GS[m, c].astype(F32)
        for oc in range(1, C):
            if s.padded:
                fetch = pltpu.make_async_copy(r.GR.at[m, oc - 1], r.gst, r.lsem.at[8])
                fetch.start()
                fetch.wait()
            part = r.gst[...] if s.padded else r.GR[m, oc - 1]
            total = total + part.astype(F32)
        r.ZS[m] = total.astype(BF)
        for o in range(1, W):
            remote(
                r.ZS.at[m, pl.ds(aligned(flip(z, o) * s.pr, 16), s.pr)],
                r.ZR.at[m, o - 1],
                r.x_rb.at[m],
                r.rb.at[m],
                zpeer(o),
            ).start()

    def spread(m):
        got(r.ZR.at[m], r.rb.at[m])
        total = r.ZS[m, pl.ds(aligned(z * s.pr, 16), s.pr), :].astype(F32)
        for o in range(1, W):
            total = total + r.ZR[m, o - 1].astype(F32)
        mine = pl.ds(aligned(c * s.pr, 16), s.pr)
        r.FG[m, mine, here] = total.astype(BF)
        part = r.FG.at[m, mine, here]
        for oc in range(1, C):
            remote(part, part, r.x_rc.at[m], r.rc.at[m], cpeer(oc)).start()

    def share_sum(m):
        got(r.FG.at[m, pl.ds(0, (C - 1) * s.pr), here], r.rc.at[m])
        part = r.FG.at[m, :, here]
        remote(part, part, r.x_rd.at[m], r.rd.at[m], sib).start()

    normed_grad = (
        dot_rt(r.dq[...], r.wfull[0]) + dot_rt(r.dk[...], r.wfull[1]) + dot_rt(r.dv[...], r.wfull[2])
    )
    plane_sum(0, r.nT, r.dq)
    shard_sum(3)
    x = r.xb[...].astype(F32)
    along = normed_grad * r.rows[0:1, :]
    r.tokens_grad[...] = (
        r.mg[...]
        + scale1 * along
        - x * (scale1 * scale1 * scale1 * jnp.mean(along * x, axis=1, keepdims=True))
    )
    r.rows[3:4, :] = jnp.sum(normed_grad * x * scale1, axis=0, keepdims=True)
    r.bt[...] = jnp.zeros_like(r.bt)
    mirror = (iota((T, T), 0) + iota((T, T), 1) == T - 1).astype(F32).astype(BF)

    def bias_back(h, carry):
        mirrored = dot(r.probs[h].astype(BF), mirror)
        wide = jnp.concatenate([mirrored, jnp.zeros((T, T), F32)], axis=1)
        turned = pltpu.roll(wide, 0, 1, stride=1, stride_axis=0)
        r.bt[pl.ds(REL_LANE + h, 1), :] = jnp.sum(turned, axis=0, keepdims=True)
        return carry

    lax.fori_loop(0, s.H, bias_back, 0)
    plane_sum(1, r.nT, r.dk)
    shard_sum(2)
    high, rest = two_parts(r.bt[...])
    rel_grad = dot_rt(r.ohm[...], high) + dot_rt(r.ohm[...], rest)
    lane_col = iota((LANES, 1), 0)
    small = jnp.where(
        lane_col == GAIN_ATTN_LANE,
        r.rows[3:4, :],
        jnp.where(lane_col == GAIN_FFN_LANE, r.rows[2:3, :], router_grad),
    ).T
    blocks = []
    for block in range(W):
        part = small[block * s.SR : (block + 1) * s.SR]
        head = part[: s.NBP] + rel_grad[block * s.NBP : (block + 1) * s.NBP]
        blocks.append(jnp.concatenate([head, part[s.NBP :]], axis=0))
    small = jnp.concatenate(blocks, axis=0).astype(BF)
    r.smo[...] = spread_rows(small)
    remote(r.smo, r.sms, r.x_rd.at[4], r.rd.at[4], sib).start()
    spread(3)
    got(r.sms, r.rd.at[4])
    pair = (r.smo[...].astype(F32) + r.sms[...].astype(F32)).astype(BF)
    for block in range(W):
        for chip in range(C):
            at = block * s.CP + chip * s.pr
            r.hGS[chip, block * s.pr : (block + 1) * s.pr, :] = pair[at : at + s.pr]
    for oc in range(1, C):
        remote(r.hGS.at[flip(c, oc)], r.hGR.at[oc - 1], r.x_ra.at[4], r.ra.at[4], cpeer(oc)).start()
    line_sent(r.Gr, r.x_gu, r.x_gd)
    for o in range(1, W):
        got(r.Tr.at[pl.ds(0, R)], r.t2.at[o])

    def scale_rows(step, carry):
        at = pl.ds(aligned(step * R, 16), R)
        gates = jnp.sum(r.Tr[at, :].astype(F32), axis=1, keepdims=True)
        r.Gr[at, :] = (r.Gr[at, :].astype(F32) * gates).astype(BF)
        r.ig[at, :] = (r.ig[at, :].astype(F32) * gates).astype(BF)
        return carry

    lax.fori_loop(0, W, scale_rows, 0)
    tile, slots = s.tile, s.slots

    def save_out(step):
        slot = lax.rem(step, slots)
        at = pl.ds(aligned(step * tile, LANES), tile)
        return pltpu.make_async_copy(r.gwo.at[slot], r.grad_w_out.at[at], r.gwo_sem.at[slot])

    def save_in(step):
        slot = lax.rem(step, slots)
        at = pl.ds(aligned(step * tile, LANES), tile)
        return pltpu.make_async_copy(r.gwi.at[slot], r.grad_w_in.at[at], r.gwi_sem.at[slot])

    def grad_out_tile(step, carry):
        @pl.when(step >= slots)
        def _():
            save_out(step - slots).wait()

        at = pl.ds(aligned(step * tile, LANES), tile)
        r.gwo[lax.rem(step, slots)] = dot_lt(r.act[:, at], r.Gr[...]).astype(BF)
        save_out(step).start()
        return carry

    def grad_in_tile(step, carry):
        @pl.when(step >= slots)
        def _():
            save_in(step - slots).wait()

        at = pl.ds(aligned(step * tile, LANES), tile)
        r.gwi[lax.rem(step, slots)] = dot_lt(r.Nr[:, at], r.ig[...]).astype(BF)
        save_in(step).start()
        return carry


    lax.fori_loop(0, s.F // tile, grad_out_tile, 0)
    shard_sum(0)
    spread(2)
    share_sum(3)
    lax.fori_loop(0, D // tile, grad_in_tile, 0)
    shard_sum(1)
    spread(0)
    share_sum(2)
    for step in passes:
        results_pass(step)
    pl.when(z < W - 1)(functools.partial(result_merge, z, z, r.rdn.at[0]))
    pl.when(z > 0)(functools.partial(result_merge, z, z + 1, r.ru.at[0]))
    r.Rb[...] = RS[z].astype(s.dt)
    plane_back(1, r.Rb, r.Rk, range(E))

    got(r.hGR, r.ra.at[4])
    total = r.hGS[c].astype(F32)
    for oc in range(1, C):
        total = total + r.hGR[oc - 1].astype(F32)
    r.hZS[...] = total.astype(BF)
    for o in range(1, W):
        remote(
            r.hZS.at[pl.ds(aligned(flip(z, o) * s.pr, 16), s.pr)],
            r.hZR.at[o - 1],
            r.x_rb.at[4],
            r.rb.at[4],
            zpeer(o),
        ).start()
    spread(1)
    share_sum(0)
    got(r.hZR, r.rb.at[4])
    total = r.hZS[pl.ds(aligned(z * s.pr, 16), s.pr), :].astype(F32)
    for o in range(1, W):
        total = total + r.hZR[o - 1].astype(F32)
    mine = pl.ds(aligned(c * s.pr, 16), s.pr)
    r.hFG[mine, :] = total.astype(BF)
    for oc in range(1, C):
        part = r.hFG.at[mine]
        remote(part, part, r.x_rc.at[4], r.rc.at[4], cpeer(oc)).start()

    got(r.Rk.at[pl.ds(0, (E - 1) * cp)], r.back.at[1])
    r.layer_out[...] = (r.middle[...] + gate * dot(r.pt[...], r.Rk[...].astype(BF))).astype(BF)

    share_sum(1)
    got(r.hFG.at[pl.ds(0, (C - 1) * s.pr)], r.rc.at[4])

    def unpad(value):
        return dot(r.unsel[...], value) if s.padded else value.astype(F32)

    r.smalls[...] = unpad(r.hFG[...])
    for m in (3, 0, 1, 2):
        got(r.FG.at[m, :, there], r.rd.at[m])
        r.grads[m] = unpad(r.FG[m]).astype(r.grads.dtype)

    for step in range(max(0, s.F // tile - slots), s.F // tile):
        save_out(step).wait()
    for step in range(max(0, D // tile - slots), D // tile):
        save_in(step).wait()
    sent(r.smg.at[pl.ds(0, W - 1)], r.x_sm)
    for m in range(4):
        part = r.wfull.at[m, pl.ds(0, s.pw), here]
        for d in range(W - 1):
            pl.when((z >= d) & (z < W - 1))(functools.partial(sent, part, r.x_wu.at[m, d]))
            pl.when((z + d <= W - 1) & (z > 0))(functools.partial(sent, part, r.x_wd.at[m, d]))
        if s.team > 1:
            sent(r.wfull.at[m, pl.ds(0, (W - 1) * (s.team - 1) * s.pw), here], r.x_wb.at[m])
        sent(r.wfull.at[m, others, here], r.x_wc.at[m])
        sent(r.fac.at[m], r.x_sibF.at[m])
        sent(r.GR.at[m], r.x_ra.at[m])
        sent(r.ZR.at[m], r.x_rb.at[m])
        sent(r.FG.at[m, pl.ds(0, (C - 1) * s.pr), here], r.x_rc.at[m])
        sent(r.FG.at[m, :, here], r.x_rd.at[m])
    for index, buffer in enumerate((r.gsend, r.nsend, r.tsend)):
        sent(buffer.at[pl.ds(0, E - 1)], r.x_d1.at[index])
    line_sent(r.Nr, r.x_nu, r.x_nd)
    sent(r.Tr.at[pl.ds(0, (W - 1) * R)], r.x_t2)
    for d in range(1, W):
        if early:
            pl.when(z >= d)(functools.partial(sent, r.SS.at[0], r.x_sd.at[d]))
            pl.when(z + d <= W - 1)(functools.partial(sent, r.SS.at[0], r.x_su.at[d]))
        pl.when(z >= d)(functools.partial(sent, r.SS.at[0], r.x_rdn.at[d]))
        pl.when(z + d <= W - 1)(functools.partial(sent, r.SS.at[0], r.x_ru.at[d]))
    for plane in range(W):
        pl.when(z != plane)(functools.partial(sent, r.HS.at[0], r.x_hz.at[plane]))
    sent(r.Hk.at[pl.ds(0, E - 1)], r.x_hp)
    sent(r.Sk.at[pl.ds(0, (E - 1) * cp)], r.x_back.at[0])
    sent(r.Rk.at[pl.ds(0, (E - 1) * cp)], r.x_back.at[1])
    sent(r.nT.at[:, pl.ds(0, T)], r.x_sibT.at[0])
    sent(r.mT.at[:, pl.ds(0, T)], r.x_sibT.at[1])
    sent(r.hGR, r.x_ra.at[4])
    sent(r.hZR, r.x_rb.at[4])
    sent(r.hFG.at[pl.ds(0, (C - 1) * s.pr)], r.x_rc.at[4])
    sent(r.smo, r.x_rd.at[4])


def selection(s):
    share = s.SR // s.C
    unsel = np.zeros((s.SR, s.CP), np.float32)
    for chip in range(s.C):
        for at in range(share):
            unsel[chip * share + at, chip * s.pr + at] = 1
    return jnp.asarray(unsel, BF)


PARTS = 3


def finish(s, *refs):
    layer_out, tokens_grad, grads, smalls, grad_in, grad_out = refs[:6]
    out_layer, out_tokens, *out_mixers = refs[6:12]
    out_in, out_out, out_gain1, out_gain2, out_rel, out_router = refs[12:18]
    low_mix, low_in, low_out, mix, into, outof, held_layer, held_tokens = refs[18:26]
    pass_sem, load_sem, save_sem, load2, save2 = refs[26:]
    through = (
        (layer_out, held_layer, out_layer),
        (tokens_grad, held_tokens, out_tokens),
    )
    loads = [
        pltpu.make_async_copy(source, held, pass_sem.at[0, index])
        for index, (source, held, _) in enumerate(through)
    ]
    saves = [
        pltpu.make_async_copy(held, target, pass_sem.at[1, index])
        for index, (_, held, target) in enumerate(through)
    ]
    for m in range(4):
        loads.append(pltpu.make_async_copy(grads.at[m], low_mix.at[m], load_sem.at[m]))
        saves.append(pltpu.make_async_copy(mix.at[m], out_mixers[m], save_sem.at[m]))
    steps = [None, None] + [(low_mix, mix, m) for m in range(4)]
    for index, (source, low, high, target) in enumerate(
        ((grad_in, low_in, into, out_in), (grad_out, low_out, outof, out_out))
    ):
        rows = source.shape[0] // PARTS
        for part in range(PARTS):
            at = pl.ds(part * rows, rows)
            loads.append(
                pltpu.make_async_copy(source.at[at], low.at[at], load2.at[index, part])
            )
            saves.append(
                pltpu.make_async_copy(high.at[at], target.at[0, at], save2.at[index, part])
            )
            steps.append((low, high, at))
    for copy in loads:
        copy.start()
    turned = smalls[...].T
    out_router[...] = turned[: s.NX]
    out_gain1[...] = turned[GAIN_ATTN_LANE : GAIN_ATTN_LANE + 1]
    out_gain2[...] = turned[GAIN_FFN_LANE : GAIN_FFN_LANE + 1]
    out_rel[...] = smalls[: s.NBH, REL_LANE : REL_LANE + s.H]
    for load, save, step in zip(loads, saves, steps, strict=True):
        load.wait()
        if step is not None:
            low, high, at = step
            high[at] = low[at].astype(F32)
        save.start()
    for copy in saves:
        copy.wait()


def local(
    tokens,
    norm_gain_attn,
    w_query,
    w_key,
    w_value,
    w_output,
    rel_bias,
    norm_gain_ffn,
    w_router,
    w_in,
    w_out,
    out_grad,
    expert_ids,
    priority,
    lengths,
    seq_order,
    relpos_table,
):
    tok_count, width = tokens.shape
    buckets_here, heads = rel_bias.shape
    n_experts = w_router.shape[1]
    s = plan(
        lax.axis_size("expert"),
        lax.axis_size("wshard"),
        tok_count,
        width,
        heads,
        buckets_here,
        n_experts,
        w_in.shape[2],
    )
    operands = [
        lengths, seq_order, expert_ids.reshape(1, tok_count), priority.reshape(1, tok_count),
        relpos_table.reshape(1, -1), w_router.T, norm_gain_attn,
        norm_gain_ffn, rel_bias,
        tokens, out_grad, w_query, w_key, w_value, w_output, w_in, w_out,
    ]
    smem, vmem, anywhere = (
        pl.BlockSpec(memory_space=space) for space in (pltpu.SMEM, pltpu.VMEM, pl.ANY)
    )
    in_specs = [smem] * 2 + [vmem] * 7 + [anywhere] * 8
    names = IN_NAMES
    if s.padded:
        operands.append(selection(s))
        in_specs.append(vmem)
        names = names + PAD_NAMES
    spilled = (jax.ShapeDtypeStruct(pieces_shape(s), BF),) if s.padded else ()
    scratch = scratch_list(s)
    names = names + OUT_NAMES + ("GR",) * len(spilled) + tuple(name for name, _ in scratch)
    outs = pl.pallas_call(
        functools.partial(kernel, s, names),
        name="layer",
        out_shape=(
            jax.ShapeDtypeStruct((s.T, s.D), BF),
            jax.ShapeDtypeStruct((s.T, s.D), F32),
            jax.ShapeDtypeStruct((4, s.SR, s.D), BF),
            jax.ShapeDtypeStruct((s.SR, LANES), F32),
            jax.ShapeDtypeStruct((s.D, s.F), BF),
            jax.ShapeDtypeStruct((s.F, s.D), BF),
            *spilled,
        ),
        in_specs=in_specs,
        out_specs=(vmem, vmem, vmem, vmem, anywhere, anywhere) + (anywhere,) * len(spilled),
        scratch_shapes=[shape for _, shape in scratch],
        compiler_params=pltpu.CompilerParams(
            collective_id=0, has_side_effects=True, vmem_limit_bytes=62 * 2**20
        ),
    )(*operands)
    done = pl.pallas_call(
        functools.partial(finish, s),
        name="finish",
        out_shape=(
            jax.ShapeDtypeStruct((s.T, s.D), BF),
            jax.ShapeDtypeStruct((s.T, s.D), F32),
            *[jax.ShapeDtypeStruct((s.SR, s.D), F32)] * 4,
            jax.ShapeDtypeStruct((1, s.D, s.F), F32),
            jax.ShapeDtypeStruct((1, s.F, s.D), F32),
            jax.ShapeDtypeStruct((1, s.SR), F32),
            jax.ShapeDtypeStruct((1, s.SR), F32),
            jax.ShapeDtypeStruct((buckets_here, heads), F32),
            jax.ShapeDtypeStruct((n_experts, s.SR), F32),
        ),
        in_specs=[anywhere, anywhere, anywhere, vmem, anywhere, anywhere],
        out_specs=(anywhere,) * 8 + (vmem,) * 4,
        scratch_shapes=[
            pltpu.VMEM((4, s.SR, s.D), BF),
            pltpu.VMEM((s.D, s.F), BF),
            pltpu.VMEM((s.F, s.D), BF),
            pltpu.VMEM((4, s.SR, s.D), F32),
            pltpu.VMEM((s.D, s.F), F32),
            pltpu.VMEM((s.F, s.D), F32),
            pltpu.VMEM((s.T, s.D), BF),
            pltpu.VMEM((s.T, s.D), F32),
            pltpu.SemaphoreType.DMA((2, 2)),
            pltpu.SemaphoreType.DMA((4,)),
            pltpu.SemaphoreType.DMA((4,)),
            pltpu.SemaphoreType.DMA((2, PARTS)),
            pltpu.SemaphoreType.DMA((2, PARTS)),
        ],
        compiler_params=pltpu.CompilerParams(vmem_limit_bytes=62 * 2**20),
    )(*outs[:6])
    layer_out, tokens_grad, gq, gk, gv, go, grad_w_in, grad_w_out, gain1, gain2, rel, router = done
    return (
        layer_out,
        tokens_grad,
        gain1.reshape(s.SR),
        gq,
        gk,
        gv,
        go,
        rel,
        gain2.reshape(s.SR),
        router.T,
        grad_w_in,
        grad_w_out,
    )


def solution(mesh):
    rows = P(("expert", "wshard"), None)
    shard = P("wshard", None)
    into, outof = P("expert", None, "wshard"), P("expert", "wshard", None)
    return jax.shard_map(
        local,
        mesh=mesh,
        in_specs=(
            rows,
            P("wshard"),
            shard,
            shard,
            shard,
            shard,
            shard,
            P("wshard"),
            shard,
            into,
            outof,
            rows,
            rows,
            P(("expert", "wshard")),
            P(),
            P(),
            P(),
        ),
        out_specs=(
            rows,
            rows,
            P("wshard"),
            shard,
            shard,
            shard,
            shard,
            shard,
            P("wshard"),
            shard,
            into,
            outof,
        ),
        check_vma=False,
    )
```

```python
import functools
import types

import jax
import jax.numpy as jnp
import numpy as np
from jax import lax
from jax.experimental import pallas as pl
from jax.experimental.pallas import tpu as pltpu
from jax.sharding import PartitionSpec as P

EPSILON = 1e-06
NEG_FILL = -1e30
GELU_A = 0.79788456
GELU_B = 0.044715
LANES = 128
REL_LANE = 64
GAIN_ATTN_LANE = 126
GAIN_FFN_LANE = 127
MESH = pl.DeviceIdType.MESH
BF = jnp.bfloat16
F32 = jnp.float32
I32 = jnp.int32


def up16(count):
    return -(-count // 16) * 16


def dot(a, b):
    return jnp.dot(a, b, preferred_element_type=F32)


def dot_rt(a, b):
    return lax.dot_general(a, b, (((1,), (1,)), ((), ())), preferred_element_type=F32)


def dot_lt(a, b):
    return lax.dot_general(a, b, (((0,), (0,)), ((), ())), preferred_element_type=F32)


def iota(shape, axis):
    return lax.broadcasted_iota(I32, shape, axis)


def flip(index, offset):
    out = index
    bit = 1
    while bit <= offset:
        if offset & bit:
            out = out + bit * (1 - 2 * lax.rem(lax.div(index, bit), 2))
        bit *= 2
    return out


def aligned(value, step):
    return pl.multiple_of(value, step)


def two_parts(value):
    high = value.astype(BF)
    return high, (value - high.astype(F32)).astype(BF)


def plan(expert_size, shard_size, tok_count, width, heads, buckets_here, n_experts, hidden):
    s = types.SimpleNamespace()
    s.E, s.W = expert_size, shard_size
    s.C = expert_size // 2
    s.T, s.D, s.H = tok_count, width, heads
    s.HD = width // heads
    s.F = hidden
    s.NX = n_experts
    s.cap = tok_count // n_experts
    s.cp = s.cap if s.cap % 8 == 0 else up16(s.cap)
    s.dt = BF if s.cp % 16 == 0 else F32
    s.S = n_experts * s.cp
    s.R = s.E * s.cp
    s.SR = width // shard_size
    s.NBH = buckets_here
    s.NBP = up16(buckets_here)
    s.half = width // 2
    s.P1 = up16(n_experts + 2)
    s.LW = -(-s.SR // LANES) * LANES
    team = s.C
    while s.SR % team or (s.SR // team) % 16:
        team //= 2
    s.team = team
    s.pw = s.SR // team
    s.pr = up16(s.SR // s.C)
    s.CP = s.C * s.pr
    s.Dp = s.W * s.CP
    s.padded = s.CP != s.SR
    s.tile = LANES
    s.slots = 2 if s.padded else max(width, hidden) // s.tile
    return s


def pieces_shape(s):
    return (4, s.C - 1, s.W * s.pr, s.half)


def arrivals(s):
    return (("Ga", s.D), ("Na", s.D)) if s.dt == F32 else ()


def scratch_list(s):
    V = pltpu.VMEM
    dma = pltpu.SemaphoreType.DMA
    return [
        ("wfull", V((4, s.D, s.D), BF)),
        ("smf", V((s.P1 + s.NBP, s.LW), F32)),
        ("smg", V((s.W, s.P1 + s.NBP, s.LW), BF)),
        ("tab", V((8, 2 * s.T), I32)),
        ("xb", V((s.T, s.D), BF)),
        ("og", V((s.T, s.D), BF)),
        ("wi", V((s.D, s.F), BF)),
        ("wo", V((s.F, s.D), BF)),
        ("pm", V((s.S, s.T), BF)),
        ("pt", V((s.T, s.S), BF)),
        ("gsend", V((s.NX, s.cp, s.D), s.dt)),
        ("nsend", V((s.NX, s.cp, s.D), s.dt)),
        ("Qs", V((8, s.S), F32)),
        ("Qk", V((s.E, 8, s.S), F32)),
        ("Qr", V((s.W, 8, s.R), F32)),
        ("Gr", V((s.W * s.R, s.D), BF)),
        ("Nr", V((s.W * s.R, s.D), BF)),
        ("agr", V((s.W * s.R, s.F), BF)),
        ("act", V((s.W * s.R, s.F), BF)),
        ("ig", V((s.W * s.R, s.F), BF)),
        ("SS", V((s.W, s.R, s.D), BF)),
        ("Sin", V((s.W + 1, s.R, s.D), BF)),
        ("Sb", V((s.R, s.D), s.dt)),
        ("Sk", V((s.S, s.D), s.dt)),
        ("HS", V((s.W, 8, s.R), F32)),
        ("Hr", V((s.W, 8, s.R), F32)),
        ("Hb", V((8, s.R), F32)),
        ("Hk", V((s.E, 8, s.R), F32)),
        ("Hm", V((LANES, s.R), F32)),
        ("Rb", V((s.R, s.D), s.dt)),
        ("Rk", V((s.S, s.D), s.dt)),
        ("tb", V((LANES, 2 * s.T), F32)),
        ("ohm", V((s.W * s.NBP, 2 * s.T), BF)),
        ("rows", V((8, s.D), F32)),
        ("RwT", V((LANES, s.D), BF)),
        ("probs", V((s.H, s.T, s.T), F32)),
        ("q", V((s.T, s.D), BF)),
        ("kk", V((s.T, s.D), BF)),
        ("v", V((s.T, s.D), BF)),
        ("mixed", V((s.T, s.D), BF)),
        ("nf", V((s.T, s.D), BF)),
        ("middle", V((s.T, s.D), F32)),
        ("mg", V((s.T, s.D), F32)),
        ("att", V((s.T, s.D), BF)),
        ("dq", V((s.T, s.D), BF)),
        ("dk", V((s.T, s.D), BF)),
        ("dv", V((s.T, s.D), BF)),
        ("nT", V((s.Dp, 2 * s.T), BF)),
        ("mT", V((s.Dp, 2 * s.T), BF)),
        ("fac", V((4, s.T, s.half), BF)),
        ("GS", V((4, s.C, s.W * s.pr, s.half), BF)),
        ("ZS", V((4, s.W * s.pr, s.half), BF)),
        ("ZR", V((4, s.W - 1, s.pr, s.half), BF)),
        ("FG", V((4, s.CP, s.D), BF)),
        ("smo", V((s.Dp, LANES), BF)),
        ("sms", V((s.Dp, LANES), BF)),
        ("hGS", V((s.C, s.W * s.pr, LANES), BF)),
        ("hGR", V((s.C - 1, s.W * s.pr, LANES), BF)),
        ("hZS", V((s.W * s.pr, LANES), BF)),
        ("hZR", V((s.W - 1, s.pr, LANES), BF)),
        ("hFG", V((s.CP, LANES), BF)),
        ("bt", V((LANES, 2 * s.T), F32)),
        ("gwi", V((s.slots, s.tile, s.F), BF)),
        ("gwo", V((s.slots, s.tile, s.D), BF)),
        ("gwi_sem", dma((s.slots,))),
        ("gwo_sem", dma((s.slots,))),
        ("lsem", dma((9,))),
        ("osem", dma((7,))),
        ("smallest", V((s.SR, LANES), F32)),
        ("smr", dma((s.W,))),
        ("wu", dma((4, s.W))),
        ("wd", dma((4, s.W))),
        ("wbu", dma((4, s.W))),
        ("wbd", dma((4, s.W))),
        ("wc", dma((4,))),
        ("g1", dma((s.C,))),
        ("gu", dma((s.W, s.C))),
        ("gd", dma((s.W, s.C))),
        ("n1", dma((s.C,))),
        ("nu", dma((s.W, s.C))),
        ("nd", dma((s.W, s.C))),
        ("t1", dma),
        ("t2", dma((s.W,))),
        ("hz", dma((s.W,))),
        ("hp", dma),
        ("x_hz", dma((s.W,))),
        ("x_hp", dma),
        ("su", dma((s.W, s.C))),
        ("sd", dma((s.W, s.C))),
        ("ru", dma((s.W,))),
        ("rdn", dma((s.W,))),
        ("back", dma((2,))),
        ("sibT", dma((2,))),
        ("sibF", dma((4,))),
        ("ra", dma((5,))),
        ("rb", dma((5,))),
        ("rc", dma((5,))),
        ("rd", dma((5,))),
        ("x_sm", dma),
        ("x_wu", dma((4, s.W))),
        ("x_wd", dma((4, s.W))),
        ("x_wb", dma((4,))),
        ("x_wc", dma((4,))),
        ("x_d1", dma((2,))),
        ("x_t1", dma),
        ("x_t2", dma),
        ("x_gu", dma((s.W,))),
        ("x_gd", dma((s.W,))),
        ("x_nu", dma((s.W,))),
        ("x_nd", dma((s.W,))),
        ("x_su", dma((s.W,))),
        ("x_sd", dma((s.W,))),
        ("x_ru", dma((s.W,))),
        ("x_rdn", dma((s.W,))),
        ("x_back", dma((2,))),
        ("x_sibT", dma((2,))),
        ("x_sibF", dma((4,))),
        ("x_ra", dma((5,))),
        ("x_rb", dma((5,))),
        ("x_rc", dma((5,))),
        ("x_rd", dma((5,))),
        ("credit", pltpu.SemaphoreType.REGULAR),
    ] + (
        [("gst", V((s.W * s.pr, s.half), BF)), ("unpadded", V((4, s.SR, s.D), BF))]
        + [(name, V((s.R, width), F32)) for name, width in arrivals(s)]
        if s.padded
        else [
            ("GR", V(pieces_shape(s), BF)),
            ("GX", V((4, 2, 2, s.W * s.pr // 2, s.half), BF)),
            ("GY", V((4, s.W * s.pr, s.half), BF)),
            ("gx", dma((4, 2))),
            ("gy", dma((4, 2))),
            ("x_gx", dma((4, 2))),
            ("x_gy", dma((4, 2))),
            ("RS", V((s.W, s.R, s.D), BF)),
            ("Rin", V((s.W + 1, s.R, s.D), BF)),
        ]
    )


IN_NAMES = (
    "lengths", "seq", "ids", "prio", "table", "router", "gain_attn", "gain_ffn", "bias",
    "tokens", "out_grad", "w0", "w1", "w2", "w3", "w_in", "w_out",
)
PAD_NAMES = ("unsel",)
OUT_NAMES = ("layer_out", "tokens_grad", "grads", "smalls", "grad_w_in", "grad_w_out")


def kernel(s, names, *refs):
    r = types.SimpleNamespace(**dict(zip(names, refs, strict=True)))
    e = lax.axis_index("expert")
    z = lax.axis_index("wshard")
    c = lax.div(e, 2)
    k = lax.rem(e, 2)
    T, D, E, W, C, R, cp, half = s.T, s.D, s.E, s.W, s.C, s.R, s.cp, s.half
    sib = (flip(e, 1), z)
    here = pl.ds(aligned(k * half, LANES), half)
    there = pl.ds(aligned((1 - k) * half, LANES), half)

    def zpeer(offset):
        return (e, flip(z, offset))

    def cpeer(offset):
        return (flip(c, offset) * 2 + k, z)

    def remote(src, dst, send, recv, device):
        return pltpu.make_async_remote_copy(
            src_ref=src, dst_ref=dst, send_sem=send, recv_sem=recv, device_id=device, device_id_type=MESH
        )

    def got(ref, sem):
        remote(ref, ref, sem, sem, sib).wait_recv()

    def sent(ref, sem):
        remote(ref, ref, sem, sem, sib).wait_send()

    barrier = pltpu.get_barrier_semaphore()
    peers = [(flip(e, o), z) for o in range(1, E)] + [zpeer(o) for o in range(1, W)]
    for peer in peers:
        pl.semaphore_signal(barrier, inc=1, device_id=peer, device_id_type=MESH)

    shards = (r.w0, r.w1, r.w2, r.w3)
    own_rows = pl.ds(aligned(z * s.SR, 16), s.SR)
    load_w = [
        pltpu.make_async_copy(shards[m], r.wfull.at[m, own_rows], r.lsem.at[m])
        for m in range(4)
    ]
    load_og = pltpu.make_async_copy(r.out_grad, r.og, r.lsem.at[4])
    load_x = pltpu.make_async_copy(r.tokens, r.xb, r.lsem.at[5])
    load_wo = pltpu.make_async_copy(r.w_out.at[0], r.wo, r.lsem.at[6])
    load_wi = pltpu.make_async_copy(r.w_in.at[0], r.wi, r.lsem.at[7])
    load_og.start()

    r.smf[...] = jnp.zeros_like(r.smf)
    r.smf[0 : s.NX, 0 : s.SR] = r.router[...].astype(F32)
    r.smf[s.NX : s.NX + 1, 0 : s.SR] = r.gain_attn[...].astype(F32).reshape(1, s.SR)
    r.smf[s.NX + 1 : s.NX + 2, 0 : s.SR] = r.gain_ffn[...].astype(F32).reshape(1, s.SR)
    r.smf[s.P1 : s.P1 + s.NBH, 0 : s.H] = r.bias[...].astype(F32)
    r.smg[z] = r.smf[...].astype(BF)
    pl.semaphore_wait(barrier, len(peers))

    team_c = lax.rem(c, s.team)
    for o in range(1, W):
        remote(r.smg.at[z], r.smg.at[z], r.x_sm, r.smr.at[o], zpeer(o)).start()
    share_rows = pl.ds(aligned(team_c * s.pw, 16), s.pw)
    def weight_at(plane):
        return pl.ds(aligned(plane * s.SR + team_c * s.pw, 16), s.pw)

    def weight_own(m):
        def send(sender, receiver, to):
            source = shards[m].at[share_rows, here]
            remote(source, r.wfull.at[m, weight_at(z), here], sender, receiver, (e, to)).start()

        pl.when(z < W - 1)(functools.partial(send, r.x_wu.at[m, 0], r.wu.at[m, 1], z + 1))
        pl.when(z > 0)(functools.partial(send, r.x_wd.at[m, 0], r.wd.at[m, 1], z - 1))

    for m in range(3):
        weight_own(m)
    for copy in (load_x, *load_w, load_wo, load_wi):
        copy.start()
    device = e * W + z
    first = r.lengths[r.seq[2 * device]]
    both = first + r.lengths[r.seq[2 * device + 1]]
    col = iota((T, 1), 0)
    row = iota((1, T), 1)
    seg_col = (col >= first).astype(I32) + (col >= both).astype(I32)
    seg_row = (row >= first).astype(I32) + (row >= both).astype(I32)
    same = seg_col == seg_row
    valid = (col < both).astype(F32)
    eye = iota((T, T), 0) == iota((T, T), 1)
    id_row = r.ids[...].astype(F32)
    id_col = jnp.sum(jnp.where(eye, id_row, 0.0), axis=1, keepdims=True)
    prio_row = r.prio[...].astype(F32)
    prio_col = jnp.sum(jnp.where(eye, prio_row, 0.0), axis=1, keepdims=True)
    ahead = (id_col == id_row) & (prio_col < prio_row)
    slot_row = jnp.sum(jnp.where(ahead, valid, 0.0), axis=0, keepdims=True)
    kept = (row < both) & (slot_row < s.cap)
    flat_row = jnp.where(kept, id_row * cp + slot_row, -1.0)
    flat_col = jnp.sum(jnp.where(eye, flat_row, 0.0), axis=1, keepdims=True)
    r.pm[...] = (iota((s.S, T), 0).astype(F32) == flat_row).astype(F32).astype(BF)
    r.pt[...] = (iota((T, s.S), 1).astype(F32) == flat_col).astype(F32).astype(BF)

    plane_step = 16 if s.dt == BF else 8
    plane_rows = z * R if s.dt == BF else 0

    def dispatch(index, send, rows, first_sem, value):
        width = rows.shape[1]
        buffer = dot(r.pm[...], value)
        send[...] = buffer.astype(s.dt).reshape(s.NX, cp, width)
        mine = pl.ds(aligned(plane_rows + e * cp, plane_step), cp)
        for o in range(1, E):
            x = flip(e, o)
            remote(
                send.at[x], rows.at[mine], r.x_d1.at[index], first_sem.at[o // 2], (x, z)
            ).start()
        rows[mine, :] = send[e]

    def block_at(plane, oc):
        return pl.ds(aligned(plane * R + flip(c, oc) * 2 * cp, 16), 2 * cp)

    def landed(rows, arrived, first_sem, oc):
        got(arrived.at[pl.ds(0, (2 if oc else 1) * cp)], first_sem.at[oc])
        if s.dt != BF:
            rows[block_at(z, oc), :] = arrived[block_at(0, oc), :].astype(BF)

    def move(part, send, recv, to):
        remote(part, part, send, recv, (e, to)).start()

    def line_own(rows, arrived, first_sem, up, down, x_up, x_down):
        for oc in range(C):
            landed(rows, arrived, first_sem, oc)
            part = rows.at[block_at(z, oc)]
            pl.when(z < W - 1)(functools.partial(move, part, x_up.at[0], up.at[1, oc], z + 1))
            pl.when(z > 0)(functools.partial(move, part, x_down.at[0], down.at[1, oc], z - 1))

    def line_pass(rows, d, up, down, x_up, x_down):
        for oc in range(C):

            @pl.when(z >= d)
            def _():
                part = rows.at[block_at(z - d, oc)]
                got(part, up.at[d, oc])
                if d < W - 1:
                    pl.when(z < W - 1)(
                        functools.partial(move, part, x_up.at[d], up.at[d + 1, oc], z + 1)
                    )

            @pl.when(z + d <= W - 1)
            def _():
                part = rows.at[block_at(z + d, oc)]
                got(part, down.at[d, oc])
                if d < W - 1:
                    pl.when(z > 0)(
                        functools.partial(move, part, x_down.at[d], down.at[d + 1, oc], z - 1)
                    )

    def line_sent(rows, x_up, x_down):
        for d in range(W - 1):
            whole = rows.at[pl.ds(0, R)]
            pl.when((z >= d) & (z < W - 1))(functools.partial(sent, whole, x_up.at[d]))
            pl.when((z + d <= W - 1) & (z > 0))(functools.partial(sent, whole, x_down.at[d]))

    g_line = (r.gu, r.gd, r.x_gu, r.x_gd)
    n_line = (r.nu, r.nd, r.x_nu, r.x_nd)
    Ga, Na = (r.Gr, r.Nr) if s.dt == BF else (r.Ga, r.Na)
    load_og.wait()
    dispatch(0, r.gsend, Ga, r.g1, r.og[...])

    def weight_pass(m, d):
        def handle(plane, arrived, onward, sender, receiver, to, beside):
            part = r.wfull.at[m, weight_at(plane), here]
            got(part, arrived)
            if d < W - 1:
                pl.when(onward)(functools.partial(move, part, sender, receiver, to))
            for oc in range(1, s.team):
                remote(part, part, r.x_wb.at[m], beside, cpeer(oc)).start()

        up, down, after = (m, d), (m, d), (m, min(d + 1, W - 1))
        pl.when(z >= d)(
            functools.partial(
                handle, z - d, r.wu.at[up], z < W - 1, r.x_wu.at[up], r.wu.at[after], z + 1, r.wbu.at[up]
            )
        )
        pl.when(z + d <= W - 1)(
            functools.partial(
                handle, z + d, r.wd.at[down], z > 0, r.x_wd.at[down], r.wd.at[after], z - 1, r.wbd.at[down]
            )
        )

    def weight_share(m, d):
        def handle(plane, beside):
            if s.team > 1:
                got(r.wfull.at[m, pl.ds(0, (s.team - 1) * s.pw), here], beside)
            part = r.wfull.at[m, pl.ds(aligned(plane * s.SR, 16), s.SR), here]
            remote(part, part, r.x_wc.at[m], r.wc.at[m], sib).start()

        pl.when(z >= d)(functools.partial(handle, z - d, r.wbu.at[m, d]))
        pl.when(z + d <= W - 1)(functools.partial(handle, z + d, r.wbd.at[m, d]))

    others = pl.ds(0, (W - 1) * s.SR)

    def weight_ready(m):
        load_w[m].wait()
        got(r.wfull.at[m, others, there], r.wc.at[m])

    for d in range(1, W):
        for m in range(3):
            weight_pass(m, d)
        if d == 1:
            weight_own(3)
        else:
            weight_pass(3, d - 1)
            for m in range(3):
                weight_share(m, d - 1)
        if d == min(2, W - 1):
            line_own(r.Gr, Ga, r.g1, *g_line)
    weight_pass(3, W - 1)
    for m in range(3):
        weight_share(m, W - 1)
    for o in range(1, W):
        got(r.smg.at[0], r.smr.at[o])
    gathered = jnp.concatenate(
        [r.smg[w, : s.P1, : s.SR].astype(F32) for w in range(W)], axis=1
    )
    r.rows[0:1, :] = gathered[s.NX : s.NX + 1]
    r.rows[1:2, :] = gathered[s.NX + 1 : s.NX + 2]
    r.RwT[...] = jnp.zeros_like(r.RwT)
    r.RwT[: s.P1, :] = jnp.where(iota((s.P1, D), 0) < s.NX, gathered, 0.0).astype(BF)
    lane_row = iota((1, LANES), 1)
    r.tab[...] = jnp.full(r.tab.shape, -1, I32)
    r.tab[0:1, 0 : 2 * T - 1] = r.table[...]
    bucket = r.tab[0:1, :]
    shift = s.NBH.bit_length() - 1
    bucket = lax.shift_right_logical(bucket, shift) * s.NBP + lax.bitwise_and(bucket, s.NBH - 1)
    bucket = jnp.where(r.tab[0:1, :] < 0, -1, bucket)
    hot = (iota((W * s.NBP, 2 * T), 0) == bucket).astype(F32).astype(BF)
    backwards = (iota((2 * T, 2 * T), 0) + iota((2 * T, 2 * T), 1) == 2 * T - 2).astype(F32)
    r.ohm[...] = dot(hot, backwards.astype(BF)).astype(BF)
    bias_rows = r.smg[:, s.P1 :, :LANES].reshape(W * s.NBP, LANES)
    r.tb[...] = dot_lt(bias_rows, hot)

    def bias_head(h, carry):
        wide = jnp.broadcast_to(r.tb[pl.ds(h, 1), :], (T, 2 * T))
        turned = pltpu.roll(wide, T + 1, 1, stride=1, stride_axis=0)
        r.probs[h] = jnp.where(same, turned[:, :T], NEG_FILL)
        return carry

    lax.fori_loop(0, s.H, bias_head, 0)
    load_x.wait()
    x = r.xb[...].astype(F32)
    scale1 = lax.rsqrt(jnp.mean(x * x, axis=1, keepdims=True) + EPSILON)
    normed = (x * scale1 * r.rows[0:1, :]).astype(BF)

    def spread_rows(value):
        if not s.padded:
            return value
        shards = [value[at : at + s.SR] for at in range(0, D, s.SR)]
        return jnp.concatenate([dot_lt(r.unsel[...], shard) for shard in shards], axis=0).astype(BF)

    def turn_out(index, value, target):
        target[:, :T] = spread_rows(value.T)
        remote(
            target.at[:, pl.ds(0, T)], target.at[:, pl.ds(T, T)], r.x_sibT.at[index], r.sibT.at[index], sib
        ).start()

    turn_out(0, normed, r.nT)
    weight_ready(0)
    r.q[...] = dot(normed, r.wfull[0]).astype(BF)
    weight_ready(1)
    r.kk[...] = dot(normed, r.wfull[1]).astype(BF)
    weight_ready(2)
    r.v[...] = dot(normed, r.wfull[2]).astype(BF)
    for d in range(1, W):
        weight_share(3, d)
    line_pass(r.Gr, 1, *g_line)

    scale = s.HD ** (-0.5)
    low_lane = (lane_row < s.HD).astype(F32)
    lane_masks = (low_lane.astype(BF), (1.0 - low_lane).astype(BF))

    def attend(p, carry):
        cols = pl.ds(aligned(p * LANES, LANES), LANES)
        q, kk, v = r.q[:, cols], r.kk[:, cols], r.v[:, cols]
        outs = []
        for side in range(2):
            h = 2 * p + side
            scores = dot_rt(q * lane_masks[side], kk) * scale + r.probs[h]
            expo = jnp.exp(scores - jnp.max(scores, axis=1, keepdims=True))
            probs = expo * (1.0 / jnp.sum(expo, axis=1, keepdims=True))
            r.probs[h] = probs
            outs.append(dot(probs.astype(BF), v))
        r.mixed[:, cols] = jnp.where(lane_row < s.HD, outs[0], outs[1]).astype(BF)
        return carry

    lax.fori_loop(0, s.H // 2, attend, 0)
    mixed = r.mixed[...]
    weight_ready(3)
    middle = r.xb[...].astype(F32) + dot(mixed, r.wfull[3]) * valid
    r.middle[...] = middle
    scale2 = lax.rsqrt(jnp.mean(middle * middle, axis=1, keepdims=True) + EPSILON)
    nf = (middle * scale2 * r.rows[1:2, :]).astype(BF)
    r.nf[...] = nf
    dispatch(1, r.nsend, Na, r.n1, nf)
    logits = jnp.where(lane_row < s.NX, dot_rt(nf, r.RwT[...]), NEG_FILL)
    raised = jnp.exp(logits - jnp.max(logits, axis=1, keepdims=True))
    router = raised / jnp.sum(raised, axis=1, keepdims=True)
    picked = (lane_row.astype(F32) == id_col).astype(F32)
    gate = jnp.sum(router * picked, axis=1, keepdims=True)
    slot_gates = jnp.sum(jnp.where(r.pt[...] > 0, gate, 0.0), axis=0, keepdims=True)
    r.Qs[...] = jnp.broadcast_to(slot_gates, r.Qs.shape)
    r.Qk[e] = r.Qs[...]
    for o in range(1, E):
        remote(r.Qs, r.Qk.at[e], r.x_t1, r.t1, (flip(e, o), z)).start()
    if W > 2:
        line_pass(r.Gr, 2, *g_line)
    line_own(r.Nr, Na, r.n1, *n_line)
    got(r.Qk.at[pl.ds(0, E - 1)], r.t1)
    repeated = jnp.concatenate(
        [jnp.broadcast_to(r.Qk[x, 0:1, :], (cp, s.S)) for x in range(E)], axis=0
    )
    wanted = e * cp + lax.rem(iota((R, s.S), 0), cp)
    gate_col = jnp.sum(
        jnp.where(iota((R, s.S), 1) == wanted, repeated, 0.0), axis=1, keepdims=True
    )
    diagonal = iota((R, R), 0) == iota((R, R), 1)
    gate_line = jnp.sum(jnp.where(diagonal, gate_col, 0.0), axis=0, keepdims=True)
    r.Qr[z] = jnp.broadcast_to(gate_line, (8, R))
    for o in range(1, W):
        remote(r.Qr.at[z], r.Qr.at[z], r.x_t2, r.t2.at[o], zpeer(o)).start()
    turn_out(1, mixed, r.mT)

    load_wo.wait()
    for d in range(3, W):
        line_pass(r.Gr, d, *g_line)

    def back_rows(step, carry):
        at = pl.ds(aligned(step * R, 16), R)
        r.agr[at, :] = dot_rt(r.Gr[at, :], r.wo[...]).astype(BF)
        return carry

    lax.fori_loop(0, W, back_rows, 0)
    load_wi.wait()

    def expert_rows(plane, at, block):
        inner = dot(r.Nr[at, :], r.wi[...])
        square = inner * inner
        tanh = jnp.tanh(GELU_A * inner * (1.0 + GELU_B * square))
        active = (0.5 * inner * (1.0 + tanh)).astype(BF)
        slope = 0.5 * (1.0 + tanh) + (0.5 * GELU_A) * inner * (1.0 - tanh * tanh) * (
            1.0 + (3.0 * GELU_B) * square
        )
        inner_grad = (r.agr[at, :].astype(F32) * slope).astype(BF)
        r.act[at, :] = active
        r.ig[at, :] = inner_grad
        r.SS[plane, block, :] = dot_rt(inner_grad, r.wi[...]).astype(BF)

    def expert(plane):
        expert_rows(plane, pl.ds(aligned(plane * R, 16), R), pl.ds(0, R))

    def gate_sums(plane, carry):
        at = pl.ds(aligned(plane * R, 16), R)
        part = jnp.sum(
            r.act[at, :].astype(F32) * r.agr[at, :].astype(F32), axis=1, keepdims=True
        )
        r.HS[plane, 0:1, :] = jnp.sum(jnp.where(diagonal, part, 0.0), axis=0, keepdims=True)

        @pl.when(plane != z)
        def _():
            remote(r.HS.at[plane], r.Hr.at[z], r.x_hz.at[plane], r.hz.at[z], (e, plane)).start()

        return carry

    def merge(plane, slot, block):
        r.SS[plane, block, :] = (
            r.SS[plane, block, :].astype(F32) + r.Sin[slot, block, :].astype(F32)
        ).astype(BF)

    def sum_down(plane, gap, oc):
        block = block_at(0, oc)
        remote(
            r.SS.at[plane, block],
            r.Sin.at[plane, block],
            r.x_sd.at[gap],
            r.sd.at[gap - 1, oc],
            (e, z - 1),
        ).start()

    def sum_up(plane, gap, oc):
        block = block_at(0, oc)
        remote(
            r.SS.at[plane, block],
            r.Sin.at[plane + 1, block],
            r.x_su.at[gap],
            r.su.at[gap - 1, oc],
            (e, z + 1),
        ).start()

    def plane_back(index, source, target, offsets):
        mine = pl.ds(aligned(e * cp, plane_step), cp)
        for o in offsets:
            if o == 0:
                target[mine, :] = source[mine, :]
                continue
            x = flip(e, o)
            remote(
                source.at[pl.ds(aligned(x * cp, plane_step), cp)],
                target.at[mine],
                r.x_back.at[index],
                r.back.at[index],
                (x, z),
            ).start()

    early = not s.padded
    RS, Rin = (r.RS, r.Rin) if early else (r.SS, r.Sin)

    def results_begin():
        if not early:
            for d in range(1, W):
                pl.when(z >= d)(functools.partial(sent, r.SS.at[0], r.x_sd.at[d]))
                pl.when(z + d <= W - 1)(functools.partial(sent, r.SS.at[0], r.x_su.at[d]))
            pl.semaphore_wait(r.credit, W - 1)

        def results(step, carry):
            at = pl.ds(aligned(step * R, 16), R)
            RS[step] = dot(r.act[at, :], r.wo[...]).astype(BF)
            return carry

        lax.fori_loop(0, W, results, 0)

    def result_merge(plane, slot, sem):
        got(Rin.at[slot], sem)
        RS[plane] = (RS[plane].astype(F32) + Rin[slot].astype(F32)).astype(BF)

    def results_pass(step):
        below = step - (W - 1 - z)
        above = W - 1 - step + z

        @pl.when((below >= 0) & (below < z))
        def _():
            @pl.when(z < W - 1)
            def _():
                result_merge(below, below, r.rdn.at[z - below])

            remote(
                RS.at[below],
                Rin.at[below],
                r.x_rdn.at[z - below],
                r.rdn.at[z - below - 1],
                (e, z - 1),
            ).start()

        @pl.when((above <= W - 1) & (above > z))
        def _():
            @pl.when(z > 0)
            def _():
                result_merge(above, above + 1, r.ru.at[above - z])

            remote(
                RS.at[above],
                Rin.at[above + 1],
                r.x_ru.at[above - z],
                r.ru.at[above - z - 1],
                (e, z + 1),
            ).start()

    passes = iter(range(W - 1))

    def next_pass():
        for step in passes:
            results_pass(step)
            break

    expert(z)
    for step in range(1, 2 * W - 2):
        if step < W - 1:
            line_pass(r.Nr, step, *n_line)

            def sides(side, carry, step=step):
                plane = z + (2 * side - 1) * step
                pl.when((plane >= 0) & (plane < W))(functools.partial(expert, plane))
                return carry

            lax.fori_loop(0, 2, sides, 0)

        if step == W - 1:
            @pl.when((z == 0) | (z == W - 1))
            def _():
                plane = W - 1 - z
                for oc in range(C):
                    at = block_at(plane, oc)
                    top = functools.partial(got, r.Nr.at[at], r.nu.at[W - 1, oc])
                    bottom = functools.partial(got, r.Nr.at[at], r.nd.at[W - 1, oc])
                    pl.when(z > 0)(top)
                    pl.when(z == 0)(bottom)
                    expert_rows(plane, at, block_at(0, oc))
                    pl.when(z > 0)(functools.partial(sum_down, plane, W - 1, oc))
                    pl.when(z == 0)(functools.partial(sum_up, plane, W - 1, oc))

        plane_down = 2 * W - 2 - z - step
        gap_down = z - plane_down
        plane_up = step - z
        gap_up = plane_up - z
        inner_down = (plane_down >= 0) & (gap_down >= 1)
        inner_up = (plane_up <= W - 1) & (gap_up >= 1)
        if step == W - 1:
            inner_down, inner_up = inner_down & (z < W - 1), inner_up & (z > 0)

        @pl.when(inner_down)
        def _():
            for oc in range(C):

                @pl.when(z < W - 1)
                def _():
                    got(r.Sin.at[plane_down, block_at(0, oc)], r.sd.at[gap_down, oc])
                    merge(plane_down, plane_down, block_at(0, oc))

                sum_down(plane_down, gap_down, oc)

        @pl.when(inner_up)
        def _():
            for oc in range(C):

                @pl.when(z > 0)
                def _():
                    got(r.Sin.at[plane_up + 1, block_at(0, oc)], r.su.at[gap_up, oc])
                    merge(plane_up, plane_up + 1, block_at(0, oc))

                sum_up(plane_up, gap_up, oc)

        if step == W - 1:
            if early:
                results_begin()
                next_pass()
            lax.fori_loop(0, W, gate_sums, 0)

    for oc in range(C):
        block = block_at(0, oc)

        @pl.when(z < W - 1)
        def _():
            got(r.Sin.at[z, block], r.sd.at[0, oc])
            merge(z, z, block)

        @pl.when(z > 0)
        def _():
            got(r.Sin.at[z + 1, block], r.su.at[0, oc])
            merge(z, z + 1, block)

        r.Sb[block, :] = r.SS[z, block, :].astype(s.dt)
        plane_back(0, r.Sb, r.Sk, (2 * oc, 2 * oc + 1))

    total = r.HS[z]
    for o in range(1, W):
        other = flip(z, o)
        got(r.Hr.at[0], r.hz.at[other])
        total = total + r.Hr[other]
    r.Hb[...] = total
    r.Hk[e] = total
    for o in range(1, E):
        remote(r.Hb, r.Hk.at[e], r.x_hp, r.hp, (flip(e, o), z)).start()

    if not early:
        for o in range(1, W):
            pl.semaphore_signal(r.credit, inc=1, device_id=zpeer(o), device_id_type=MESH)
        results_begin()
    next_pass()
    got(r.Sk.at[pl.ds(0, (E - 1) * cp)], r.back.at[0])
    got(r.Hk.at[pl.ds(0, E - 1)], r.hp)
    r.Hm[...] = jnp.zeros_like(r.Hm)
    for x in range(E):
        r.Hm[x : x + 1, :] = r.Hk[x, 0:1, :]
    slot_col = jnp.sum(jnp.where(eye, jnp.where(kept, slot_row, -1.0), 0.0), axis=1, keepdims=True)
    slot_lane = jnp.where(slot_col < 0, -1.0, slot_col + (e * cp).astype(F32))
    chosen = (iota((T, R), 1).astype(F32) == slot_lane).astype(F32).astype(BF)
    high, rest = two_parts(r.Hm[...])
    gate_grad = jnp.sum(
        picked * (dot_rt(chosen, high) + dot_rt(chosen, rest)), axis=1, keepdims=True
    )
    returned = dot(r.pt[...], r.Sk[...].astype(BF))
    logit_grad = (gate * gate_grad * (picked - router)).astype(BF)
    nf_grad = dot(logit_grad, r.RwT[...]) + gate * returned
    middle = r.middle[...]
    along = nf_grad * r.rows[1:2, :]
    middle_grad = (
        r.og[...].astype(F32)
        + scale2 * along
        - middle * (scale2 * scale2 * scale2 * jnp.mean(along * middle, axis=1, keepdims=True))
    )
    r.mg[...] = middle_grad
    r.rows[2:3, :] = jnp.sum(nf_grad * middle * scale2, axis=0, keepdims=True)
    r.att[...] = (middle_grad * valid).astype(BF)
    attended_grad = r.att[...]

    def share(m, source):
        remote(source.at[:, there], r.fac.at[m], r.x_sibF.at[m], r.sibF.at[m], sib).start()

    share(3, r.att)
    r.mixed[...] = dot_rt(attended_grad, r.wfull[3]).astype(BF)
    router_grad = dot_lt(logit_grad, r.nf[...])
    two_step = C == 4 and not s.padded
    half_rows = W * s.pr // 2
    row_sides = (pl.ds(0, half_rows), pl.ds(half_rows, half_rows))

    def plane_sum(m, left, source):
        got(r.fac.at[m], r.sibF.at[m])

        def block(step, carry):
            at = pl.ds(aligned(step * s.CP, 16), s.CP)
            part = dot(left[at, :T], source[:, here]) + dot(left[at, T:], r.fac[m])
            part = part.astype(BF)
            for chip in range(C):
                r.GS[m, chip, pl.ds(aligned(step * s.pr, 16), s.pr), :] = part[
                    chip * s.pr : (chip + 1) * s.pr
                ]
            return carry

        lax.fori_loop(0, W, block, 0)
        if two_step:
            for side in range(2):
                near, far = 1 + side, 2 - side
                for slot, oc in enumerate((near, near + far)):
                    remote(
                        r.GS.at[m, flip(c, oc), row_sides[side]],
                        r.GX.at[m, side, slot],
                        r.x_gx.at[m, side],
                        r.gx.at[m, side],
                        cpeer(near),
                    ).start()
            return
        for oc in range(1, C):
            remote(
                r.GS.at[m, flip(c, oc)], r.GR.at[m, oc - 1], r.x_ra.at[m], r.ra.at[m], cpeer(oc)
            ).start()

    def plane_fold(m):
        if not two_step:
            return
        for side in range(2):
            far, rows = 2 - side, row_sides[side]
            got(r.GX.at[m, side], r.gx.at[m, side])
            for slot, chip in ((1, flip(c, far)), (0, c)):
                r.GS[m, chip, rows, :] = (
                    r.GS[m, chip, rows, :].astype(F32) + r.GX[m, side, slot].astype(F32)
                ).astype(BF)
                if slot:
                    remote(
                        r.GS.at[m, chip, rows],
                        r.GY.at[m, rows],
                        r.x_gy.at[m, side],
                        r.gy.at[m, side],
                        cpeer(far),
                    ).start()

    low_side = lane_row < s.HD

    def values_back(p, carry):
        cols = pl.ds(aligned(p * LANES, LANES), LANES)
        mixg = r.mixed[:, cols]
        outs = [dot_lt(r.probs[2 * p + side].astype(BF), mixg) for side in range(2)]
        r.dv[:, cols] = jnp.where(low_side, outs[0], outs[1]).astype(BF)
        return carry

    lax.fori_loop(0, s.H // 2, values_back, 0)
    share(2, r.dv)
    got(r.mT.at[:, pl.ds(T, T)], r.sibT.at[1])
    plane_sum(3, r.mT, r.att)
    got(r.nT.at[:, pl.ds(T, T)], r.sibT.at[0])
    plane_sum(2, r.nT, r.dv)

    def attend_back(p, carry):
        cols = pl.ds(aligned(p * LANES, LANES), LANES)
        q, kk, v, mixg = r.q[:, cols], r.kk[:, cols], r.v[:, cols], r.mixed[:, cols]
        outs = []
        for side in range(2):
            h = 2 * p + side
            probs = r.probs[h]
            prob_grad = dot_rt(mixg * lane_masks[side], v)
            inside = jnp.sum(probs * prob_grad, axis=1, keepdims=True)
            score_grad = (probs * (prob_grad - inside)).astype(BF)
            r.probs[h] = score_grad.astype(F32)
            outs.append((dot(score_grad, kk) * scale, dot_lt(score_grad, q) * scale))
        r.dq[:, cols] = jnp.where(low_side, outs[0][0], outs[1][0]).astype(BF)
        r.dk[:, cols] = jnp.where(low_side, outs[0][1], outs[1][1]).astype(BF)
        return carry

    lax.fori_loop(0, s.H // 2, attend_back, 0)
    share(0, r.dq)
    share(1, r.dk)
    plane_fold(3)
    plane_fold(2)
    next_pass()

    def shard_sum(m):
        total = r.GS[m, c].astype(F32)
        if two_step:
            for side in range(2):
                got(r.GY.at[m, row_sides[side]], r.gy.at[m, side])
            total = total + r.GY[m].astype(F32)
        else:
            got(r.GR.at[m], r.ra.at[m])
        for oc in range(1, 1 if two_step else C):
            if s.padded:
                fetch = pltpu.make_async_copy(r.GR.at[m, oc - 1], r.gst, r.lsem.at[8])
                fetch.start()
                fetch.wait()
            part = r.gst[...] if s.padded else r.GR[m, oc - 1]
            total = total + part.astype(F32)
        r.ZS[m] = total.astype(BF)
        for o in range(1, W):
            remote(
                r.ZS.at[m, pl.ds(aligned(flip(z, o) * s.pr, 16), s.pr)],
                r.ZR.at[m, o - 1],
                r.x_rb.at[m],
                r.rb.at[m],
                zpeer(o),
            ).start()

    def spread(m):
        got(r.ZR.at[m], r.rb.at[m])
        total = r.ZS[m, pl.ds(aligned(z * s.pr, 16), s.pr), :].astype(F32)
        for o in range(1, W):
            total = total + r.ZR[m, o - 1].astype(F32)
        mine = pl.ds(aligned(c * s.pr, 16), s.pr)
        r.FG[m, mine, here] = total.astype(BF)
        part = r.FG.at[m, mine, here]
        for oc in range(1, C):
            remote(part, part, r.x_rc.at[m], r.rc.at[m], cpeer(oc)).start()

    def share_sum(m):
        got(r.FG.at[m, pl.ds(0, (C - 1) * s.pr), here], r.rc.at[m])
        part = r.FG.at[m, :, here]
        remote(part, part, r.x_rd.at[m], r.rd.at[m], sib).start()

    normed_grad = (
        dot_rt(r.dq[...], r.wfull[0]) + dot_rt(r.dk[...], r.wfull[1]) + dot_rt(r.dv[...], r.wfull[2])
    )
    plane_sum(0, r.nT, r.dq)
    shard_sum(3)
    x = r.xb[...].astype(F32)
    along = normed_grad * r.rows[0:1, :]
    r.mg[...] = (
        r.mg[...]
        + scale1 * along
        - x * (scale1 * scale1 * scale1 * jnp.mean(along * x, axis=1, keepdims=True))
    )
    r.rows[3:4, :] = jnp.sum(normed_grad * x * scale1, axis=0, keepdims=True)
    save_tokens = pltpu.make_async_copy(r.mg, r.tokens_grad, r.osem.at[0])
    save_tokens.start()
    r.bt[...] = jnp.zeros_like(r.bt)
    mirror = (iota((T, T), 0) + iota((T, T), 1) == T - 1).astype(F32).astype(BF)

    def bias_back(h, carry):
        mirrored = dot(r.probs[h].astype(BF), mirror)
        wide = jnp.concatenate([mirrored, jnp.zeros((T, T), F32)], axis=1)
        turned = pltpu.roll(wide, 0, 1, stride=1, stride_axis=0)
        r.bt[pl.ds(REL_LANE + h, 1), :] = jnp.sum(turned, axis=0, keepdims=True)
        return carry

    lax.fori_loop(0, s.H, bias_back, 0)
    plane_sum(1, r.nT, r.dk)
    shard_sum(2)
    plane_fold(0)
    high, rest = two_parts(r.bt[...])
    rel_grad = dot_rt(r.ohm[...], high) + dot_rt(r.ohm[...], rest)
    lane_col = iota((LANES, 1), 0)
    small = jnp.where(
        lane_col == GAIN_ATTN_LANE,
        r.rows[3:4, :],
        jnp.where(lane_col == GAIN_FFN_LANE, r.rows[2:3, :], router_grad),
    ).T
    blocks = []
    for block in range(W):
        part = small[block * s.SR : (block + 1) * s.SR]
        head = part[: s.NBP] + rel_grad[block * s.NBP : (block + 1) * s.NBP]
        blocks.append(jnp.concatenate([head, part[s.NBP :]], axis=0))
    small = jnp.concatenate(blocks, axis=0).astype(BF)
    r.smo[...] = spread_rows(small)
    remote(r.smo, r.sms, r.x_rd.at[4], r.rd.at[4], sib).start()
    spread(3)
    got(r.sms, r.rd.at[4])
    pair = (r.smo[...].astype(F32) + r.sms[...].astype(F32)).astype(BF)
    for block in range(W):
        for chip in range(C):
            at = block * s.CP + chip * s.pr
            r.hGS[chip, block * s.pr : (block + 1) * s.pr, :] = pair[at : at + s.pr]
    for oc in range(1, C):
        remote(r.hGS.at[flip(c, oc)], r.hGR.at[oc - 1], r.x_ra.at[4], r.ra.at[4], cpeer(oc)).start()
    line_sent(r.Gr, r.x_gu, r.x_gd)
    for o in range(1, W):
        got(r.Qr.at[0], r.t2.at[o])

    def scale_rows(step, carry):
        at = pl.ds(aligned(step * R, 16), R)
        gates = jnp.sum(jnp.where(diagonal, r.Qr[step, 0:1, :], 0.0), axis=1, keepdims=True)
        r.Gr[at, :] = (r.Gr[at, :].astype(F32) * gates).astype(BF)
        r.ig[at, :] = (r.ig[at, :].astype(F32) * gates).astype(BF)
        return carry

    lax.fori_loop(0, W, scale_rows, 0)
    tile, slots = s.tile, s.slots

    def save_out(step):
        slot = lax.rem(step, slots)
        at = pl.ds(aligned(step * tile, LANES), tile)
        return pltpu.make_async_copy(r.gwo.at[slot], r.grad_w_out.at[at], r.gwo_sem.at[slot])

    def save_in(step):
        slot = lax.rem(step, slots)
        at = pl.ds(aligned(step * tile, LANES), tile)
        return pltpu.make_async_copy(r.gwi.at[slot], r.grad_w_in.at[at], r.gwi_sem.at[slot])

    def grad_out_tile(step, carry):
        @pl.when(step >= slots)
        def _():
            save_out(step - slots).wait()

        at = pl.ds(aligned(step * tile, LANES), tile)
        r.gwo[lax.rem(step, slots)] = dot_lt(r.act[:, at], r.Gr[...]).astype(BF)
        save_out(step).start()
        return carry

    def grad_in_tile(step, carry):
        @pl.when(step >= slots)
        def _():
            save_in(step - slots).wait()

        at = pl.ds(aligned(step * tile, LANES), tile)
        r.gwi[lax.rem(step, slots)] = dot_lt(r.Nr[:, at], r.ig[...]).astype(BF)
        save_in(step).start()
        return carry


    plane_fold(1)
    lax.fori_loop(0, s.F // tile, grad_out_tile, 0)
    shard_sum(0)
    spread(2)
    share_sum(3)
    lax.fori_loop(0, D // tile, grad_in_tile, 0)
    shard_sum(1)
    spread(0)
    share_sum(2)
    for step in passes:
        results_pass(step)
    pl.when(z < W - 1)(functools.partial(result_merge, z, z, r.rdn.at[0]))
    pl.when(z > 0)(functools.partial(result_merge, z, z + 1, r.ru.at[0]))
    r.Rb[...] = RS[z].astype(s.dt)
    plane_back(1, r.Rb, r.Rk, range(E))

    got(r.hGR, r.ra.at[4])
    total = r.hGS[c].astype(F32)
    for oc in range(1, C):
        total = total + r.hGR[oc - 1].astype(F32)
    r.hZS[...] = total.astype(BF)
    for o in range(1, W):
        remote(
            r.hZS.at[pl.ds(aligned(flip(z, o) * s.pr, 16), s.pr)],
            r.hZR.at[o - 1],
            r.x_rb.at[4],
            r.rb.at[4],
            zpeer(o),
        ).start()
    spread(1)
    share_sum(0)
    got(r.hZR, r.rb.at[4])
    total = r.hZS[pl.ds(aligned(z * s.pr, 16), s.pr), :].astype(F32)
    for o in range(1, W):
        total = total + r.hZR[o - 1].astype(F32)
    mine = pl.ds(aligned(c * s.pr, 16), s.pr)
    r.hFG[mine, :] = total.astype(BF)
    for oc in range(1, C):
        part = r.hFG.at[mine]
        remote(part, part, r.x_rc.at[4], r.rc.at[4], cpeer(oc)).start()

    got(r.Rk.at[pl.ds(0, (E - 1) * cp)], r.back.at[1])
    r.nf[...] = (r.middle[...] + gate * dot(r.pt[...], r.Rk[...].astype(BF))).astype(BF)
    save_layer = pltpu.make_async_copy(r.nf, r.layer_out, r.osem.at[1])
    save_layer.start()

    share_sum(1)
    got(r.hFG.at[pl.ds(0, (C - 1) * s.pr)], r.rc.at[4])

    def unpad(value):
        return dot(r.unsel[...], value) if s.padded else value.astype(F32)

    r.smallest[...] = unpad(r.hFG[...])
    saves = [save_tokens, save_layer, pltpu.make_async_copy(r.smallest, r.smalls, r.osem.at[2])]
    saves[-1].start()
    for m in (3, 2, 0, 1):
        got(r.FG.at[m, :, there], r.rd.at[m])
        complete = r.FG.at[m]
        if s.padded:
            r.unpadded[m] = unpad(r.FG[m]).astype(BF)
            complete = r.unpadded.at[m]
        saves.append(pltpu.make_async_copy(complete, r.grads.at[m], r.osem.at[3 + m]))
        saves[-1].start()

    for save in saves:
        save.wait()
    for step in range(max(0, s.F // tile - slots), s.F // tile):
        save_out(step).wait()
    for step in range(max(0, D // tile - slots), D // tile):
        save_in(step).wait()
    sent(r.smg.at[pl.ds(0, W - 1)], r.x_sm)
    for m in range(4):
        part = r.wfull.at[m, pl.ds(0, s.pw), here]
        for d in range(W - 1):
            pl.when((z >= d) & (z < W - 1))(functools.partial(sent, part, r.x_wu.at[m, d]))
            pl.when((z + d <= W - 1) & (z > 0))(functools.partial(sent, part, r.x_wd.at[m, d]))
        if s.team > 1:
            sent(r.wfull.at[m, pl.ds(0, (W - 1) * (s.team - 1) * s.pw), here], r.x_wb.at[m])
        sent(r.wfull.at[m, others, here], r.x_wc.at[m])
        sent(r.fac.at[m], r.x_sibF.at[m])
        if two_step:
            for side in range(2):
                sent(r.GX.at[m, side], r.x_gx.at[m, side])
                sent(r.GY.at[m, row_sides[side]], r.x_gy.at[m, side])
        else:
            sent(r.GR.at[m], r.x_ra.at[m])
        sent(r.ZR.at[m], r.x_rb.at[m])
        sent(r.FG.at[m, pl.ds(0, (C - 1) * s.pr), here], r.x_rc.at[m])
        sent(r.FG.at[m, :, here], r.x_rd.at[m])
    sent(r.Qk.at[pl.ds(0, E - 1)], r.x_t1)
    for index, buffer in enumerate((r.gsend, r.nsend)):
        sent(buffer.at[pl.ds(0, E - 1)], r.x_d1.at[index])
    line_sent(r.Nr, r.x_nu, r.x_nd)
    sent(r.Qr.at[pl.ds(0, W - 1)], r.x_t2)
    for d in range(1, W):
        if early:
            pl.when(z >= d)(functools.partial(sent, r.SS.at[0], r.x_sd.at[d]))
            pl.when(z + d <= W - 1)(functools.partial(sent, r.SS.at[0], r.x_su.at[d]))
        pl.when(z >= d)(functools.partial(sent, r.SS.at[0], r.x_rdn.at[d]))
        pl.when(z + d <= W - 1)(functools.partial(sent, r.SS.at[0], r.x_ru.at[d]))
    for plane in range(W):
        pl.when(z != plane)(functools.partial(sent, r.HS.at[0], r.x_hz.at[plane]))
    sent(r.Hk.at[pl.ds(0, E - 1)], r.x_hp)
    sent(r.Sk.at[pl.ds(0, (E - 1) * cp)], r.x_back.at[0])
    sent(r.Rk.at[pl.ds(0, (E - 1) * cp)], r.x_back.at[1])
    sent(r.nT.at[:, pl.ds(0, T)], r.x_sibT.at[0])
    sent(r.mT.at[:, pl.ds(0, T)], r.x_sibT.at[1])
    sent(r.hGR, r.x_ra.at[4])
    sent(r.hZR, r.x_rb.at[4])
    sent(r.hFG.at[pl.ds(0, (C - 1) * s.pr)], r.x_rc.at[4])
    sent(r.smo, r.x_rd.at[4])


def selection(s):
    share = s.SR // s.C
    unsel = np.zeros((s.SR, s.CP), np.float32)
    for chip in range(s.C):
        for at in range(share):
            unsel[chip * share + at, chip * s.pr + at] = 1
    return jnp.asarray(unsel, BF)


PARTS = 3


def finish(s, *refs):
    layer_out, tokens_grad, grads, smalls, grad_in, grad_out = refs[:6]
    out_layer, out_tokens, *out_mixers = refs[6:12]
    out_in, out_out, out_gain1, out_gain2, out_rel, out_router = refs[12:18]
    low_mix, low_in, low_out, mix, into, outof, held_layer, held_tokens = refs[18:26]
    pass_sem, load_sem, save_sem, load2, save2 = refs[26:]
    through = (
        (layer_out, held_layer, out_layer),
        (tokens_grad, held_tokens, out_tokens),
    )
    loads = [
        pltpu.make_async_copy(source, held, pass_sem.at[0, index])
        for index, (source, held, _) in enumerate(through)
    ]
    saves = [
        pltpu.make_async_copy(held, target, pass_sem.at[1, index])
        for index, (_, held, target) in enumerate(through)
    ]
    for m in range(4):
        loads.append(pltpu.make_async_copy(grads.at[m], low_mix.at[m], load_sem.at[m]))
        saves.append(pltpu.make_async_copy(mix.at[m], out_mixers[m], save_sem.at[m]))
    steps = [None, None] + [(low_mix, mix, m) for m in range(4)]
    for index, (source, low, high, target) in enumerate(
        ((grad_in, low_in, into, out_in), (grad_out, low_out, outof, out_out))
    ):
        rows = source.shape[0] // PARTS
        for part in range(PARTS):
            at = pl.ds(part * rows, rows)
            loads.append(
                pltpu.make_async_copy(source.at[at], low.at[at], load2.at[index, part])
            )
            saves.append(
                pltpu.make_async_copy(high.at[at], target.at[0, at], save2.at[index, part])
            )
            steps.append((low, high, at))
    for copy in loads:
        copy.start()
    turned = smalls[...].T
    out_router[...] = turned[: s.NX]
    out_gain1[...] = turned[GAIN_ATTN_LANE : GAIN_ATTN_LANE + 1]
    out_gain2[...] = turned[GAIN_FFN_LANE : GAIN_FFN_LANE + 1]
    out_rel[...] = smalls[: s.NBH, REL_LANE : REL_LANE + s.H]
    for load, save, step in zip(loads, saves, steps, strict=True):
        load.wait()
        if step is not None:
            low, high, at = step
            high[at] = low[at].astype(F32)
        save.start()
    for copy in saves:
        copy.wait()


def local(
    tokens,
    norm_gain_attn,
    w_query,
    w_key,
    w_value,
    w_output,
    rel_bias,
    norm_gain_ffn,
    w_router,
    w_in,
    w_out,
    out_grad,
    expert_ids,
    priority,
    lengths,
    seq_order,
    relpos_table,
):
    tok_count, width = tokens.shape
    buckets_here, heads = rel_bias.shape
    n_experts = w_router.shape[1]
    s = plan(
        lax.axis_size("expert"),
        lax.axis_size("wshard"),
        tok_count,
        width,
        heads,
        buckets_here,
        n_experts,
        w_in.shape[2],
    )
    operands = [
        lengths, seq_order, expert_ids.reshape(1, tok_count), priority.reshape(1, tok_count),
        relpos_table.reshape(1, -1), w_router.T, norm_gain_attn,
        norm_gain_ffn, rel_bias,
        tokens, out_grad, w_query, w_key, w_value, w_output, w_in, w_out,
    ]
    smem, vmem, anywhere = (
        pl.BlockSpec(memory_space=space) for space in (pltpu.SMEM, pltpu.VMEM, pl.ANY)
    )
    in_specs = [smem] * 2 + [vmem] * 7 + [anywhere] * 8
    names = IN_NAMES
    if s.padded:
        operands.append(selection(s))
        in_specs.append(vmem)
        names = names + PAD_NAMES
    spilled = (jax.ShapeDtypeStruct(pieces_shape(s), BF),) if s.padded else ()
    scratch = scratch_list(s)
    names = names + OUT_NAMES + ("GR",) * len(spilled) + tuple(name for name, _ in scratch)
    outs = pl.pallas_call(
        functools.partial(kernel, s, names),
        name="layer",
        out_shape=(
            jax.ShapeDtypeStruct((s.T, s.D), BF),
            jax.ShapeDtypeStruct((s.T, s.D), F32),
            jax.ShapeDtypeStruct((4, s.SR, s.D), BF),
            jax.ShapeDtypeStruct((s.SR, LANES), F32),
            jax.ShapeDtypeStruct((s.D, s.F), BF),
            jax.ShapeDtypeStruct((s.F, s.D), BF),
            *spilled,
        ),
        in_specs=in_specs,
        out_specs=(anywhere,) * (6 + len(spilled)),
        scratch_shapes=[shape for _, shape in scratch],
        compiler_params=pltpu.CompilerParams(
            collective_id=0, has_side_effects=True, vmem_limit_bytes=62 * 2**20
        ),
    )(*operands)
    done = pl.pallas_call(
        functools.partial(finish, s),
        name="finish",
        out_shape=(
            jax.ShapeDtypeStruct((s.T, s.D), BF),
            jax.ShapeDtypeStruct((s.T, s.D), F32),
            *[jax.ShapeDtypeStruct((s.SR, s.D), F32)] * 4,
            jax.ShapeDtypeStruct((1, s.D, s.F), F32),
            jax.ShapeDtypeStruct((1, s.F, s.D), F32),
            jax.ShapeDtypeStruct((1, s.SR), F32),
            jax.ShapeDtypeStruct((1, s.SR), F32),
            jax.ShapeDtypeStruct((buckets_here, heads), F32),
            jax.ShapeDtypeStruct((n_experts, s.SR), F32),
        ),
        in_specs=[anywhere, anywhere, anywhere, vmem, anywhere, anywhere],
        out_specs=(anywhere,) * 8 + (vmem,) * 4,
        scratch_shapes=[
            pltpu.VMEM((4, s.SR, s.D), BF),
            pltpu.VMEM((s.D, s.F), BF),
            pltpu.VMEM((s.F, s.D), BF),
            pltpu.VMEM((4, s.SR, s.D), F32),
            pltpu.VMEM((s.D, s.F), F32),
            pltpu.VMEM((s.F, s.D), F32),
            pltpu.VMEM((s.T, s.D), BF),
            pltpu.VMEM((s.T, s.D), F32),
            pltpu.SemaphoreType.DMA((2, 2)),
            pltpu.SemaphoreType.DMA((4,)),
            pltpu.SemaphoreType.DMA((4,)),
            pltpu.SemaphoreType.DMA((2, PARTS)),
            pltpu.SemaphoreType.DMA((2, PARTS)),
        ],
        compiler_params=pltpu.CompilerParams(vmem_limit_bytes=62 * 2**20),
    )(*outs[:6])
    layer_out, tokens_grad, gq, gk, gv, go, grad_w_in, grad_w_out, gain1, gain2, rel, router = done
    return (
        layer_out,
        tokens_grad,
        gain1.reshape(s.SR),
        gq,
        gk,
        gv,
        go,
        rel,
        gain2.reshape(s.SR),
        router.T,
        grad_w_in,
        grad_w_out,
    )


def solution(mesh):
    rows = P(("expert", "wshard"), None)
    shard = P("wshard", None)
    into, outof = P("expert", None, "wshard"), P("expert", "wshard", None)
    return jax.shard_map(
        local,
        mesh=mesh,
        in_specs=(
            rows,
            P("wshard"),
            shard,
            shard,
            shard,
            shard,
            shard,
            P("wshard"),
            shard,
            into,
            outof,
            rows,
            rows,
            P(("expert", "wshard")),
            P(),
            P(),
            P(),
        ),
        out_specs=(
            rows,
            rows,
            P("wshard"),
            shard,
            shard,
            shard,
            shard,
            shard,
            P("wshard"),
            shard,
            into,
            outof,
        ),
        check_vma=False,
    )
```

```python
import functools
import types

import jax
import jax.numpy as jnp
import numpy as np
from jax import lax
from jax.experimental import pallas as pl
from jax.experimental.pallas import tpu as pltpu
from jax.sharding import PartitionSpec as P

EPSILON = 1e-06
NEG_FILL = -1e30
GELU_A = 0.79788456
GELU_B = 0.044715
LANES = 128
REL_LANE = 64
GAIN_ATTN_LANE = 126
GAIN_FFN_LANE = 127
MESH = pl.DeviceIdType.MESH
BF = jnp.bfloat16
F32 = jnp.float32
I32 = jnp.int32


def up16(count):
    return -(-count // 16) * 16


def dot(a, b):
    return jnp.dot(a, b, preferred_element_type=F32)


def dot_rt(a, b):
    return lax.dot_general(a, b, (((1,), (1,)), ((), ())), preferred_element_type=F32)


def dot_lt(a, b):
    return lax.dot_general(a, b, (((0,), (0,)), ((), ())), preferred_element_type=F32)


def iota(shape, axis):
    return lax.broadcasted_iota(I32, shape, axis)


def flip(index, offset):
    out = index
    bit = 1
    while bit <= offset:
        if offset & bit:
            out = out + bit * (1 - 2 * lax.rem(lax.div(index, bit), 2))
        bit *= 2
    return out


def aligned(value, step):
    return pl.multiple_of(value, step)


def two_parts(value):
    high = value.astype(BF)
    return high, (value - high.astype(F32)).astype(BF)


def plan(expert_size, shard_size, tok_count, width, heads, buckets_here, n_experts, hidden):
    s = types.SimpleNamespace()
    s.E, s.W = expert_size, shard_size
    s.C = expert_size // 2
    s.T, s.D, s.H = tok_count, width, heads
    s.HD = width // heads
    s.F = hidden
    s.NX = n_experts
    s.cap = tok_count // n_experts
    s.cp = s.cap if s.cap % 8 == 0 else up16(s.cap)
    s.dt = BF if s.cp % 16 == 0 else F32
    s.S = n_experts * s.cp
    s.R = s.E * s.cp
    s.SR = width // shard_size
    s.NBH = buckets_here
    s.NBP = up16(buckets_here)
    s.half = width // 2
    s.P1 = up16(n_experts + 2)
    s.LW = -(-s.SR // LANES) * LANES
    team = s.C
    while s.SR % team or (s.SR // team) % 16:
        team //= 2
    s.team = team
    s.pw = s.SR // team
    s.pr = up16(s.SR // s.C)
    s.CP = s.C * s.pr
    s.Dp = s.W * s.CP
    s.padded = s.CP != s.SR
    s.tile = LANES
    s.slots = 2 if s.padded else max(width, hidden) // s.tile
    return s


def pieces_shape(s):
    return (4, s.C - 1, s.W * s.pr, s.half)


def arrivals(s):
    return (("Ga", s.D), ("Na", s.D)) if s.dt == F32 else ()


def scratch_list(s):
    V = pltpu.VMEM
    dma = pltpu.SemaphoreType.DMA
    return [
        ("wfull", V((4, s.D, s.D), BF)),
        ("smf", V((s.P1 + s.NBP, s.LW), F32)),
        ("smg", V((s.W, s.P1 + s.NBP, s.LW), BF)),
        ("tab", V((8, 2 * s.T), I32)),
        ("xb", V((s.T, s.D), BF)),
        ("og", V((s.T, s.D), BF)),
        ("wi", V((s.D, s.F), BF)),
        ("wo", V((s.F, s.D), BF)),
        ("pm", V((s.S, s.T), BF)),
        ("pt", V((s.T, s.S), BF)),
        ("gsend", V((s.NX, s.cp, s.D), s.dt)),
        ("nsend", V((s.NX, s.cp, s.D), s.dt)),
        ("Qs", V((8, s.S), F32)),
        ("Qk", V((s.E, 8, s.S), F32)),
        ("Qr", V((s.W, 8, s.R), F32)),
        ("Gr", V((s.W * s.R, s.D), BF)),
        ("Nr", V((s.W * s.R, s.D), BF)),
        ("agr", V((s.W * s.R, s.F), BF)),
        ("act", V((s.W * s.R, s.F), BF)),
        ("ig", V((s.W * s.R, s.F), BF)),
        ("SS", V((s.W, s.R, s.D), BF)),
        ("Sin", V((s.W + 1, s.R, s.D), BF)),
        ("Sb", V((s.R, s.D), s.dt)),
        ("Sk", V((s.S, s.D), s.dt)),
        ("HS", V((s.W, 8, s.R), F32)),
        ("Hr", V((s.W, 8, s.R), F32)),
        ("Hb", V((8, s.R), F32)),
        ("Hk", V((s.E, 8, s.R), F32)),
        ("Hm", V((LANES, s.R), F32)),
        ("Rb", V((s.R, s.D), s.dt)),
        ("Rk", V((s.S, s.D), s.dt)),
        ("tb", V((LANES, 2 * s.T), F32)),
        ("ohm", V((s.W * s.NBP, 2 * s.T), BF)),
        ("rows", V((8, s.D), F32)),
        ("RwT", V((LANES, s.D), BF)),
        ("probs", V((s.H, s.T, s.T), F32)),
        ("q", V((s.T, s.D), BF)),
        ("kk", V((s.T, s.D), BF)),
        ("v", V((s.T, s.D), BF)),
        ("mixed", V((s.T, s.D), BF)),
        ("nf", V((s.T, s.D), BF)),
        ("middle", V((s.T, s.D), F32)),
        ("mg", V((s.T, s.D), F32)),
        ("att", V((s.T, s.D), BF)),
        ("dq", V((s.T, s.D), BF)),
        ("dk", V((s.T, s.D), BF)),
        ("dv", V((s.T, s.D), BF)),
        ("nT", V((s.Dp, 2 * s.T), BF)),
        ("mT", V((s.Dp, 2 * s.T), BF)),
        ("fac", V((4, s.T, s.half), BF)),
        ("GS", V((4, s.C, s.W * s.pr, s.half), BF)),
        ("ZS", V((4, s.W * s.pr, s.half), BF)),
        ("ZR", V((4, s.W - 1, s.pr, s.half), BF)),
        ("FG", V((4, s.CP, s.D), BF)),
        ("smo", V((s.Dp, LANES), BF)),
        ("sms", V((s.Dp, LANES), BF)),
        ("hGS", V((s.C, s.W * s.pr, LANES), BF)),
        ("hGR", V((s.C - 1, s.W * s.pr, LANES), BF)),
        ("hZS", V((s.W * s.pr, LANES), BF)),
        ("hZR", V((s.W - 1, s.pr, LANES), BF)),
        ("hFG", V((s.CP, LANES), BF)),
        ("bt", V((LANES, 2 * s.T), F32)),
        ("gwi", V((s.slots, s.tile, s.F), BF)),
        ("gwo", V((s.slots, s.tile, s.D), BF)),
        ("gwi_sem", dma((s.slots,))),
        ("gwo_sem", dma((s.slots,))),
        ("lsem", dma((9,))),
        ("osem", dma((7,))),
        ("smallest", V((s.SR, LANES), F32)),
        ("smr", dma((s.W,))),
        ("wu", dma((4, s.W))),
        ("wd", dma((4, s.W))),
        ("wbu", dma((4, s.W))),
        ("wbd", dma((4, s.W))),
        ("wc", dma((4,))),
        ("g1", dma((s.C,))),
        ("gu", dma((s.W, s.C))),
        ("gd", dma((s.W, s.C))),
        ("n1", dma((s.C,))),
        ("nu", dma((s.W, s.C))),
        ("nd", dma((s.W, s.C))),
        ("t1", dma),
        ("t2", dma((s.W,))),
        ("hz", dma((s.W,))),
        ("hp", dma),
        ("x_hz", dma((s.W,))),
        ("x_hp", dma),
        ("su", dma((s.W, s.C))),
        ("sd", dma((s.W, s.C))),
        ("ru", dma((s.W,))),
        ("rdn", dma((s.W,))),
        ("back", dma((2,))),
        ("sibT", dma((2,))),
        ("sibF", dma((4,))),
        ("ra", dma((5,))),
        ("rb", dma((5,))),
        ("rc", dma((5,))),
        ("rd", dma((5,))),
        ("x_sm", dma),
        ("x_wu", dma((4, s.W))),
        ("x_wd", dma((4, s.W))),
        ("x_wb", dma((4,))),
        ("x_wc", dma((4,))),
        ("x_d1", dma((2,))),
        ("x_t1", dma),
        ("x_t2", dma),
        ("x_gu", dma((s.W,))),
        ("x_gd", dma((s.W,))),
        ("x_nu", dma((s.W,))),
        ("x_nd", dma((s.W,))),
        ("x_su", dma((s.W,))),
        ("x_sd", dma((s.W,))),
        ("x_ru", dma((s.W,))),
        ("x_rdn", dma((s.W,))),
        ("x_back", dma((2,))),
        ("x_sibT", dma((2,))),
        ("x_sibF", dma((4,))),
        ("x_ra", dma((5,))),
        ("x_rb", dma((5,))),
        ("x_rc", dma((5,))),
        ("x_rd", dma((5,))),
        ("credit", pltpu.SemaphoreType.REGULAR),
    ] + (
        [("gst", V((s.W * s.pr, s.half), BF)), ("unpadded", V((4, s.SR, s.D), BF))]
        + [(name, V((s.R, width), F32)) for name, width in arrivals(s)]
        if s.padded
        else [
            ("GR", V(pieces_shape(s), BF)),
            ("GX", V((4, 2, 2, s.W * s.pr // 2, s.half), BF)),
            ("GY", V((4, s.W * s.pr, s.half), BF)),
            ("gx", dma((4, 2))),
            ("gy", dma((4, 2))),
            ("x_gx", dma((4, 2))),
            ("x_gy", dma((4, 2))),
            ("RS", V((s.W, s.R, s.D), BF)),
            ("Rin", V((s.W + 1, s.R, s.D), BF)),
        ]
    )


IN_NAMES = (
    "lengths", "seq", "ids", "prio", "table", "router", "gain_attn", "gain_ffn", "bias",
    "tokens", "out_grad", "w0", "w1", "w2", "w3", "w_in", "w_out",
)
PAD_NAMES = ("unsel",)
OUT_NAMES = ("layer_out", "tokens_grad", "grads", "smalls", "grad_w_in", "grad_w_out")


def kernel(s, names, *refs):
    r = types.SimpleNamespace(**dict(zip(names, refs, strict=True)))
    e = lax.axis_index("expert")
    z = lax.axis_index("wshard")
    c = lax.div(e, 2)
    k = lax.rem(e, 2)
    T, D, E, W, C, R, cp, half = s.T, s.D, s.E, s.W, s.C, s.R, s.cp, s.half
    sib = (flip(e, 1), z)
    here = pl.ds(aligned(k * half, LANES), half)
    there = pl.ds(aligned((1 - k) * half, LANES), half)

    def zpeer(offset):
        return (e, flip(z, offset))

    def cpeer(offset):
        return (flip(c, offset) * 2 + k, z)

    def remote(src, dst, send, recv, device):
        return pltpu.make_async_remote_copy(
            src_ref=src, dst_ref=dst, send_sem=send, recv_sem=recv, device_id=device, device_id_type=MESH
        )

    def got(ref, sem):
        remote(ref, ref, sem, sem, sib).wait_recv()

    def sent(ref, sem):
        remote(ref, ref, sem, sem, sib).wait_send()

    barrier = pltpu.get_barrier_semaphore()
    peers = [(flip(e, o), z) for o in range(1, E)] + [zpeer(o) for o in range(1, W)]
    for peer in peers:
        pl.semaphore_signal(barrier, inc=1, device_id=peer, device_id_type=MESH)

    shards = (r.w0, r.w1, r.w2, r.w3)
    own_rows = pl.ds(aligned(z * s.SR, 16), s.SR)
    load_w = [
        pltpu.make_async_copy(shards[m], r.wfull.at[m, own_rows], r.lsem.at[m])
        for m in range(4)
    ]
    load_og = pltpu.make_async_copy(r.out_grad, r.og, r.lsem.at[4])
    load_x = pltpu.make_async_copy(r.tokens, r.xb, r.lsem.at[5])
    load_wo = pltpu.make_async_copy(r.w_out.at[0], r.wo, r.lsem.at[6])
    load_wi = pltpu.make_async_copy(r.w_in.at[0], r.wi, r.lsem.at[7])
    load_og.start()

    r.smf[...] = jnp.zeros_like(r.smf)
    r.smf[0 : s.NX, 0 : s.SR] = r.router[...].astype(F32)
    r.smf[s.NX : s.NX + 1, 0 : s.SR] = r.gain_attn[...].astype(F32).reshape(1, s.SR)
    r.smf[s.NX + 1 : s.NX + 2, 0 : s.SR] = r.gain_ffn[...].astype(F32).reshape(1, s.SR)
    r.smf[s.P1 : s.P1 + s.NBH, 0 : s.H] = r.bias[...].astype(F32)
    r.smg[z] = r.smf[...].astype(BF)
    device = e * W + z
    first = r.lengths[r.seq[2 * device]]
    both = first + r.lengths[r.seq[2 * device + 1]]
    col = iota((T, 1), 0)
    row = iota((1, T), 1)
    seg_col = (col >= first).astype(I32) + (col >= both).astype(I32)
    seg_row = (row >= first).astype(I32) + (row >= both).astype(I32)
    same = seg_col == seg_row
    valid = (col < both).astype(F32)
    eye = iota((T, T), 0) == iota((T, T), 1)
    id_row = r.ids[...].astype(F32)
    id_col = jnp.sum(jnp.where(eye, id_row, 0.0), axis=1, keepdims=True)
    prio_row = r.prio[...].astype(F32)
    prio_col = jnp.sum(jnp.where(eye, prio_row, 0.0), axis=1, keepdims=True)
    ahead = (id_col == id_row) & (prio_col < prio_row)
    slot_row = jnp.sum(jnp.where(ahead, valid, 0.0), axis=0, keepdims=True)
    kept = (row < both) & (slot_row < s.cap)
    flat_row = jnp.where(kept, id_row * cp + slot_row, -1.0)
    flat_col = jnp.sum(jnp.where(eye, flat_row, 0.0), axis=1, keepdims=True)
    r.pm[...] = (iota((s.S, T), 0).astype(F32) == flat_row).astype(F32).astype(BF)
    r.pt[...] = (iota((T, s.S), 1).astype(F32) == flat_col).astype(F32).astype(BF)

    def fill(send, value):
        send[...] = dot(r.pm[...], value).astype(s.dt).reshape(send.shape)

    load_og.wait()
    fill(r.gsend, r.og[...])
    pl.semaphore_wait(barrier, len(peers))

    team_c = lax.rem(c, s.team)
    for o in range(1, W):
        remote(r.smg.at[z], r.smg.at[z], r.x_sm, r.smr.at[o], zpeer(o)).start()
    share_rows = pl.ds(aligned(team_c * s.pw, 16), s.pw)
    def weight_at(plane):
        return pl.ds(aligned(plane * s.SR + team_c * s.pw, 16), s.pw)

    def weight_own(m):
        def send(sender, receiver, to):
            source = shards[m].at[share_rows, here]
            remote(source, r.wfull.at[m, weight_at(z), here], sender, receiver, (e, to)).start()

        pl.when(z < W - 1)(functools.partial(send, r.x_wu.at[m, 0], r.wu.at[m, 1], z + 1))
        pl.when(z > 0)(functools.partial(send, r.x_wd.at[m, 0], r.wd.at[m, 1], z - 1))

    for m in range(3):
        weight_own(m)
    for copy in (load_x, *load_w, load_wo, load_wi):
        copy.start()
    plane_step = 16 if s.dt == BF else 8
    plane_rows = z * R if s.dt == BF else 0

    def dispatch(index, send, rows, first_sem, value):
        if value is not None:
            fill(send, value)
        mine = pl.ds(aligned(plane_rows + e * cp, plane_step), cp)
        for o in range(1, E):
            x = flip(e, o)
            remote(
                send.at[x], rows.at[mine], r.x_d1.at[index], first_sem.at[o // 2], (x, z)
            ).start()
        rows[mine, :] = send[e]

    def block_at(plane, oc):
        return pl.ds(aligned(plane * R + flip(c, oc) * 2 * cp, 16), 2 * cp)

    def landed(rows, arrived, first_sem, oc):
        got(arrived.at[pl.ds(0, (2 if oc else 1) * cp)], first_sem.at[oc])
        if s.dt != BF:
            rows[block_at(z, oc), :] = arrived[block_at(0, oc), :].astype(BF)

    def move(part, send, recv, to):
        remote(part, part, send, recv, (e, to)).start()

    def line_own(rows, arrived, first_sem, up, down, x_up, x_down):
        for oc in range(C):
            landed(rows, arrived, first_sem, oc)
            part = rows.at[block_at(z, oc)]
            pl.when(z < W - 1)(functools.partial(move, part, x_up.at[0], up.at[1, oc], z + 1))
            pl.when(z > 0)(functools.partial(move, part, x_down.at[0], down.at[1, oc], z - 1))

    def line_pass(rows, d, up, down, x_up, x_down):
        for oc in range(C):

            @pl.when(z >= d)
            def _():
                part = rows.at[block_at(z - d, oc)]
                got(part, up.at[d, oc])
                if d < W - 1:
                    pl.when(z < W - 1)(
                        functools.partial(move, part, x_up.at[d], up.at[d + 1, oc], z + 1)
                    )

            @pl.when(z + d <= W - 1)
            def _():
                part = rows.at[block_at(z + d, oc)]
                got(part, down.at[d, oc])
                if d < W - 1:
                    pl.when(z > 0)(
                        functools.partial(move, part, x_down.at[d], down.at[d + 1, oc], z - 1)
                    )

    def line_sent(rows, x_up, x_down):
        for d in range(W - 1):
            whole = rows.at[pl.ds(0, R)]
            pl.when((z >= d) & (z < W - 1))(functools.partial(sent, whole, x_up.at[d]))
            pl.when((z + d <= W - 1) & (z > 0))(functools.partial(sent, whole, x_down.at[d]))

    g_line = (r.gu, r.gd, r.x_gu, r.x_gd)
    n_line = (r.nu, r.nd, r.x_nu, r.x_nd)
    Ga, Na = (r.Gr, r.Nr) if s.dt == BF else (r.Ga, r.Na)
    dispatch(0, r.gsend, Ga, r.g1, None)

    def weight_pass(m, d):
        def handle(plane, arrived, onward, sender, receiver, to, beside):
            part = r.wfull.at[m, weight_at(plane), here]
            got(part, arrived)
            if d < W - 1:
                pl.when(onward)(functools.partial(move, part, sender, receiver, to))
            for oc in range(1, s.team):
                remote(part, part, r.x_wb.at[m], beside, cpeer(oc)).start()

        up, down, after = (m, d), (m, d), (m, min(d + 1, W - 1))
        pl.when(z >= d)(
            functools.partial(
                handle, z - d, r.wu.at[up], z < W - 1, r.x_wu.at[up], r.wu.at[after], z + 1, r.wbu.at[up]
            )
        )
        pl.when(z + d <= W - 1)(
            functools.partial(
                handle, z + d, r.wd.at[down], z > 0, r.x_wd.at[down], r.wd.at[after], z - 1, r.wbd.at[down]
            )
        )

    def weight_share(m, d):
        def handle(plane, beside):
            if s.team > 1:
                got(r.wfull.at[m, pl.ds(0, (s.team - 1) * s.pw), here], beside)
            part = r.wfull.at[m, pl.ds(aligned(plane * s.SR, 16), s.SR), here]
            remote(part, part, r.x_wc.at[m], r.wc.at[m], sib).start()

        pl.when(z >= d)(functools.partial(handle, z - d, r.wbu.at[m, d]))
        pl.when(z + d <= W - 1)(functools.partial(handle, z + d, r.wbd.at[m, d]))

    others = pl.ds(0, (W - 1) * s.SR)

    def weight_ready(m):
        load_w[m].wait()
        got(r.wfull.at[m, others, there], r.wc.at[m])

    for d in range(1, W):
        for m in range(3):
            weight_pass(m, d)
        if d == 1:
            weight_own(3)
        else:
            weight_pass(3, d - 1)
            for m in range(3):
                weight_share(m, d - 1)
        if d == min(2, W - 1):
            line_own(r.Gr, Ga, r.g1, *g_line)
    weight_pass(3, W - 1)
    for m in range(3):
        weight_share(m, W - 1)
    for o in range(1, W):
        got(r.smg.at[0], r.smr.at[o])
    gathered = jnp.concatenate(
        [r.smg[w, : s.P1, : s.SR].astype(F32) for w in range(W)], axis=1
    )
    r.rows[0:1, :] = gathered[s.NX : s.NX + 1]
    r.rows[1:2, :] = gathered[s.NX + 1 : s.NX + 2]
    r.RwT[...] = jnp.zeros_like(r.RwT)
    r.RwT[: s.P1, :] = jnp.where(iota((s.P1, D), 0) < s.NX, gathered, 0.0).astype(BF)
    lane_row = iota((1, LANES), 1)
    r.tab[...] = jnp.full(r.tab.shape, -1, I32)
    r.tab[0:1, 0 : 2 * T - 1] = r.table[...]
    bucket = r.tab[0:1, :]
    shift = s.NBH.bit_length() - 1
    bucket = lax.shift_right_logical(bucket, shift) * s.NBP + lax.bitwise_and(bucket, s.NBH - 1)
    bucket = jnp.where(r.tab[0:1, :] < 0, -1, bucket)
    hot = (iota((W * s.NBP, 2 * T), 0) == bucket).astype(F32).astype(BF)
    backwards = (iota((2 * T, 2 * T), 0) + iota((2 * T, 2 * T), 1) == 2 * T - 2).astype(F32)
    r.ohm[...] = dot(hot, backwards.astype(BF)).astype(BF)
    bias_rows = r.smg[:, s.P1 :, :LANES].reshape(W * s.NBP, LANES)
    r.tb[...] = dot_lt(bias_rows, hot)

    def bias_head(h, carry):
        wide = jnp.broadcast_to(r.tb[pl.ds(h, 1), :], (T, 2 * T))
        turned = pltpu.roll(wide, T + 1, 1, stride=1, stride_axis=0)
        r.probs[h] = jnp.where(same, turned[:, :T], NEG_FILL)
        return carry

    lax.fori_loop(0, s.H, bias_head, 0)
    load_x.wait()
    x = r.xb[...].astype(F32)
    scale1 = lax.rsqrt(jnp.mean(x * x, axis=1, keepdims=True) + EPSILON)
    normed = (x * scale1 * r.rows[0:1, :]).astype(BF)

    def spread_rows(value):
        if not s.padded:
            return value
        shards = [value[at : at + s.SR] for at in range(0, D, s.SR)]
        return jnp.concatenate([dot_lt(r.unsel[...], shard) for shard in shards], axis=0).astype(BF)

    def turn_out(index, value, target):
        target[:, :T] = spread_rows(value.T)
        remote(
            target.at[:, pl.ds(0, T)], target.at[:, pl.ds(T, T)], r.x_sibT.at[index], r.sibT.at[index], sib
        ).start()

    turn_out(0, normed, r.nT)
    weight_ready(0)
    r.q[...] = dot(normed, r.wfull[0]).astype(BF)
    weight_ready(1)
    r.kk[...] = dot(normed, r.wfull[1]).astype(BF)
    weight_ready(2)
    r.v[...] = dot(normed, r.wfull[2]).astype(BF)
    for d in range(1, W):
        weight_share(3, d)
    line_pass(r.Gr, 1, *g_line)

    scale = s.HD ** (-0.5)
    low_lane = (lane_row < s.HD).astype(F32)
    lane_masks = (low_lane.astype(BF), (1.0 - low_lane).astype(BF))

    def attend(p, carry):
        cols = pl.ds(aligned(p * LANES, LANES), LANES)
        q, kk, v = r.q[:, cols], r.kk[:, cols], r.v[:, cols]
        outs = []
        for side in range(2):
            h = 2 * p + side
            scores = dot_rt(q * lane_masks[side], kk) * scale + r.probs[h]
            expo = jnp.exp(scores - jnp.max(scores, axis=1, keepdims=True))
            probs = expo * (1.0 / jnp.sum(expo, axis=1, keepdims=True))
            r.probs[h] = probs
            outs.append(dot(probs.astype(BF), v))
        r.mixed[:, cols] = jnp.where(lane_row < s.HD, outs[0], outs[1]).astype(BF)
        return carry

    lax.fori_loop(0, s.H // 2, attend, 0)
    mixed = r.mixed[...]
    weight_ready(3)
    middle = r.xb[...].astype(F32) + dot(mixed, r.wfull[3]) * valid
    r.middle[...] = middle
    scale2 = lax.rsqrt(jnp.mean(middle * middle, axis=1, keepdims=True) + EPSILON)
    nf = (middle * scale2 * r.rows[1:2, :]).astype(BF)
    r.nf[...] = nf
    dispatch(1, r.nsend, Na, r.n1, nf)
    logits = jnp.where(lane_row < s.NX, dot_rt(nf, r.RwT[...]), NEG_FILL)
    raised = jnp.exp(logits - jnp.max(logits, axis=1, keepdims=True))
    router = raised / jnp.sum(raised, axis=1, keepdims=True)
    picked = (lane_row.astype(F32) == id_col).astype(F32)
    gate = jnp.sum(router * picked, axis=1, keepdims=True)
    slot_gates = jnp.sum(jnp.where(r.pt[...] > 0, gate, 0.0), axis=0, keepdims=True)
    r.Qs[...] = jnp.broadcast_to(slot_gates, r.Qs.shape)
    r.Qk[e] = r.Qs[...]
    for o in range(1, E):
        remote(r.Qs, r.Qk.at[e], r.x_t1, r.t1, (flip(e, o), z)).start()
    if W > 2:
        line_pass(r.Gr, 2, *g_line)
    line_own(r.Nr, Na, r.n1, *n_line)
    got(r.Qk.at[pl.ds(0, E - 1)], r.t1)
    repeated = jnp.concatenate(
        [jnp.broadcast_to(r.Qk[x, 0:1, :], (cp, s.S)) for x in range(E)], axis=0
    )
    wanted = e * cp + lax.rem(iota((R, s.S), 0), cp)
    gate_col = jnp.sum(
        jnp.where(iota((R, s.S), 1) == wanted, repeated, 0.0), axis=1, keepdims=True
    )
    diagonal = iota((R, R), 0) == iota((R, R), 1)
    gate_line = jnp.sum(jnp.where(diagonal, gate_col, 0.0), axis=0, keepdims=True)
    r.Qr[z] = jnp.broadcast_to(gate_line, (8, R))
    for o in range(1, W):
        remote(r.Qr.at[z], r.Qr.at[z], r.x_t2, r.t2.at[o], zpeer(o)).start()
    turn_out(1, mixed, r.mT)

    load_wo.wait()
    for d in range(3, W):
        line_pass(r.Gr, d, *g_line)

    def back_rows(step, carry):
        at = pl.ds(aligned(step * R, 16), R)
        r.agr[at, :] = dot_rt(r.Gr[at, :], r.wo[...]).astype(BF)
        return carry

    lax.fori_loop(0, W, back_rows, 0)
    load_wi.wait()

    def expert_rows(plane, at, block):
        inner = dot(r.Nr[at, :], r.wi[...])
        square = inner * inner
        tanh = jnp.tanh(GELU_A * inner * (1.0 + GELU_B * square))
        active = (0.5 * inner * (1.0 + tanh)).astype(BF)
        slope = 0.5 * (1.0 + tanh) + (0.5 * GELU_A) * inner * (1.0 - tanh * tanh) * (
            1.0 + (3.0 * GELU_B) * square
        )
        inner_grad = (r.agr[at, :].astype(F32) * slope).astype(BF)
        r.act[at, :] = active
        r.ig[at, :] = inner_grad
        r.SS[plane, block, :] = dot_rt(inner_grad, r.wi[...]).astype(BF)

    def expert(plane):
        expert_rows(plane, pl.ds(aligned(plane * R, 16), R), pl.ds(0, R))

    def gate_sums(plane, carry):
        at = pl.ds(aligned(plane * R, 16), R)
        part = jnp.sum(
            r.act[at, :].astype(F32) * r.agr[at, :].astype(F32), axis=1, keepdims=True
        )
        r.HS[plane, 0:1, :] = jnp.sum(jnp.where(diagonal, part, 0.0), axis=0, keepdims=True)

        @pl.when(plane != z)
        def _():
            remote(r.HS.at[plane], r.Hr.at[z], r.x_hz.at[plane], r.hz.at[z], (e, plane)).start()

        return carry

    def merge(plane, slot, block):
        r.SS[plane, block, :] = (
            r.SS[plane, block, :].astype(F32) + r.Sin[slot, block, :].astype(F32)
        ).astype(BF)

    def sum_down(plane, gap, oc):
        block = block_at(0, oc)
        remote(
            r.SS.at[plane, block],
            r.Sin.at[plane, block],
            r.x_sd.at[gap],
            r.sd.at[gap - 1, oc],
            (e, z - 1),
        ).start()

    def sum_up(plane, gap, oc):
        block = block_at(0, oc)
        remote(
            r.SS.at[plane, block],
            r.Sin.at[plane + 1, block],
            r.x_su.at[gap],
            r.su.at[gap - 1, oc],
            (e, z + 1),
        ).start()

    def plane_back(index, source, target, offsets):
        mine = pl.ds(aligned(e * cp, plane_step), cp)
        for o in offsets:
            if o == 0:
                target[mine, :] = source[mine, :]
                continue
            x = flip(e, o)
            remote(
                source.at[pl.ds(aligned(x * cp, plane_step), cp)],
                target.at[mine],
                r.x_back.at[index],
                r.back.at[index],
                (x, z),
            ).start()

    early = not s.padded
    RS, Rin = (r.RS, r.Rin) if early else (r.SS, r.Sin)

    def results_begin():
        if not early:
            for d in range(1, W):
                pl.when(z >= d)(functools.partial(sent, r.SS.at[0], r.x_sd.at[d]))
                pl.when(z + d <= W - 1)(functools.partial(sent, r.SS.at[0], r.x_su.at[d]))
            pl.semaphore_wait(r.credit, W - 1)

        def results(step, carry):
            at = pl.ds(aligned(step * R, 16), R)
            RS[step] = dot(r.act[at, :], r.wo[...]).astype(BF)
            return carry

        lax.fori_loop(0, W, results, 0)

    def result_merge(plane, slot, sem):
        got(Rin.at[slot], sem)
        RS[plane] = (RS[plane].astype(F32) + Rin[slot].astype(F32)).astype(BF)

    def results_pass(step):
        below = step - (W - 1 - z)
        above = W - 1 - step + z

        @pl.when((below >= 0) & (below < z))
        def _():
            @pl.when(z < W - 1)
            def _():
                result_merge(below, below, r.rdn.at[z - below])

            remote(
                RS.at[below],
                Rin.at[below],
                r.x_rdn.at[z - below],
                r.rdn.at[z - below - 1],
                (e, z - 1),
            ).start()

        @pl.when((above <= W - 1) & (above > z))
        def _():
            @pl.when(z > 0)
            def _():
                result_merge(above, above + 1, r.ru.at[above - z])

            remote(
                RS.at[above],
                Rin.at[above + 1],
                r.x_ru.at[above - z],
                r.ru.at[above - z - 1],
                (e, z + 1),
            ).start()

    passes = iter(range(W - 1))

    def next_pass():
        for step in passes:
            results_pass(step)
            break

    expert(z)
    for step in range(1, 2 * W - 2):
        if step < W - 1:
            line_pass(r.Nr, step, *n_line)

            def sides(side, carry, step=step):
                plane = z + (2 * side - 1) * step
                pl.when((plane >= 0) & (plane < W))(functools.partial(expert, plane))
                return carry

            lax.fori_loop(0, 2, sides, 0)

        if step == W - 1:
            @pl.when((z == 0) | (z == W - 1))
            def _():
                plane = W - 1 - z
                for oc in range(C):
                    at = block_at(plane, oc)
                    top = functools.partial(got, r.Nr.at[at], r.nu.at[W - 1, oc])
                    bottom = functools.partial(got, r.Nr.at[at], r.nd.at[W - 1, oc])
                    pl.when(z > 0)(top)
                    pl.when(z == 0)(bottom)
                    expert_rows(plane, at, block_at(0, oc))
                    pl.when(z > 0)(functools.partial(sum_down, plane, W - 1, oc))
                    pl.when(z == 0)(functools.partial(sum_up, plane, W - 1, oc))

        plane_down = 2 * W - 2 - z - step
        gap_down = z - plane_down
        plane_up = step - z
        gap_up = plane_up - z
        inner_down = (plane_down >= 0) & (gap_down >= 1)
        inner_up = (plane_up <= W - 1) & (gap_up >= 1)
        if step == W - 1:
            inner_down, inner_up = inner_down & (z < W - 1), inner_up & (z > 0)

        @pl.when(inner_down)
        def _():
            for oc in range(C):

                @pl.when(z < W - 1)
                def _():
                    got(r.Sin.at[plane_down, block_at(0, oc)], r.sd.at[gap_down, oc])
                    merge(plane_down, plane_down, block_at(0, oc))

                sum_down(plane_down, gap_down, oc)

        @pl.when(inner_up)
        def _():
            for oc in range(C):

                @pl.when(z > 0)
                def _():
                    got(r.Sin.at[plane_up + 1, block_at(0, oc)], r.su.at[gap_up, oc])
                    merge(plane_up, plane_up + 1, block_at(0, oc))

                sum_up(plane_up, gap_up, oc)

        if step == W - 1:
            if early:
                pass
            lax.fori_loop(0, W, gate_sums, 0)
            if early:
                results_begin()
                next_pass()

    for oc in range(C):
        block = block_at(0, oc)

        @pl.when(z < W - 1)
        def _():
            got(r.Sin.at[z, block], r.sd.at[0, oc])
            merge(z, z, block)

        @pl.when(z > 0)
        def _():
            got(r.Sin.at[z + 1, block], r.su.at[0, oc])
            merge(z, z + 1, block)

        r.Sb[block, :] = r.SS[z, block, :].astype(s.dt)
        plane_back(0, r.Sb, r.Sk, (2 * oc, 2 * oc + 1))

    total = r.HS[z]
    for o in range(1, W):
        other = flip(z, o)
        got(r.Hr.at[0], r.hz.at[other])
        total = total + r.Hr[other]
    r.Hb[...] = total
    r.Hk[e] = total
    for o in range(1, E):
        remote(r.Hb, r.Hk.at[e], r.x_hp, r.hp, (flip(e, o), z)).start()

    if not early:
        for o in range(1, W):
            pl.semaphore_signal(r.credit, inc=1, device_id=zpeer(o), device_id_type=MESH)
        results_begin()
    next_pass()
    got(r.Sk.at[pl.ds(0, (E - 1) * cp)], r.back.at[0])
    got(r.Hk.at[pl.ds(0, E - 1)], r.hp)
    r.Hm[...] = jnp.zeros_like(r.Hm)
    for x in range(E):
        r.Hm[x : x + 1, :] = r.Hk[x, 0:1, :]
    slot_col = jnp.sum(jnp.where(eye, jnp.where(kept, slot_row, -1.0), 0.0), axis=1, keepdims=True)
    slot_lane = jnp.where(slot_col < 0, -1.0, slot_col + (e * cp).astype(F32))
    chosen = (iota((T, R), 1).astype(F32) == slot_lane).astype(F32).astype(BF)
    high, rest = two_parts(r.Hm[...])
    gate_grad = jnp.sum(
        picked * (dot_rt(chosen, high) + dot_rt(chosen, rest)), axis=1, keepdims=True
    )
    returned = dot(r.pt[...], r.Sk[...].astype(BF))
    logit_grad = (gate * gate_grad * (picked - router)).astype(BF)
    nf_grad = dot(logit_grad, r.RwT[...]) + gate * returned
    middle = r.middle[...]
    along = nf_grad * r.rows[1:2, :]
    middle_grad = (
        r.og[...].astype(F32)
        + scale2 * along
        - middle * (scale2 * scale2 * scale2 * jnp.mean(along * middle, axis=1, keepdims=True))
    )
    r.mg[...] = middle_grad
    r.rows[2:3, :] = jnp.sum(nf_grad * middle * scale2, axis=0, keepdims=True)
    r.att[...] = (middle_grad * valid).astype(BF)
    attended_grad = r.att[...]

    def share(m, source):
        remote(source.at[:, there], r.fac.at[m], r.x_sibF.at[m], r.sibF.at[m], sib).start()

    share(3, r.att)
    r.mixed[...] = dot_rt(attended_grad, r.wfull[3]).astype(BF)
    router_grad = dot_lt(logit_grad, r.nf[...])
    two_step = C == 4 and not s.padded
    half_rows = W * s.pr // 2
    row_sides = (pl.ds(0, half_rows), pl.ds(half_rows, half_rows))

    def plane_sum(m, left, source):
        got(r.fac.at[m], r.sibF.at[m])

        def block(step, carry):
            at = pl.ds(aligned(step * s.CP, 16), s.CP)
            part = dot(left[at, :T], source[:, here]) + dot(left[at, T:], r.fac[m])
            part = part.astype(BF)
            for chip in range(C):
                r.GS[m, chip, pl.ds(aligned(step * s.pr, 16), s.pr), :] = part[
                    chip * s.pr : (chip + 1) * s.pr
                ]
            return carry

        lax.fori_loop(0, W, block, 0)
        if two_step:
            for side in range(2):
                near, far = 1 + side, 2 - side
                for slot, oc in enumerate((near, near + far)):
                    remote(
                        r.GS.at[m, flip(c, oc), row_sides[side]],
                        r.GX.at[m, side, slot],
                        r.x_gx.at[m, side],
                        r.gx.at[m, side],
                        cpeer(near),
                    ).start()
            return
        for oc in range(1, C):
            remote(
                r.GS.at[m, flip(c, oc)], r.GR.at[m, oc - 1], r.x_ra.at[m], r.ra.at[m], cpeer(oc)
            ).start()

    def plane_fold(m):
        if not two_step:
            return
        for side in range(2):
            far, rows = 2 - side, row_sides[side]
            got(r.GX.at[m, side], r.gx.at[m, side])
            for slot, chip in ((1, flip(c, far)), (0, c)):
                r.GS[m, chip, rows, :] = (
                    r.GS[m, chip, rows, :].astype(F32) + r.GX[m, side, slot].astype(F32)
                ).astype(BF)
                if slot:
                    remote(
                        r.GS.at[m, chip, rows],
                        r.GY.at[m, rows],
                        r.x_gy.at[m, side],
                        r.gy.at[m, side],
                        cpeer(far),
                    ).start()

    low_side = lane_row < s.HD

    def values_back(p, carry):
        cols = pl.ds(aligned(p * LANES, LANES), LANES)
        mixg = r.mixed[:, cols]
        outs = [dot_lt(r.probs[2 * p + side].astype(BF), mixg) for side in range(2)]
        r.dv[:, cols] = jnp.where(low_side, outs[0], outs[1]).astype(BF)
        return carry

    lax.fori_loop(0, s.H // 2, values_back, 0, unroll=2)
    share(2, r.dv)
    got(r.mT.at[:, pl.ds(T, T)], r.sibT.at[1])
    plane_sum(3, r.mT, r.att)
    got(r.nT.at[:, pl.ds(T, T)], r.sibT.at[0])
    plane_sum(2, r.nT, r.dv)

    def attend_back(p, carry):
        cols = pl.ds(aligned(p * LANES, LANES), LANES)
        q, kk, v, mixg = r.q[:, cols], r.kk[:, cols], r.v[:, cols], r.mixed[:, cols]
        outs = []
        for side in range(2):
            h = 2 * p + side
            probs = r.probs[h]
            prob_grad = dot_rt(mixg * lane_masks[side], v)
            inside = jnp.sum(probs * prob_grad, axis=1, keepdims=True)
            score_grad = (probs * (prob_grad - inside)).astype(BF)
            r.probs[h] = score_grad.astype(F32)
            outs.append((dot(score_grad, kk) * scale, dot_lt(score_grad, q) * scale))
        r.dq[:, cols] = jnp.where(low_side, outs[0][0], outs[1][0]).astype(BF)
        r.dk[:, cols] = jnp.where(low_side, outs[0][1], outs[1][1]).astype(BF)
        return carry

    lax.fori_loop(0, s.H // 2, attend_back, 0, unroll=2)
    share(0, r.dq)
    share(1, r.dk)
    plane_fold(3)
    plane_fold(2)
    next_pass()

    def shard_sum(m):
        total = r.GS[m, c].astype(F32)
        if two_step:
            for side in range(2):
                got(r.GY.at[m, row_sides[side]], r.gy.at[m, side])
            total = total + r.GY[m].astype(F32)
        else:
            got(r.GR.at[m], r.ra.at[m])
        for oc in range(1, 1 if two_step else C):
            if s.padded:
                fetch = pltpu.make_async_copy(r.GR.at[m, oc - 1], r.gst, r.lsem.at[8])
                fetch.start()
                fetch.wait()
            part = r.gst[...] if s.padded else r.GR[m, oc - 1]
            total = total + part.astype(F32)
        r.ZS[m] = total.astype(BF)
        for o in range(1, W):
            remote(
                r.ZS.at[m, pl.ds(aligned(flip(z, o) * s.pr, 16), s.pr)],
                r.ZR.at[m, o - 1],
                r.x_rb.at[m],
                r.rb.at[m],
                zpeer(o),
            ).start()

    def spread(m):
        got(r.ZR.at[m], r.rb.at[m])
        total = r.ZS[m, pl.ds(aligned(z * s.pr, 16), s.pr), :].astype(F32)
        for o in range(1, W):
            total = total + r.ZR[m, o - 1].astype(F32)
        mine = pl.ds(aligned(c * s.pr, 16), s.pr)
        r.FG[m, mine, here] = total.astype(BF)
        part = r.FG.at[m, mine, here]
        for oc in range(1, C):
            remote(part, part, r.x_rc.at[m], r.rc.at[m], cpeer(oc)).start()

    def share_sum(m):
        got(r.FG.at[m, pl.ds(0, (C - 1) * s.pr), here], r.rc.at[m])
        part = r.FG.at[m, :, here]
        remote(part, part, r.x_rd.at[m], r.rd.at[m], sib).start()

    normed_grad = (
        dot_rt(r.dq[...], r.wfull[0]) + dot_rt(r.dk[...], r.wfull[1]) + dot_rt(r.dv[...], r.wfull[2])
    )
    plane_sum(0, r.nT, r.dq)
    shard_sum(3)
    x = r.xb[...].astype(F32)
    along = normed_grad * r.rows[0:1, :]
    r.mg[...] = (
        r.mg[...]
        + scale1 * along
        - x * (scale1 * scale1 * scale1 * jnp.mean(along * x, axis=1, keepdims=True))
    )
    r.rows[3:4, :] = jnp.sum(normed_grad * x * scale1, axis=0, keepdims=True)
    save_tokens = pltpu.make_async_copy(r.mg, r.tokens_grad, r.osem.at[0])
    save_tokens.start()
    r.bt[...] = jnp.zeros_like(r.bt)
    mirror = (iota((T, T), 0) + iota((T, T), 1) == T - 1).astype(F32).astype(BF)

    def bias_back(h, carry):
        mirrored = dot(r.probs[h].astype(BF), mirror)
        wide = jnp.concatenate([mirrored, jnp.zeros((T, T), F32)], axis=1)
        turned = pltpu.roll(wide, 0, 1, stride=1, stride_axis=0)
        r.bt[pl.ds(REL_LANE + h, 1), :] = jnp.sum(turned, axis=0, keepdims=True)
        return carry

    lax.fori_loop(0, s.H, bias_back, 0)
    plane_sum(1, r.nT, r.dk)
    shard_sum(2)
    plane_fold(0)
    high, rest = two_parts(r.bt[...])
    rel_grad = dot_rt(r.ohm[...], high) + dot_rt(r.ohm[...], rest)
    lane_col = iota((LANES, 1), 0)
    small = jnp.where(
        lane_col == GAIN_ATTN_LANE,
        r.rows[3:4, :],
        jnp.where(lane_col == GAIN_FFN_LANE, r.rows[2:3, :], router_grad),
    ).T
    blocks = []
    for block in range(W):
        part = small[block * s.SR : (block + 1) * s.SR]
        head = part[: s.NBP] + rel_grad[block * s.NBP : (block + 1) * s.NBP]
        blocks.append(jnp.concatenate([head, part[s.NBP :]], axis=0))
    small = jnp.concatenate(blocks, axis=0).astype(BF)
    r.smo[...] = spread_rows(small)
    remote(r.smo, r.sms, r.x_rd.at[4], r.rd.at[4], sib).start()
    spread(3)
    got(r.sms, r.rd.at[4])
    pair = (r.smo[...].astype(F32) + r.sms[...].astype(F32)).astype(BF)
    for block in range(W):
        for chip in range(C):
            at = block * s.CP + chip * s.pr
            r.hGS[chip, block * s.pr : (block + 1) * s.pr, :] = pair[at : at + s.pr]
    for oc in range(1, C):
        remote(r.hGS.at[flip(c, oc)], r.hGR.at[oc - 1], r.x_ra.at[4], r.ra.at[4], cpeer(oc)).start()
    line_sent(r.Gr, r.x_gu, r.x_gd)
    for o in range(1, W):
        got(r.Qr.at[0], r.t2.at[o])

    def scale_rows(step, carry):
        at = pl.ds(aligned(step * R, 16), R)
        gates = jnp.sum(jnp.where(diagonal, r.Qr[step, 0:1, :], 0.0), axis=1, keepdims=True)
        r.Gr[at, :] = (r.Gr[at, :].astype(F32) * gates).astype(BF)
        r.ig[at, :] = (r.ig[at, :].astype(F32) * gates).astype(BF)
        return carry

    lax.fori_loop(0, W, scale_rows, 0)
    tile, slots = s.tile, s.slots

    def save_out(step):
        slot = lax.rem(step, slots)
        at = pl.ds(aligned(step * tile, LANES), tile)
        return pltpu.make_async_copy(r.gwo.at[slot], r.grad_w_out.at[at], r.gwo_sem.at[slot])

    def save_in(step):
        slot = lax.rem(step, slots)
        at = pl.ds(aligned(step * tile, LANES), tile)
        return pltpu.make_async_copy(r.gwi.at[slot], r.grad_w_in.at[at], r.gwi_sem.at[slot])

    def grad_out_tile(step, carry):
        @pl.when(step >= slots)
        def _():
            save_out(step - slots).wait()

        at = pl.ds(aligned(step * tile, LANES), tile)
        r.gwo[lax.rem(step, slots)] = dot_lt(r.act[:, at], r.Gr[...]).astype(BF)
        save_out(step).start()
        return carry

    def grad_in_tile(step, carry):
        @pl.when(step >= slots)
        def _():
            save_in(step - slots).wait()

        at = pl.ds(aligned(step * tile, LANES), tile)
        r.gwi[lax.rem(step, slots)] = dot_lt(r.Nr[:, at], r.ig[...]).astype(BF)
        save_in(step).start()
        return carry


    plane_fold(1)
    lax.fori_loop(0, s.F // tile, grad_out_tile, 0)
    shard_sum(0)
    spread(2)
    share_sum(3)
    lax.fori_loop(0, D // tile, grad_in_tile, 0)
    shard_sum(1)
    spread(0)
    share_sum(2)
    for step in passes:
        results_pass(step)
    pl.when(z < W - 1)(functools.partial(result_merge, z, z, r.rdn.at[0]))
    pl.when(z > 0)(functools.partial(result_merge, z, z + 1, r.ru.at[0]))
    r.Rb[...] = RS[z].astype(s.dt)
    plane_back(1, r.Rb, r.Rk, range(E))

    got(r.hGR, r.ra.at[4])
    total = r.hGS[c].astype(F32)
    for oc in range(1, C):
        total = total + r.hGR[oc - 1].astype(F32)
    r.hZS[...] = total.astype(BF)
    for o in range(1, W):
        remote(
            r.hZS.at[pl.ds(aligned(flip(z, o) * s.pr, 16), s.pr)],
            r.hZR.at[o - 1],
            r.x_rb.at[4],
            r.rb.at[4],
            zpeer(o),
        ).start()
    spread(1)
    share_sum(0)
    got(r.hZR, r.rb.at[4])
    total = r.hZS[pl.ds(aligned(z * s.pr, 16), s.pr), :].astype(F32)
    for o in range(1, W):
        total = total + r.hZR[o - 1].astype(F32)
    mine = pl.ds(aligned(c * s.pr, 16), s.pr)
    r.hFG[mine, :] = total.astype(BF)
    for oc in range(1, C):
        part = r.hFG.at[mine]
        remote(part, part, r.x_rc.at[4], r.rc.at[4], cpeer(oc)).start()

    got(r.Rk.at[pl.ds(0, (E - 1) * cp)], r.back.at[1])
    r.nf[...] = (r.middle[...] + gate * dot(r.pt[...], r.Rk[...].astype(BF))).astype(BF)
    save_layer = pltpu.make_async_copy(r.nf, r.layer_out, r.osem.at[1])
    save_layer.start()

    share_sum(1)
    got(r.hFG.at[pl.ds(0, (C - 1) * s.pr)], r.rc.at[4])

    def unpad(value):
        return dot(r.unsel[...], value) if s.padded else value.astype(F32)

    r.smallest[...] = unpad(r.hFG[...])
    saves = [save_tokens, save_layer, pltpu.make_async_copy(r.smallest, r.smalls, r.osem.at[2])]
    saves[-1].start()
    for m in (3, 2, 0, 1):
        got(r.FG.at[m, :, there], r.rd.at[m])
        complete = r.FG.at[m]
        if s.padded:
            r.unpadded[m] = unpad(r.FG[m]).astype(BF)
            complete = r.unpadded.at[m]
        saves.append(pltpu.make_async_copy(complete, r.grads.at[m], r.osem.at[3 + m]))
        saves[-1].start()

    for save in saves:
        save.wait()
    for step in range(max(0, s.F // tile - slots), s.F // tile):
        save_out(step).wait()
    for step in range(max(0, D // tile - slots), D // tile):
        save_in(step).wait()
    sent(r.smg.at[pl.ds(0, W - 1)], r.x_sm)
    for m in range(4):
        part = r.wfull.at[m, pl.ds(0, s.pw), here]
        for d in range(W - 1):
            pl.when((z >= d) & (z < W - 1))(functools.partial(sent, part, r.x_wu.at[m, d]))
            pl.when((z + d <= W - 1) & (z > 0))(functools.partial(sent, part, r.x_wd.at[m, d]))
        if s.team > 1:
            sent(r.wfull.at[m, pl.ds(0, (W - 1) * (s.team - 1) * s.pw), here], r.x_wb.at[m])
        sent(r.wfull.at[m, others, here], r.x_wc.at[m])
        sent(r.fac.at[m], r.x_sibF.at[m])
        if two_step:
            for side in range(2):
                sent(r.GX.at[m, side], r.x_gx.at[m, side])
                sent(r.GY.at[m, row_sides[side]], r.x_gy.at[m, side])
        else:
            sent(r.GR.at[m], r.x_ra.at[m])
        sent(r.ZR.at[m], r.x_rb.at[m])
        sent(r.FG.at[m, pl.ds(0, (C - 1) * s.pr), here], r.x_rc.at[m])
        sent(r.FG.at[m, :, here], r.x_rd.at[m])
    sent(r.Qk.at[pl.ds(0, E - 1)], r.x_t1)
    for index, buffer in enumerate((r.gsend, r.nsend)):
        sent(buffer.at[pl.ds(0, E - 1)], r.x_d1.at[index])
    line_sent(r.Nr, r.x_nu, r.x_nd)
    sent(r.Qr.at[pl.ds(0, W - 1)], r.x_t2)
    for d in range(1, W):
        if early:
            pl.when(z >= d)(functools.partial(sent, r.SS.at[0], r.x_sd.at[d]))
            pl.when(z + d <= W - 1)(functools.partial(sent, r.SS.at[0], r.x_su.at[d]))
        pl.when(z >= d)(functools.partial(sent, r.SS.at[0], r.x_rdn.at[d]))
        pl.when(z + d <= W - 1)(functools.partial(sent, r.SS.at[0], r.x_ru.at[d]))
    for plane in range(W):
        pl.when(z != plane)(functools.partial(sent, r.HS.at[0], r.x_hz.at[plane]))
    sent(r.Hk.at[pl.ds(0, E - 1)], r.x_hp)
    sent(r.Sk.at[pl.ds(0, (E - 1) * cp)], r.x_back.at[0])
    sent(r.Rk.at[pl.ds(0, (E - 1) * cp)], r.x_back.at[1])
    sent(r.nT.at[:, pl.ds(0, T)], r.x_sibT.at[0])
    sent(r.mT.at[:, pl.ds(0, T)], r.x_sibT.at[1])
    sent(r.hGR, r.x_ra.at[4])
    sent(r.hZR, r.x_rb.at[4])
    sent(r.hFG.at[pl.ds(0, (C - 1) * s.pr)], r.x_rc.at[4])
    sent(r.smo, r.x_rd.at[4])


def selection(s):
    share = s.SR // s.C
    unsel = np.zeros((s.SR, s.CP), np.float32)
    for chip in range(s.C):
        for at in range(share):
            unsel[chip * share + at, chip * s.pr + at] = 1
    return jnp.asarray(unsel, BF)


PARTS = 3


def finish(s, *refs):
    layer_out, tokens_grad, grads, smalls, grad_in, grad_out = refs[:6]
    out_layer, out_tokens, *out_mixers = refs[6:12]
    out_in, out_out, out_gain1, out_gain2, out_rel, out_router = refs[12:18]
    low_mix, low_in, low_out, mix, into, outof, held_layer, held_tokens = refs[18:26]
    pass_sem, load_sem, save_sem, load2, save2 = refs[26:]
    through = (
        (layer_out, held_layer, out_layer),
        (tokens_grad, held_tokens, out_tokens),
    )
    loads = [
        pltpu.make_async_copy(source, held, pass_sem.at[0, index])
        for index, (source, held, _) in enumerate(through)
    ]
    saves = [
        pltpu.make_async_copy(held, target, pass_sem.at[1, index])
        for index, (_, held, target) in enumerate(through)
    ]
    for m in range(4):
        loads.append(pltpu.make_async_copy(grads.at[m], low_mix.at[m], load_sem.at[m]))
        saves.append(pltpu.make_async_copy(mix.at[m], out_mixers[m], save_sem.at[m]))
    steps = [None, None] + [(low_mix, mix, m) for m in range(4)]
    for index, (source, low, high, target) in enumerate(
        ((grad_in, low_in, into, out_in), (grad_out, low_out, outof, out_out))
    ):
        rows = source.shape[0] // PARTS
        for part in range(PARTS):
            at = pl.ds(part * rows, rows)
            loads.append(
                pltpu.make_async_copy(source.at[at], low.at[at], load2.at[index, part])
            )
            saves.append(
                pltpu.make_async_copy(high.at[at], target.at[0, at], save2.at[index, part])
            )
            steps.append((low, high, at))
    order = [6, 9, 7, 10, 8, 11, 2, 3, 4, 5, 1, 0]
    loads, saves, steps = ([items[at] for at in order] for items in (loads, saves, steps))
    for copy in loads:
        copy.start()
    turned = smalls[...].T
    out_router[...] = turned[: s.NX]
    out_gain1[...] = turned[GAIN_ATTN_LANE : GAIN_ATTN_LANE + 1]
    out_gain2[...] = turned[GAIN_FFN_LANE : GAIN_FFN_LANE + 1]
    out_rel[...] = smalls[: s.NBH, REL_LANE : REL_LANE + s.H]
    for load, save, step in zip(loads, saves, steps, strict=True):
        load.wait()
        if step is not None:
            low, high, at = step
            high[at] = low[at].astype(F32)
        save.start()
    for copy in saves:
        copy.wait()


def local(
    tokens,
    norm_gain_attn,
    w_query,
    w_key,
    w_value,
    w_output,
    rel_bias,
    norm_gain_ffn,
    w_router,
    w_in,
    w_out,
    out_grad,
    expert_ids,
    priority,
    lengths,
    seq_order,
    relpos_table,
):
    tok_count, width = tokens.shape
    buckets_here, heads = rel_bias.shape
    n_experts = w_router.shape[1]
    s = plan(
        lax.axis_size("expert"),
        lax.axis_size("wshard"),
        tok_count,
        width,
        heads,
        buckets_here,
        n_experts,
        w_in.shape[2],
    )
    operands = [
        lengths, seq_order, expert_ids.reshape(1, tok_count), priority.reshape(1, tok_count),
        relpos_table.reshape(1, -1), w_router.T, norm_gain_attn,
        norm_gain_ffn, rel_bias,
        tokens, out_grad, w_query, w_key, w_value, w_output, w_in, w_out,
    ]
    smem, vmem, anywhere = (
        pl.BlockSpec(memory_space=space) for space in (pltpu.SMEM, pltpu.VMEM, pl.ANY)
    )
    in_specs = [smem] * 2 + [vmem] * 7 + [anywhere] * 8
    names = IN_NAMES
    if s.padded:
        operands.append(selection(s))
        in_specs.append(vmem)
        names = names + PAD_NAMES
    spilled = (jax.ShapeDtypeStruct(pieces_shape(s), BF),) if s.padded else ()
    scratch = scratch_list(s)
    names = names + OUT_NAMES + ("GR",) * len(spilled) + tuple(name for name, _ in scratch)
    outs = pl.pallas_call(
        functools.partial(kernel, s, names),
        name="layer",
        out_shape=(
            jax.ShapeDtypeStruct((s.T, s.D), BF),
            jax.ShapeDtypeStruct((s.T, s.D), F32),
            jax.ShapeDtypeStruct((4, s.SR, s.D), BF),
            jax.ShapeDtypeStruct((s.SR, LANES), F32),
            jax.ShapeDtypeStruct((s.D, s.F), BF),
            jax.ShapeDtypeStruct((s.F, s.D), BF),
            *spilled,
        ),
        in_specs=in_specs,
        out_specs=(anywhere,) * (6 + len(spilled)),
        scratch_shapes=[shape for _, shape in scratch],
        compiler_params=pltpu.CompilerParams(
            collective_id=0, has_side_effects=True, vmem_limit_bytes=62 * 2**20
        ),
    )(*operands)
    done = pl.pallas_call(
        functools.partial(finish, s),
        name="finish",
        out_shape=(
            jax.ShapeDtypeStruct((s.T, s.D), BF),
            jax.ShapeDtypeStruct((s.T, s.D), F32),
            *[jax.ShapeDtypeStruct((s.SR, s.D), F32)] * 4,
            jax.ShapeDtypeStruct((1, s.D, s.F), F32),
            jax.ShapeDtypeStruct((1, s.F, s.D), F32),
            jax.ShapeDtypeStruct((1, s.SR), F32),
            jax.ShapeDtypeStruct((1, s.SR), F32),
            jax.ShapeDtypeStruct((buckets_here, heads), F32),
            jax.ShapeDtypeStruct((n_experts, s.SR), F32),
        ),
        in_specs=[anywhere, anywhere, anywhere, vmem, anywhere, anywhere],
        out_specs=(anywhere,) * 8 + (vmem,) * 4,
        scratch_shapes=[
            pltpu.VMEM((4, s.SR, s.D), BF),
            pltpu.VMEM((s.D, s.F), BF),
            pltpu.VMEM((s.F, s.D), BF),
            pltpu.VMEM((4, s.SR, s.D), F32),
            pltpu.VMEM((s.D, s.F), F32),
            pltpu.VMEM((s.F, s.D), F32),
            pltpu.VMEM((s.T, s.D), BF),
            pltpu.VMEM((s.T, s.D), F32),
            pltpu.SemaphoreType.DMA((2, 2)),
            pltpu.SemaphoreType.DMA((4,)),
            pltpu.SemaphoreType.DMA((4,)),
            pltpu.SemaphoreType.DMA((2, PARTS)),
            pltpu.SemaphoreType.DMA((2, PARTS)),
        ],
        compiler_params=pltpu.CompilerParams(vmem_limit_bytes=62 * 2**20),
    )(*outs[:6])
    layer_out, tokens_grad, gq, gk, gv, go, grad_w_in, grad_w_out, gain1, gain2, rel, router = done
    return (
        layer_out,
        tokens_grad,
        gain1.reshape(s.SR),
        gq,
        gk,
        gv,
        go,
        rel,
        gain2.reshape(s.SR),
        router.T,
        grad_w_in,
        grad_w_out,
    )


def solution(mesh):
    rows = P(("expert", "wshard"), None)
    shard = P("wshard", None)
    into, outof = P("expert", None, "wshard"), P("expert", "wshard", None)
    return jax.shard_map(
        local,
        mesh=mesh,
        in_specs=(
            rows,
            P("wshard"),
            shard,
            shard,
            shard,
            shard,
            shard,
            P("wshard"),
            shard,
            into,
            outof,
            rows,
            rows,
            P(("expert", "wshard")),
            P(),
            P(),
            P(),
        ),
        out_specs=(
            rows,
            rows,
            P("wshard"),
            shard,
            shard,
            shard,
            shard,
            shard,
            P("wshard"),
            shard,
            into,
            outof,
        ),
        check_vma=False,
    )
```

```python
import functools
import types

import jax
import jax.numpy as jnp
import numpy as np
from jax import lax
from jax.experimental import pallas as pl
from jax.experimental.pallas import tpu as pltpu
from jax.sharding import PartitionSpec as P

EPSILON = 1e-06
NEG_FILL = -1e30
GELU_A = 0.79788456
GELU_B = 0.044715
LANES = 128
REL_LANE = 64
GAIN_ATTN_LANE = 126
GAIN_FFN_LANE = 127
MESH = pl.DeviceIdType.MESH
BF = jnp.bfloat16
F32 = jnp.float32
I32 = jnp.int32


def up16(count):
    return -(-count // 16) * 16


def dot(a, b):
    return jnp.dot(a, b, preferred_element_type=F32)


def dot_rt(a, b):
    return lax.dot_general(a, b, (((1,), (1,)), ((), ())), preferred_element_type=F32)


def dot_lt(a, b):
    return lax.dot_general(a, b, (((0,), (0,)), ((), ())), preferred_element_type=F32)


def iota(shape, axis):
    return lax.broadcasted_iota(I32, shape, axis)


def flip(index, offset):
    out = index
    bit = 1
    while bit <= offset:
        if offset & bit:
            out = out + bit * (1 - 2 * lax.rem(lax.div(index, bit), 2))
        bit *= 2
    return out


def aligned(value, step):
    return pl.multiple_of(value, step)


def two_parts(value):
    high = value.astype(BF)
    return high, (value - high.astype(F32)).astype(BF)


def plan(expert_size, shard_size, tok_count, width, heads, buckets_here, n_experts, hidden):
    s = types.SimpleNamespace()
    s.E, s.W = expert_size, shard_size
    s.C = expert_size // 2
    s.T, s.D, s.H = tok_count, width, heads
    s.HD = width // heads
    s.F = hidden
    s.NX = n_experts
    s.cap = tok_count // n_experts
    s.cp = s.cap if s.cap % 8 == 0 else up16(s.cap)
    s.dt = BF if s.cp % 16 == 0 else F32
    s.S = n_experts * s.cp
    s.R = s.E * s.cp
    s.SR = width // shard_size
    s.NBH = buckets_here
    s.NBP = up16(buckets_here)
    s.half = width // 2
    s.P1 = up16(n_experts + 2)
    s.LW = -(-s.SR // LANES) * LANES
    team = s.C
    while s.SR % team or (s.SR // team) % 16:
        team //= 2
    s.team = team
    s.pw = s.SR // team
    s.pr = up16(s.SR // s.C)
    s.CP = s.C * s.pr
    s.Dp = s.W * s.CP
    s.padded = s.CP != s.SR
    s.tile = 2 * LANES if hidden % (2 * LANES) == 0 and width % (2 * LANES) == 0 else LANES
    s.slots = 2 if s.padded else max(width, hidden) // s.tile
    return s


def pieces_shape(s):
    return (4, s.C - 1, s.W * s.pr, s.half)


def arrivals(s):
    return (("Ga", s.D), ("Na", s.D)) if s.dt == F32 else ()


def scratch_list(s):
    V = pltpu.VMEM
    dma = pltpu.SemaphoreType.DMA
    return [
        ("wfull", V((4, s.D, s.D), BF)),
        ("smf", V((s.P1 + s.NBP, s.LW), F32)),
        ("smg", V((s.W, s.P1 + s.NBP, s.LW), BF)),
        ("tab", V((8, 2 * s.T), I32)),
        ("xb", V((s.T, s.D), BF)),
        ("og", V((s.T, s.D), BF)),
        ("wi", V((s.D, s.F), BF)),
        ("wo", V((s.F, s.D), BF)),
        ("pm", V((s.S, s.T), BF)),
        ("pt", V((s.T, s.S), BF)),
        ("gsend", V((s.NX, s.cp, s.D), s.dt)),
        ("nsend", V((s.NX, s.cp, s.D), s.dt)),
        ("Qs", V((8, s.S), F32)),
        ("Qk", V((s.E, 8, s.S), F32)),
        ("Qr", V((s.W, 8, s.R), F32)),
        ("Gr", V((s.W * s.R, s.D), BF)),
        ("Nr", V((s.W * s.R, s.D), BF)),
        ("agr", V((s.W * s.R, s.F), BF)),
        ("act", V((s.W * s.R, s.F), BF)),
        ("ig", V((s.W * s.R, s.F), BF)),
        ("SS", V((s.W, s.R, s.D), BF)),
        ("Sin", V((s.W + 1, s.R, s.D), BF)),
        ("Sb", V((s.R, s.D), s.dt)),
        ("Sk", V((s.S, s.D), s.dt)),
        ("HS", V((s.W, 8, s.R), F32)),
        ("Hr", V((s.W, 8, s.R), F32)),
        ("Hb", V((8, s.R), F32)),
        ("Hk", V((s.E, 8, s.R), F32)),
        ("Hm", V((LANES, s.R), F32)),
        ("Rb", V((s.R, s.D), s.dt)),
        ("Rk", V((s.S, s.D), s.dt)),
        ("tb", V((LANES, 2 * s.T), F32)),
        ("ohm", V((s.W * s.NBP, 2 * s.T), BF)),
        ("rows", V((8, s.D), F32)),
        ("RwT", V((LANES, s.D), BF)),
        ("probs", V((s.H, s.T, s.T), F32)),
        ("q", V((s.T, s.D), BF)),
        ("kk", V((s.T, s.D), BF)),
        ("v", V((s.T, s.D), BF)),
        ("mixed", V((s.T, s.D), BF)),
        ("nf", V((s.T, s.D), BF)),
        ("middle", V((s.T, s.D), F32)),
        ("mg", V((s.T, s.D), F32)),
        ("att", V((s.T, s.D), BF)),
        ("dq", V((s.T, s.D), BF)),
        ("dk", V((s.T, s.D), BF)),
        ("dv", V((s.T, s.D), BF)),
        ("nT", V((s.Dp, 2 * s.T), BF)),
        ("mT", V((s.Dp, 2 * s.T), BF)),
        ("fac", V((4, s.T, s.half), BF)),
        ("GS", V((4, s.C, s.W * s.pr, s.half), BF)),
        ("ZS", V((4, s.W * s.pr, s.half), BF)),
        ("ZR", V((4, s.W - 1, s.pr, s.half), BF)),
        ("FG", V((4, s.CP, s.D), BF)),
        ("smo", V((s.Dp, LANES), BF)),
        ("sms", V((s.Dp, LANES), BF)),
        ("hGS", V((s.C, s.W * s.pr, LANES), BF)),
        ("hGR", V((s.C - 1, s.W * s.pr, LANES), BF)),
        ("hZS", V((s.W * s.pr, LANES), BF)),
        ("hZR", V((s.W - 1, s.pr, LANES), BF)),
        ("hFG", V((s.CP, LANES), BF)),
        ("bt", V((LANES, 2 * s.T), F32)),
        ("gwi", V((s.slots, s.tile, s.F), BF)),
        ("gwo", V((s.slots, s.tile, s.D), BF)),
        ("gwi_sem", dma((s.slots,))),
        ("gwo_sem", dma((s.slots,))),
        ("lsem", dma((9,))),
        ("osem", dma((7,))),
        ("smallest", V((s.SR, LANES), F32)),
        ("smr", dma((s.W,))),
        ("wu", dma((4, s.W))),
        ("wd", dma((4, s.W))),
        ("wbu", dma((4, s.W))),
        ("wbd", dma((4, s.W))),
        ("wc", dma((4,))),
        ("g1", dma((s.C,))),
        ("gu", dma((s.W, s.C))),
        ("gd", dma((s.W, s.C))),
        ("n1", dma((s.C,))),
        ("nu", dma((s.W, s.C))),
        ("nd", dma((s.W, s.C))),
        ("t1", dma),
        ("t2", dma((s.W,))),
        ("hz", dma((s.W,))),
        ("hp", dma),
        ("x_hz", dma((s.W,))),
        ("x_hp", dma),
        ("su", dma((s.W, s.C))),
        ("sd", dma((s.W, s.C))),
        ("ru", dma((s.W,))),
        ("rdn", dma((s.W,))),
        ("back", dma((2,))),
        ("sibT", dma((2,))),
        ("sibF", dma((4,))),
        ("ra", dma((5,))),
        ("rb", dma((5,))),
        ("rc", dma((5,))),
        ("rd", dma((5,))),
        ("x_sm", dma),
        ("x_wu", dma((4, s.W))),
        ("x_wd", dma((4, s.W))),
        ("x_wb", dma((4,))),
        ("x_wc", dma((4,))),
        ("x_d1", dma((2,))),
        ("x_t1", dma),
        ("x_t2", dma),
        ("x_gu", dma((s.W,))),
        ("x_gd", dma((s.W,))),
        ("x_nu", dma((s.W,))),
        ("x_nd", dma((s.W,))),
        ("x_su", dma((s.W,))),
        ("x_sd", dma((s.W,))),
        ("x_ru", dma((s.W,))),
        ("x_rdn", dma((s.W,))),
        ("x_back", dma((2,))),
        ("x_sibT", dma((2,))),
        ("x_sibF", dma((4,))),
        ("x_ra", dma((5,))),
        ("x_rb", dma((5,))),
        ("x_rc", dma((5,))),
        ("x_rd", dma((5,))),
        ("credit", pltpu.SemaphoreType.REGULAR),
    ] + (
        [("gst", V((s.W * s.pr, s.half), BF)), ("unpadded", V((4, s.SR, s.D), BF))]
        + [(name, V((s.R, width), F32)) for name, width in arrivals(s)]
        if s.padded
        else [
            ("GR", V(pieces_shape(s), BF)),
            ("GX", V((4, 2, 2, s.W * s.pr // 2, s.half), BF)),
            ("GY", V((4, s.W * s.pr, s.half), BF)),
            ("gx", dma((4, 2))),
            ("gy", dma((4, 2))),
            ("x_gx", dma((4, 2))),
            ("x_gy", dma((4, 2))),
            ("RS", V((s.W, s.R, s.D), BF)),
            ("Rin", V((s.W + 1, s.R, s.D), BF)),
        ]
    )


IN_NAMES = (
    "lengths", "seq", "ids", "prio", "table", "router", "gain_attn", "gain_ffn", "bias",
    "tokens", "out_grad", "w0", "w1", "w2", "w3", "w_in", "w_out",
)
PAD_NAMES = ("unsel",)
OUT_NAMES = ("layer_out", "tokens_grad", "grads", "smalls", "grad_w_in", "grad_w_out")


def kernel(s, names, *refs):
    r = types.SimpleNamespace(**dict(zip(names, refs, strict=True)))
    e = lax.axis_index("expert")
    z = lax.axis_index("wshard")
    c = lax.div(e, 2)
    k = lax.rem(e, 2)
    T, D, E, W, C, R, cp, half = s.T, s.D, s.E, s.W, s.C, s.R, s.cp, s.half
    sib = (flip(e, 1), z)
    here = pl.ds(aligned(k * half, LANES), half)
    there = pl.ds(aligned((1 - k) * half, LANES), half)

    def zpeer(offset):
        return (e, flip(z, offset))

    def cpeer(offset):
        return (flip(c, offset) * 2 + k, z)

    def remote(src, dst, send, recv, device):
        return pltpu.make_async_remote_copy(
            src_ref=src, dst_ref=dst, send_sem=send, recv_sem=recv, device_id=device, device_id_type=MESH
        )

    def got(ref, sem):
        remote(ref, ref, sem, sem, sib).wait_recv()

    def sent(ref, sem):
        remote(ref, ref, sem, sem, sib).wait_send()

    barrier = pltpu.get_barrier_semaphore()
    peers = [(flip(e, o), z) for o in range(1, E)] + [zpeer(o) for o in range(1, W)]
    for peer in peers:
        pl.semaphore_signal(barrier, inc=1, device_id=peer, device_id_type=MESH)

    shards = (r.w0, r.w1, r.w2, r.w3)
    own_rows = pl.ds(aligned(z * s.SR, 16), s.SR)
    load_w = [
        pltpu.make_async_copy(shards[m], r.wfull.at[m, own_rows], r.lsem.at[m])
        for m in range(4)
    ]
    load_og = pltpu.make_async_copy(r.out_grad, r.og, r.lsem.at[4])
    load_x = pltpu.make_async_copy(r.tokens, r.xb, r.lsem.at[5])
    load_wo = pltpu.make_async_copy(r.w_out.at[0], r.wo, r.lsem.at[6])
    load_wi = pltpu.make_async_copy(r.w_in.at[0], r.wi, r.lsem.at[7])
    load_og.start()

    r.smf[...] = jnp.zeros_like(r.smf)
    r.smf[0 : s.NX, 0 : s.SR] = r.router[...].astype(F32)
    r.smf[s.NX : s.NX + 1, 0 : s.SR] = r.gain_attn[...].astype(F32).reshape(1, s.SR)
    r.smf[s.NX + 1 : s.NX + 2, 0 : s.SR] = r.gain_ffn[...].astype(F32).reshape(1, s.SR)
    r.smf[s.P1 : s.P1 + s.NBH, 0 : s.H] = r.bias[...].astype(F32)
    r.smg[z] = r.smf[...].astype(BF)
    device = e * W + z
    first = r.lengths[r.seq[2 * device]]
    both = first + r.lengths[r.seq[2 * device + 1]]
    col = iota((T, 1), 0)
    row = iota((1, T), 1)
    seg_col = (col >= first).astype(I32) + (col >= both).astype(I32)
    seg_row = (row >= first).astype(I32) + (row >= both).astype(I32)
    same = seg_col == seg_row
    valid = (col < both).astype(F32)
    eye = iota((T, T), 0) == iota((T, T), 1)
    id_row = r.ids[...].astype(F32)
    id_col = jnp.sum(jnp.where(eye, id_row, 0.0), axis=1, keepdims=True)
    prio_row = r.prio[...].astype(F32)
    prio_col = jnp.sum(jnp.where(eye, prio_row, 0.0), axis=1, keepdims=True)
    ahead = (id_col == id_row) & (prio_col < prio_row)
    slot_row = jnp.sum(jnp.where(ahead, valid, 0.0), axis=0, keepdims=True)
    kept = (row < both) & (slot_row < s.cap)
    flat_row = jnp.where(kept, id_row * cp + slot_row, -1.0)
    flat_col = jnp.sum(jnp.where(eye, flat_row, 0.0), axis=1, keepdims=True)
    r.pm[...] = (iota((s.S, T), 0).astype(F32) == flat_row).astype(F32).astype(BF)
    r.pt[...] = (iota((T, s.S), 1).astype(F32) == flat_col).astype(F32).astype(BF)

    def fill(send, value):
        send[...] = dot(r.pm[...], value).astype(s.dt).reshape(send.shape)

    load_og.wait()
    fill(r.gsend, r.og[...])
    pl.semaphore_wait(barrier, len(peers))

    team_c = lax.rem(c, s.team)
    for o in range(1, W):
        remote(r.smg.at[z], r.smg.at[z], r.x_sm, r.smr.at[o], zpeer(o)).start()
    share_rows = pl.ds(aligned(team_c * s.pw, 16), s.pw)
    def weight_at(plane):
        return pl.ds(aligned(plane * s.SR + team_c * s.pw, 16), s.pw)

    def weight_own(m):
        def send(sender, receiver, to):
            source = shards[m].at[share_rows, here]
            remote(source, r.wfull.at[m, weight_at(z), here], sender, receiver, (e, to)).start()

        pl.when(z < W - 1)(functools.partial(send, r.x_wu.at[m, 0], r.wu.at[m, 1], z + 1))
        pl.when(z > 0)(functools.partial(send, r.x_wd.at[m, 0], r.wd.at[m, 1], z - 1))

    for m in range(3):
        weight_own(m)
    for copy in (load_x, *load_w, load_wo, load_wi):
        copy.start()
    plane_step = 16 if s.dt == BF else 8
    plane_rows = z * R if s.dt == BF else 0

    def dispatch(index, send, rows, first_sem, value):
        if value is not None:
            fill(send, value)
        mine = pl.ds(aligned(plane_rows + e * cp, plane_step), cp)
        for o in range(1, E):
            x = flip(e, o)
            remote(
                send.at[x], rows.at[mine], r.x_d1.at[index], first_sem.at[o // 2], (x, z)
            ).start()
        rows[mine, :] = send[e]

    def block_at(plane, oc):
        return pl.ds(aligned(plane * R + flip(c, oc) * 2 * cp, 16), 2 * cp)

    def landed(rows, arrived, first_sem, oc):
        got(arrived.at[pl.ds(0, (2 if oc else 1) * cp)], first_sem.at[oc])
        if s.dt != BF:
            rows[block_at(z, oc), :] = arrived[block_at(0, oc), :].astype(BF)

    def move(part, send, recv, to):
        remote(part, part, send, recv, (e, to)).start()

    def line_own(rows, arrived, first_sem, up, down, x_up, x_down):
        for oc in range(C):
            landed(rows, arrived, first_sem, oc)
            part = rows.at[block_at(z, oc)]
            pl.when(z < W - 1)(functools.partial(move, part, x_up.at[0], up.at[1, oc], z + 1))
            pl.when(z > 0)(functools.partial(move, part, x_down.at[0], down.at[1, oc], z - 1))

    def line_pass(rows, d, up, down, x_up, x_down):
        for oc in range(C):

            @pl.when(z >= d)
            def _():
                part = rows.at[block_at(z - d, oc)]
                got(part, up.at[d, oc])
                if d < W - 1:
                    pl.when(z < W - 1)(
                        functools.partial(move, part, x_up.at[d], up.at[d + 1, oc], z + 1)
                    )

            @pl.when(z + d <= W - 1)
            def _():
                part = rows.at[block_at(z + d, oc)]
                got(part, down.at[d, oc])
                if d < W - 1:
                    pl.when(z > 0)(
                        functools.partial(move, part, x_down.at[d], down.at[d + 1, oc], z - 1)
                    )

    def line_sent(rows, x_up, x_down):
        for d in range(W - 1):
            whole = rows.at[pl.ds(0, R)]
            pl.when((z >= d) & (z < W - 1))(functools.partial(sent, whole, x_up.at[d]))
            pl.when((z + d <= W - 1) & (z > 0))(functools.partial(sent, whole, x_down.at[d]))

    g_line = (r.gu, r.gd, r.x_gu, r.x_gd)
    n_line = (r.nu, r.nd, r.x_nu, r.x_nd)
    Ga, Na = (r.Gr, r.Nr) if s.dt == BF else (r.Ga, r.Na)
    dispatch(0, r.gsend, Ga, r.g1, None)

    def weight_pass(m, d):
        def handle(plane, arrived, onward, sender, receiver, to, beside):
            part = r.wfull.at[m, weight_at(plane), here]
            got(part, arrived)
            if d < W - 1:
                pl.when(onward)(functools.partial(move, part, sender, receiver, to))
            for oc in range(1, s.team):
                remote(part, part, r.x_wb.at[m], beside, cpeer(oc)).start()

        up, down, after = (m, d), (m, d), (m, min(d + 1, W - 1))
        pl.when(z >= d)(
            functools.partial(
                handle, z - d, r.wu.at[up], z < W - 1, r.x_wu.at[up], r.wu.at[after], z + 1, r.wbu.at[up]
            )
        )
        pl.when(z + d <= W - 1)(
            functools.partial(
                handle, z + d, r.wd.at[down], z > 0, r.x_wd.at[down], r.wd.at[after], z - 1, r.wbd.at[down]
            )
        )

    def weight_share(m, d):
        def handle(plane, beside):
            if s.team > 1:
                got(r.wfull.at[m, pl.ds(0, (s.team - 1) * s.pw), here], beside)
            part = r.wfull.at[m, pl.ds(aligned(plane * s.SR, 16), s.SR), here]
            remote(part, part, r.x_wc.at[m], r.wc.at[m], sib).start()

        pl.when(z >= d)(functools.partial(handle, z - d, r.wbu.at[m, d]))
        pl.when(z + d <= W - 1)(functools.partial(handle, z + d, r.wbd.at[m, d]))

    others = pl.ds(0, (W - 1) * s.SR)

    def weight_ready(m):
        load_w[m].wait()
        got(r.wfull.at[m, others, there], r.wc.at[m])

    for d in range(1, W):
        for m in range(3):
            weight_pass(m, d)
        if d == 1:
            weight_own(3)
        else:
            weight_pass(3, d - 1)
            for m in range(3):
                weight_share(m, d - 1)
        if d == min(2, W - 1):
            line_own(r.Gr, Ga, r.g1, *g_line)
    weight_pass(3, W - 1)
    for m in range(3):
        weight_share(m, W - 1)
    for o in range(1, W):
        got(r.smg.at[0], r.smr.at[o])
    gathered = jnp.concatenate(
        [r.smg[w, : s.P1, : s.SR].astype(F32) for w in range(W)], axis=1
    )
    r.rows[0:1, :] = gathered[s.NX : s.NX + 1]
    r.rows[1:2, :] = gathered[s.NX + 1 : s.NX + 2]
    r.RwT[...] = jnp.zeros_like(r.RwT)
    r.RwT[: s.P1, :] = jnp.where(iota((s.P1, D), 0) < s.NX, gathered, 0.0).astype(BF)
    lane_row = iota((1, LANES), 1)
    r.tab[...] = jnp.full(r.tab.shape, -1, I32)
    r.tab[0:1, 0 : 2 * T - 1] = r.table[...]
    bucket = r.tab[0:1, :]
    shift = s.NBH.bit_length() - 1
    bucket = lax.shift_right_logical(bucket, shift) * s.NBP + lax.bitwise_and(bucket, s.NBH - 1)
    bucket = jnp.where(r.tab[0:1, :] < 0, -1, bucket)
    hot = (iota((W * s.NBP, 2 * T), 0) == bucket).astype(F32).astype(BF)
    backwards = (iota((2 * T, 2 * T), 0) + iota((2 * T, 2 * T), 1) == 2 * T - 2).astype(F32)
    r.ohm[...] = dot(hot, backwards.astype(BF)).astype(BF)
    bias_rows = r.smg[:, s.P1 :, :LANES].reshape(W * s.NBP, LANES)
    r.tb[...] = dot_lt(bias_rows, hot)

    def bias_head(h, carry):
        wide = jnp.broadcast_to(r.tb[pl.ds(h, 1), :], (T, 2 * T))
        turned = pltpu.roll(wide, T + 1, 1, stride=1, stride_axis=0)
        r.probs[h] = jnp.where(same, turned[:, :T], NEG_FILL)
        return carry

    lax.fori_loop(0, s.H, bias_head, 0)
    load_x.wait()
    x = r.xb[...].astype(F32)
    scale1 = lax.rsqrt(jnp.mean(x * x, axis=1, keepdims=True) + EPSILON)
    normed = (x * scale1 * r.rows[0:1, :]).astype(BF)

    def spread_rows(value):
        if not s.padded:
            return value
        shards = [value[at : at + s.SR] for at in range(0, D, s.SR)]
        return jnp.concatenate([dot_lt(r.unsel[...], shard) for shard in shards], axis=0).astype(BF)

    def turn_out(index, value, target):
        target[:, :T] = spread_rows(value.T)
        remote(
            target.at[:, pl.ds(0, T)], target.at[:, pl.ds(T, T)], r.x_sibT.at[index], r.sibT.at[index], sib
        ).start()

    turn_out(0, normed, r.nT)
    weight_ready(0)
    r.q[...] = dot(normed, r.wfull[0]).astype(BF)
    weight_ready(1)
    r.kk[...] = dot(normed, r.wfull[1]).astype(BF)
    weight_ready(2)
    r.v[...] = dot(normed, r.wfull[2]).astype(BF)
    for d in range(1, W):
        weight_share(3, d)
    line_pass(r.Gr, 1, *g_line)

    scale = s.HD ** (-0.5)
    low_lane = (lane_row < s.HD).astype(F32)
    lane_masks = (low_lane.astype(BF), (1.0 - low_lane).astype(BF))

    def attend(p, carry):
        cols = pl.ds(aligned(p * LANES, LANES), LANES)
        q, kk, v = r.q[:, cols], r.kk[:, cols], r.v[:, cols]
        outs = []
        for side in range(2):
            h = 2 * p + side
            scores = dot_rt(q * lane_masks[side], kk) * scale + r.probs[h]
            expo = jnp.exp(scores - jnp.max(scores, axis=1, keepdims=True))
            probs = expo * (1.0 / jnp.sum(expo, axis=1, keepdims=True))
            r.probs[h] = probs
            outs.append(dot(probs.astype(BF), v))
        r.mixed[:, cols] = jnp.where(lane_row < s.HD, outs[0], outs[1]).astype(BF)
        return carry

    lax.fori_loop(0, s.H // 2, attend, 0)
    mixed = r.mixed[...]
    weight_ready(3)
    middle = r.xb[...].astype(F32) + dot(mixed, r.wfull[3]) * valid
    r.middle[...] = middle
    scale2 = lax.rsqrt(jnp.mean(middle * middle, axis=1, keepdims=True) + EPSILON)
    nf = (middle * scale2 * r.rows[1:2, :]).astype(BF)
    r.nf[...] = nf
    dispatch(1, r.nsend, Na, r.n1, nf)
    logits = jnp.where(lane_row < s.NX, dot_rt(nf, r.RwT[...]), NEG_FILL)
    raised = jnp.exp(logits - jnp.max(logits, axis=1, keepdims=True))
    router = raised / jnp.sum(raised, axis=1, keepdims=True)
    picked = (lane_row.astype(F32) == id_col).astype(F32)
    gate = jnp.sum(router * picked, axis=1, keepdims=True)
    slot_gates = jnp.sum(jnp.where(r.pt[...] > 0, gate, 0.0), axis=0, keepdims=True)
    r.Qs[...] = jnp.broadcast_to(slot_gates, r.Qs.shape)
    r.Qk[e] = r.Qs[...]
    for o in range(1, E):
        remote(r.Qs, r.Qk.at[e], r.x_t1, r.t1, (flip(e, o), z)).start()
    if W > 2:
        line_pass(r.Gr, 2, *g_line)
    line_own(r.Nr, Na, r.n1, *n_line)
    got(r.Qk.at[pl.ds(0, E - 1)], r.t1)
    repeated = jnp.concatenate(
        [jnp.broadcast_to(r.Qk[x, 0:1, :], (cp, s.S)) for x in range(E)], axis=0
    )
    wanted = e * cp + lax.rem(iota((R, s.S), 0), cp)
    gate_col = jnp.sum(
        jnp.where(iota((R, s.S), 1) == wanted, repeated, 0.0), axis=1, keepdims=True
    )
    diagonal = iota((R, R), 0) == iota((R, R), 1)
    gate_line = jnp.sum(jnp.where(diagonal, gate_col, 0.0), axis=0, keepdims=True)
    r.Qr[z] = jnp.broadcast_to(gate_line, (8, R))
    for o in range(1, W):
        remote(r.Qr.at[z], r.Qr.at[z], r.x_t2, r.t2.at[o], zpeer(o)).start()
    turn_out(1, mixed, r.mT)

    load_wo.wait()
    for d in range(3, W):
        line_pass(r.Gr, d, *g_line)

    def back_rows(step, carry):
        at = pl.ds(aligned(step * R, 16), R)
        r.agr[at, :] = dot_rt(r.Gr[at, :], r.wo[...]).astype(BF)
        return carry

    lax.fori_loop(0, W, back_rows, 0)
    load_wi.wait()

    def expert_rows(plane, at, block):
        inner = dot(r.Nr[at, :], r.wi[...])
        square = inner * inner
        tanh = jnp.tanh(GELU_A * inner * (1.0 + GELU_B * square))
        active = (0.5 * inner * (1.0 + tanh)).astype(BF)
        slope = 0.5 * (1.0 + tanh) + (0.5 * GELU_A) * inner * (1.0 - tanh * tanh) * (
            1.0 + (3.0 * GELU_B) * square
        )
        inner_grad = (r.agr[at, :].astype(F32) * slope).astype(BF)
        r.act[at, :] = active
        r.ig[at, :] = inner_grad
        r.SS[plane, block, :] = dot_rt(inner_grad, r.wi[...]).astype(BF)

    def expert(plane):
        expert_rows(plane, pl.ds(aligned(plane * R, 16), R), pl.ds(0, R))

    def gate_sums(plane, carry):
        at = pl.ds(aligned(plane * R, 16), R)
        part = jnp.sum(
            r.act[at, :].astype(F32) * r.agr[at, :].astype(F32), axis=1, keepdims=True
        )
        r.HS[plane, 0:1, :] = jnp.sum(jnp.where(diagonal, part, 0.0), axis=0, keepdims=True)

        @pl.when(plane != z)
        def _():
            remote(r.HS.at[plane], r.Hr.at[z], r.x_hz.at[plane], r.hz.at[z], (e, plane)).start()

        return carry

    def merge(plane, slot, block):
        r.SS[plane, block, :] = (
            r.SS[plane, block, :].astype(F32) + r.Sin[slot, block, :].astype(F32)
        ).astype(BF)

    def sum_down(plane, gap, oc):
        block = block_at(0, oc)
        remote(
            r.SS.at[plane, block],
            r.Sin.at[plane, block],
            r.x_sd.at[gap],
            r.sd.at[gap - 1, oc],
            (e, z - 1),
        ).start()

    def sum_up(plane, gap, oc):
        block = block_at(0, oc)
        remote(
            r.SS.at[plane, block],
            r.Sin.at[plane + 1, block],
            r.x_su.at[gap],
            r.su.at[gap - 1, oc],
            (e, z + 1),
        ).start()

    def plane_back(index, source, target, offsets):
        mine = pl.ds(aligned(e * cp, plane_step), cp)
        for o in offsets:
            if o == 0:
                target[mine, :] = source[mine, :]
                continue
            x = flip(e, o)
            remote(
                source.at[pl.ds(aligned(x * cp, plane_step), cp)],
                target.at[mine],
                r.x_back.at[index],
                r.back.at[index],
                (x, z),
            ).start()

    early = not s.padded
    RS, Rin = (r.RS, r.Rin) if early else (r.SS, r.Sin)

    def results_begin():
        if not early:
            for d in range(1, W):
                pl.when(z >= d)(functools.partial(sent, r.SS.at[0], r.x_sd.at[d]))
                pl.when(z + d <= W - 1)(functools.partial(sent, r.SS.at[0], r.x_su.at[d]))
            pl.semaphore_wait(r.credit, W - 1)

        def results(step, carry):
            at = pl.ds(aligned(step * R, 16), R)
            RS[step] = dot(r.act[at, :], r.wo[...]).astype(BF)
            return carry

        lax.fori_loop(0, W, results, 0)

    def result_merge(plane, slot, sem):
        got(Rin.at[slot], sem)
        RS[plane] = (RS[plane].astype(F32) + Rin[slot].astype(F32)).astype(BF)

    def results_pass(step):
        below = step - (W - 1 - z)
        above = W - 1 - step + z

        @pl.when((below >= 0) & (below < z))
        def _():
            @pl.when(z < W - 1)
            def _():
                result_merge(below, below, r.rdn.at[z - below])

            remote(
                RS.at[below],
                Rin.at[below],
                r.x_rdn.at[z - below],
                r.rdn.at[z - below - 1],
                (e, z - 1),
            ).start()

        @pl.when((above <= W - 1) & (above > z))
        def _():
            @pl.when(z > 0)
            def _():
                result_merge(above, above + 1, r.ru.at[above - z])

            remote(
                RS.at[above],
                Rin.at[above + 1],
                r.x_ru.at[above - z],
                r.ru.at[above - z - 1],
                (e, z + 1),
            ).start()

    passes = iter(range(W - 1))

    def next_pass():
        for step in passes:
            results_pass(step)
            break

    expert(z)
    for step in range(1, 2 * W - 2):
        if step < W - 1:
            line_pass(r.Nr, step, *n_line)

            def sides(side, carry, step=step):
                plane = z + (2 * side - 1) * step
                pl.when((plane >= 0) & (plane < W))(functools.partial(expert, plane))
                return carry

            lax.fori_loop(0, 2, sides, 0)

        if step == W - 1:
            @pl.when((z == 0) | (z == W - 1))
            def _():
                plane = W - 1 - z
                for oc in range(C):
                    at = block_at(plane, oc)
                    top = functools.partial(got, r.Nr.at[at], r.nu.at[W - 1, oc])
                    bottom = functools.partial(got, r.Nr.at[at], r.nd.at[W - 1, oc])
                    pl.when(z > 0)(top)
                    pl.when(z == 0)(bottom)
                    expert_rows(plane, at, block_at(0, oc))
                    pl.when(z > 0)(functools.partial(sum_down, plane, W - 1, oc))
                    pl.when(z == 0)(functools.partial(sum_up, plane, W - 1, oc))

        plane_down = 2 * W - 2 - z - step
        gap_down = z - plane_down
        plane_up = step - z
        gap_up = plane_up - z
        inner_down = (plane_down >= 0) & (gap_down >= 1)
        inner_up = (plane_up <= W - 1) & (gap_up >= 1)
        if step == W - 1:
            inner_down, inner_up = inner_down & (z < W - 1), inner_up & (z > 0)

        @pl.when(inner_down)
        def _():
            for oc in range(C):

                @pl.when(z < W - 1)
                def _():
                    got(r.Sin.at[plane_down, block_at(0, oc)], r.sd.at[gap_down, oc])
                    merge(plane_down, plane_down, block_at(0, oc))

                sum_down(plane_down, gap_down, oc)

        @pl.when(inner_up)
        def _():
            for oc in range(C):

                @pl.when(z > 0)
                def _():
                    got(r.Sin.at[plane_up + 1, block_at(0, oc)], r.su.at[gap_up, oc])
                    merge(plane_up, plane_up + 1, block_at(0, oc))

                sum_up(plane_up, gap_up, oc)

        if step == W - 1:
            if early:
                pass
            lax.fori_loop(0, W, gate_sums, 0)
            if early:
                results_begin()
                next_pass()

    for oc in range(C):
        block = block_at(0, oc)

        @pl.when(z < W - 1)
        def _():
            got(r.Sin.at[z, block], r.sd.at[0, oc])
            merge(z, z, block)

        @pl.when(z > 0)
        def _():
            got(r.Sin.at[z + 1, block], r.su.at[0, oc])
            merge(z, z + 1, block)

        r.Sb[block, :] = r.SS[z, block, :].astype(s.dt)
        plane_back(0, r.Sb, r.Sk, (2 * oc, 2 * oc + 1))

    total = r.HS[z]
    for o in range(1, W):
        other = flip(z, o)
        got(r.Hr.at[0], r.hz.at[other])
        total = total + r.Hr[other]
    r.Hb[...] = total
    r.Hk[e] = total
    for o in range(1, E):
        remote(r.Hb, r.Hk.at[e], r.x_hp, r.hp, (flip(e, o), z)).start()

    if not early:
        for o in range(1, W):
            pl.semaphore_signal(r.credit, inc=1, device_id=zpeer(o), device_id_type=MESH)
        results_begin()
    next_pass()
    got(r.Sk.at[pl.ds(0, (E - 1) * cp)], r.back.at[0])
    got(r.Hk.at[pl.ds(0, E - 1)], r.hp)
    r.Hm[...] = jnp.zeros_like(r.Hm)
    for x in range(E):
        r.Hm[x : x + 1, :] = r.Hk[x, 0:1, :]
    slot_col = jnp.sum(jnp.where(eye, jnp.where(kept, slot_row, -1.0), 0.0), axis=1, keepdims=True)
    slot_lane = jnp.where(slot_col < 0, -1.0, slot_col + (e * cp).astype(F32))
    chosen = (iota((T, R), 1).astype(F32) == slot_lane).astype(F32).astype(BF)
    high, rest = two_parts(r.Hm[...])
    gate_grad = jnp.sum(
        picked * (dot_rt(chosen, high) + dot_rt(chosen, rest)), axis=1, keepdims=True
    )
    returned = dot(r.pt[...], r.Sk[...].astype(BF))
    logit_grad = (gate * gate_grad * (picked - router)).astype(BF)
    nf_grad = dot(logit_grad, r.RwT[...]) + gate * returned
    middle = r.middle[...]
    along = nf_grad * r.rows[1:2, :]
    middle_grad = (
        r.og[...].astype(F32)
        + scale2 * along
        - middle * (scale2 * scale2 * scale2 * jnp.mean(along * middle, axis=1, keepdims=True))
    )
    r.mg[...] = middle_grad
    r.rows[2:3, :] = jnp.sum(nf_grad * middle * scale2, axis=0, keepdims=True)
    r.att[...] = (middle_grad * valid).astype(BF)
    attended_grad = r.att[...]

    def share(m, source):
        remote(source.at[:, there], r.fac.at[m], r.x_sibF.at[m], r.sibF.at[m], sib).start()

    share(3, r.att)
    r.mixed[...] = dot_rt(attended_grad, r.wfull[3]).astype(BF)
    router_grad = dot_lt(logit_grad, r.nf[...])
    two_step = C == 4 and not s.padded
    half_rows = W * s.pr // 2
    row_sides = (pl.ds(0, half_rows), pl.ds(half_rows, half_rows))

    def plane_sum(m, left, source):
        got(r.fac.at[m], r.sibF.at[m])

        def block(step, carry):
            at = pl.ds(aligned(step * s.CP, 16), s.CP)
            part = dot(left[at, :T], source[:, here]) + dot(left[at, T:], r.fac[m])
            part = part.astype(BF)
            for chip in range(C):
                r.GS[m, chip, pl.ds(aligned(step * s.pr, 16), s.pr), :] = part[
                    chip * s.pr : (chip + 1) * s.pr
                ]
            return carry

        lax.fori_loop(0, W, block, 0, unroll=2)
        if two_step:
            for side in range(2):
                near, far = 1 + side, 2 - side
                for slot, oc in enumerate((near, near + far)):
                    remote(
                        r.GS.at[m, flip(c, oc), row_sides[side]],
                        r.GX.at[m, side, slot],
                        r.x_gx.at[m, side],
                        r.gx.at[m, side],
                        cpeer(near),
                    ).start()
            return
        for oc in range(1, C):
            remote(
                r.GS.at[m, flip(c, oc)], r.GR.at[m, oc - 1], r.x_ra.at[m], r.ra.at[m], cpeer(oc)
            ).start()

    def plane_fold(m):
        if not two_step:
            return
        for side in range(2):
            far, rows = 2 - side, row_sides[side]
            got(r.GX.at[m, side], r.gx.at[m, side])
            for slot, chip in ((1, flip(c, far)), (0, c)):
                r.GS[m, chip, rows, :] = (
                    r.GS[m, chip, rows, :].astype(F32) + r.GX[m, side, slot].astype(F32)
                ).astype(BF)
                if slot:
                    remote(
                        r.GS.at[m, chip, rows],
                        r.GY.at[m, rows],
                        r.x_gy.at[m, side],
                        r.gy.at[m, side],
                        cpeer(far),
                    ).start()

    low_side = lane_row < s.HD

    def values_back(p, carry):
        cols = pl.ds(aligned(p * LANES, LANES), LANES)
        mixg = r.mixed[:, cols]
        outs = [dot_lt(r.probs[2 * p + side].astype(BF), mixg) for side in range(2)]
        r.dv[:, cols] = jnp.where(low_side, outs[0], outs[1]).astype(BF)
        return carry

    lax.fori_loop(0, s.H // 2, values_back, 0, unroll=2)
    share(2, r.dv)
    got(r.mT.at[:, pl.ds(T, T)], r.sibT.at[1])
    plane_sum(3, r.mT, r.att)
    got(r.nT.at[:, pl.ds(T, T)], r.sibT.at[0])
    plane_sum(2, r.nT, r.dv)

    def attend_back(p, carry):
        cols = pl.ds(aligned(p * LANES, LANES), LANES)
        q, kk, v, mixg = r.q[:, cols], r.kk[:, cols], r.v[:, cols], r.mixed[:, cols]
        outs = []
        for side in range(2):
            h = 2 * p + side
            probs = r.probs[h]
            prob_grad = dot_rt(mixg * lane_masks[side], v)
            inside = jnp.sum(probs * prob_grad, axis=1, keepdims=True)
            score_grad = (probs * (prob_grad - inside)).astype(BF)
            r.probs[h] = score_grad.astype(F32)
            outs.append((dot(score_grad, kk) * scale, dot_lt(score_grad, q) * scale))
        r.dq[:, cols] = jnp.where(low_side, outs[0][0], outs[1][0]).astype(BF)
        r.dk[:, cols] = jnp.where(low_side, outs[0][1], outs[1][1]).astype(BF)
        return carry

    lax.fori_loop(0, s.H // 2, attend_back, 0, unroll=2)
    share(0, r.dq)
    share(1, r.dk)
    plane_fold(3)
    plane_fold(2)
    next_pass()

    def shard_sum(m):
        total = r.GS[m, c].astype(F32)
        if two_step:
            for side in range(2):
                got(r.GY.at[m, row_sides[side]], r.gy.at[m, side])
            total = total + r.GY[m].astype(F32)
        else:
            got(r.GR.at[m], r.ra.at[m])
        for oc in range(1, 1 if two_step else C):
            if s.padded:
                fetch = pltpu.make_async_copy(r.GR.at[m, oc - 1], r.gst, r.lsem.at[8])
                fetch.start()
                fetch.wait()
            part = r.gst[...] if s.padded else r.GR[m, oc - 1]
            total = total + part.astype(F32)
        r.ZS[m] = total.astype(BF)
        for o in range(1, W):
            remote(
                r.ZS.at[m, pl.ds(aligned(flip(z, o) * s.pr, 16), s.pr)],
                r.ZR.at[m, o - 1],
                r.x_rb.at[m],
                r.rb.at[m],
                zpeer(o),
            ).start()

    def spread(m):
        got(r.ZR.at[m], r.rb.at[m])
        total = r.ZS[m, pl.ds(aligned(z * s.pr, 16), s.pr), :].astype(F32)
        for o in range(1, W):
            total = total + r.ZR[m, o - 1].astype(F32)
        mine = pl.ds(aligned(c * s.pr, 16), s.pr)
        r.FG[m, mine, here] = total.astype(BF)
        part = r.FG.at[m, mine, here]
        for oc in range(1, C):
            remote(part, part, r.x_rc.at[m], r.rc.at[m], cpeer(oc)).start()

    def share_sum(m):
        got(r.FG.at[m, pl.ds(0, (C - 1) * s.pr), here], r.rc.at[m])
        part = r.FG.at[m, :, here]
        remote(part, part, r.x_rd.at[m], r.rd.at[m], sib).start()

    normed_grad = (
        dot_rt(r.dq[...], r.wfull[0]) + dot_rt(r.dk[...], r.wfull[1]) + dot_rt(r.dv[...], r.wfull[2])
    )
    plane_sum(0, r.nT, r.dq)
    shard_sum(3)
    x = r.xb[...].astype(F32)
    along = normed_grad * r.rows[0:1, :]
    r.mg[...] = (
        r.mg[...]
        + scale1 * along
        - x * (scale1 * scale1 * scale1 * jnp.mean(along * x, axis=1, keepdims=True))
    )
    r.rows[3:4, :] = jnp.sum(normed_grad * x * scale1, axis=0, keepdims=True)
    save_tokens = pltpu.make_async_copy(r.mg, r.tokens_grad, r.osem.at[0])
    save_tokens.start()
    r.bt[...] = jnp.zeros_like(r.bt)
    mirror = (iota((T, T), 0) + iota((T, T), 1) == T - 1).astype(F32).astype(BF)

    def bias_back(h, carry):
        mirrored = dot(r.probs[h].astype(BF), mirror)
        wide = jnp.concatenate([mirrored, jnp.zeros((T, T), F32)], axis=1)
        turned = pltpu.roll(wide, 0, 1, stride=1, stride_axis=0)
        r.bt[pl.ds(REL_LANE + h, 1), :] = jnp.sum(turned, axis=0, keepdims=True)
        return carry

    lax.fori_loop(0, s.H, bias_back, 0)
    plane_sum(1, r.nT, r.dk)
    shard_sum(2)
    plane_fold(0)
    high, rest = two_parts(r.bt[...])
    rel_grad = dot_rt(r.ohm[...], high) + dot_rt(r.ohm[...], rest)
    lane_col = iota((LANES, 1), 0)
    small = jnp.where(
        lane_col == GAIN_ATTN_LANE,
        r.rows[3:4, :],
        jnp.where(lane_col == GAIN_FFN_LANE, r.rows[2:3, :], router_grad),
    ).T
    blocks = []
    for block in range(W):
        part = small[block * s.SR : (block + 1) * s.SR]
        head = part[: s.NBP] + rel_grad[block * s.NBP : (block + 1) * s.NBP]
        blocks.append(jnp.concatenate([head, part[s.NBP :]], axis=0))
    small = jnp.concatenate(blocks, axis=0).astype(BF)
    r.smo[...] = spread_rows(small)
    remote(r.smo, r.sms, r.x_rd.at[4], r.rd.at[4], sib).start()
    spread(3)
    got(r.sms, r.rd.at[4])
    pair = (r.smo[...].astype(F32) + r.sms[...].astype(F32)).astype(BF)
    for block in range(W):
        for chip in range(C):
            at = block * s.CP + chip * s.pr
            r.hGS[chip, block * s.pr : (block + 1) * s.pr, :] = pair[at : at + s.pr]
    for oc in range(1, C):
        remote(r.hGS.at[flip(c, oc)], r.hGR.at[oc - 1], r.x_ra.at[4], r.ra.at[4], cpeer(oc)).start()
    line_sent(r.Gr, r.x_gu, r.x_gd)
    for o in range(1, W):
        got(r.Qr.at[0], r.t2.at[o])

    def scale_rows(step, carry):
        at = pl.ds(aligned(step * R, 16), R)
        gates = jnp.sum(jnp.where(diagonal, r.Qr[step, 0:1, :], 0.0), axis=1, keepdims=True)
        r.Gr[at, :] = (r.Gr[at, :].astype(F32) * gates).astype(BF)
        r.ig[at, :] = (r.ig[at, :].astype(F32) * gates).astype(BF)
        return carry

    lax.fori_loop(0, W, scale_rows, 0)
    tile, slots = s.tile, s.slots

    def save_out(step):
        slot = lax.rem(step, slots)
        at = pl.ds(aligned(step * tile, LANES), tile)
        return pltpu.make_async_copy(r.gwo.at[slot], r.grad_w_out.at[at], r.gwo_sem.at[slot])

    def save_in(step):
        slot = lax.rem(step, slots)
        at = pl.ds(aligned(step * tile, LANES), tile)
        return pltpu.make_async_copy(r.gwi.at[slot], r.grad_w_in.at[at], r.gwi_sem.at[slot])

    def grad_out_tile(step, carry):
        @pl.when(step >= slots)
        def _():
            save_out(step - slots).wait()

        at = pl.ds(aligned(step * tile, LANES), tile)
        r.gwo[lax.rem(step, slots)] = dot_lt(r.act[:, at], r.Gr[...]).astype(BF)
        save_out(step).start()
        return carry

    def grad_in_tile(step, carry):
        @pl.when(step >= slots)
        def _():
            save_in(step - slots).wait()

        at = pl.ds(aligned(step * tile, LANES), tile)
        r.gwi[lax.rem(step, slots)] = dot_lt(r.Nr[:, at], r.ig[...]).astype(BF)
        save_in(step).start()
        return carry


    plane_fold(1)
    lax.fori_loop(0, s.F // tile, grad_out_tile, 0)
    shard_sum(0)
    spread(2)
    share_sum(3)
    lax.fori_loop(0, D // tile, grad_in_tile, 0)
    shard_sum(1)
    spread(0)
    share_sum(2)
    for step in passes:
        results_pass(step)
    pl.when(z < W - 1)(functools.partial(result_merge, z, z, r.rdn.at[0]))
    pl.when(z > 0)(functools.partial(result_merge, z, z + 1, r.ru.at[0]))
    r.Rb[...] = RS[z].astype(s.dt)
    plane_back(1, r.Rb, r.Rk, range(E))

    got(r.hGR, r.ra.at[4])
    total = r.hGS[c].astype(F32)
    for oc in range(1, C):
        total = total + r.hGR[oc - 1].astype(F32)
    r.hZS[...] = total.astype(BF)
    for o in range(1, W):
        remote(
            r.hZS.at[pl.ds(aligned(flip(z, o) * s.pr, 16), s.pr)],
            r.hZR.at[o - 1],
            r.x_rb.at[4],
            r.rb.at[4],
            zpeer(o),
        ).start()
    spread(1)
    share_sum(0)
    got(r.hZR, r.rb.at[4])
    total = r.hZS[pl.ds(aligned(z * s.pr, 16), s.pr), :].astype(F32)
    for o in range(1, W):
        total = total + r.hZR[o - 1].astype(F32)
    mine = pl.ds(aligned(c * s.pr, 16), s.pr)
    r.hFG[mine, :] = total.astype(BF)
    for oc in range(1, C):
        part = r.hFG.at[mine]
        remote(part, part, r.x_rc.at[4], r.rc.at[4], cpeer(oc)).start()

    got(r.Rk.at[pl.ds(0, (E - 1) * cp)], r.back.at[1])
    r.nf[...] = (r.middle[...] + gate * dot(r.pt[...], r.Rk[...].astype(BF))).astype(BF)
    save_layer = pltpu.make_async_copy(r.nf, r.layer_out, r.osem.at[1])
    save_layer.start()

    share_sum(1)
    got(r.hFG.at[pl.ds(0, (C - 1) * s.pr)], r.rc.at[4])

    def unpad(value):
        return dot(r.unsel[...], value) if s.padded else value.astype(F32)

    r.smallest[...] = unpad(r.hFG[...])
    saves = [save_tokens, save_layer, pltpu.make_async_copy(r.smallest, r.smalls, r.osem.at[2])]
    saves[-1].start()
    for m in (3, 2, 0, 1):
        got(r.FG.at[m, :, there], r.rd.at[m])
        complete = r.FG.at[m]
        if s.padded:
            r.unpadded[m] = unpad(r.FG[m]).astype(BF)
            complete = r.unpadded.at[m]
        saves.append(pltpu.make_async_copy(complete, r.grads.at[m], r.osem.at[3 + m]))
        saves[-1].start()

    for save in saves:
        save.wait()
    for step in range(max(0, s.F // tile - slots), s.F // tile):
        save_out(step).wait()
    for step in range(max(0, D // tile - slots), D // tile):
        save_in(step).wait()
    sent(r.smg.at[pl.ds(0, W - 1)], r.x_sm)
    for m in range(4):
        part = r.wfull.at[m, pl.ds(0, s.pw), here]
        for d in range(W - 1):
            pl.when((z >= d) & (z < W - 1))(functools.partial(sent, part, r.x_wu.at[m, d]))
            pl.when((z + d <= W - 1) & (z > 0))(functools.partial(sent, part, r.x_wd.at[m, d]))
        if s.team > 1:
            sent(r.wfull.at[m, pl.ds(0, (W - 1) * (s.team - 1) * s.pw), here], r.x_wb.at[m])
        sent(r.wfull.at[m, others, here], r.x_wc.at[m])
        sent(r.fac.at[m], r.x_sibF.at[m])
        if two_step:
            for side in range(2):
                sent(r.GX.at[m, side], r.x_gx.at[m, side])
                sent(r.GY.at[m, row_sides[side]], r.x_gy.at[m, side])
        else:
            sent(r.GR.at[m], r.x_ra.at[m])
        sent(r.ZR.at[m], r.x_rb.at[m])
        sent(r.FG.at[m, pl.ds(0, (C - 1) * s.pr), here], r.x_rc.at[m])
        sent(r.FG.at[m, :, here], r.x_rd.at[m])
    sent(r.Qk.at[pl.ds(0, E - 1)], r.x_t1)
    for index, buffer in enumerate((r.gsend, r.nsend)):
        sent(buffer.at[pl.ds(0, E - 1)], r.x_d1.at[index])
    line_sent(r.Nr, r.x_nu, r.x_nd)
    sent(r.Qr.at[pl.ds(0, W - 1)], r.x_t2)
    for d in range(1, W):
        if early:
            pl.when(z >= d)(functools.partial(sent, r.SS.at[0], r.x_sd.at[d]))
            pl.when(z + d <= W - 1)(functools.partial(sent, r.SS.at[0], r.x_su.at[d]))
        pl.when(z >= d)(functools.partial(sent, r.SS.at[0], r.x_rdn.at[d]))
        pl.when(z + d <= W - 1)(functools.partial(sent, r.SS.at[0], r.x_ru.at[d]))
    for plane in range(W):
        pl.when(z != plane)(functools.partial(sent, r.HS.at[0], r.x_hz.at[plane]))
    sent(r.Hk.at[pl.ds(0, E - 1)], r.x_hp)
    sent(r.Sk.at[pl.ds(0, (E - 1) * cp)], r.x_back.at[0])
    sent(r.Rk.at[pl.ds(0, (E - 1) * cp)], r.x_back.at[1])
    sent(r.nT.at[:, pl.ds(0, T)], r.x_sibT.at[0])
    sent(r.mT.at[:, pl.ds(0, T)], r.x_sibT.at[1])
    sent(r.hGR, r.x_ra.at[4])
    sent(r.hZR, r.x_rb.at[4])
    sent(r.hFG.at[pl.ds(0, (C - 1) * s.pr)], r.x_rc.at[4])
    sent(r.smo, r.x_rd.at[4])


def selection(s):
    share = s.SR // s.C
    unsel = np.zeros((s.SR, s.CP), np.float32)
    for chip in range(s.C):
        for at in range(share):
            unsel[chip * share + at, chip * s.pr + at] = 1
    return jnp.asarray(unsel, BF)


PARTS = 3


def finish(s, *refs):
    layer_out, tokens_grad, grads, smalls, grad_in, grad_out = refs[:6]
    out_layer, out_tokens, *out_mixers = refs[6:12]
    out_in, out_out, out_gain1, out_gain2, out_rel, out_router = refs[12:18]
    low_mix, low_in, low_out, mix, into, outof, held_layer, held_tokens = refs[18:26]
    pass_sem, load_sem, save_sem, load2, save2 = refs[26:]
    through = (
        (layer_out, held_layer, out_layer),
        (tokens_grad, held_tokens, out_tokens),
    )
    loads = [
        pltpu.make_async_copy(source, held, pass_sem.at[0, index])
        for index, (source, held, _) in enumerate(through)
    ]
    saves = [
        pltpu.make_async_copy(held, target, pass_sem.at[1, index])
        for index, (_, held, target) in enumerate(through)
    ]
    for m in range(4):
        loads.append(pltpu.make_async_copy(grads.at[m], low_mix.at[m], load_sem.at[m]))
        saves.append(pltpu.make_async_copy(mix.at[m], out_mixers[m], save_sem.at[m]))
    steps = [None, None] + [(low_mix, mix, m) for m in range(4)]
    for index, (source, low, high, target) in enumerate(
        ((grad_in, low_in, into, out_in), (grad_out, low_out, outof, out_out))
    ):
        rows = source.shape[0] // PARTS
        for part in range(PARTS):
            at = pl.ds(part * rows, rows)
            loads.append(
                pltpu.make_async_copy(source.at[at], low.at[at], load2.at[index, part])
            )
            saves.append(
                pltpu.make_async_copy(high.at[at], target.at[0, at], save2.at[index, part])
            )
            steps.append((low, high, at))
    order = [6, 9, 7, 10, 8, 11, 2, 3, 4, 5, 1, 0]
    loads, saves, steps = ([items[at] for at in order] for items in (loads, saves, steps))
    for copy in loads:
        copy.start()
    turned = smalls[...].T
    out_router[...] = turned[: s.NX]
    out_gain1[...] = turned[GAIN_ATTN_LANE : GAIN_ATTN_LANE + 1]
    out_gain2[...] = turned[GAIN_FFN_LANE : GAIN_FFN_LANE + 1]
    out_rel[...] = smalls[: s.NBH, REL_LANE : REL_LANE + s.H]
    for load, save, step in zip(loads, saves, steps, strict=True):
        load.wait()
        if step is not None:
            low, high, at = step
            high[at] = low[at].astype(F32)
        save.start()
    for copy in saves:
        copy.wait()


def local(
    tokens,
    norm_gain_attn,
    w_query,
    w_key,
    w_value,
    w_output,
    rel_bias,
    norm_gain_ffn,
    w_router,
    w_in,
    w_out,
    out_grad,
    expert_ids,
    priority,
    lengths,
    seq_order,
    relpos_table,
):
    tok_count, width = tokens.shape
    buckets_here, heads = rel_bias.shape
    n_experts = w_router.shape[1]
    s = plan(
        lax.axis_size("expert"),
        lax.axis_size("wshard"),
        tok_count,
        width,
        heads,
        buckets_here,
        n_experts,
        w_in.shape[2],
    )
    operands = [
        lengths, seq_order, expert_ids.reshape(1, tok_count), priority.reshape(1, tok_count),
        relpos_table.reshape(1, -1), w_router.T, norm_gain_attn,
        norm_gain_ffn, rel_bias,
        tokens, out_grad, w_query, w_key, w_value, w_output, w_in, w_out,
    ]
    smem, vmem, anywhere = (
        pl.BlockSpec(memory_space=space) for space in (pltpu.SMEM, pltpu.VMEM, pl.ANY)
    )
    in_specs = [smem] * 2 + [vmem] * 7 + [anywhere] * 8
    names = IN_NAMES
    if s.padded:
        operands.append(selection(s))
        in_specs.append(vmem)
        names = names + PAD_NAMES
    spilled = (jax.ShapeDtypeStruct(pieces_shape(s), BF),) if s.padded else ()
    scratch = scratch_list(s)
    names = names + OUT_NAMES + ("GR",) * len(spilled) + tuple(name for name, _ in scratch)
    outs = pl.pallas_call(
        functools.partial(kernel, s, names),
        name="layer",
        out_shape=(
            jax.ShapeDtypeStruct((s.T, s.D), BF),
            jax.ShapeDtypeStruct((s.T, s.D), F32),
            jax.ShapeDtypeStruct((4, s.SR, s.D), BF),
            jax.ShapeDtypeStruct((s.SR, LANES), F32),
            jax.ShapeDtypeStruct((s.D, s.F), BF),
            jax.ShapeDtypeStruct((s.F, s.D), BF),
            *spilled,
        ),
        in_specs=in_specs,
        out_specs=(anywhere,) * (6 + len(spilled)),
        scratch_shapes=[shape for _, shape in scratch],
        compiler_params=pltpu.CompilerParams(
            collective_id=0, has_side_effects=True, vmem_limit_bytes=62 * 2**20
        ),
    )(*operands)
    done = pl.pallas_call(
        functools.partial(finish, s),
        name="finish",
        out_shape=(
            jax.ShapeDtypeStruct((s.T, s.D), BF),
            jax.ShapeDtypeStruct((s.T, s.D), F32),
            *[jax.ShapeDtypeStruct((s.SR, s.D), F32)] * 4,
            jax.ShapeDtypeStruct((1, s.D, s.F), F32),
            jax.ShapeDtypeStruct((1, s.F, s.D), F32),
            jax.ShapeDtypeStruct((1, s.SR), F32),
            jax.ShapeDtypeStruct((1, s.SR), F32),
            jax.ShapeDtypeStruct((buckets_here, heads), F32),
            jax.ShapeDtypeStruct((n_experts, s.SR), F32),
        ),
        in_specs=[anywhere, anywhere, anywhere, vmem, anywhere, anywhere],
        out_specs=(anywhere,) * 8 + (vmem,) * 4,
        scratch_shapes=[
            pltpu.VMEM((4, s.SR, s.D), BF),
            pltpu.VMEM((s.D, s.F), BF),
            pltpu.VMEM((s.F, s.D), BF),
            pltpu.VMEM((4, s.SR, s.D), F32),
            pltpu.VMEM((s.D, s.F), F32),
            pltpu.VMEM((s.F, s.D), F32),
            pltpu.VMEM((s.T, s.D), BF),
            pltpu.VMEM((s.T, s.D), F32),
            pltpu.SemaphoreType.DMA((2, 2)),
            pltpu.SemaphoreType.DMA((4,)),
            pltpu.SemaphoreType.DMA((4,)),
            pltpu.SemaphoreType.DMA((2, PARTS)),
            pltpu.SemaphoreType.DMA((2, PARTS)),
        ],
        compiler_params=pltpu.CompilerParams(vmem_limit_bytes=62 * 2**20),
    )(*outs[:6])
    layer_out, tokens_grad, gq, gk, gv, go, grad_w_in, grad_w_out, gain1, gain2, rel, router = done
    return (
        layer_out,
        tokens_grad,
        gain1.reshape(s.SR),
        gq,
        gk,
        gv,
        go,
        rel,
        gain2.reshape(s.SR),
        router.T,
        grad_w_in,
        grad_w_out,
    )


def solution(mesh):
    rows = P(("expert", "wshard"), None)
    shard = P("wshard", None)
    into, outof = P("expert", None, "wshard"), P("expert", "wshard", None)
    return jax.shard_map(
        local,
        mesh=mesh,
        in_specs=(
            rows,
            P("wshard"),
            shard,
            shard,
            shard,
            shard,
            shard,
            P("wshard"),
            shard,
            into,
            outof,
            rows,
            rows,
            P(("expert", "wshard")),
            P(),
            P(),
            P(),
        ),
        out_specs=(
            rows,
            rows,
            P("wshard"),
            shard,
            shard,
            shard,
            shard,
            shard,
            P("wshard"),
            shard,
            into,
            outof,
        ),
        check_vma=False,
    )
```
